32 devices in a mesh: seq: 8 (over z, x), head: 4 (over y, core).
Axes of the slice: x: 2, y: 2, z: 4, core: 2. Of those that a mesh axis runs over, the one named last changes fastest.
Arguments:
- tokens: bfloat16 [4, 2048, 2048], P(None, 'seq', 'head'), may hold values from -6 to 6
- cotangent: bfloat16 [4, 2048, 2048], P(None, 'seq', 'head'), may hold values from -6 to 6
- norm_gain: float32 [2048], replicated, may hold values from 0.1 to 1.9
- gate_matrix: bfloat16 [2048, 4096], P(None, 'head'), may hold values from -0.125 to 0.125
- value_matrix: bfloat16 [2048, 4096], P(None, 'head'), may hold values from -0.125 to 0.125
- state_matrix: bfloat16 [2048, 256], replicated, may hold values from -0.125 to 0.125
- step_matrix: bfloat16 [2048, 64], P(None, 'head'), may hold values from -0.125 to 0.125
- value_kernel: float32 [4, 4096], P(None, 'head'), may hold values from -3 to 3
- value_bias: float32 [4096], P('head'), may hold values from -3 to 3
- state_kernel: float32 [4, 256], replicated, may hold values from -3 to 3
- state_bias: float32 [256], replicated, may hold values from -3 to 3
- step_bias: float32 [64], P('head'), may hold values from -9 to -2
- log_rate: float32 [64], P('head'), may hold values from -1 to 1.5
- skip_gain: float32 [64], P('head'), may hold values from 0.5 to 1.5
- gate_gain: float32 [4096], P('head'), may hold values from 0.1 to 1.9
- output_matrix: bfloat16 [4096, 2048], P('head'), may hold values from -0.09375 to 0.09375
Outputs:
- layer_out: bfloat16 [4, 2048, 2048], P(None, 'seq', 'head')
- token_grad: float32 [4, 2048, 2048], P(None, 'seq', 'head')
- norm_gain_grad: float32 [2048], P('head')
- gate_matrix_grad: float32 [2048, 4096], P('seq', 'head')
- value_matrix_grad: float32 [2048, 4096], P('seq', 'head')
- state_matrix_grad: float32 [2048, 256], P('head')
- step_matrix_grad: float32 [2048, 64], P('seq', 'head')
- value_kernel_grad: float32 [4, 4096], P(None, 'head')
- value_bias_grad: float32 [4096], P('head')
- state_kernel_grad: float32 [4, 256], replicated
- state_bias_grad: float32 [256], replicated
- step_bias_grad: float32 [64], P('head')
- log_rate_grad: float32 [64], P('head')
- skip_gain_grad: float32 [64], P('head')
- gate_gain_grad: float32 [4096], P('head')
- output_matrix_grad: float32 [4096, 2048], P('head', 'seq')
The draws below stay inside these ranges and needn't reach their ends.
All inputs are finite; a program needn't handle non-finite values.
Results may differ from the reference program's by a relative error of at most 0.012.
The reference program's roundings to bfloat16 on the way count: a program that leaves them out, or rounds other values in their place, can miss the bound.
Values may be sent and summed in bfloat16 or wider, within the bound.
A program may use at most 192 MiB of HBM per device.

```python
import jax
import jax.numpy as jnp
from jax import lax

D = 2048
HEADS = 64
HEAD_DIM = 64
STATE = 128
BLOCK = 256
CONV = 4
SEQS = 4
INNER = 4096
LENGTH = 2048
N_SEQ = 8


def block_levels(own_key, extent, shards, smallest, high):
    def one(dim, blocks):
        steps = jax.random.uniform(jax.random.fold_in(jax.random.fold_in(own_key, 6), dim), (blocks,), jnp.float32, smallest / len(shards), high / len(shards))
        return jnp.repeat(jnp.exp(steps), extent[dim] // blocks).reshape((-1,) + (1,) * (len(extent) - dim - 1))

    gain = one(*shards[0])
    for cut in shards[1:]:
        gain = gain * one(*cut)
    return gain


def centred(own_key, shape, deviation, most, cuts=(), dtype=jnp.bfloat16):
    factor_of = block_levels(own_key, shape, cuts, -0.22, 0.18) if cuts else 1.0
    entries = jax.random.normal(own_key, shape, jnp.float32) * deviation * factor_of
    return jnp.minimum(jnp.maximum(entries, -most), most).astype(dtype)


def setup_inputs(seed: int = 0) -> dict:
    key_list = jax.random.split(jax.random.key(seed), 17)
    tokens = centred(key_list[0], (SEQS, LENGTH, D), 1.0, 6.0, ((1, 8), (2, 4)))
    cotangent = centred(key_list[1], (SEQS, LENGTH, D), 1.0, 6.0, ((1, 8), (2, 4)))
    norm_gain = jnp.clip(1.0 + 0.18 * jax.random.normal(key_list[2], (D,), jnp.float32), 0.1, 1.9)
    gate_matrix = centred(key_list[3], (D, INNER), D ** -0.5, 0.125, ((1, 4),))
    value_matrix = centred(key_list[4], (D, INNER), D ** -0.5, 0.125, ((1, 4),))
    state_matrix = centred(key_list[5], (D, 2 * STATE), D ** -0.5, 0.125)
    step_matrix = centred(key_list[6], (D, HEADS), D ** -0.5, 0.125, ((1, 4),))
    value_kernel = centred(key_list[7], (CONV, INNER), 0.5, 3.0, ((1, 4),), jnp.float32)
    value_bias = centred(key_list[8], (INNER,), 0.5, 3.0, ((0, 4),), jnp.float32)
    state_kernel = centred(key_list[9], (CONV, 2 * STATE), 0.5, 3.0, (), jnp.float32)
    state_bias = centred(key_list[10], (2 * STATE,), 0.5, 3.0, (), jnp.float32)
    step_bias = jnp.clip(-9.0 + 7.0 * jax.random.uniform(key_list[11], (HEADS,), jnp.float32) ** block_levels(key_list[11], (HEADS,), ((0, 4),), -0.2, 0.2), -9.0, -2.0)
    log_rate = jnp.clip(-1.0 + 2.5 * jax.random.uniform(key_list[12], (HEADS,), jnp.float32) ** block_levels(key_list[12], (HEADS,), ((0, 4),), -0.2, 0.2), -1.0, 1.5)
    skip_gain = jnp.clip(0.5 + 1.0 * jax.random.uniform(key_list[13], (HEADS,), jnp.float32) ** block_levels(key_list[13], (HEADS,), ((0, 4),), -0.2, 0.2), 0.5, 1.5)
    gate_gain = jnp.clip(1.0 + 0.18 * jax.random.normal(key_list[14], (INNER,), jnp.float32), 0.1, 1.9)
    output_matrix = centred(key_list[15], (INNER, D), INNER ** -0.5, 0.09375, ((0, 4),))
    return dict(tokens=tokens, cotangent=cotangent, norm_gain=norm_gain, gate_matrix=gate_matrix, value_matrix=value_matrix, state_matrix=state_matrix, step_matrix=step_matrix, value_kernel=value_kernel, value_bias=value_bias, state_kernel=state_kernel, state_bias=state_bias, step_bias=step_bias, log_rate=log_rate, skip_gain=skip_gain, gate_gain=gate_gain, output_matrix=output_matrix)


HIGH = lax.Precision.HIGHEST
EPSILON = 1e-05

@jax.custom_vjp
def low(v):
    return lax.optimization_barrier(v.astype(jnp.bfloat16)).astype(jnp.float32)

@jax.custom_vjp
def low_back(v):
    return v

def low_keep(v):
    return (low(v), None)

def low_pass(kept, grad):
    return (grad,)

def back_keep(v):
    return (v, None)

def back_low(kept, grad):
    return (low(grad),)
low.defvjp(low_keep, low_pass)
low_back.defvjp(back_keep, back_low)

def causal(values, kernel, offset):
    padded = jnp.pad(values, ((CONV - 1, 0), (0, 0)))
    summed = offset + kernel[0] * padded[0:LENGTH]
    for tap_index in range(1, CONV):
        summed = summed + kernel[tap_index] * padded[tap_index:tap_index + LENGTH]
    return summed

def block_step(incoming, pieces):
    values, in_basis, out_basis, step_size, decay_log = pieces
    cumulative = jnp.cumsum(decay_log, axis=0)
    final = cumulative[-1]
    scores = jnp.dot(out_basis, in_basis.T, precision=HIGH)
    lower = jnp.arange(BLOCK)[:, None] >= jnp.arange(BLOCK)[None, :]
    lower = lower[None]
    gap = cumulative.T[:, :, None] - cumulative.T[:, None, :]
    decay = jnp.where(lower, jnp.exp(jnp.where(lower, gap, 0.0)), 0.0)
    weights = low(scores[None] * decay * step_size.T[:, None, :])
    heads_x = values.reshape(BLOCK, HEADS, HEAD_DIM)
    intra = jnp.einsum('htr,rhp->thp', weights, heads_x, precision=HIGH)
    inner_v = low_back(jnp.einsum('tn,hpn->thp', out_basis, low(incoming), precision=HIGH))
    inter = jnp.exp(cumulative)[:, :, None] * inner_v
    factor = jnp.exp(final[None, :] - cumulative) * step_size
    scaled_x = low(heads_x * factor[:, :, None])
    local_state = low_back(jnp.einsum('rhp,rn->hpn', scaled_x, in_basis, precision=HIGH))
    leaving = jnp.exp(final)[:, None, None] * incoming + local_state
    return (leaving, intra + inter)

def blocks(value):
    return value.reshape((N_SEQ, BLOCK) + value.shape[1:])

def block_forward(tokens, norm_gain, gate_matrix, value_matrix, state_matrix, step_matrix, value_kernel, value_bias, state_kernel, state_bias, step_bias, log_rate, skip_gain, gate_gain, output_matrix):
    rstd = lax.rsqrt(lax.optimization_barrier(jnp.mean(tokens * tokens, axis=-1, keepdims=True)) + EPSILON)
    normal_in = low(tokens * rstd * norm_gain)
    gate_pre = low_back(jnp.dot(normal_in, gate_matrix, precision=HIGH))
    value_pre = low_back(jnp.dot(normal_in, value_matrix, precision=HIGH))
    state_pre = low_back(jnp.dot(normal_in, state_matrix, precision=HIGH))
    step_pre = low_back(jnp.dot(normal_in, step_matrix, precision=HIGH))
    values = low(jax.nn.silu(causal(value_pre, value_kernel, value_bias)))
    basis = low(jax.nn.silu(causal(state_pre, state_kernel, state_bias)))
    step_size = jax.nn.softplus(step_pre + step_bias)
    decay_log = step_size * -jnp.exp(log_rate)
    start = jnp.zeros((HEADS, HEAD_DIM, STATE), jnp.float32)
    leaving, mixed = lax.scan(jax.checkpoint(block_step), start, (blocks(values), blocks(basis[:, :STATE]), blocks(basis[:, STATE:]), blocks(step_size), blocks(decay_log)))
    heads_x = values.reshape(LENGTH, HEADS, HEAD_DIM)
    mixed = mixed.reshape(LENGTH, HEADS, HEAD_DIM) + skip_gain[None, :, None] * heads_x
    output_y = low_back(mixed.reshape(LENGTH, INNER))
    gated = output_y * jax.nn.silu(gate_pre)
    grstd = lax.rsqrt(lax.optimization_barrier(jnp.mean(gated * gated, axis=-1, keepdims=True)) + EPSILON)
    normed = low(gated * grstd * gate_gain)
    return tokens + jnp.dot(normed, output_matrix, precision=HIGH)

def reference(tokens, cotangent, norm_gain, gate_matrix, value_matrix, state_matrix, step_matrix, value_kernel, value_bias, state_kernel, state_bias, step_bias, log_rate, skip_gain, gate_gain, output_matrix):
    params = tuple((item.astype(jnp.float32) for item in (norm_gain, gate_matrix, value_matrix, state_matrix, step_matrix, value_kernel, value_bias, state_kernel, state_bias, step_bias, log_rate, skip_gain, gate_gain, output_matrix)))

    def one_sequence(totals, paired):
        result, pullback = jax.vjp(block_forward, paired[0].astype(jnp.float32), *params)
        grads = pullback(paired[1].astype(jnp.float32))
        totals = tuple((first + second for first, second in zip(totals, grads[1:])))
        return (totals, (result.astype(jnp.bfloat16), grads[0]))
    zeros = tuple((jnp.zeros_like(item) for item in params))
    totals, (layer_out, token_grad) = lax.scan(one_sequence, zeros, (tokens, cotangent))
    return (layer_out, token_grad, totals[0], totals[1], totals[2], totals[3], totals[4], totals[5], totals[6], totals[7], totals[8], totals[9], totals[10], totals[11], totals[12], totals[13])
```

```python
import jax
import jax.numpy as jnp
from jax import lax
from jax.sharding import PartitionSpec as P

HIGH = lax.Precision.HIGHEST
EPSILON = 1e-05


def shifted(block, axis, distance):
    devices = range(lax.axis_size(axis))
    route = [(i - distance, i) for i in devices if i - distance in devices]
    return lax.ppermute(block, axis, route)


def regroup(block):
    members = block.shape[0]
    count = lax.axis_size("seq")
    groups = [list(range(i, i + members)) for i in range(0, count, members)]
    return lax.all_to_all(block, "seq", 0, 0, axis_index_groups=groups, tiled=True)


def carried(part, decay, hops, distance):
    carry = jnp.zeros_like(part)
    for _ in range(hops):
        leaving = (decay[..., None, None] * carry + part).astype(jnp.bfloat16)
        carry = shifted(leaving, "seq", distance).astype(jnp.float32)
    return carry


def silu_slope(value):
    sigma = jax.nn.sigmoid(value)
    return sigma * (1.0 + value * (1.0 - sigma))


def depthwise(padded, kernel, offset, length):
    summed = offset + kernel[0] * padded[:, 0:length]
    for tap_index in range(1, kernel.shape[0]):
        summed = summed + kernel[tap_index] * padded[:, tap_index : tap_index + length]
    return summed


def depthwise_back(extended, kernel, length):
    margin = kernel.shape[0] - 1
    summed = kernel[0] * extended[:, margin : margin + length]
    for tap_index in range(1, kernel.shape[0]):
        summed = (
            summed
            + kernel[tap_index] * extended[:, margin - tap_index : margin - tap_index + length]
        )
    return summed


def kernel_sums(padded, pre_grad, length, taps):
    return jnp.stack(
        [
            jnp.sum(pre_grad * padded[:, tap_index : tap_index + length], axis=(0, 1))
            for tap_index in range(taps)
        ]
    )


def back_product(grad_rows, matrix):
    return jnp.einsum("rc,dc->rd", grad_rows, matrix, preferred_element_type=jnp.float32)


def row_product(rows_in, grad_rows):
    return jnp.einsum("rd,rc->dc", rows_in, grad_rows, preferred_element_type=jnp.float32)


def summed_low(part, dim):
    low = part.astype(jnp.bfloat16)
    return lax.psum_scatter(low, "seq", scatter_dimension=dim, tiled=True).astype(jnp.float32)


def local(
    tokens,
    cotangent,
    norm_gain,
    gate_matrix,
    value_matrix,
    state_matrix,
    step_matrix,
    value_kernel,
    value_bias,
    state_kernel,
    state_bias,
    step_bias,
    log_rate,
    skip_gain,
    gate_gain,
    output_matrix,
):
    seq_count, block_len, share = tokens.shape
    chain = lax.axis_size("seq") // seq_count
    width = gate_matrix.shape[0]
    inner_local = gate_matrix.shape[1]
    heads_local = step_bias.shape[0]
    head_width = inner_local // heads_local
    states = state_matrix.shape[1] // 2
    taps = value_kernel.shape[0]
    row_count = seq_count * block_len
    head_count = lax.axis_size("head")
    head_rank = lax.axis_index("head")
    inner_total = inner_local * head_count
    whole_in, whole_cot = (
        lax.all_gather(regroup(tokens), "head", axis=2, tiled=True),
        lax.all_gather(regroup(cotangent), "head", axis=2, tiled=True),
    )
    plain = whole_in.astype(jnp.float32)
    rstd = lax.rsqrt(jnp.mean(plain * plain, axis=-1, keepdims=True) + EPSILON)
    normal_in = (plain * rstd * norm_gain).astype(jnp.bfloat16)
    flat_in = normal_in.reshape(row_count, width)
    gate_pre = jnp.dot(flat_in, gate_matrix, preferred_element_type=jnp.float32).reshape(
        seq_count, block_len, inner_local
    )
    value_pre = jnp.dot(flat_in, value_matrix, preferred_element_type=jnp.float32).reshape(
        seq_count, block_len, inner_local
    )
    state_pre = jnp.dot(flat_in, state_matrix, preferred_element_type=jnp.float32).reshape(
        seq_count, block_len, 2 * states
    )
    step_pre = jnp.dot(flat_in, step_matrix, preferred_element_type=jnp.float32).reshape(
        seq_count, block_len, heads_local
    )
    value_flat = value_pre.reshape(1, row_count, inner_local)
    state_flat = state_pre.reshape(1, row_count, 2 * states)
    cut = row_count - taps + 1
    value_edge, state_edge = shifted((value_flat[:, cut:], state_flat[:, cut:]), "seq", seq_count)
    value_padded = jnp.concatenate([value_edge, value_flat], axis=1)
    state_padded = jnp.concatenate([state_edge, state_flat], axis=1)
    value_conv = depthwise(value_padded, value_kernel, value_bias, row_count).reshape(
        seq_count, block_len, inner_local
    )
    state_conv = depthwise(state_padded, state_kernel, state_bias, row_count).reshape(
        seq_count, block_len, 2 * states
    )
    values = jax.nn.silu(value_conv).astype(jnp.bfloat16)
    basis = jax.nn.silu(state_conv).astype(jnp.bfloat16)
    in_basis = basis[..., :states]
    out_basis = basis[..., states:]
    step_in = step_pre + step_bias
    step_size = jax.nn.softplus(step_in)
    rate = -jnp.exp(log_rate)
    cumulative = jnp.cumsum(step_size * rate, axis=1)
    final = cumulative[:, -1]
    cum_heads = jnp.transpose(cumulative, (0, 2, 1))
    step_heads = jnp.transpose(step_size, (0, 2, 1))
    lower = lax.broadcasted_iota(jnp.int32, (block_len, block_len), 0) >= lax.broadcasted_iota(
        jnp.int32, (block_len, block_len), 1
    )
    scores = jnp.einsum("stn,srn->str", out_basis, in_basis, preferred_element_type=jnp.float32)
    gap = cum_heads[:, :, :, None] - cum_heads[:, :, None, :]
    decay = jnp.where(lower, jnp.exp(jnp.where(lower, gap, 0.0)), 0.0)
    weights = (scores[:, None] * decay * step_heads[:, :, None, :]).astype(jnp.bfloat16)
    heads_x = values.reshape(seq_count, block_len, heads_local, head_width)
    heads_plain = heads_x.astype(jnp.float32)
    intra = jnp.einsum("shtr,srhp->sthp", weights, heads_x, preferred_element_type=jnp.float32)
    factor = jnp.exp(final[:, None, :] - cumulative) * step_size
    scaled_x = (heads_plain * factor[..., None]).astype(jnp.bfloat16)
    local_state = jnp.einsum(
        "srhp,srn->shpn", scaled_x, in_basis, preferred_element_type=jnp.float32
    )
    block_decay = jnp.exp(final)
    whole_decay = jnp.exp(jnp.sum(final, axis=0))
    ending = local_state[0]
    for i in range(1, seq_count):
        ending = block_decay[i][:, None, None] * ending + local_state[i]
    entering = [carried(ending, whole_decay, chain - 1, seq_count)]
    for i in range(seq_count - 1):
        entering.append(block_decay[i][:, None, None] * entering[i] + local_state[i])
    incoming = jnp.stack(entering)
    incoming_low = incoming.astype(jnp.bfloat16)
    inner_v = jnp.einsum(
        "stn,shpn->sthp", out_basis, incoming_low, preferred_element_type=jnp.float32
    )
    growth = jnp.exp(cumulative)[..., None]
    mixed = intra + growth * inner_v + skip_gain[:, None] * heads_plain
    mixed = mixed.reshape(seq_count, block_len, inner_local)
    gate_act = jax.nn.silu(gate_pre)
    gated = mixed * gate_act
    flat_cot = whole_cot.reshape(row_count, width)
    normed_grad = back_product(flat_cot, output_matrix).reshape(seq_count, block_len, inner_local)
    gained = normed_grad * gate_gain
    square_sum, cross_sum = lax.psum(
        jnp.stack([jnp.sum(gated * gated, axis=-1), jnp.sum(gained * gated, axis=-1)]), "head"
    )
    grstd = lax.rsqrt(square_sum / inner_total + EPSILON)[..., None]
    normed = (gated * grstd * gate_gain).astype(jnp.bfloat16)
    flat_normed = normed.reshape(row_count, inner_local)
    partial_value = jnp.dot(flat_normed, output_matrix, preferred_element_type=jnp.float32).reshape(
        seq_count, block_len, width
    )
    branch = lax.psum_scatter(
        partial_value.astype(jnp.bfloat16), "head", scatter_dimension=2, tiled=True
    )
    layer_out = (tokens.astype(jnp.float32) + regroup(branch).astype(jnp.float32)).astype(
        jnp.bfloat16
    )
    output_partial = jnp.einsum(
        "ri,rd->id", flat_normed, flat_cot, preferred_element_type=jnp.float32
    )
    gate_gain_part = jnp.sum(normed_grad * gated * grstd, axis=(0, 1))
    gated_grad = (
        grstd * gained - gated * (grstd * grstd * grstd) * (cross_sum / inner_total)[..., None]
    )
    mixed_grad = (gated_grad * gate_act).astype(jnp.bfloat16)
    gate_grad_low = (gated_grad * mixed * silu_slope(gate_pre)).astype(jnp.bfloat16)
    dy_heads = mixed_grad.reshape(seq_count, block_len, heads_local, head_width)
    dy_plain = dy_heads.astype(jnp.float32)
    weight_grad = jnp.einsum(
        "sthp,srhp->shtr", dy_heads, heads_x, preferred_element_type=jnp.float32
    )
    through = weight_grad * decay
    score_grad = jnp.sum(through * step_heads[:, :, None, :], axis=1)
    with_scores = through * scores[:, None]
    log_part = with_scores * step_heads[:, :, None, :]
    step_from_weights = jnp.sum(with_scores, axis=2)
    cum_grad = jnp.sum(log_part, axis=3) - jnp.sum(log_part, axis=2)
    x_grad = jnp.einsum("shtr,sthp->srhp", weights, dy_heads, preferred_element_type=jnp.float32)
    v_grad = (dy_plain * growth).astype(jnp.bfloat16)
    inter_cum = jnp.sum(dy_plain * growth * inner_v, axis=3)
    incoming_grad = jnp.einsum(
        "sthp,stn->shpn", v_grad, out_basis, preferred_element_type=jnp.float32
    )
    out_basis_grad = jnp.einsum(
        "sthp,shpn->stn", v_grad, incoming_low, preferred_element_type=jnp.float32
    )
    starting = incoming_grad[-1]
    for i in range(seq_count - 2, -1, -1):
        starting = block_decay[i][:, None, None] * starting + incoming_grad[i]
    returning = [carried(starting, whole_decay, chain - 1, -seq_count)]
    for i in range(seq_count - 1, 0, -1):
        returning.insert(0, block_decay[i][:, None, None] * returning[0] + incoming_grad[i])
    chain_grad = jnp.stack(returning)
    total_grad = block_decay * jnp.sum(chain_grad * incoming, axis=(2, 3))
    chain_low = chain_grad.astype(jnp.bfloat16)
    scaled_grad = jnp.einsum(
        "shpn,srn->srhp", chain_low, in_basis, preferred_element_type=jnp.float32
    )
    in_basis_grad = jnp.einsum(
        "shpn,srhp->srn", chain_low, scaled_x, preferred_element_type=jnp.float32
    )
    factor_grad = jnp.sum(scaled_grad * heads_plain, axis=3)
    x_grad = x_grad + scaled_grad * factor[..., None] + skip_gain[:, None] * dy_plain
    skip_part = jnp.sum(dy_plain * heads_plain, axis=(0, 1, 3))
    via_factor = factor_grad * factor
    total_grad = total_grad + jnp.sum(via_factor, axis=1)
    last_token = lax.broadcasted_iota(jnp.int32, (1, block_len, 1), 1) == block_len - 1
    cum_tokens = jnp.transpose(cum_grad, (0, 2, 1)) + inter_cum - via_factor
    cum_tokens = cum_tokens + jnp.where(last_token, total_grad[:, None, :], 0.0)
    rate_grad_tok = jnp.flip(jnp.cumsum(jnp.flip(cum_tokens, 1), axis=1), 1)
    step_grad = (
        jnp.transpose(step_from_weights, (0, 2, 1))
        + factor_grad * jnp.exp(final[:, None, :] - cumulative)
        + rate_grad_tok * rate
    )
    log_rate_part = jnp.sum(rate_grad_tok * step_size, axis=(0, 1)) * rate
    pre_step_grad = step_grad * jax.nn.sigmoid(step_in)
    step_bias_part = jnp.sum(pre_step_grad, axis=(0, 1))
    step_low_flat = pre_step_grad.astype(jnp.bfloat16).reshape(row_count, heads_local)
    out_basis_grad = out_basis_grad + jnp.einsum(
        "str,srn->stn", score_grad, in_basis.astype(jnp.float32), precision=HIGH
    )
    in_basis_grad = in_basis_grad + jnp.einsum(
        "str,stn->srn", score_grad, out_basis.astype(jnp.float32), precision=HIGH
    )
    basis_grad = lax.psum(jnp.concatenate([in_basis_grad, out_basis_grad], axis=-1), "head")
    value_pre_grad = x_grad.reshape(1, row_count, inner_local) * silu_slope(value_conv).reshape(
        1, row_count, inner_local
    )
    state_pre_grad = (basis_grad * silu_slope(state_conv)).reshape(1, row_count, 2 * states)
    value_next, state_next = shifted(
        (value_pre_grad[:, : taps - 1], state_pre_grad[:, : taps - 1]), "seq", -seq_count
    )
    value_extended = jnp.concatenate([value_pre_grad, value_next], axis=1)
    state_extended = jnp.concatenate([state_pre_grad, state_next], axis=1)
    value_low_flat = (
        depthwise_back(value_extended, value_kernel, row_count)
        .astype(jnp.bfloat16)
        .reshape(row_count, inner_local)
    )
    state_low_flat = (
        depthwise_back(state_extended, state_kernel, row_count)
        .astype(jnp.bfloat16)
        .reshape(row_count, 2 * states)
    )
    value_kernel_part = kernel_sums(value_padded, value_pre_grad, row_count, taps)
    value_bias_part = jnp.sum(value_pre_grad, axis=(0, 1))
    state_kernel_part = kernel_sums(state_padded, state_pre_grad, row_count, taps)
    state_bias_part = jnp.sum(state_pre_grad, axis=(0, 1))
    gate_low_flat = gate_grad_low.reshape(row_count, inner_local)
    column_share = 2 * states // head_count
    state_columns = lax.dynamic_slice_in_dim(
        state_low_flat, head_rank * column_share, column_share, 1
    )
    matrix_columns = lax.dynamic_slice_in_dim(
        state_matrix, head_rank * column_share, column_share, 1
    )
    normal_partial = back_product(gate_low_flat, gate_matrix) + back_product(
        value_low_flat, value_matrix
    )
    normal_partial = (
        normal_partial
        + back_product(state_columns, matrix_columns)
        + back_product(step_low_flat, step_matrix)
    )
    normal_partial = normal_partial.reshape(seq_count, block_len, width)
    gain_share = lax.dynamic_slice_in_dim(norm_gain, head_rank * share, share, 0)
    own_hat = lax.dynamic_slice_in_dim(plain, head_rank * share, share, 2) * rstd
    row_total = lax.psum(
        jnp.sum(normal_partial * norm_gain * (plain * rstd), axis=-1, keepdims=True), "head"
    )
    normal_grad = lax.psum_scatter(
        normal_partial.astype(jnp.bfloat16), "head", scatter_dimension=2, tiled=True
    ).astype(jnp.float32)
    back = rstd * (normal_grad * gain_share - own_hat * row_total / width)
    token_grad = cotangent.astype(jnp.float32) + regroup(back.astype(jnp.bfloat16)).astype(
        jnp.float32
    )
    norm_gain_part = jnp.sum(normal_grad * own_hat, axis=(0, 1))
    gate_partial = row_product(flat_in, gate_low_flat)
    value_partial = row_product(flat_in, value_low_flat)
    step_partial = row_product(flat_in, step_low_flat)
    own_rows = lax.dynamic_slice_in_dim(normal_in, head_rank * share, share, 2).reshape(
        row_count, share
    )
    state_partial = row_product(own_rows, state_low_flat)
    gate_matrix_grad, value_matrix_grad, step_matrix_grad, output_matrix_grad = (
        summed_low(gate_partial, 0),
        summed_low(value_partial, 0),
        lax.psum_scatter(step_partial, "seq", scatter_dimension=0, tiled=True),
        summed_low(output_partial, 1),
    )
    summed = lax.psum(
        (
            state_partial,
            norm_gain_part,
            value_kernel_part,
            value_bias_part,
            state_kernel_part,
            state_bias_part,
            step_bias_part,
            log_rate_part,
            skip_part,
            gate_gain_part,
        ),
        "seq",
    )
    return (
        layer_out,
        token_grad,
        summed[1],
        gate_matrix_grad,
        value_matrix_grad,
        summed[0],
        step_matrix_grad,
        summed[2],
        summed[3],
        summed[4],
        summed[5],
        summed[6],
        summed[7],
        summed[8],
        summed[9],
        output_matrix_grad,
    )


def solution(mesh):
    in_specs = (
        P(None, "seq", "head"),
        P(None, "seq", "head"),
        P(),
        P(None, "head"),
        P(None, "head"),
        P(),
        P(None, "head"),
        P(None, "head"),
        P("head"),
        P(),
        P(),
        P("head"),
        P("head"),
        P("head"),
        P("head"),
        P("head", None),
    )
    out_specs = (
        P(None, "seq", "head"),
        P(None, "seq", "head"),
        P("head"),
        P("seq", "head"),
        P("seq", "head"),
        P("head", None),
        P("seq", "head"),
        P(None, "head"),
        P("head"),
        P(),
        P(),
        P("head"),
        P("head"),
        P("head"),
        P("head"),
        P("head", "seq"),
    )
    return jax.shard_map(local, mesh=mesh, in_specs=in_specs, out_specs=out_specs, check_vma=False)
```

```python
import jax
import jax.numpy as jnp
from jax import lax
from jax.experimental import pallas as pl
from jax.experimental.pallas import tpu as pltpu
from jax.sharding import PartitionSpec as P

HIGH = lax.Precision.HIGHEST
EPSILON = 1e-05
F32 = jnp.float32
BF16 = jnp.bfloat16
LANES = 128
EDGE = 8
VMEM_BYTES = 56 * 1024 * 1024

NN = (((1,), (0,)), ((), ()))
NT = (((1,), (1,)), ((), ()))
TN = (((0,), (0,)), ((), ()))


def dot(a, b, dims=NN, precision=None):
    return lax.dot_general(a, b, dims, precision=precision, preferred_element_type=F32)


def dot_split(a, b, dims=NN):
    high = a.astype(BF16)
    rest = (a - high.astype(F32)).astype(BF16)
    return dot(high, b, dims) + dot(rest, b, dims)


def sigmoid(v):
    return 1.0 / (1.0 + jnp.exp(-v))


def silu(v):
    return v * sigmoid(v)


def slope(v):
    sigma = sigmoid(v)
    return sigma * (1.0 + v * (1.0 - sigma))


def softplus(v):
    return jnp.maximum(v, 0.0) + jnp.log1p(jnp.exp(-jnp.abs(v)))


def ones_where(shape, rule):
    rows = lax.broadcasted_iota(jnp.int32, shape, 0)
    cols = lax.broadcasted_iota(jnp.int32, shape, 1)
    return rule(rows, cols)


def head_picker(channels, heads):
    wide = channels // heads
    return ones_where((channels, heads), lambda r, c: r // wide == c).astype(F32).astype(BF16)


def pair_spread(cols, j, rows):
    lane = lax.broadcasted_iota(jnp.int32, (rows, LANES), 1)
    first = jnp.broadcast_to(cols[:, 2 * j : 2 * j + 1], (rows, LANES))
    second = jnp.broadcast_to(cols[:, 2 * j + 1 : 2 * j + 2], (rows, LANES))
    return jnp.where(lane < LANES // 2, first, second)


def spread(cols, rows, heads):
    return jnp.concatenate([pair_spread(cols, j, rows) for j in range(heads // 2)], axis=1)


def call(kernel, name, grid, in_specs, out_specs, out_shape, scratch, flops, args, transcendentals=0):
    moved = sum(a.size * a.dtype.itemsize for a in args) + sum(
        o.size * o.dtype.itemsize for o in out_shape
    )
    return pl.pallas_call(
        kernel,
        grid=grid,
        in_specs=in_specs,
        out_specs=out_specs,
        out_shape=out_shape,
        scratch_shapes=scratch,
        compiler_params=pltpu.CompilerParams(
            dimension_semantics=("arbitrary",) * len(grid), vmem_limit_bytes=VMEM_BYTES
        ),
        cost_estimate=pl.CostEstimate(
            flops=int(flops), bytes_accessed=int(moved), transcendentals=int(transcendentals)
        ),
        name=name,
    )(*args)


def shape(dims, dtype):
    return jax.ShapeDtypeStruct(dims, dtype)


def prepare(value_pre, value_edge, state_pre, state_edge, step_pre, value_kernel, value_bias,
            state_kernel, state_bias, step_bias, log_rate, length):
    rows, channels = value_pre.shape
    heads = step_pre.shape[1]
    both = state_pre.shape[1]
    states = both // 2
    wide = channels // heads
    count = rows // length
    taps = value_kernel.shape[0]
    unit = length // EDGE

    def kernel(xr, xr_before, xr_edge, bc, bc_before, bc_edge, dtr, vk, vb, sk, sb, tb, lr,
               xs_o, xdt_o, xw_o, bcs_o, dt_o, cum_o, cumt_o, hin_o, pre_o, dec_o, end_o,
               padded, padded_bc, state, ahead):
        i = pl.program_id(0)

        @pl.when(i == 0)
        def _():
            padded[0:EDGE] = xr_edge[...]
            padded_bc[0:EDGE] = bc_edge[...]
            state[...] = jnp.zeros_like(state)
            ahead[...] = jnp.ones_like(ahead)

        @pl.when(i > 0)
        def _():
            padded[0:EDGE] = xr_before[...]
            padded_bc[0:EDGE] = bc_before[...]

        padded[EDGE:] = xr[...]
        padded_bc[EDGE:] = bc[...]
        start = EDGE - taps + 1
        summed = sb[...] + sk[0:1] * padded_bc[pl.ds(start, length)]
        for k in range(1, taps):
            summed = summed + sk[k : k + 1] * padded_bc[pl.ds(start + k, length)]
        basis = silu(summed).astype(BF16)
        bcs_o[...] = basis
        dt = softplus(dtr[...] + tb[...])
        da = dt * -jnp.exp(lr[...])
        lower = ones_where((length, length), lambda r, c: r >= c).astype(F32)
        upper = ones_where((length, length), lambda r, c: r <= c).astype(F32)
        cum = dot(lower, da, precision=HIGH)
        cumt = dot(da, upper, TN, precision=HIGH)
        dt_o[...] = dt
        cum_o[...] = cum
        cumt_o[...] = cumt
        factor = jnp.exp(cum[length - 1 : length] - cum) * dt
        decay = jnp.exp(jnp.broadcast_to(cumt[:, length - 1 : length], (heads, LANES)))
        dec_o[0] = decay
        pre_o[0] = ahead[...]
        ahead[...] = ahead[...] * decay
        hin_o[0] = state[...]
        for j in range(channels // LANES):
            at = slice(j * LANES, (j + 1) * LANES)
            total = vb[:, at] + vk[0:1, at] * padded[pl.ds(start, length), at]
            for k in range(1, taps):
                total = total + vk[k : k + 1, at] * padded[pl.ds(start + k, length), at]
            xs = silu(total).astype(BF16)
            xs_o[:, at] = xs
            plain = xs.astype(F32)
            xdt_o[:, at] = (plain * pair_spread(dt, j, length)).astype(BF16)
            xw_o[:, at] = (plain * pair_spread(factor, j, length)).astype(BF16)
        local = dot(xw_o[...], basis[:, :states], TN)
        for h in range(heads):
            at = slice(h * wide, (h + 1) * wide)
            state[at] = decay[h : h + 1] * state[at] + local[at]
        end_o[...] = state[...].astype(BF16)

    whole = lambda *dims: pl.BlockSpec(dims, lambda i: (0,) * len(dims))
    tokens = lambda n: pl.BlockSpec((length, n), lambda i: (i, 0))
    before = lambda n: pl.BlockSpec((EDGE, n), lambda i: (jnp.maximum(i * unit - 1, 0), 0))
    per = lambda *dims: pl.BlockSpec((1,) + dims, lambda i: (i, 0, 0))
    return call(
        kernel, "conv_and_local_states", (count,),
        [tokens(channels), before(channels), whole(EDGE, channels), tokens(both), before(both),
         whole(EDGE, both), tokens(heads), whole(taps, channels), whole(1, channels),
         whole(taps, both), whole(1, both), whole(1, heads), whole(1, heads)],
        [tokens(channels), tokens(channels), tokens(channels), tokens(both), tokens(heads),
         tokens(heads), pl.BlockSpec((heads, length), lambda i: (0, i)), per(channels, states),
         per(heads, LANES), per(heads, LANES), whole(channels, states)],
        [shape((rows, channels), BF16), shape((rows, channels), BF16), shape((rows, channels), BF16),
         shape((rows, both), BF16), shape((rows, heads), F32), shape((rows, heads), F32),
         shape((heads, rows), F32), shape((count, channels, states), F32),
         shape((count, heads, LANES), F32), shape((count, heads, LANES), F32),
         shape((channels, states), BF16)],
        [pltpu.VMEM((length + EDGE, channels), F32), pltpu.VMEM((length + EDGE, both), F32),
         pltpu.VMEM((channels, states), F32), pltpu.VMEM((heads, LANES), F32)],
        2 * rows * channels * states,
        (value_pre, value_pre, value_edge, state_pre, state_pre, state_edge, step_pre, value_kernel,
         value_bias, state_kernel, state_bias, step_bias, log_rate),
        4 * rows * channels,
    )


def decays(cum, cumt, h, half):
    top = jnp.exp(jnp.minimum(cum[:half, h : h + 1] - cumt[h : h + 1, :half], 0.0))
    low = jnp.exp(jnp.minimum(cum[half:, h : h + 1] - cumt[h : h + 1, :], 0.0))
    return top, low


def lower_scores(basis, states, length):
    scores = dot(basis[:, states:], basis[:, :states], NT)
    return jnp.where(ones_where((length, length), lambda r, c: r >= c), scores, 0.0)


def intra(bcs, xdt, cum, cumt, length):
    rows, channels = xdt.shape
    heads = cum.shape[1]
    both = bcs.shape[1]
    states = both // 2
    half = length // 2

    def kernel(bcs_r, xdt_r, cum_r, cumt_r, y_o):
        scores = lower_scores(bcs_r[...], states, length)
        cum_v, cumt_v = cum_r[...], cumt_r[...]
        lane = lax.broadcasted_iota(jnp.int32, (length, LANES), 1)
        for j in range(heads // 2):
            at = slice(j * LANES, (j + 1) * LANES)
            pair = xdt_r[:, at]
            y_top = jnp.zeros((half, LANES), F32)
            y_low = jnp.zeros((half, LANES), F32)
            for s in range(2):
                own = jnp.where((lane < LANES // 2) == (s == 0), pair, jnp.zeros_like(pair))
                top, low = decays(cum_v, cumt_v, 2 * j + s, half)
                y_top += dot((scores[:half, :half] * top).astype(BF16), own[:half])
                y_low += dot((scores[half:] * low).astype(BF16), own)
            y_o[:half, at] = y_top
            y_o[half:, at] = y_low

    tokens = lambda n: pl.BlockSpec((length, n), lambda i: (i, 0))
    return call(
        kernel, "within_blocks", (rows // length,),
        [tokens(both), tokens(channels), tokens(heads), pl.BlockSpec((heads, length), lambda i: (0, i))],
        [tokens(channels)], [shape((rows, channels), F32)], [],
        2 * rows * length * channels * 4, (bcs, xdt, cum, cumt), rows * length * heads,
    )[0]


def finish(y_intra, xs, bcs, gate_pre, normed_grad, cum, hin0, pre, carry, skip_row, gate_gain, length):
    rows, channels = xs.shape
    heads = cum.shape[1]
    both = bcs.shape[1]
    states = both // 2
    wide = channels // heads
    count = rows // length

    def kernel(yi, xs_r, bcs_r, z, dn, cum_r, hin_r, pre_r, carry_r, skip, gain, y_o, low_o, sums_o):
        for h in range(heads):
            at = slice(h * wide, (h + 1) * wide)
            low_o[0, at] = (hin_r[0, at] + pre_r[0, h : h + 1] * carry_r[at].astype(F32)).astype(BF16)
        growth = jnp.exp(cum_r[...])
        squares = jnp.zeros((length, LANES), F32)
        crosses = jnp.zeros((length, LANES), F32)
        out_basis = bcs_r[:, states:]
        for j in range(channels // LANES):
            at = slice(j * LANES, (j + 1) * LANES)
            v = dot(out_basis, low_o[0, at], NT)
            y = yi[:, at] + pair_spread(growth, j, length) * v + skip[:, at] * xs_r[:, at].astype(F32)
            y_o[:, at] = y
            gated = y * silu(z[:, at])
            squares += gated * gated
            crosses += dn[:, at] * gain[:, at] * gated
        sums_o[...] = jnp.concatenate(
            [jnp.sum(squares, axis=1, keepdims=True), jnp.sum(crosses, axis=1, keepdims=True)], axis=1
        )

    whole = lambda *dims: pl.BlockSpec(dims, lambda i: (0,) * len(dims))
    tokens = lambda n: pl.BlockSpec((length, n), lambda i: (i, 0))
    per = lambda *dims: pl.BlockSpec((1,) + dims, lambda i: (i, 0, 0))
    return call(
        kernel, "across_blocks", (count,),
        [tokens(channels), tokens(channels), tokens(both), tokens(channels), tokens(channels),
         tokens(heads), per(channels, states), per(heads, LANES), whole(channels, states),
         whole(1, channels), whole(1, channels)],
        [tokens(channels), per(channels, states), tokens(2)],
        [shape((rows, channels), F32), shape((count, channels, states), BF16), shape((rows, 2), F32)],
        [], 2 * rows * channels * states,
        (y_intra, xs, bcs, gate_pre, normed_grad, cum, hin0, pre, carry, skip_row, gate_gain),
        2 * rows * channels,
    )


def turn(y, gate_pre, normed_grad, xs, bcs, cum, sums, gate_gain, output_matrix, dec, length, inner):
    rows, channels = xs.shape
    heads = cum.shape[1]
    both = bcs.shape[1]
    states = both // 2
    wide = channels // heads
    count = rows // length
    width = output_matrix.shape[1]

    def kernel(y_r, z_r, dn_r, xs_r, bcs_r, cum_r, sums_r, gain, wo, dec_r,
               normed_o, part_o, dy_o, dz_o, dv_o, ab_o, ds_o, post_o, start_o, ggain_o,
               state, behind, prod_a, prod_b):
        i = pl.program_id(0)

        @pl.when(i == 0)
        def _():
            state[...] = jnp.zeros_like(state)
            behind[...] = jnp.ones_like(behind)
            ggain_o[...] = jnp.zeros_like(ggain_o)

        grstd = lax.rsqrt(sums_r[:, 0:1] / inner + EPSILON)
        cross = (grstd * grstd * grstd) * (sums_r[:, 1:2] / inner)
        growth = jnp.exp(cum_r[...])
        for j in range(channels // LANES):
            at = slice(j * LANES, (j + 1) * LANES)
            y, z, dn = y_r[:, at], z_r[:, at], dn_r[:, at]
            sigma = sigmoid(z)
            act = z * sigma
            gated = y * act
            scaled = gated * grstd
            normed_o[:, at] = (scaled * gain[:, at]).astype(BF16)
            ggain_o[:, at] += jnp.sum(dn * scaled, axis=0, keepdims=True)
            dgated = grstd * (dn * gain[:, at]) - gated * cross
            dy = (dgated * act).astype(BF16)
            dy_o[:, at] = dy
            dz_o[:, at] = (dgated * y * (sigma * (1.0 + z * (1.0 - sigma)))).astype(BF16)
            plain = dy.astype(F32)
            dv_o[:, at] = (plain * pair_spread(growth, j, length)).astype(BF16)
            prod_a[:, at] = plain * y
            prod_b[:, at] = plain * xs_r[:, at].astype(F32)
        picker = head_picker(channels, heads)
        ab_o[:, :heads] = dot_split(prod_a[...], picker)
        ab_o[:, heads:] = dot_split(prod_b[...], picker)
        part_o[...] = dot(normed_o[...], wo[...]).astype(BF16)
        dhin = dot(dv_o[...], bcs_r[:, states:], TN)
        ds_o[0] = state[...]
        post_o[0] = behind[...]
        behind[...] = behind[...] * dec_r[0]
        for h in range(heads):
            at = slice(h * wide, (h + 1) * wide)
            state[at] = dec_r[0, h : h + 1] * state[at] + dhin[at]
        start_o[...] = state[...].astype(BF16)

    last = count - 1
    whole = lambda *dims: pl.BlockSpec(dims, lambda i: (0,) * len(dims))
    tokens = lambda n: pl.BlockSpec((length, n), lambda i: (last - i, 0))
    per = lambda *dims: pl.BlockSpec((1,) + dims, lambda i: (last - i, 0, 0))
    return call(
        kernel, "gate_and_turn", (count,),
        [tokens(channels), tokens(channels), tokens(channels), tokens(channels), tokens(both),
         tokens(heads), tokens(2), whole(1, channels), whole(channels, width), per(heads, LANES)],
        [tokens(channels), tokens(width), tokens(channels), tokens(channels), tokens(channels),
         tokens(2 * heads), per(channels, states), per(heads, LANES), whole(channels, states),
         whole(1, channels)],
        [shape((rows, channels), BF16), shape((rows, width), BF16), shape((rows, channels), BF16),
         shape((rows, channels), BF16), shape((rows, channels), BF16), shape((rows, 2 * heads), F32),
         shape((count, channels, states), F32), shape((count, heads, LANES), F32),
         shape((channels, states), BF16), shape((1, channels), F32)],
        [pltpu.VMEM((channels, states), F32), pltpu.VMEM((heads, LANES), F32),
         pltpu.VMEM((length, channels), F32), pltpu.VMEM((length, channels), F32)],
        2 * rows * channels * (width + states),
        (y, gate_pre, normed_grad, xs, bcs, cum, sums, gate_gain, output_matrix, dec),
        rows * channels,
    )


def intra_back(bcs, xdt, dy, cum, cumt, length):
    rows, channels = xdt.shape
    heads = cum.shape[1]
    both = bcs.shape[1]
    states = both // 2
    half = length // 2

    def kernel(bcs_r, xdt_r, dy_r, cum_r, cumt_r, g_o, dbc_o, grad):
        scores = lower_scores(bcs_r[...], states, length)
        cum_v, cumt_v = cum_r[...], cumt_r[...]
        lane = lax.broadcasted_iota(jnp.int32, (length, LANES), 1)
        grad[...] = jnp.zeros_like(grad)
        for j in range(heads // 2):
            at = slice(j * LANES, (j + 1) * LANES)
            pair, dpair = xdt_r[:, at], dy_r[:, at]
            g_top = jnp.zeros((half, LANES), F32)
            g_low = jnp.zeros((half, LANES), F32)
            for s in range(2):
                own = jnp.where((lane < LANES // 2) == (s == 0), dpair, jnp.zeros_like(dpair))
                top, low = decays(cum_v, cumt_v, 2 * j + s, half)
                grad[:half, :half] += dot(own[:half], pair[:half], NT) * top
                grad[half:] += dot(own[half:], pair, NT) * low
                w_top = (scores[:half, :half] * top).astype(BF16)
                w_low = (scores[half:] * low).astype(BF16)
                g_top += dot(w_top, own[:half], TN) + dot(w_low[:, :half], own[half:], TN)
                g_low += dot(w_low[:, half:], own[half:], TN)
            g_o[:half, at] = g_top
            g_o[half:, at] = g_low
        masked = jnp.where(ones_where((length, length), lambda r, c: r >= c), grad[...], 0.0)
        high = masked.astype(BF16)
        rest = (masked - high.astype(F32)).astype(BF16)
        in_b, out_b = bcs_r[:, :states], bcs_r[:, states:]
        dbc_o[:, :states] = dot(high, out_b, TN) + dot(rest, out_b, TN)
        dbc_o[:, states:] = dot(high, in_b) + dot(rest, in_b)

    tokens = lambda n: pl.BlockSpec((length, n), lambda i: (i, 0))
    return call(
        kernel, "within_blocks_back", (rows // length,),
        [tokens(both), tokens(channels), tokens(channels), tokens(heads),
         pl.BlockSpec((heads, length), lambda i: (0, i))],
        [tokens(channels), tokens(both)],
        [shape((rows, channels), F32), shape((rows, both), F32)],
        [pltpu.VMEM((length, length), F32)],
        2 * rows * length * channels * 8, (bcs, xdt, dy, cum, cumt), rows * length * heads,
    )


def finish_back(value_pre, value_edge, value_kernel, value_bias, xs, xdt, xw, g, dy, dv, bcs, step_pre, dt,
                cum, ab, hin0, pre, carry, hin_low, ds0, post, back, dec, dbc_intra, skip_row, skip_gain,
                step_bias, log_rate, length):
    rows, channels = xs.shape
    heads = cum.shape[1]
    both = bcs.shape[1]
    states = both // 2
    wide = channels // heads
    count = rows // length
    taps = value_kernel.shape[0]
    unit = length // EDGE

    def kernel(xr, xr_before, xr_edge, vk, vb, xs_r, xdt_r, xw_r, g_r, dy_r, dv_r, bcs_r, dtr, dt_r, cum_r,
               ab_r, hin_r, pre_r, carry_r, low_r, ds_r, post_r, back_r, dec_r, dbci, skip, skipg, tb,
               lr, dxr_o, tail_o, head_o, vkg_o, vbg_o, ddtr_o, dbc_o, small_o,
               padded, ext, ds_low, inner_sums):
        i = pl.program_id(0)
        block = count - 1 - i

        @pl.when(i == 0)
        def _():
            vkg_o[...] = jnp.zeros_like(vkg_o)
            vbg_o[...] = jnp.zeros_like(vbg_o)
            small_o[...] = jnp.zeros_like(small_o)
            ext[0:EDGE] = jnp.zeros((EDGE, channels), F32)

        @pl.when(block == 0)
        def _():
            padded[0:EDGE] = xr_edge[...]

        @pl.when(block > 0)
        def _():
            padded[0:EDGE] = xr_before[...]

        padded[EDGE:] = xr[...]
        ext[length:] = ext[0:EDGE]
        for h in range(heads):
            at = slice(h * wide, (h + 1) * wide)
            ds = ds_r[0, at] + post_r[0, h : h + 1] * back_r[at].astype(F32)
            ds_low[at] = ds.astype(BF16)
            hin = hin_r[0, at] + pre_r[0, h : h + 1] * carry_r[at].astype(F32)
            inner_sums[h : h + 1] = jnp.sum(ds * hin, axis=0, keepdims=True) * dec_r[0, h : h + 1]
        in_b = bcs_r[:, :states]
        dt_v, cum_v = dt_r[...], cum_r[...]
        fade = jnp.exp(cum_v[length - 1 : length] - cum_v)
        factor = fade * dt_v
        start = EDGE - taps + 1
        picker = head_picker(channels, heads)
        c_sum = jnp.zeros((length, heads), F32)
        d_sum = jnp.zeros((length, heads), F32)
        w_sum = jnp.zeros((length, heads), F32)
        for j in range(channels // LANES):
            at = slice(j * LANES, (j + 1) * LANES)
            xs_v = xs_r[:, at].astype(F32)
            dxw = dot(in_b, ds_low[at], NT)
            g_v = g_r[:, at]
            c_sum += dot_split(xs_v * g_v, picker[at])
            d_sum += dot_split(xs_v * dxw, picker[at])
            w_sum += dot_split(xdt_r[:, at].astype(F32) * g_v, picker[at])
            dxs = (
                pair_spread(dt_v, j, length) * g_v
                + pair_spread(factor, j, length) * dxw
                + skip[:, at] * dy_r[:, at].astype(F32)
            )
            total = vb[:, at] + vk[0:1, at] * padded[pl.ds(start, length), at]
            for k in range(1, taps):
                total = total + vk[k : k + 1, at] * padded[pl.ds(start + k, length), at]
            dpre = dxs * slope(total)
            ext[0:length, at] = dpre
            vbg_o[:, at] += jnp.sum(dpre, axis=0, keepdims=True)
            for k in range(taps):
                vkg_o[k : k + 1, at] += jnp.sum(
                    dpre * padded[pl.ds(start + k, length), at], axis=0, keepdims=True
                )
            dxr = vk[0:1, at] * ext[pl.ds(taps - 1, length), at]
            for k in range(1, taps):
                dxr = dxr + vk[k : k + 1, at] * ext[pl.ds(taps - 1 - k, length), at]
            dxr_o[:, at] = dxr.astype(BF16)

            @pl.when(i == 0)
            def _():
                tail_o[:, at] = dxr[length - EDGE :]

        head_o[...] = ext[0:EDGE]
        dbc_o[:, :states] = dbci[:, :states] + dot(xw_r[...], ds_low[...])
        dbc_o[:, states:] = dbci[:, states:] + dot(dv_r[...], low_r[0])
        rate = -jnp.exp(lr[...])
        a_sum, b_sum = ab_r[:, :heads], ab_r[:, heads:]
        e_sum = d_sum * factor
        ones = jnp.ones((1, LANES), F32)
        dtotal = jnp.sum(e_sum, axis=0, keepdims=True) + dot(ones, inner_sums[...], NT, precision=HIGH)
        row = lax.broadcasted_iota(jnp.int32, (length, heads), 0)
        dcum = a_sum - skipg[...] * b_sum - w_sum - e_sum
        dcum = dcum + jnp.where(row == length - 1, dtotal, 0.0)
        upper = ones_where((length, length), lambda r, c: r <= c).astype(F32)
        dda = dot(upper, dcum, precision=HIGH)
        ddt = c_sum + d_sum * fade + dda * rate
        dpre_dt = ddt * sigmoid(dtr[...] + tb[...])
        ddtr_o[...] = dpre_dt.astype(BF16)
        small_o[0:1] += jnp.sum(dpre_dt, axis=0, keepdims=True)
        small_o[1:2] += jnp.sum(dda * dt_v, axis=0, keepdims=True) * rate
        small_o[2:3] += jnp.sum(b_sum, axis=0, keepdims=True)

    last = count - 1
    whole = lambda *dims: pl.BlockSpec(dims, lambda i: (0,) * len(dims))
    tokens = lambda n: pl.BlockSpec((length, n), lambda i: (last - i, 0))
    before = lambda n: pl.BlockSpec((EDGE, n), lambda i: (jnp.maximum((last - i) * unit - 1, 0), 0))
    per = lambda *dims: pl.BlockSpec((1,) + dims, lambda i: (last - i, 0, 0))
    return call(
        kernel, "across_blocks_back", (count,),
        [tokens(channels), before(channels), whole(EDGE, channels), whole(taps, channels),
         whole(1, channels), tokens(channels), tokens(channels), tokens(channels), tokens(channels),
         tokens(channels), tokens(channels), tokens(both), tokens(heads), tokens(heads), tokens(heads),
         tokens(2 * heads), per(channels, states), per(heads, LANES), whole(channels, states),
         per(channels, states), per(channels, states), per(heads, LANES), whole(channels, states),
         per(heads, LANES), tokens(both), whole(1, channels), whole(1, heads), whole(1, heads),
         whole(1, heads)],
        [tokens(channels), whole(EDGE, channels), whole(EDGE, channels), whole(taps, channels),
         whole(1, channels), tokens(heads), tokens(both), whole(EDGE, heads)],
        [shape((rows, channels), BF16), shape((EDGE, channels), F32), shape((EDGE, channels), F32),
         shape((taps, channels), F32), shape((1, channels), F32), shape((rows, heads), BF16),
         shape((rows, both), F32), shape((EDGE, heads), F32)],
        [pltpu.VMEM((length + EDGE, channels), F32), pltpu.VMEM((length + EDGE, channels), F32),
         pltpu.VMEM((channels, states), BF16), pltpu.VMEM((heads, LANES), F32)],
        2 * rows * channels * states * 3,
        (value_pre, value_pre, value_edge, value_kernel, value_bias, xs, xdt, xw, g, dy, dv, bcs, step_pre,
         dt, cum, ab, hin0, pre, carry, hin_low, ds0, post, back, dec, dbc_intra, skip_row, skip_gain,
         step_bias, log_rate),
        2 * rows * channels,
    )


def shifted(block, axis, distance):
    devices = range(lax.axis_size(axis))
    route = [(i - distance, i) for i in devices if i - distance in devices]
    return lax.ppermute(block, axis, route)


def regroup(block):
    members = block.shape[0]
    count = lax.axis_size("seq")
    groups = [list(range(i, i + members)) for i in range(0, count, members)]
    return lax.all_to_all(block, "seq", 0, 0, axis_index_groups=groups, tiled=True)


def carried(part, decay, hops, distance):
    carry = shifted(part, "seq", distance)
    for _ in range(hops - 1):
        leaving = decay * carry.astype(F32) + part.astype(F32)
        carry = shifted(leaving.astype(BF16), "seq", distance)
    return carry


def depthwise(padded, kernel, offset, length):
    summed = offset + kernel[0] * padded[0:length]
    for tap_index in range(1, kernel.shape[0]):
        summed = summed + kernel[tap_index] * padded[tap_index : tap_index + length]
    return summed


def depthwise_back(extended, kernel, length):
    margin = kernel.shape[0] - 1
    summed = kernel[0] * extended[margin : margin + length]
    for k in range(1, kernel.shape[0]):
        summed = summed + kernel[k] * extended[margin - k : margin - k + length]
    return summed


def kernel_sums(padded, pre_grad, length, taps):
    return jnp.stack([jnp.sum(pre_grad * padded[k : k + length], axis=0) for k in range(taps)])


def summed_low(part, dim):
    low = part.astype(BF16)
    return lax.psum_scatter(low, "seq", scatter_dimension=dim, tiled=True).astype(F32)


def local(
    tokens,
    cotangent,
    norm_gain,
    gate_matrix,
    value_matrix,
    state_matrix,
    step_matrix,
    value_kernel,
    value_bias,
    state_kernel,
    state_bias,
    step_bias,
    log_rate,
    skip_gain,
    gate_gain,
    output_matrix,
):
    seq_count, length, share = tokens.shape
    hops = lax.axis_size("seq") // seq_count - 1
    width, channels = gate_matrix.shape
    heads = step_bias.shape[0]
    wide = channels // heads
    both = state_matrix.shape[1]
    taps = value_kernel.shape[0]
    rows = seq_count * length
    head_count = lax.axis_size("head")
    head_rank = lax.axis_index("head")
    inner = channels * head_count
    row = lambda v: v.reshape(1, -1)

    whole_in = lax.all_gather(regroup(tokens), "head", axis=2, tiled=True).reshape(rows, width)
    flat_cot = lax.all_gather(regroup(cotangent), "head", axis=2, tiled=True).reshape(rows, width)
    plain = whole_in.astype(F32)
    rstd = lax.rsqrt(jnp.mean(plain * plain, axis=-1, keepdims=True) + EPSILON)
    normal_in = (plain * rstd * norm_gain).astype(BF16)
    state_pre = dot(normal_in, state_matrix)
    step_pre = dot(normal_in, step_matrix)
    value_pre = dot(normal_in, value_matrix)
    gate_pre = dot(normal_in, gate_matrix)

    edge = shifted(
        jnp.concatenate([value_pre[rows - EDGE :], state_pre[rows - EDGE :]], axis=1), "seq", seq_count
    )
    value_edge, state_edge = edge[:, :channels], edge[:, channels:]
    xs, xdt, xw, bcs, dt, cum, cumt, hin0, pre, dec, ending = prepare(
        value_pre, value_edge, state_pre, state_edge, step_pre, value_kernel, row(value_bias),
        state_kernel, row(state_bias), row(step_bias), row(log_rate), length,
    )
    whole_decay = jnp.repeat(pre[-1] * dec[-1], wide, axis=0)
    carry = carried(ending, whole_decay, hops, seq_count)
    y_intra = intra(bcs, xdt, cum, cumt, length)
    normed_grad = dot(flat_cot, output_matrix, NT)
    skip_row = row(jnp.repeat(skip_gain, wide))
    y, hin_low, sums = finish(
        y_intra, xs, bcs, gate_pre, normed_grad, cum, hin0, pre, carry, skip_row, row(gate_gain), length
    )
    sums = lax.psum(sums, "head")
    normed, part, dy, dz, dv, ab, ds0, post, starting, gate_gain_part = turn(
        y, gate_pre, normed_grad, xs, bcs, cum, sums, row(gate_gain), output_matrix, dec, length, inner
    )
    back = carried(starting, whole_decay, hops, -seq_count)
    branch = lax.psum_scatter(part, "head", scatter_dimension=1, tiled=True)
    layer_out = (
        tokens.astype(F32) + regroup(branch.reshape(tokens.shape)).astype(F32)
    ).astype(BF16)
    output_partial = dot(normed, flat_cot, TN)
    gate_partial = dot(normal_in, dz, TN)
    g, dbc_intra = intra_back(bcs, xdt, dy, cum, cumt, length)
    dxr, tail, head_rows, value_kernel_part, value_bias_part, ddtr, dbc, small = finish_back(
        value_pre, value_edge, value_kernel, row(value_bias), xs, xdt, xw, g, dy, dv, bcs, step_pre, dt, cum,
        ab, hin0, pre, carry, hin_low, ds0, post, back, dec, dbc_intra, skip_row, row(skip_gain),
        row(step_bias), row(log_rate), length,
    )
    dbc = lax.psum(dbc, "head")
    state_padded = jnp.concatenate([state_edge[EDGE - taps + 1 :], state_pre], axis=0)
    state_conv = depthwise(state_padded, state_kernel, state_bias, rows)
    dpre_bc = dbc * slope(state_conv)
    after = shifted(jnp.concatenate([head_rows, dpre_bc[:EDGE]], axis=1), "seq", -seq_count)
    value_after, state_after = after[:, :channels], after[:, channels:]
    zeros = jnp.zeros_like(value_after)
    fixed = tail + depthwise_back(
        jnp.concatenate([zeros, value_after[: taps - 1]], axis=0), value_kernel, EDGE
    )
    dxr = lax.dynamic_update_slice(dxr, fixed.astype(BF16), (rows - EDGE, 0))
    dbc_low = depthwise_back(
        jnp.concatenate([dpre_bc, state_after[: taps - 1]], axis=0), state_kernel, rows
    ).astype(BF16)
    state_kernel_part = kernel_sums(state_padded, dpre_bc, rows, taps)
    state_bias_part = jnp.sum(dpre_bc, axis=0)

    column_share = both // head_count
    state_columns = lax.dynamic_slice_in_dim(dbc_low, head_rank * column_share, column_share, 1)
    matrix_columns = lax.dynamic_slice_in_dim(
        state_matrix, head_rank * column_share, column_share, 1
    )
    value_partial = dot(normal_in, dxr, TN)
    normal_partial = (
        dot(dz, gate_matrix, NT)
        + dot(dxr, value_matrix, NT)
        + dot(state_columns, matrix_columns, NT)
        + dot(ddtr, step_matrix, NT)
    )
    gain_share = lax.dynamic_slice_in_dim(norm_gain, head_rank * share, share, 0)
    own_hat = lax.dynamic_slice_in_dim(plain, head_rank * share, share, 1) * rstd
    row_total = lax.psum(
        jnp.sum(normal_partial * norm_gain * (plain * rstd), axis=-1, keepdims=True), "head"
    )
    normal_grad = lax.psum_scatter(
        normal_partial.astype(BF16), "head", scatter_dimension=1, tiled=True
    ).astype(F32)
    up = rstd * (normal_grad * gain_share - own_hat * row_total / width)
    token_grad = cotangent.astype(F32) + regroup(up.astype(BF16).reshape(tokens.shape)).astype(F32)
    norm_gain_part = jnp.sum(normal_grad * own_hat, axis=0)
    step_partial = dot(normal_in, ddtr, TN)
    own_rows = lax.dynamic_slice_in_dim(normal_in, head_rank * share, share, 1)
    state_partial = dot(own_rows, dbc_low, TN)
    gate_matrix_grad, value_matrix_grad, step_matrix_grad, output_matrix_grad = (
        summed_low(gate_partial, 0),
        summed_low(value_partial, 0),
        lax.psum_scatter(step_partial, "seq", scatter_dimension=0, tiled=True),
        summed_low(output_partial, 1),
    )
    summed = lax.psum(
        (
            state_partial,
            norm_gain_part,
            value_kernel_part,
            value_bias_part[0],
            state_kernel_part,
            state_bias_part,
            small[0],
            small[1],
            small[2],
            gate_gain_part[0],
        ),
        "seq",
    )
    return (
        layer_out,
        token_grad,
        summed[1],
        gate_matrix_grad,
        value_matrix_grad,
        summed[0],
        step_matrix_grad,
        summed[2],
        summed[3],
        summed[4],
        summed[5],
        summed[6],
        summed[7],
        summed[8],
        summed[9],
        output_matrix_grad,
    )


def solution(mesh):
    in_specs = (
        P(None, "seq", "head"),
        P(None, "seq", "head"),
        P(),
        P(None, "head"),
        P(None, "head"),
        P(),
        P(None, "head"),
        P(None, "head"),
        P("head"),
        P(),
        P(),
        P("head"),
        P("head"),
        P("head"),
        P("head"),
        P("head", None),
    )
    out_specs = (
        P(None, "seq", "head"),
        P(None, "seq", "head"),
        P("head"),
        P("seq", "head"),
        P("seq", "head"),
        P("head", None),
        P("seq", "head"),
        P(None, "head"),
        P("head"),
        P(),
        P(),
        P("head"),
        P("head"),
        P("head"),
        P("head"),
        P("head", "seq"),
    )
    return jax.shard_map(local, mesh=mesh, in_specs=in_specs, out_specs=out_specs, check_vma=False)
```

```python
import jax
import jax.numpy as jnp
from jax import lax
from jax.experimental import pallas as pl
from jax.experimental.pallas import tpu as pltpu
from jax.sharding import PartitionSpec as P

HIGH = lax.Precision.HIGHEST
EPSILON = 1e-05
F32 = jnp.float32
BF16 = jnp.bfloat16
LANES = 128
EDGE = 8
VMEM_BYTES = 56 * 1024 * 1024

NN = (((1,), (0,)), ((), ()))
NT = (((1,), (1,)), ((), ()))
TN = (((0,), (0,)), ((), ()))


def dot(a, b, dims=NN, precision=None):
    return lax.dot_general(a, b, dims, precision=precision, preferred_element_type=F32)


def dot_split(a, b, dims=NN):
    high = a.astype(BF16)
    rest = (a - high.astype(F32)).astype(BF16)
    return dot(high, b, dims) + dot(rest, b, dims)


def sigmoid(v):
    return 1.0 / (1.0 + jnp.exp(-v))


def silu(v):
    return v * sigmoid(v)


def slope(v):
    sigma = sigmoid(v)
    return sigma * (1.0 + v * (1.0 - sigma))


def softplus(v):
    return jnp.maximum(v, 0.0) + jnp.log1p(jnp.exp(-jnp.abs(v)))


def ones_where(shape, rule):
    rows = lax.broadcasted_iota(jnp.int32, shape, 0)
    cols = lax.broadcasted_iota(jnp.int32, shape, 1)
    return rule(rows, cols)


def head_picker(channels, heads):
    wide = channels // heads
    return ones_where((channels, heads), lambda r, c: r // wide == c).astype(F32).astype(BF16)


def pair_spread(cols, j, rows):
    lane = lax.broadcasted_iota(jnp.int32, (rows, LANES), 1)
    first = jnp.broadcast_to(cols[:, 2 * j : 2 * j + 1], (rows, LANES))
    second = jnp.broadcast_to(cols[:, 2 * j + 1 : 2 * j + 2], (rows, LANES))
    return jnp.where(lane < LANES // 2, first, second)


def spread(cols, rows, heads):
    return jnp.concatenate([pair_spread(cols, j, rows) for j in range(heads // 2)], axis=1)


def call(kernel, name, grid, in_specs, out_specs, out_shape, scratch, flops, args, transcendentals=0):
    moved = sum(a.size * a.dtype.itemsize for a in args) + sum(
        o.size * o.dtype.itemsize for o in out_shape
    )
    return pl.pallas_call(
        kernel,
        grid=grid,
        in_specs=in_specs,
        out_specs=out_specs,
        out_shape=out_shape,
        scratch_shapes=scratch,
        compiler_params=pltpu.CompilerParams(
            dimension_semantics=("arbitrary",) * len(grid), vmem_limit_bytes=VMEM_BYTES
        ),
        cost_estimate=pl.CostEstimate(
            flops=int(flops), bytes_accessed=int(moved), transcendentals=int(transcendentals)
        ),
        name=name,
    )(*args)


def shape(dims, dtype):
    return jax.ShapeDtypeStruct(dims, dtype)


def prepare(value_pre, value_edge, state_pre, state_edge, step_pre, value_kernel, value_bias,
            state_kernel, state_bias, step_bias, log_rate, length):
    rows, channels = value_pre.shape
    heads = step_pre.shape[1]
    both = state_pre.shape[1]
    states = both // 2
    wide = channels // heads
    count = rows // length
    taps = value_kernel.shape[0]
    unit = length // EDGE

    def kernel(xr, xr_before, xr_edge, bc, bc_before, bc_edge, dtr, vk, vb, sk, sb, tb, lr,
               xs_o, xdt_o, xw_o, bcs_o, dt_o, cum_o, cumt_o, hin_o, pre_o, dec_o, end_o,
               padded, padded_bc, state, ahead):
        i = pl.program_id(0)

        @pl.when(i == 0)
        def _():
            padded[0:EDGE] = xr_edge[...]
            padded_bc[0:EDGE] = bc_edge[...]
            state[...] = jnp.zeros_like(state)
            ahead[...] = jnp.ones_like(ahead)

        @pl.when(i > 0)
        def _():
            padded[0:EDGE] = xr_before[...]
            padded_bc[0:EDGE] = bc_before[...]

        padded[EDGE:] = xr[...]
        padded_bc[EDGE:] = bc[...]
        start = EDGE - taps + 1
        summed = sb[...] + sk[0:1] * padded_bc[pl.ds(start, length)]
        for k in range(1, taps):
            summed = summed + sk[k : k + 1] * padded_bc[pl.ds(start + k, length)]
        basis = silu(summed).astype(BF16)
        bcs_o[...] = basis
        dt = softplus(dtr[...] + tb[...])
        da = dt * -jnp.exp(lr[...])
        lower = ones_where((length, length), lambda r, c: r >= c).astype(F32)
        upper = ones_where((length, length), lambda r, c: r <= c).astype(F32)
        cum = dot(lower, da, precision=HIGH)
        cumt = dot(da, upper, TN, precision=HIGH)
        dt_o[...] = dt
        cum_o[...] = cum
        cumt_o[...] = cumt
        factor = jnp.exp(cum[length - 1 : length] - cum) * dt
        decay = jnp.exp(jnp.broadcast_to(cumt[:, length - 1 : length], (heads, LANES)))
        dec_o[0] = decay
        pre_o[0] = ahead[...]
        ahead[...] = ahead[...] * decay
        hin_o[0] = state[...]
        for j in range(channels // LANES):
            at = slice(j * LANES, (j + 1) * LANES)
            total = vb[:, at] + vk[0:1, at] * padded[pl.ds(start, length), at]
            for k in range(1, taps):
                total = total + vk[k : k + 1, at] * padded[pl.ds(start + k, length), at]
            xs = silu(total).astype(BF16)
            xs_o[:, at] = xs
            plain = xs.astype(F32)
            xdt_o[:, at] = (plain * pair_spread(dt, j, length)).astype(BF16)
            xw_o[:, at] = (plain * pair_spread(factor, j, length)).astype(BF16)
        local = dot(xw_o[...], basis[:, :states], TN)
        for h in range(heads):
            at = slice(h * wide, (h + 1) * wide)
            state[at] = decay[h : h + 1] * state[at] + local[at]
        end_o[...] = state[...].astype(BF16)

    whole = lambda *dims: pl.BlockSpec(dims, lambda i: (0,) * len(dims))
    tokens = lambda n: pl.BlockSpec((length, n), lambda i: (i, 0))
    before = lambda n: pl.BlockSpec((EDGE, n), lambda i: (jnp.maximum(i * unit - 1, 0), 0))
    per = lambda *dims: pl.BlockSpec((1,) + dims, lambda i: (i, 0, 0))
    return call(
        kernel, "conv_and_local_states", (count,),
        [tokens(channels), before(channels), whole(EDGE, channels), tokens(both), before(both),
         whole(EDGE, both), tokens(heads), whole(taps, channels), whole(1, channels),
         whole(taps, both), whole(1, both), whole(1, heads), whole(1, heads)],
        [tokens(channels), tokens(channels), tokens(channels), tokens(both), tokens(heads),
         tokens(heads), pl.BlockSpec((heads, length), lambda i: (0, i)), per(channels, states),
         per(heads, LANES), per(heads, LANES), whole(channels, states)],
        [shape((rows, channels), BF16), shape((rows, channels), BF16), shape((rows, channels), BF16),
         shape((rows, both), BF16), shape((rows, heads), F32), shape((rows, heads), F32),
         shape((heads, rows), F32), shape((count, channels, states), F32),
         shape((count, heads, LANES), F32), shape((count, heads, LANES), F32),
         shape((channels, states), BF16)],
        [pltpu.VMEM((length + EDGE, channels), F32), pltpu.VMEM((length + EDGE, both), F32),
         pltpu.VMEM((channels, states), F32), pltpu.VMEM((heads, LANES), F32)],
        2 * rows * channels * states,
        (value_pre, value_pre, value_edge, state_pre, state_pre, state_edge, step_pre, value_kernel,
         value_bias, state_kernel, state_bias, step_bias, log_rate),
        4 * rows * channels,
    )


def decays(cum, cumt, h, half):
    top = jnp.exp(jnp.minimum(cum[:half, h : h + 1] - cumt[h : h + 1, :half], 0.0))
    low = jnp.exp(jnp.minimum(cum[half:, h : h + 1] - cumt[h : h + 1, :], 0.0))
    return top, low


def lower_scores(basis, states, length):
    scores = dot(basis[:, states:], basis[:, :states], NT)
    return jnp.where(ones_where((length, length), lambda r, c: r >= c), scores, 0.0)


def intra(bcs, xdt, cum, cumt, length):
    rows, channels = xdt.shape
    heads = cum.shape[1]
    both = bcs.shape[1]
    states = both // 2
    half = length // 2

    def kernel(bcs_r, xdt_r, cum_r, cumt_r, y_o):
        scores = lower_scores(bcs_r[...], states, length)
        cum_v, cumt_v = cum_r[...], cumt_r[...]
        lane = lax.broadcasted_iota(jnp.int32, (length, LANES), 1)
        for j in range(heads // 2):
            at = slice(j * LANES, (j + 1) * LANES)
            pair = xdt_r[:, at]
            y_top = jnp.zeros((half, LANES), F32)
            y_low = jnp.zeros((half, LANES), F32)
            for s in range(2):
                own = jnp.where((lane < LANES // 2) == (s == 0), pair, jnp.zeros_like(pair))
                top, low = decays(cum_v, cumt_v, 2 * j + s, half)
                y_top += dot((scores[:half, :half] * top).astype(BF16), own[:half])
                y_low += dot((scores[half:] * low).astype(BF16), own)
            y_o[:half, at] = y_top
            y_o[half:, at] = y_low

    tokens = lambda n: pl.BlockSpec((length, n), lambda i: (i, 0))
    return call(
        kernel, "within_blocks", (rows // length,),
        [tokens(both), tokens(channels), tokens(heads), pl.BlockSpec((heads, length), lambda i: (0, i))],
        [tokens(channels)], [shape((rows, channels), F32)], [],
        2 * rows * length * channels * 4, (bcs, xdt, cum, cumt), rows * length * heads,
    )[0]


def finish(y_intra, xs, bcs, gate_pre, normed_grad, cum, hin0, pre, carry, skip_row, gate_gain, length):
    rows, channels = xs.shape
    heads = cum.shape[1]
    both = bcs.shape[1]
    states = both // 2
    wide = channels // heads
    count = rows // length

    def kernel(yi, xs_r, bcs_r, z, dn, cum_r, hin_r, pre_r, carry_r, skip, gain, y_o, low_o, sums_o):
        for h in range(heads):
            at = slice(h * wide, (h + 1) * wide)
            low_o[0, at] = (hin_r[0, at] + pre_r[0, h : h + 1] * carry_r[at].astype(F32)).astype(BF16)
        growth = jnp.exp(cum_r[...])
        squares = jnp.zeros((length, LANES), F32)
        crosses = jnp.zeros((length, LANES), F32)
        out_basis = bcs_r[:, states:]
        for j in range(channels // LANES):
            at = slice(j * LANES, (j + 1) * LANES)
            v = dot(out_basis, low_o[0, at], NT)
            y = yi[:, at] + pair_spread(growth, j, length) * v + skip[:, at] * xs_r[:, at].astype(F32)
            y_o[:, at] = y
            gated = y * silu(z[:, at])
            squares += gated * gated
            crosses += dn[:, at] * gain[:, at] * gated
        sums_o[...] = jnp.concatenate(
            [jnp.sum(squares, axis=1, keepdims=True), jnp.sum(crosses, axis=1, keepdims=True)], axis=1
        )

    whole = lambda *dims: pl.BlockSpec(dims, lambda i: (0,) * len(dims))
    tokens = lambda n: pl.BlockSpec((length, n), lambda i: (i, 0))
    per = lambda *dims: pl.BlockSpec((1,) + dims, lambda i: (i, 0, 0))
    return call(
        kernel, "across_blocks", (count,),
        [tokens(channels), tokens(channels), tokens(both), tokens(channels), tokens(channels),
         tokens(heads), per(channels, states), per(heads, LANES), whole(channels, states),
         whole(1, channels), whole(1, channels)],
        [tokens(channels), per(channels, states), tokens(2)],
        [shape((rows, channels), F32), shape((count, channels, states), BF16), shape((rows, 2), F32)],
        [], 2 * rows * channels * states,
        (y_intra, xs, bcs, gate_pre, normed_grad, cum, hin0, pre, carry, skip_row, gate_gain),
        2 * rows * channels,
    )


def turn(y, gate_pre, normed_grad, xs, bcs, cum, sums, gate_gain, output_matrix, dec, length, shares):
    rows, channels = xs.shape
    heads = cum.shape[1]
    both = bcs.shape[1]
    states = both // 2
    wide = channels // heads
    count = rows // length
    width = output_matrix.shape[1]
    share = width // shares
    inner = channels * shares

    def kernel(y_r, z_r, dn_r, xs_r, bcs_r, cum_r, sums_r, gain, wo, dec_r,
               normed_o, part_o, dy_o, dz_o, dv_o, ab_o, ds_o, post_o, start_o, ggain_o,
               state, behind, prod_a, prod_b):
        i = pl.program_id(0)

        @pl.when(i == 0)
        def _():
            state[...] = jnp.zeros_like(state)
            behind[...] = jnp.ones_like(behind)
            ggain_o[...] = jnp.zeros_like(ggain_o)

        grstd = lax.rsqrt(sums_r[:, 0:1] / inner + EPSILON)
        cross = (grstd * grstd * grstd) * (sums_r[:, 1:2] / inner)
        growth = jnp.exp(cum_r[...])
        for j in range(channels // LANES):
            at = slice(j * LANES, (j + 1) * LANES)
            y, z, dn = y_r[:, at], z_r[:, at], dn_r[:, at]
            sigma = sigmoid(z)
            act = z * sigma
            gated = y * act
            scaled = gated * grstd
            normed_o[:, at] = (scaled * gain[:, at]).astype(BF16)
            ggain_o[:, at] += jnp.sum(dn * scaled, axis=0, keepdims=True)
            dgated = grstd * (dn * gain[:, at]) - gated * cross
            dy = (dgated * act).astype(BF16)
            dy_o[:, at] = dy
            dz_o[:, at] = (dgated * y * (sigma * (1.0 + z * (1.0 - sigma)))).astype(BF16)
            plain = dy.astype(F32)
            dv_o[:, at] = (plain * pair_spread(growth, j, length)).astype(BF16)
            prod_a[:, at] = plain * y
            prod_b[:, at] = plain * xs_r[:, at].astype(F32)
        picker = head_picker(channels, heads)
        ab_o[:, :heads] = dot_split(prod_a[...], picker)
        ab_o[:, heads:] = dot_split(prod_b[...], picker)
        for q in range(shares):
            at = slice(q * share, (q + 1) * share)
            part_o[q] = dot(normed_o[...], wo[:, at]).astype(BF16)
        dhin = dot(dv_o[...], bcs_r[:, states:], TN)
        ds_o[0] = state[...]
        post_o[0] = behind[...]
        behind[...] = behind[...] * dec_r[0]
        for h in range(heads):
            at = slice(h * wide, (h + 1) * wide)
            state[at] = dec_r[0, h : h + 1] * state[at] + dhin[at]
        start_o[...] = state[...].astype(BF16)

    last = count - 1
    whole = lambda *dims: pl.BlockSpec(dims, lambda i: (0,) * len(dims))
    tokens = lambda n: pl.BlockSpec((length, n), lambda i: (last - i, 0))
    per = lambda *dims: pl.BlockSpec((1,) + dims, lambda i: (last - i, 0, 0))
    return call(
        kernel, "gate_and_turn", (count,),
        [tokens(channels), tokens(channels), tokens(channels), tokens(channels), tokens(both),
         tokens(heads), tokens(2), whole(1, channels), whole(channels, width), per(heads, LANES)],
        [tokens(channels), pl.BlockSpec((shares, length, share), lambda i: (0, last - i, 0)),
         tokens(channels), tokens(channels), tokens(channels), tokens(2 * heads), per(channels, states), per(heads, LANES), whole(channels, states),
         whole(1, channels)],
        [shape((rows, channels), BF16), shape((shares, rows, share), BF16), shape((rows, channels), BF16),
         shape((rows, channels), BF16), shape((rows, channels), BF16), shape((rows, 2 * heads), F32),
         shape((count, channels, states), F32), shape((count, heads, LANES), F32),
         shape((channels, states), BF16), shape((1, channels), F32)],
        [pltpu.VMEM((channels, states), F32), pltpu.VMEM((heads, LANES), F32),
         pltpu.VMEM((length, channels), F32), pltpu.VMEM((length, channels), F32)],
        2 * rows * channels * (width + states),
        (y, gate_pre, normed_grad, xs, bcs, cum, sums, gate_gain, output_matrix, dec),
        rows * channels,
    )


def intra_back(bcs, xdt, dy, cum, cumt, length):
    rows, channels = xdt.shape
    heads = cum.shape[1]
    both = bcs.shape[1]
    states = both // 2
    half = length // 2

    def kernel(bcs_r, xdt_r, dy_r, cum_r, cumt_r, g_o, dbc_o, grad):
        scores = lower_scores(bcs_r[...], states, length)
        cum_v, cumt_v = cum_r[...], cumt_r[...]
        lane = lax.broadcasted_iota(jnp.int32, (length, LANES), 1)
        grad[...] = jnp.zeros_like(grad)
        for j in range(heads // 2):
            at = slice(j * LANES, (j + 1) * LANES)
            pair, dpair = xdt_r[:, at], dy_r[:, at]
            g_top = jnp.zeros((half, LANES), F32)
            g_low = jnp.zeros((half, LANES), F32)
            for s in range(2):
                own = jnp.where((lane < LANES // 2) == (s == 0), dpair, jnp.zeros_like(dpair))
                top, low = decays(cum_v, cumt_v, 2 * j + s, half)
                grad[:half, :half] += dot(own[:half], pair[:half], NT) * top
                grad[half:] += dot(own[half:], pair, NT) * low
                w_top = (scores[:half, :half] * top).astype(BF16)
                w_low = (scores[half:] * low).astype(BF16)
                g_top += dot(w_top, own[:half], TN) + dot(w_low[:, :half], own[half:], TN)
                g_low += dot(w_low[:, half:], own[half:], TN)
            g_o[:half, at] = g_top
            g_o[half:, at] = g_low
        masked = jnp.where(ones_where((length, length), lambda r, c: r >= c), grad[...], 0.0)
        high = masked.astype(BF16)
        rest = (masked - high.astype(F32)).astype(BF16)
        in_b, out_b = bcs_r[:, :states], bcs_r[:, states:]
        dbc_o[:, :states] = dot(high, out_b, TN) + dot(rest, out_b, TN)
        dbc_o[:, states:] = dot(high, in_b) + dot(rest, in_b)

    tokens = lambda n: pl.BlockSpec((length, n), lambda i: (i, 0))
    return call(
        kernel, "within_blocks_back", (rows // length,),
        [tokens(both), tokens(channels), tokens(channels), tokens(heads),
         pl.BlockSpec((heads, length), lambda i: (0, i))],
        [tokens(channels), tokens(both)],
        [shape((rows, channels), F32), shape((rows, both), F32)],
        [pltpu.VMEM((length, length), F32)],
        2 * rows * length * channels * 8, (bcs, xdt, dy, cum, cumt), rows * length * heads,
    )


def finish_back(value_pre, value_edge, value_kernel, value_bias, xs, xdt, xw, g, dy, dv, bcs, step_pre, dt,
                cum, ab, hin0, pre, carry, hin_low, ds0, post, back, dec, dbc_intra, skip_row, skip_gain,
                step_bias, log_rate, length):
    rows, channels = xs.shape
    heads = cum.shape[1]
    both = bcs.shape[1]
    states = both // 2
    wide = channels // heads
    count = rows // length
    taps = value_kernel.shape[0]
    unit = length // EDGE

    def kernel(xr, xr_before, xr_edge, vk, vb, xs_r, xdt_r, xw_r, g_r, dy_r, dv_r, bcs_r, dtr, dt_r, cum_r,
               ab_r, hin_r, pre_r, carry_r, low_r, ds_r, post_r, back_r, dec_r, dbci, skip, skipg, tb,
               lr, dxr_o, tail_o, head_o, vkg_o, vbg_o, ddtr_o, dbc_o, small_o,
               padded, ext, ds_low, inner_sums):
        i = pl.program_id(0)
        block = count - 1 - i

        @pl.when(i == 0)
        def _():
            vkg_o[...] = jnp.zeros_like(vkg_o)
            vbg_o[...] = jnp.zeros_like(vbg_o)
            small_o[...] = jnp.zeros_like(small_o)
            ext[0:EDGE] = jnp.zeros((EDGE, channels), F32)

        @pl.when(block == 0)
        def _():
            padded[0:EDGE] = xr_edge[...]

        @pl.when(block > 0)
        def _():
            padded[0:EDGE] = xr_before[...]

        padded[EDGE:] = xr[...]
        ext[length:] = ext[0:EDGE]
        for h in range(heads):
            at = slice(h * wide, (h + 1) * wide)
            ds = ds_r[0, at] + post_r[0, h : h + 1] * back_r[at].astype(F32)
            ds_low[at] = ds.astype(BF16)
            hin = hin_r[0, at] + pre_r[0, h : h + 1] * carry_r[at].astype(F32)
            inner_sums[h : h + 1] = jnp.sum(ds * hin, axis=0, keepdims=True) * dec_r[0, h : h + 1]
        in_b = bcs_r[:, :states]
        dt_v, cum_v = dt_r[...], cum_r[...]
        fade = jnp.exp(cum_v[length - 1 : length] - cum_v)
        factor = fade * dt_v
        start = EDGE - taps + 1
        picker = head_picker(channels, heads)
        c_sum = jnp.zeros((length, heads), F32)
        d_sum = jnp.zeros((length, heads), F32)
        w_sum = jnp.zeros((length, heads), F32)
        for j in range(channels // LANES):
            at = slice(j * LANES, (j + 1) * LANES)
            xs_v = xs_r[:, at].astype(F32)
            dxw = dot(in_b, ds_low[at], NT)
            g_v = g_r[:, at]
            c_sum += dot_split(xs_v * g_v, picker[at])
            d_sum += dot_split(xs_v * dxw, picker[at])
            w_sum += dot_split(xdt_r[:, at].astype(F32) * g_v, picker[at])
            dxs = (
                pair_spread(dt_v, j, length) * g_v
                + pair_spread(factor, j, length) * dxw
                + skip[:, at] * dy_r[:, at].astype(F32)
            )
            total = vb[:, at] + vk[0:1, at] * padded[pl.ds(start, length), at]
            for k in range(1, taps):
                total = total + vk[k : k + 1, at] * padded[pl.ds(start + k, length), at]
            dpre = dxs * slope(total)
            ext[0:length, at] = dpre
            vbg_o[:, at] += jnp.sum(dpre, axis=0, keepdims=True)
            for k in range(taps):
                vkg_o[k : k + 1, at] += jnp.sum(
                    dpre * padded[pl.ds(start + k, length), at], axis=0, keepdims=True
                )
            dxr = vk[0:1, at] * ext[pl.ds(taps - 1, length), at]
            for k in range(1, taps):
                dxr = dxr + vk[k : k + 1, at] * ext[pl.ds(taps - 1 - k, length), at]
            dxr_o[:, at] = dxr.astype(BF16)

            @pl.when(i == 0)
            def _():
                tail_o[:, at] = dxr[length - EDGE :]

        head_o[...] = ext[0:EDGE]
        dbc_o[:, :states] = dbci[:, :states] + dot(xw_r[...], ds_low[...])
        dbc_o[:, states:] = dbci[:, states:] + dot(dv_r[...], low_r[0])
        rate = -jnp.exp(lr[...])
        a_sum, b_sum = ab_r[:, :heads], ab_r[:, heads:]
        e_sum = d_sum * factor
        ones = jnp.ones((1, LANES), F32)
        dtotal = jnp.sum(e_sum, axis=0, keepdims=True) + dot(ones, inner_sums[...], NT, precision=HIGH)
        row = lax.broadcasted_iota(jnp.int32, (length, heads), 0)
        dcum = a_sum - skipg[...] * b_sum - w_sum - e_sum
        dcum = dcum + jnp.where(row == length - 1, dtotal, 0.0)
        upper = ones_where((length, length), lambda r, c: r <= c).astype(F32)
        dda = dot(upper, dcum, precision=HIGH)
        ddt = c_sum + d_sum * fade + dda * rate
        dpre_dt = ddt * sigmoid(dtr[...] + tb[...])
        ddtr_o[...] = dpre_dt.astype(BF16)
        small_o[0:1] += jnp.sum(dpre_dt, axis=0, keepdims=True)
        small_o[1:2] += jnp.sum(dda * dt_v, axis=0, keepdims=True) * rate
        small_o[2:3] += jnp.sum(b_sum, axis=0, keepdims=True)

    last = count - 1
    whole = lambda *dims: pl.BlockSpec(dims, lambda i: (0,) * len(dims))
    tokens = lambda n: pl.BlockSpec((length, n), lambda i: (last - i, 0))
    before = lambda n: pl.BlockSpec((EDGE, n), lambda i: (jnp.maximum((last - i) * unit - 1, 0), 0))
    per = lambda *dims: pl.BlockSpec((1,) + dims, lambda i: (last - i, 0, 0))
    return call(
        kernel, "across_blocks_back", (count,),
        [tokens(channels), before(channels), whole(EDGE, channels), whole(taps, channels),
         whole(1, channels), tokens(channels), tokens(channels), tokens(channels), tokens(channels),
         tokens(channels), tokens(channels), tokens(both), tokens(heads), tokens(heads), tokens(heads),
         tokens(2 * heads), per(channels, states), per(heads, LANES), whole(channels, states),
         per(channels, states), per(channels, states), per(heads, LANES), whole(channels, states),
         per(heads, LANES), tokens(both), whole(1, channels), whole(1, heads), whole(1, heads),
         whole(1, heads)],
        [tokens(channels), whole(EDGE, channels), whole(EDGE, channels), whole(taps, channels),
         whole(1, channels), tokens(heads), tokens(both), whole(EDGE, heads)],
        [shape((rows, channels), BF16), shape((EDGE, channels), F32), shape((EDGE, channels), F32),
         shape((taps, channels), F32), shape((1, channels), F32), shape((rows, heads), BF16),
         shape((rows, both), F32), shape((EDGE, heads), F32)],
        [pltpu.VMEM((length + EDGE, channels), F32), pltpu.VMEM((length + EDGE, channels), F32),
         pltpu.VMEM((channels, states), BF16), pltpu.VMEM((heads, LANES), F32)],
        2 * rows * channels * states * 3,
        (value_pre, value_pre, value_edge, value_kernel, value_bias, xs, xdt, xw, g, dy, dv, bcs, step_pre,
         dt, cum, ab, hin0, pre, carry, hin_low, ds0, post, back, dec, dbc_intra, skip_row, skip_gain,
         step_bias, log_rate),
        2 * rows * channels,
    )


def halves(normal_in, grad, outer):
    rows, width = normal_in.shape
    channels = grad.shape[1]
    strip = width // (2 * outer)

    def kernel(xn, grad_r, keep_o, give_o):
        side = lax.rem(lax.axis_index("seq"), 2)
        product = dot(xn[...], grad_r[...], TN).astype(BF16)

        @pl.when(side == 0)
        def _():
            keep_o[0] = product[:strip]
            give_o[0] = product[strip:]

        @pl.when(side == 1)
        def _():
            keep_o[0] = product[strip:]
            give_o[0] = product[:strip]

    out = pl.BlockSpec((1, strip, channels), lambda i: (i, 0, 0))
    return call(
        kernel, "gate_strips", (outer,),
        [pl.BlockSpec((rows, 2 * strip), lambda i: (0, i)),
         pl.BlockSpec((rows, channels), lambda i: (0, 0))],
        [out, out], [shape((outer, strip, channels), BF16)] * 2, [], 2 * rows * width * channels,
        (normal_in, grad),
    )


def remote(src, dst, send, recv, seq, head):
    return pltpu.make_async_remote_copy(
        src_ref=src, dst_ref=dst, send_sem=send, recv_sem=recv, device_id=(seq, head),
        device_id_type=pl.DeviceIdType.MESH,
    )


def greet(seq, head, seq_size, head_size):
    barrier = pltpu.get_barrier_semaphore()
    for d in range(1, seq_size):
        pl.semaphore_signal(
            barrier, inc=1, device_id=(lax.rem(seq + d, seq_size), head),
            device_id_type=pl.DeviceIdType.MESH,
        )
    for d in range(1, head_size):
        pl.semaphore_signal(
            barrier, inc=1, device_id=(seq, lax.rem(head + d, head_size)),
            device_id_type=pl.DeviceIdType.MESH,
        )
    pl.semaphore_wait(barrier, seq_size - 1 + head_size - 1)


def closing(normal_in, dz, dxr, tail, head_rows, gate_matrix, value_matrix, state_matrix, step_matrix,
            value_kernel, state_kernel, state_bias, state_pre, state_edge, dbc, ddtr, vectors, small,
            part, mine, rstd, gain_share, gate_half, length, seq_size, head_size):
    rows, width = normal_in.shape
    channels = dz.shape[1]
    heads = ddtr.shape[1]
    both = dbc.shape[1]
    share = mine.shape[1]
    taps = value_kernel.shape[0]
    members = rows // length
    outer = seq_size // 2
    half_heads = head_size // 2
    strip = width // seq_size
    chunk = rows // head_size
    per = head_size // members
    piece = share // seq_size
    piece_type = BF16 if piece % 16 == 0 else F32
    packed = channels + both + LANES
    groups = seq_size // members

    def kernel(xn, dz_r, dxr_h, tail_r, head_r, gate_h, value_h, state_m, step_m, vk, sk, sb, bc_h,
               bc_edge, dbc_h, ddtr_r, vec, small_r, part_h, mine_r, rstd_r, gain, half_h,
               gate_o, value_o, state_o, step_o, vec_o, norm_o, up_o, branch_o,
               dxr_r, duo, xrecv, zrecv, gown, grecv, weights, weight, csend, cown, crecv, yrecv, rsend,
               rrecv, up, nsend, nrecv,
               pown, precv, pyrecv, drecv, dsum, ext, hrecv, hbrecv, low, spart, srecv, ssum, sall,
               tsend, trecv, vsend, vrecv,
               xs_sem, xr_sem, zs_sem, zr_sem, cs_sem, cr_sem, ys_sem, yr_sem, rs_sem, rr_sem,
               us_sem, ur_sem, ns_sem, nr_sem, ps_sem, pr_sem, pys_sem, pyr_sem, ds_sem, dr_sem,
               as_sem, ar_sem, h_sem, hb_sem, ss_sem, sr_sem, sas_sem, sar_sem, ts_sem, tr_sem,
               vs_sem, vr_sem, bs_sem, br_sem, gs_sem, gr_sem, w_sem, copy_sem):
        seq, head = lax.axis_index("seq"), lax.axis_index("head")
        place, side = seq // 2, lax.rem(seq, 2)
        lane, core = head // 2, lax.rem(head, 2)
        group, member = seq // members, lax.rem(seq, members)
        base = seq - member
        load_dxr = pltpu.make_async_copy(dxr_h, dxr_r, copy_sem.at[0])
        load_dxr.start()
        load_bc = pltpu.make_async_copy(bc_h, low.at[pl.ds(EDGE, rows)], copy_sem.at[1 + half_heads])
        load_bc.start()
        low[0:EDGE] = bc_edge[...]

        def outer_at(k):
            return lax.rem(place + 1 + k, outer)

        def lane_at(k):
            return lax.rem(lane + 1 + k, half_heads)

        def seq_at(d):
            return lax.rem(seq + d, seq_size)

        def head_at(d):
            return lax.rem(head + d, head_size)

        loads = [
            pltpu.make_async_copy(part_h.at[2 * lane_at(k) + core], pown.at[k], copy_sem.at[1 + k])
            for k in range(half_heads)
        ]
        for load in loads:
            load.start()
        own_rows = pl.ds(pl.multiple_of(head * chunk, chunk), chunk)
        load_dbc = pltpu.make_async_copy(
            dbc_h.at[own_rows], dsum.at[own_rows], copy_sem.at[2 + half_heads]
        )
        load_dbc.start()
        load_half = pltpu.make_async_copy(half_h.at[place], gown, copy_sem.at[3 + half_heads])
        load_half.start()
        greet(seq, head, seq_size, head_size)

        def cross(k):
            return remote(duo.at[k, 1 - side], xrecv.at[k], xs_sem.at[k], xr_sem.at[k],
                          2 * place + 1 - side, head)

        def along(k):
            return remote(duo.at[k, side], zrecv.at[k], zs_sem.at[k], zr_sem.at[k],
                          2 * outer_at(k) + side, head)

        def along_gate(k):
            return remote(half_h.at[outer_at(k)], grecv.at[k], gs_sem.at[k], gr_sem.at[k],
                          2 * outer_at(k) + side, head)

        def edge_back(src, dst, sems):
            return remote(src, dst, sems.at[0], sems.at[1], seq - members, head)

        def part_core(k):
            return remote(part_h.at[2 * lane_at(k) + 1 - core], precv.at[k], ps_sem.at[k], pr_sem.at[k],
                          seq, 2 * lane + 1 - core)

        def part_lane(k):
            return remote(pown.at[k], pyrecv.at[k], pys_sem.at[k], pyr_sem.at[k],
                          seq, 2 * lane_at(k) + core)

        def rows_of(c):
            return pl.ds(pl.multiple_of(c * chunk, chunk), chunk)

        def basis_sum(d):
            return remote(dbc_h.at[rows_of(head_at(d))], drecv.at[d - 1], ds_sem.at[d - 1],
                          dr_sem.at[d - 1], seq, head_at(d))

        def basis_share(d):
            at = rows_of(head)
            return remote(dsum.at[at], dsum.at[at], as_sem.at[d - 1], ar_sem.at[d - 1], seq, head_at(d))

        @pl.when(group > 0)
        def _():
            edge_back(head_r, hrecv, h_sem).start()

        for d in range(1, head_size):
            basis_sum(d).start()
        for k in range(half_heads):
            part_core(k).start()

        for k in range(outer - 1):
            along_gate(k).start()

        load_dxr.wait()
        ext[...] = jnp.zeros_like(ext)

        @pl.when(group < groups - 1)
        def _():
            remote(head_r, hrecv, h_sem.at[0], h_sem.at[1], seq, head).wait_recv()
            ext[EDGE:] = hrecv[...]

        fixed = tail_r[...]
        for k in range(taps):
            fixed = fixed + vk[k : k + 1] * ext[pl.ds(taps - 1 - k, EDGE)]
        last = dxr_r[rows - 2 * EDGE :].astype(F32)
        dxr_r[rows - 2 * EDGE :] = jnp.concatenate([last[:EDGE], fixed], axis=0).astype(BF16)

        def multiply(k, _):
            at = pl.ds(pl.multiple_of(outer_at(k) * 2 * strip, 2 * strip), 2 * strip)
            product = dot(xn[:, at], dxr_r[...], TN).astype(BF16)
            duo[k, 0] = product[:strip]
            duo[k, 1] = product[strip:]
            cross(k).start()
            return 0

        lax.fori_loop(0, outer, multiply, 0)

        load_dbc.wait()
        total = dsum[own_rows]
        for d in range(1, head_size):
            basis_sum(d).wait_recv()
            total = total + drecv[d - 1]
        dsum[own_rows] = total
        for d in range(1, head_size):
            basis_share(d).start()

        tsend_v = dot(ddtr_r[...], xn[...], TN)
        for o in range(outer):
            tsend[o] = tsend_v[:, o * 2 * strip : (o + 1) * 2 * strip]

        def step_piece(d):
            return remote(tsend.at[seq_at(d) // 2], trecv.at[d - 1], ts_sem.at[d - 1], tr_sem.at[d - 1],
                          seq_at(d), head)

        for d in range(1, seq_size):
            step_piece(d).start()

        def arrived(k, send=True):
            cross(k).wait_recv()
            duo[k, side] = (duo[k, side].astype(F32) + xrecv[k].astype(F32)).astype(BF16)
            if send:
                along(k).start()

        def arrived_loop(first, last):
            def one(k, _):
                arrived(k)
                return 0

            lax.fori_loop(first, last, one, 0)

        for k in range(half_heads):
            loads[k].wait()
            part_core(k).wait_recv()
            for r in range(members):
                at = slice(r * length, (r + 1) * length)
                pown[k, at] = (pown[k, at].astype(F32) + precv[k, at].astype(F32)).astype(BF16)
            if k < half_heads - 1:
                part_lane(k).start()

        for d in range(1, head_size):
            at = rows_of(head_at(d))
            remote(dsum.at[at], dsum.at[at], as_sem.at[d - 1], ar_sem.at[head_size - 1 - d],
                   seq, head).wait_recv()

        start = EDGE - taps + 1
        load_bc.wait()
        pre_bc = sb[...]
        for k in range(taps):
            pre_bc = pre_bc + sk[k : k + 1] * low[pl.ds(start + k, rows)]
        dpre = dsum[...] * slope(pre_bc)
        vsend[...] = jnp.zeros_like(vsend)
        vsend[:, :channels] = vec[...]
        vsend[:, channels + both : channels + both + heads] = small_r[...]
        for k in range(taps):
            vsend[k : k + 1, channels : channels + both] = jnp.sum(
                dpre * low[pl.ds(start + k, rows)], axis=0, keepdims=True
            )
        vsend[taps : taps + 1, channels : channels + both] = jnp.sum(dpre, axis=0, keepdims=True)
        low[0:rows] = dpre
        low[rows:] = jnp.zeros((EDGE, both), F32)

        @pl.when(group > 0)
        def _():
            edge_back(low.at[pl.ds(0, EDGE)], hbrecv, hb_sem).start()

        def vector(d):
            return remote(vsend, vrecv.at[d - 1], vs_sem.at[d - 1], vr_sem.at[d - 1], seq_at(d), head)

        for d in range(1, seq_size):
            vector(d).start()
        arrived_loop(0, outer // 4)

        @pl.when(group < groups - 1)
        def _():
            remote(low.at[pl.ds(0, EDGE)], hbrecv, hb_sem.at[0], hb_sem.at[1], seq, head).wait_recv()
            low[rows:] = hbrecv[...]

        dbc_v = sk[0:1] * low[pl.ds(taps - 1, rows)]
        for k in range(1, taps):
            dbc_v = dbc_v + sk[k : k + 1] * low[pl.ds(taps - 1 - k, rows)]
        dbc_low = dbc_v.astype(BF16)
        own_at = pl.ds(pl.multiple_of(head * share, share), share)
        own_state = dot(xn[:, own_at], dbc_low, TN)
        for s in range(seq_size):
            spart[s] = own_state[s * piece : (s + 1) * piece].astype(piece_type)
        for d in range(1, head_size):
            basis_share(d).wait_send()
        dsum[...] = dbc_low.astype(F32)

        def state_piece(d):
            return remote(spart.at[seq_at(d)], srecv.at[d - 1], ss_sem.at[d - 1], sr_sem.at[d - 1],
                          seq_at(d), head)

        for d in range(1, seq_size):
            state_piece(d).start()

        def to_core(k):
            return remote(csend.at[k], crecv.at[k], cs_sem.at[k], cr_sem.at[k], seq, 2 * lane + 1 - core)

        def to_lane(k):
            return remote(cown.at[k], yrecv.at[k], ys_sem.at[k], yr_sem.at[k],
                          seq, 2 * lane_at(k) + core)

        def columns_of(step):
            which = 1 - core if step < half_heads else core
            at = (2 * lane_at(step % half_heads) + which) * share
            return pl.ds(pl.multiple_of(at, share), share)

        def fetch(step):
            at, slot = columns_of(step), step % 2
            return [
                pltpu.make_async_copy(gate_h.at[at], weights.at[slot, 0], w_sem.at[slot, 0]),
                pltpu.make_async_copy(value_h.at[at], weights.at[slot, 1], w_sem.at[slot, 1]),
            ]

        for step in range(head_size):
            slot, at, k = step % 2, columns_of(step), step % half_heads
            keep = csend if step < half_heads else cown
            if step == 0:
                for load in fetch(0):
                    load.start()
            if step < head_size - 1:
                for load in fetch(step + 1):
                    load.start()
            for load in fetch(step):
                load.wait()

            def back_rows(c, _, slot=slot, at=at, k=k, keep=keep, first=step == 0):
                at_rows = rows_of(c)
                basis = jnp.where(c == head, dsum[at_rows], 0.0).astype(BF16)
                grad = (
                    dot(dz_r[at_rows], weights[slot, 0], NT) + dot(dxr_r[at_rows], weights[slot, 1], NT)
                    + dot(basis, state_m[at], NT) + dot(ddtr_r[at_rows], step_m[at], NT)
                )
                keep[k, at_rows] = grad.astype(BF16)
                weighed = grad * xn[at_rows, at].astype(F32)
                total = weighed[:, :LANES] if first else weight[at_rows] + weighed[:, :LANES]
                for q in range(1, share // LANES):
                    total += weighed[:, q * LANES : (q + 1) * LANES]
                weight[at_rows] = total
                return 0

            lax.fori_loop(0, head_size, back_rows, 0)
            if step < half_heads:
                to_core(k).start()
            else:
                to_core(k).wait_recv()

                def add_rows(c, _, k=k):
                    at_rows = rows_of(c)
                    cown[k, at_rows] = (
                        cown[k, at_rows].astype(F32) + crecv[k, at_rows].astype(F32)
                    ).astype(BF16)
                    return 0

                lax.fori_loop(0, head_size, add_rows, 0)
                if k < half_heads - 1:
                    to_lane(k).start()
            if step == 0:
                arrived_loop(outer // 4, outer // 2)
            if step == head_size - 2:
                arrived_loop(outer // 2, outer - 1)

        rsend[...] = dot(jnp.ones((8, LANES), F32), weight[...], NT, precision=HIGH)

        def row_sums(d):
            return remote(rsend, rrecv.at[d - 1], rs_sem.at[d - 1], rr_sem.at[d - 1], seq, head_at(d))

        for d in range(1, head_size):
            row_sums(d).start()

        state_sum = spart[seq].astype(F32)
        for d in range(1, seq_size):
            state_piece(d).wait_recv()
            state_sum = state_sum + srecv[d - 1].astype(F32)
        sall[seq] = state_sum.astype(piece_type)

        def state_share(d):
            return remote(sall.at[seq], sall.at[seq], sas_sem.at[d - 1], sar_sem.at[d - 1],
                          seq_at(d), head)

        for d in range(1, seq_size):
            state_share(d).start()
        def give(src, out, r, sems_s, sems_r):
            return remote(src.at[r], out.at[member], sems_s.at[r], sems_r.at[member], base + r, head)

        for k in range(half_heads - 1):
            part_lane(k).wait_recv()
        for r in range(members):
            at = slice(r * length, (r + 1) * length)
            total = pown[half_heads - 1, at].astype(F32)
            for k in range(half_heads - 1):
                total = total + pyrecv[k, at].astype(F32)
            precv[0, at] = total.astype(BF16)

        def branch_rows(r):
            return precv.at[0, pl.ds(r * length, length)]

        for r in range(members):
            @pl.when(r != member)
            def _(r=r):
                remote(branch_rows(r), branch_o.at[member], bs_sem.at[r], br_sem.at[member],
                       base + r, head).start()

            @pl.when(r == member)
            def _(r=r):
                pltpu.make_async_copy(branch_rows(r), branch_o.at[r], copy_sem.at[0]).start()

        arrived(outer - 1, False)
        for d in range(1, head_size):
            row_sums(d).wait_recv()
        sums = rsend[...]
        for d in range(1, head_size):
            sums = sums + rrecv[d - 1]
        pick = (lax.broadcasted_iota(jnp.int32, (8, LANES), 0) == 0).astype(F32)
        nsend[...] = jnp.zeros_like(nsend)
        rrecv[0] = sums * (1.0 / width)
        for k in range(half_heads - 1):
            to_lane(k).wait_recv()

        def finish_rows(c, _):
            at_rows = rows_of(c)
            grad = cown[half_heads - 1, at_rows].astype(F32)
            for k in range(half_heads - 1):
                grad = grad + yrecv[k, at_rows].astype(F32)
            scale = rstd_r[at_rows]
            hat = mine_r[at_rows].astype(F32) * scale
            mean = dot(rrecv[0, :, at_rows], pick, TN, precision=HIGH)
            nsend[0:1] += jnp.sum(grad * hat, axis=0, keepdims=True)
            inside = pl.ds(pl.multiple_of(lax.rem(c, per) * chunk, chunk), chunk)
            for q in range(share // LANES):
                at = slice(q * LANES, (q + 1) * LANES)
                up[c // per, inside, at] = (
                    scale * (grad[:, at] * gain[:, at] - hat[:, at] * mean)
                ).astype(BF16)
            return 0

        lax.fori_loop(0, head_size, finish_rows, 0)
        for r in range(members):
            @pl.when(r != member)
            def _(r=r):
                give(up, up_o, r, us_sem, ur_sem).start()

        keep_up = pltpu.make_async_copy(up.at[member], up_o.at[member], copy_sem.at[1])
        keep_up.start()

        def share_norm(d):
            return remote(nsend, nrecv.at[d - 1], ns_sem.at[d - 1], nr_sem.at[d - 1], seq_at(d), head)

        for d in range(1, seq_size):
            share_norm(d).start()

        vectors_sum = vsend[...]
        step_sum = tsend[place]
        for d in range(1, seq_size):
            vector(d).wait_recv()
            vectors_sum = vectors_sum + vrecv[d - 1]
            step_piece(d).wait_recv()
            step_sum = step_sum + trecv[d - 1]
        vec_o[...] = vectors_sum
        step_o[...] = step_sum
        for d in range(1, seq_size):
            source = seq_at(d)
            remote(sall.at[source], sall.at[source], sas_sem.at[d - 1], sar_sem.at[seq_size - 1 - d],
                   seq, head).wait_recv()
        state_o[...] = sall[...].astype(F32)

        def settle(out, own, copy, landed):
            def one(k, total):
                copy(k).wait_recv()
                return total + landed[k].astype(F32)

            out[...] = lax.fori_loop(0, outer - 1, one, own.astype(F32))

        load_half.wait()
        settle(gate_o, gown[...], along_gate, grecv)
        norm = nsend[...]
        for d in range(1, seq_size):
            share_norm(d).wait_recv()
            norm = norm + nrecv[d - 1]
        norm_o[...] = norm
        settle(value_o, duo[outer - 1, side], along, zrecv)

        for r in range(members):
            @pl.when(r != member)
            def _(r=r):
                remote(up.at[r], up_o.at[r], us_sem.at[r], ur_sem.at[r], base + r, head).wait()
                remote(branch_rows(r), branch_o.at[r], bs_sem.at[r], br_sem.at[r], base + r, head).wait()

            @pl.when(r == member)
            def _(r=r):
                pltpu.make_async_copy(branch_rows(r), branch_o.at[r], copy_sem.at[0]).wait()

        keep_up.wait()

        def drain(k, _):
            cross(k).wait_send()
            return 0

        def drain_along(k, _):
            along(k).wait_send()
            along_gate(k).wait_send()
            return 0

        lax.fori_loop(0, outer, drain, 0)
        lax.fori_loop(0, outer - 1, drain_along, 0)
        for k in range(half_heads):
            to_core(k).wait_send()
            if k < half_heads - 1:
                to_lane(k).wait_send()

        @pl.when(group > 0)
        def _():
            edge_back(head_r, hrecv, h_sem).wait_send()
            edge_back(low.at[pl.ds(0, EDGE)], hbrecv, hb_sem).wait_send()

        for k in range(half_heads):
            part_core(k).wait_send()
            if k < half_heads - 1:
                part_lane(k).wait_send()
        for d in range(1, head_size):
            row_sums(d).wait_send()
            basis_sum(d).wait_send()
        for d in range(1, seq_size):
            share_norm(d).wait_send()
            vector(d).wait_send()
            step_piece(d).wait_send()
            state_piece(d).wait_send()
            state_share(d).wait_send()

    vmem = pl.BlockSpec(memory_space=pltpu.VMEM)
    anywhere = pl.BlockSpec(memory_space=pl.ANY)
    dma = pltpu.SemaphoreType.DMA
    args = (normal_in, dz, dxr, tail, head_rows, gate_matrix, value_matrix, state_matrix, step_matrix,
            value_kernel, state_kernel, state_bias, state_pre, state_edge, dbc, ddtr, vectors, small,
            part, mine, rstd, gain_share, gate_half)
    far = {2, 5, 6, 12, 14, 18, 22}
    moves = lambda *dims: pltpu.VMEM(dims, BF16)
    plain = lambda *dims: pltpu.VMEM(dims, F32)
    return pl.pallas_call(
        kernel,
        in_specs=[anywhere if i in far else vmem for i in range(len(args))],
        out_specs=[vmem] * 6 + [anywhere, anywhere],
        out_shape=[
            shape((strip, channels), F32), shape((strip, channels), F32),
            shape((seq_size, piece, both), F32), shape((heads, 2 * strip), F32),
            shape((8, packed), F32), shape((8, share), F32),
            shape((members, length, share), BF16), shape((members, length, share), BF16),
        ],
        scratch_shapes=[
            moves(rows, channels), moves(outer, 2, strip, channels), moves(outer, strip, channels),
            moves(outer - 1, strip, channels), moves(strip, channels),
            moves(outer - 1, strip, channels), moves(2, 2, share, channels), plain(rows, LANES),
            moves(half_heads, rows, share), moves(half_heads, rows, share),
            moves(half_heads, rows, share), moves(half_heads - 1, rows, share),
            plain(8, rows), plain(head_size - 1, 8, rows), moves(members, length, share),
            plain(8, share), plain(seq_size - 1, 8, share),
            moves(half_heads, rows, share), moves(half_heads, rows, share),
            moves(half_heads - 1, rows, share),
            plain(head_size - 1, chunk, both), plain(rows, both), plain(2 * EDGE, channels),
            plain(EDGE, channels), plain(EDGE, both), plain(rows + EDGE, both),
            pltpu.VMEM((seq_size, piece, both), piece_type),
            pltpu.VMEM((seq_size - 1, piece, both), piece_type),
            plain(8, LANES),
            pltpu.VMEM((seq_size, piece, both), piece_type),
            plain(outer, heads, 2 * strip), plain(seq_size - 1, heads, 2 * strip),
            plain(8, packed), plain(seq_size - 1, 8, packed),
            dma((outer,)), dma((outer,)), dma((outer - 1,)), dma((outer - 1,)),
            dma((half_heads,)), dma((half_heads,)), dma((half_heads - 1,)), dma((half_heads - 1,)),
            dma((head_size - 1,)), dma((head_size - 1,)),
            dma((members,)), dma((members,)), dma((seq_size - 1,)), dma((seq_size - 1,)),
            dma((half_heads,)), dma((half_heads,)), dma((half_heads - 1,)), dma((half_heads - 1,)),
            dma((head_size - 1,)), dma((head_size - 1,)), dma((head_size - 1,)), dma((head_size - 1,)),
            dma((2,)), dma((2,)),
            dma((seq_size - 1,)), dma((seq_size - 1,)), dma((seq_size - 1,)), dma((seq_size - 1,)),
            dma((seq_size - 1,)), dma((seq_size - 1,)), dma((seq_size - 1,)), dma((seq_size - 1,)),
            dma((members,)), dma((members,)), dma((outer - 1,)), dma((outer - 1,)), dma((2, 2)),
            dma((4 + half_heads,)),
        ],
        compiler_params=pltpu.CompilerParams(
            collective_id=1, has_side_effects=True, vmem_limit_bytes=VMEM_BYTES
        ),
        cost_estimate=pl.CostEstimate(
            flops=60_000_000_000, bytes_accessed=300_000_000, transcendentals=0
        ),
        name="closing_sums",
    )(*args)

def shifted(block, axis, distance):
    devices = range(lax.axis_size(axis))
    route = [(i - distance, i) for i in devices if i - distance in devices]
    return lax.ppermute(block, axis, route)


def regroup(block):
    members = block.shape[0]
    count = lax.axis_size("seq")
    groups = [list(range(i, i + members)) for i in range(0, count, members)]
    return lax.all_to_all(block, "seq", 0, 0, axis_index_groups=groups, tiled=True)


def carried(part, decay, hops, distance):
    carry = shifted(part, "seq", distance)
    for _ in range(hops - 1):
        leaving = decay * carry.astype(F32) + part.astype(F32)
        carry = shifted(leaving.astype(BF16), "seq", distance)
    return carry


def summed_low(part, dim):
    low = part.astype(BF16)
    return lax.psum_scatter(low, "seq", scatter_dimension=dim, tiled=True).astype(F32)


def local(
    tokens,
    cotangent,
    norm_gain,
    gate_matrix,
    value_matrix,
    state_matrix,
    step_matrix,
    value_kernel,
    value_bias,
    state_kernel,
    state_bias,
    step_bias,
    log_rate,
    skip_gain,
    gate_gain,
    output_matrix,
):
    seq_count, length, share = tokens.shape
    hops = lax.axis_size("seq") // seq_count - 1
    width, channels = gate_matrix.shape
    heads = step_bias.shape[0]
    wide = channels // heads
    both = state_matrix.shape[1]
    taps = value_kernel.shape[0]
    rows = seq_count * length
    head_count = lax.axis_size("head")
    head_rank = lax.axis_index("head")
    row = lambda v: v.reshape(1, -1)

    mine = regroup(tokens)
    whole_in = lax.all_gather(mine, "head", axis=2, tiled=True).reshape(rows, width)
    mine = mine.reshape(rows, share)
    flat_cot = lax.all_gather(regroup(cotangent), "head", axis=2, tiled=True).reshape(rows, width)
    plain = whole_in.astype(F32)
    rstd = lax.rsqrt(jnp.mean(plain * plain, axis=-1, keepdims=True) + EPSILON)
    normal_in = (plain * rstd * norm_gain).astype(BF16)
    state_pre = dot(normal_in, state_matrix)
    step_pre = dot(normal_in, step_matrix)
    value_pre = dot(normal_in, value_matrix)
    gate_pre = dot(normal_in, gate_matrix)

    edge = shifted(
        jnp.concatenate([value_pre[rows - EDGE :], state_pre[rows - EDGE :]], axis=1), "seq", seq_count
    )
    value_edge, state_edge = edge[:, :channels], edge[:, channels:]
    xs, xdt, xw, bcs, dt, cum, cumt, hin0, pre, dec, ending = prepare(
        value_pre, value_edge, state_pre, state_edge, step_pre, value_kernel, row(value_bias),
        state_kernel, row(state_bias), row(step_bias), row(log_rate), length,
    )
    whole_decay = jnp.repeat(pre[-1] * dec[-1], wide, axis=0)
    carry = carried(ending, whole_decay, hops, seq_count)
    y_intra = intra(bcs, xdt, cum, cumt, length)
    normed_grad = dot(flat_cot, output_matrix, NT)
    skip_row = row(jnp.repeat(skip_gain, wide))
    y, hin_low, sums = finish(
        y_intra, xs, bcs, gate_pre, normed_grad, cum, hin0, pre, carry, skip_row, row(gate_gain), length
    )
    sums = lax.psum(sums, "head")
    normed, part, dy, dz, dv, ab, ds0, post, starting, gate_gain_part = turn(
        y, gate_pre, normed_grad, xs, bcs, cum, sums, row(gate_gain), output_matrix, dec, length, head_count
    )
    back = carried(starting, whole_decay, hops, -seq_count)
    output_partial = dot(normed, flat_cot, TN)
    seq_size = lax.axis_size("seq")
    gate_keep, gate_give = halves(normal_in, dz, seq_size // 2)
    gate_half = lax.ppermute(gate_give, "seq", [(i, i ^ 1) for i in range(seq_size)])
    gate_half = (gate_keep.astype(F32) + gate_half.astype(F32)).astype(BF16)
    g, dbc_intra = intra_back(bcs, xdt, dy, cum, cumt, length)
    dxr, tail, head_rows, value_kernel_part, value_bias_part, ddtr, dbc, small = finish_back(
        value_pre, value_edge, value_kernel, row(value_bias), xs, xdt, xw, g, dy, dv, bcs, step_pre, dt, cum,
        ab, hin0, pre, carry, hin_low, ds0, post, back, dec, dbc_intra, skip_row, row(skip_gain),
        row(step_bias), row(log_rate), length,
    )
    vectors = jnp.concatenate(
        [value_kernel_part, value_bias_part, gate_gain_part, jnp.zeros((2, channels), F32)], axis=0
    )
    gain_share = lax.dynamic_slice_in_dim(norm_gain, head_rank * share, share, 0)
    gate_grad, value_grad, state_grad, step_grad, sums_out, norm_grad, up, branch = closing(
        normal_in, dz, dxr, tail, head_rows, gate_matrix, value_matrix, state_matrix, step_matrix,
        value_kernel, state_kernel, row(state_bias), state_pre, state_edge, dbc, ddtr, vectors, small,
        part, mine, rstd, row(gain_share), gate_half, length, seq_size, head_count,
    )
    token_grad = cotangent.astype(F32) + up.astype(F32)
    layer_out = (tokens.astype(F32) + branch.astype(F32)).astype(BF16)
    output_grad = summed_low(output_partial, 1)
    strip = width // seq_size
    step_grad = lax.dynamic_slice_in_dim(
        step_grad, lax.rem(lax.axis_index("seq"), 2) * strip, strip, 1
    ).T
    state_sums = sums_out[:, channels : channels + both]
    small_sums = sums_out[:, channels + both : channels + both + heads]
    return (
        layer_out,
        token_grad,
        norm_grad[0],
        gate_grad,
        value_grad,
        state_grad.reshape(share, both),
        step_grad,
        sums_out[:taps, :channels],
        sums_out[taps, :channels],
        state_sums[:taps],
        state_sums[taps],
        small_sums[0],
        small_sums[1],
        small_sums[2],
        sums_out[taps + 1, :channels],
        output_grad,
    )


def solution(mesh):
    in_specs = (
        P(None, "seq", "head"),
        P(None, "seq", "head"),
        P(),
        P(None, "head"),
        P(None, "head"),
        P(),
        P(None, "head"),
        P(None, "head"),
        P("head"),
        P(),
        P(),
        P("head"),
        P("head"),
        P("head"),
        P("head"),
        P("head", None),
    )
    out_specs = (
        P(None, "seq", "head"),
        P(None, "seq", "head"),
        P("head"),
        P("seq", "head"),
        P("seq", "head"),
        P("head", None),
        P("seq", "head"),
        P(None, "head"),
        P("head"),
        P(),
        P(),
        P("head"),
        P("head"),
        P("head"),
        P("head"),
        P("head", "seq"),
    )
    return jax.shard_map(local, mesh=mesh, in_specs=in_specs, out_specs=out_specs, check_vma=False)
```

```python
import jax
import jax.numpy as jnp
from jax import lax
from jax.experimental import pallas as pl
from jax.experimental.pallas import tpu as pltpu
from jax.sharding import PartitionSpec as P

HIGH = lax.Precision.HIGHEST
EPSILON = 1e-05
F32 = jnp.float32
BF16 = jnp.bfloat16
LANES = 128
EDGE = 8
VMEM_BYTES = 56 * 1024 * 1024

NN = (((1,), (0,)), ((), ()))
NT = (((1,), (1,)), ((), ()))
TN = (((0,), (0,)), ((), ()))


def dot(a, b, dims=NN, precision=None):
    return lax.dot_general(a, b, dims, precision=precision, preferred_element_type=F32)


def dot_split(a, b, dims=NN):
    high = a.astype(BF16)
    rest = (a - high.astype(F32)).astype(BF16)
    return dot(high, b, dims) + dot(rest, b, dims)


def sigmoid(v):
    return 1.0 / (1.0 + jnp.exp(-v))


def silu(v):
    return v * sigmoid(v)


def slope(v):
    sigma = sigmoid(v)
    return sigma * (1.0 + v * (1.0 - sigma))


def softplus(v):
    return jnp.maximum(v, 0.0) + jnp.log1p(jnp.exp(-jnp.abs(v)))


def ones_where(shape, rule):
    rows = lax.broadcasted_iota(jnp.int32, shape, 0)
    cols = lax.broadcasted_iota(jnp.int32, shape, 1)
    return rule(rows, cols)


def head_picker(channels, heads):
    wide = channels // heads
    return ones_where((channels, heads), lambda r, c: r // wide == c).astype(F32).astype(BF16)


def pair_spread(cols, j, rows):
    lane = lax.broadcasted_iota(jnp.int32, (rows, LANES), 1)
    first = jnp.broadcast_to(cols[:, 2 * j : 2 * j + 1], (rows, LANES))
    second = jnp.broadcast_to(cols[:, 2 * j + 1 : 2 * j + 2], (rows, LANES))
    return jnp.where(lane < LANES // 2, first, second)


def spread(cols, rows, heads):
    return jnp.concatenate([pair_spread(cols, j, rows) for j in range(heads // 2)], axis=1)


def call(kernel, name, grid, in_specs, out_specs, out_shape, scratch, flops, args, transcendentals=0):
    moved = sum(a.size * a.dtype.itemsize for a in args) + sum(
        o.size * o.dtype.itemsize for o in out_shape
    )
    return pl.pallas_call(
        kernel,
        grid=grid,
        in_specs=in_specs,
        out_specs=out_specs,
        out_shape=out_shape,
        scratch_shapes=scratch,
        compiler_params=pltpu.CompilerParams(
            dimension_semantics=("arbitrary",) * len(grid), vmem_limit_bytes=VMEM_BYTES
        ),
        cost_estimate=pl.CostEstimate(
            flops=int(flops), bytes_accessed=int(moved), transcendentals=int(transcendentals)
        ),
        name=name,
    )(*args)


def shape(dims, dtype):
    return jax.ShapeDtypeStruct(dims, dtype)


def decays(cum, cumt, h, half):
    top = jnp.exp(jnp.minimum(cum[:half, h : h + 1] - cumt[h : h + 1, :half], 0.0))
    low = jnp.exp(jnp.minimum(cum[half:, h : h + 1] - cumt[h : h + 1, :], 0.0))
    return top, low


def lower_scores(basis, states, length):
    scores = dot(basis[:, states:], basis[:, :states], NT)
    return jnp.where(ones_where((length, length), lambda r, c: r >= c), scores, 0.0)


def intra_back(bcs, xdt, dy, cum, cumt, length):
    rows, channels = xdt.shape
    heads = cum.shape[1]
    both = bcs.shape[1]
    states = both // 2
    half = length // 2

    def kernel(bcs_r, xdt_r, dy_r, cum_r, cumt_r, g_o, dbc_o, grad):
        scores = lower_scores(bcs_r[...], states, length)
        cum_v, cumt_v = cum_r[...], cumt_r[...]
        lane = lax.broadcasted_iota(jnp.int32, (length, LANES), 1)
        grad[...] = jnp.zeros_like(grad)
        for j in range(heads // 2):
            at = slice(j * LANES, (j + 1) * LANES)
            pair, dpair = xdt_r[:, at], dy_r[:, at]
            g_top = jnp.zeros((half, LANES), F32)
            g_low = jnp.zeros((half, LANES), F32)
            for s in range(2):
                own = jnp.where((lane < LANES // 2) == (s == 0), dpair, jnp.zeros_like(dpair))
                top, low = decays(cum_v, cumt_v, 2 * j + s, half)
                grad[:half, :half] += dot(own[:half], pair[:half], NT) * top
                grad[half:] += dot(own[half:], pair, NT) * low
                w_top = (scores[:half, :half] * top).astype(BF16)
                w_low = (scores[half:] * low).astype(BF16)
                g_top += dot(w_top, own[:half], TN) + dot(w_low[:, :half], own[half:], TN)
                g_low += dot(w_low[:, half:], own[half:], TN)
            g_o[:half, at] = g_top
            g_o[half:, at] = g_low
        masked = jnp.where(ones_where((length, length), lambda r, c: r >= c), grad[...], 0.0)
        high = masked.astype(BF16)
        rest = (masked - high.astype(F32)).astype(BF16)
        in_b, out_b = bcs_r[:, :states], bcs_r[:, states:]
        dbc_o[:, :states] = dot(high, out_b, TN) + dot(rest, out_b, TN)
        dbc_o[:, states:] = dot(high, in_b) + dot(rest, in_b)

    tokens = lambda n: pl.BlockSpec((length, n), lambda i: (i, 0))
    return call(
        kernel, "within_blocks_back", (rows // length,),
        [tokens(both), tokens(channels), tokens(channels), tokens(heads),
         pl.BlockSpec((heads, length), lambda i: (0, i))],
        [tokens(channels), tokens(both)],
        [shape((rows, channels), F32), shape((rows, both), F32)],
        [pltpu.VMEM((length, length), F32)],
        2 * rows * length * channels * 8, (bcs, xdt, dy, cum, cumt), rows * length * heads,
    )


def finish_back(value_pre, value_edge, value_kernel, value_bias, xs, xdt, xw, g, dy, dv, bcs, step_pre, dt,
                cum, ab, hin0, pre, carry, hin_low, ds0, post, back, dec, dbc_intra, skip_row, skip_gain,
                step_bias, log_rate, length):
    rows, channels = xs.shape
    heads = cum.shape[1]
    both = bcs.shape[1]
    states = both // 2
    wide = channels // heads
    count = rows // length
    taps = value_kernel.shape[0]
    unit = length // EDGE

    def kernel(xr, xr_before, xr_edge, vk, vb, xs_r, xdt_r, xw_r, g_r, dy_r, dv_r, bcs_r, dtr, dt_r, cum_r,
               ab_r, hin_r, pre_r, carry_r, low_r, ds_r, post_r, back_r, dec_r, dbci, skip, skipg, tb,
               lr, dxr_o, tail_o, head_o, vkg_o, vbg_o, ddtr_o, dbc_o, small_o,
               padded, ext, ds_low, inner_sums):
        i = pl.program_id(0)
        block = count - 1 - i

        @pl.when(i == 0)
        def _():
            vkg_o[...] = jnp.zeros_like(vkg_o)
            vbg_o[...] = jnp.zeros_like(vbg_o)
            small_o[...] = jnp.zeros_like(small_o)
            ext[0:EDGE] = jnp.zeros((EDGE, channels), F32)

        @pl.when(block == 0)
        def _():
            padded[0:EDGE] = xr_edge[...]

        @pl.when(block > 0)
        def _():
            padded[0:EDGE] = xr_before[...]

        padded[EDGE:] = xr[...]
        ext[length:] = ext[0:EDGE]
        for h in range(heads):
            at = slice(h * wide, (h + 1) * wide)
            ds = ds_r[0, at] + post_r[0, h : h + 1] * back_r[at].astype(F32)
            ds_low[at] = ds.astype(BF16)
            hin = hin_r[0, at] + pre_r[0, h : h + 1] * carry_r[at].astype(F32)
            inner_sums[h : h + 1] = jnp.sum(ds * hin, axis=0, keepdims=True) * dec_r[0, h : h + 1]
        in_b = bcs_r[:, :states]
        dt_v, cum_v = dt_r[...], cum_r[...]
        fade = jnp.exp(cum_v[length - 1 : length] - cum_v)
        factor = fade * dt_v
        start = EDGE - taps + 1
        picker = head_picker(channels, heads)
        c_sum = jnp.zeros((length, heads), F32)
        d_sum = jnp.zeros((length, heads), F32)
        w_sum = jnp.zeros((length, heads), F32)
        for j in range(channels // LANES):
            at = slice(j * LANES, (j + 1) * LANES)
            xs_v = xs_r[:, at].astype(F32)
            dxw = dot(in_b, ds_low[at], NT)
            g_v = g_r[:, at]
            c_sum += dot_split(xs_v * g_v, picker[at])
            d_sum += dot_split(xs_v * dxw, picker[at])
            w_sum += dot_split(xdt_r[:, at].astype(F32) * g_v, picker[at])
            dxs = (
                pair_spread(dt_v, j, length) * g_v
                + pair_spread(factor, j, length) * dxw
                + skip[:, at] * dy_r[:, at].astype(F32)
            )
            total = vb[:, at] + vk[0:1, at] * padded[pl.ds(start, length), at]
            for k in range(1, taps):
                total = total + vk[k : k + 1, at] * padded[pl.ds(start + k, length), at]
            dpre = dxs * slope(total)
            ext[0:length, at] = dpre
            vbg_o[:, at] += jnp.sum(dpre, axis=0, keepdims=True)
            for k in range(taps):
                vkg_o[k : k + 1, at] += jnp.sum(
                    dpre * padded[pl.ds(start + k, length), at], axis=0, keepdims=True
                )
            dxr = vk[0:1, at] * ext[pl.ds(taps - 1, length), at]
            for k in range(1, taps):
                dxr = dxr + vk[k : k + 1, at] * ext[pl.ds(taps - 1 - k, length), at]
            dxr_o[:, at] = dxr.astype(BF16)

            @pl.when(i == 0)
            def _():
                tail_o[:, at] = dxr[length - EDGE :]

        head_o[...] = ext[0:EDGE]
        dbc_o[:, :states] = dbci[:, :states] + dot(xw_r[...], ds_low[...])
        dbc_o[:, states:] = dbci[:, states:] + dot(dv_r[...], low_r[0])
        rate = -jnp.exp(lr[...])
        a_sum, b_sum = ab_r[:, :heads], ab_r[:, heads:]
        e_sum = d_sum * factor
        ones = jnp.ones((1, LANES), F32)
        dtotal = jnp.sum(e_sum, axis=0, keepdims=True) + dot(ones, inner_sums[...], NT, precision=HIGH)
        row = lax.broadcasted_iota(jnp.int32, (length, heads), 0)
        dcum = a_sum - skipg[...] * b_sum - w_sum - e_sum
        dcum = dcum + jnp.where(row == length - 1, dtotal, 0.0)
        upper = ones_where((length, length), lambda r, c: r <= c).astype(F32)
        dda = dot(upper, dcum, precision=HIGH)
        ddt = c_sum + d_sum * fade + dda * rate
        dpre_dt = ddt * sigmoid(dtr[...] + tb[...])
        ddtr_o[...] = dpre_dt.astype(BF16)
        small_o[0:1] += jnp.sum(dpre_dt, axis=0, keepdims=True)
        small_o[1:2] += jnp.sum(dda * dt_v, axis=0, keepdims=True) * rate
        small_o[2:3] += jnp.sum(b_sum, axis=0, keepdims=True)

    last = count - 1
    whole = lambda *dims: pl.BlockSpec(dims, lambda i: (0,) * len(dims))
    tokens = lambda n: pl.BlockSpec((length, n), lambda i: (last - i, 0))
    before = lambda n: pl.BlockSpec((EDGE, n), lambda i: (jnp.maximum((last - i) * unit - 1, 0), 0))
    per = lambda *dims: pl.BlockSpec((1,) + dims, lambda i: (last - i, 0, 0))
    return call(
        kernel, "across_blocks_back", (count,),
        [tokens(channels), before(channels), whole(EDGE, channels), whole(taps, channels),
         whole(1, channels), tokens(channels), tokens(channels), tokens(channels), tokens(channels),
         tokens(channels), tokens(channels), tokens(both), tokens(heads), tokens(heads), tokens(heads),
         tokens(2 * heads), per(channels, states), per(heads, LANES), whole(channels, states),
         per(channels, states), per(channels, states), per(heads, LANES), whole(channels, states),
         per(heads, LANES), tokens(both), whole(1, channels), whole(1, heads), whole(1, heads),
         whole(1, heads)],
        [tokens(channels), whole(EDGE, channels), whole(EDGE, channels), whole(taps, channels),
         whole(1, channels), tokens(heads), tokens(both), whole(EDGE, heads)],
        [shape((rows, channels), BF16), shape((EDGE, channels), F32), shape((EDGE, channels), F32),
         shape((taps, channels), F32), shape((1, channels), F32), shape((rows, heads), BF16),
         shape((rows, both), F32), shape((EDGE, heads), F32)],
        [pltpu.VMEM((length + EDGE, channels), F32), pltpu.VMEM((length + EDGE, channels), F32),
         pltpu.VMEM((channels, states), BF16), pltpu.VMEM((heads, LANES), F32)],
        2 * rows * channels * states * 3,
        (value_pre, value_pre, value_edge, value_kernel, value_bias, xs, xdt, xw, g, dy, dv, bcs, step_pre,
         dt, cum, ab, hin0, pre, carry, hin_low, ds0, post, back, dec, dbc_intra, skip_row, skip_gain,
         step_bias, log_rate),
        2 * rows * channels,
    )


def halves(normal_in, grad, outer):
    rows, width = normal_in.shape
    channels = grad.shape[1]
    strip = width // (2 * outer)

    def kernel(xn, grad_r, keep_o, give_o):
        side = lax.rem(lax.axis_index("seq"), 2)
        product = dot(xn[...], grad_r[...], TN).astype(BF16)

        @pl.when(side == 0)
        def _():
            keep_o[0] = product[:strip]
            give_o[0] = product[strip:]

        @pl.when(side == 1)
        def _():
            keep_o[0] = product[strip:]
            give_o[0] = product[:strip]

    out = pl.BlockSpec((1, strip, channels), lambda i: (i, 0, 0))
    return call(
        kernel, "gate_strips", (outer,),
        [pl.BlockSpec((rows, 2 * strip), lambda i: (0, i)),
         pl.BlockSpec((rows, channels), lambda i: (0, 0))],
        [out, out], [shape((outer, strip, channels), BF16)] * 2, [], 2 * rows * width * channels,
        (normal_in, grad),
    )


def remote(src, dst, send, recv, seq, head):
    return pltpu.make_async_remote_copy(
        src_ref=src, dst_ref=dst, send_sem=send, recv_sem=recv, device_id=(seq, head),
        device_id_type=pl.DeviceIdType.MESH,
    )


def greet(seq, head, seq_size, head_size):
    barrier = pltpu.get_barrier_semaphore()
    for d in range(1, seq_size):
        pl.semaphore_signal(
            barrier, inc=1, device_id=(lax.rem(seq + d, seq_size), head),
            device_id_type=pl.DeviceIdType.MESH,
        )
    for d in range(1, head_size):
        pl.semaphore_signal(
            barrier, inc=1, device_id=(seq, lax.rem(head + d, head_size)),
            device_id_type=pl.DeviceIdType.MESH,
        )
    pl.semaphore_wait(barrier, seq_size - 1 + head_size - 1)


def forward(xdt, xs, bcs, gate_pre, normed_grad, cum, cumt, hin0, pre, dec, carry, skip_row, gate_gain,
            output_matrix, length, seq_size, head_size):
    rows, channels = xs.shape
    heads = cum.shape[1]
    both = bcs.shape[1]
    states = both // 2
    wide = channels // heads
    count = rows // length
    half = length // 2
    width = output_matrix.shape[1]
    share = width // head_size
    inner = channels * head_size

    def kernel(xdt_r, xs_r, bcs_r, z_r, dn_r, cum_r, cumt_r, hin_r, pre_r, dec_r, carry_r, skip, gain, wo,
               low_o, normed_o, part_o, dy_o, dz_o, dv_o, ab_o, ds_o, post_o, start_o, ggain_o,
               y_s, sums, others, state, behind, prod_a, prod_b, s_sem, r_sem):
        i = pl.program_id(0)
        seq, head = lax.axis_index("seq"), lax.axis_index("head")
        barrier = pltpu.get_barrier_semaphore()

        def head_at(d):
            return lax.rem(head + d, head_size)

        def share_sums(d):
            return remote(sums, others.at[d - 1], s_sem.at[d - 1], r_sem.at[d - 1], seq, head_at(d))

        @pl.when(i == 0)
        def _():
            for d in range(1, head_size):
                pl.semaphore_signal(
                    barrier, inc=1, device_id=(seq, head_at(d)), device_id_type=pl.DeviceIdType.MESH
                )

        @pl.when(i < count)
        def _():
            at_rows = pl.ds(pl.multiple_of(i * length, length), length)
            for h in range(heads):
                at = slice(h * wide, (h + 1) * wide)
                low_o[0, at] = (
                    hin_r[0, at] + pre_r[0, h : h + 1] * carry_r[at].astype(F32)
                ).astype(BF16)
            scores = lower_scores(bcs_r[...], states, length)
            cum_v, cumt_v = cum_r[...], cumt_r[...]
            growth = jnp.exp(cum_v)
            lane = lax.broadcasted_iota(jnp.int32, (length, LANES), 1)
            squares = jnp.zeros((length, LANES), F32)
            crosses = jnp.zeros((length, LANES), F32)
            out_basis = bcs_r[:, states:]
            for j in range(channels // LANES):
                at = slice(j * LANES, (j + 1) * LANES)
                pair = xdt_r[:, at]
                y_top = jnp.zeros((half, LANES), F32)
                y_low = jnp.zeros((half, LANES), F32)
                for s in range(2):
                    own = jnp.where((lane < LANES // 2) == (s == 0), pair, jnp.zeros_like(pair))
                    top, low = decays(cum_v, cumt_v, 2 * j + s, half)
                    y_top += dot((scores[:half, :half] * top).astype(BF16), own[:half])
                    y_low += dot((scores[half:] * low).astype(BF16), own)
                v = dot(out_basis, low_o[0, at], NT)
                y = (
                    jnp.concatenate([y_top, y_low], axis=0)
                    + pair_spread(growth, j, length) * v
                    + skip[:, at] * xs_r[:, at].astype(F32)
                )
                y_s[at_rows, at] = y
                gated = y * silu(z_r[:, at])
                squares += gated * gated
                crosses += dn_r[:, at] * gain[:, at] * gated
            first = ones_where((8, LANES), lambda r, c: r == 0).astype(F32)
            second = ones_where((8, LANES), lambda r, c: r == 1).astype(F32)
            sums[:, at_rows] = dot(first, squares, NT, HIGH) + dot(second, crosses, NT, HIGH)

        @pl.when(i == count)
        def _():
            pl.semaphore_wait(barrier, head_size - 1)
            for d in range(1, head_size):
                share_sums(d).start()
            state[...] = jnp.zeros_like(state)
            behind[...] = jnp.ones_like(behind)
            ggain_o[...] = jnp.zeros_like(ggain_o)
            for d in range(1, head_size):
                share_sums(d).wait()
            total = sums[...]
            for d in range(1, head_size):
                total = total + others[d - 1]
            others[0] = total

        @pl.when(i >= count)
        def _():
            at_rows = pl.ds(pl.multiple_of((2 * count - 1 - i) * length, length), length)
            both_sums = others[0, :, at_rows]
            first = ones_where((8, LANES), lambda r, c: r == 0).astype(F32)
            second = ones_where((8, LANES), lambda r, c: r == 1).astype(F32)
            grstd = lax.rsqrt(dot(both_sums, first, TN, HIGH) * (1.0 / inner) + EPSILON)
            cross = (grstd * grstd * grstd) * (dot(both_sums, second, TN, HIGH) * (1.0 / inner))
            growth = jnp.exp(cum_r[...])
            for j in range(channels // LANES):
                at = slice(j * LANES, (j + 1) * LANES)
                y, z, dn = y_s[at_rows, at], z_r[:, at], dn_r[:, at]
                sigma = sigmoid(z)
                act = z * sigma
                gated = y * act
                scaled = gated * grstd
                normed_o[:, at] = (scaled * gain[:, at]).astype(BF16)
                ggain_o[:, at] += jnp.sum(dn * scaled, axis=0, keepdims=True)
                dgated = grstd * (dn * gain[:, at]) - gated * cross
                dy = (dgated * act).astype(BF16)
                dy_o[:, at] = dy
                dz_o[:, at] = (dgated * y * (sigma * (1.0 + z * (1.0 - sigma)))).astype(BF16)
                plain = dy.astype(F32)
                dv_o[:, at] = (plain * pair_spread(growth, j, length)).astype(BF16)
                prod_a[:, at] = plain * y
                prod_b[:, at] = plain * xs_r[:, at].astype(F32)
            picker = head_picker(channels, heads)
            ab_o[:, :heads] = dot_split(prod_a[...], picker)
            ab_o[:, heads:] = dot_split(prod_b[...], picker)
            for q in range(head_size):
                at = slice(q * share, (q + 1) * share)
                part_o[q] = dot(normed_o[...], wo[:, at]).astype(BF16)
            dhin = dot(dv_o[...], bcs_r[:, states:], TN)
            ds_o[0] = state[...]
            post_o[0] = behind[...]
            behind[...] = behind[...] * dec_r[0]
            for h in range(heads):
                at = slice(h * wide, (h + 1) * wide)
                state[at] = dec_r[0, h : h + 1] * state[at] + dhin[at]
            start_o[...] = state[...].astype(BF16)

    last = count - 1
    ways = {
        "both": lambda i: jnp.where(i < count, i, 2 * count - 1 - i),
        "up": lambda i: jnp.minimum(i, last),
        "down": lambda i: jnp.minimum(2 * count - 1 - i, last),
    }
    whole = lambda *dims: pl.BlockSpec(dims, lambda i: (0,) * len(dims))
    tokens = lambda n, way: pl.BlockSpec((length, n), lambda i: (ways[way](i), 0))
    per = lambda way, *dims: pl.BlockSpec((1,) + dims, lambda i: (ways[way](i), 0, 0))
    args = (xdt, xs, bcs, gate_pre, normed_grad, cum, cumt, hin0, pre, dec, carry, skip_row, gate_gain,
            output_matrix)
    return pl.pallas_call(
        kernel,
        grid=(2 * count,),
        in_specs=[
            tokens(channels, "up"), tokens(channels, "both"), tokens(both, "both"),
            tokens(channels, "both"), tokens(channels, "both"), tokens(heads, "both"),
            pl.BlockSpec((heads, length), lambda i: (0, ways["up"](i))), per("up", channels, states),
            per("up", heads, LANES), per("down", heads, LANES), whole(channels, states),
            whole(1, channels), whole(1, channels), whole(channels, width),
        ],
        out_specs=[
            per("up", channels, states), tokens(channels, "down"),
            pl.BlockSpec((head_size, length, share), lambda i: (0, ways["down"](i), 0)),
            tokens(channels, "down"), tokens(channels, "down"), tokens(channels, "down"),
            tokens(2 * heads, "down"), per("down", channels, states), per("down", heads, LANES),
            whole(channels, states), whole(1, channels),
        ],
        out_shape=[
            shape((count, channels, states), BF16), shape((rows, channels), BF16),
            shape((head_size, rows, share), BF16), shape((rows, channels), BF16),
            shape((rows, channels), BF16), shape((rows, channels), BF16), shape((rows, 2 * heads), F32),
            shape((count, channels, states), F32), shape((count, heads, LANES), F32),
            shape((channels, states), BF16), shape((1, channels), F32),
        ],
        scratch_shapes=[
            pltpu.VMEM((rows, channels), F32), pltpu.VMEM((8, rows), F32),
            pltpu.VMEM((head_size - 1, 8, rows), F32), pltpu.VMEM((channels, states), F32),
            pltpu.VMEM((heads, LANES), F32), pltpu.VMEM((length, channels), F32),
            pltpu.VMEM((length, channels), F32),
            pltpu.SemaphoreType.DMA((head_size - 1,)), pltpu.SemaphoreType.DMA((head_size - 1,)),
        ],
        compiler_params=pltpu.CompilerParams(
            dimension_semantics=("arbitrary",), collective_id=3, has_side_effects=True,
            vmem_limit_bytes=VMEM_BYTES,
        ),
        cost_estimate=pl.CostEstimate(
            flops=2 * rows * channels * (width + 6 * length), bytes_accessed=60_000_000,
            transcendentals=rows * (length * heads + 2 * channels),
        ),
        name="blocks_and_gate",
    )(*args)


def opening(tokens, cotangent, norm_gain, gate_matrix, value_matrix, state_matrix, step_matrix,
            output_matrix, value_kernel, value_bias, state_kernel, state_bias, step_bias, log_rate,
            seq_size, head_size):
    members, length, share = tokens.shape
    rows = members * length
    width, channels = gate_matrix.shape
    both = state_matrix.shape[1]
    heads = step_matrix.shape[1]
    half_heads = head_size // 2
    states = both // 2
    wide = channels // heads
    taps = value_kernel.shape[0]
    groups = seq_size // members
    margin = EDGE - taps + 1

    def kernel(tokens_h, cot_h, gain, gate_h, value_h, state_h, step_m, out_h, vk, vb, sk, sb, tb, lr,
               xn_o, cot_o, mine_o, z_o, xr_o, bc_o, dn_o, xs_o, xdt_o, xw_o, hin_o,
               rstd_o, dtr_o, bcs_o, dt_o, cum_o, cumt_o, pre_o, dec_o, xedge_o, bedge_o, carry_o,
               whole, xn, z, xr, bc, dn, gate, value, state_m, out_m,
               padded, padded_bc, xs, xdt, xw, hin, state, ahead, leaving,
               gs_sem, gr_sem, ys_sem, yr_sem, cs_sem, cr_sem, w_sem, o_sem, l_sem, e_sem):
        seq, head = lax.axis_index("seq"), lax.axis_index("head")
        lane, core = head // 2, lax.rem(head, 2)
        group, member = seq // members, lax.rem(seq, members)
        base = seq - member
        sources = (tokens_h, cot_h)

        def rows_of(j):
            return pl.ds(pl.multiple_of(j * length, length), length)

        def lanes_of(h):
            return pl.ds(pl.multiple_of(h * share, share), share)

        own = [
            pltpu.make_async_copy(
                sources[a].at[member], whole.at[a, rows_of(member), lanes_of(head)], l_sem.at[a]
            )
            for a in range(2)
        ]
        loads = [
            pltpu.make_async_copy(src, dst, w_sem.at[i])
            for i, (src, dst) in enumerate(
                ((gate_h, gate), (value_h, value), (state_h, state_m), (out_h, out_m))
            )
        ]
        own[0].start()
        own[1].start()
        for load in loads:
            load.start()
        greet(seq, head, seq_size, head_size)

        def place(t):
            return lax.rem(member + t, members)

        def to_group(a, t):
            return remote(sources[a].at[place(t)], whole.at[a, rows_of(member), lanes_of(head)],
                          gs_sem.at[a, t - 1], gr_sem.at[a, members - 1 - t], base + place(t), head)

        def from_group(a, t):
            return remote(sources[a].at[place(t)], whole.at[a, rows_of(place(t)), lanes_of(head)],
                          gs_sem.at[a, t - 1], gr_sem.at[a, t - 1], seq, head)

        def to_lane(a, t, k):
            at = whole.at[a, rows_of(place(t)), lanes_of(head)]
            return remote(at, at, ys_sem.at[a, t, k], yr_sem.at[a, t, k],
                          seq, 2 * lax.rem(lane + 1 + k, half_heads) + core)

        def lane_from(k):
            return lax.rem(lane + half_heads - 1 - k, half_heads)

        def from_lane(a, t, k):
            at = whole.at[a, rows_of(place(t)), lanes_of(2 * lane_from(k) + core)]
            return remote(at, at, ys_sem.at[a, t, k], yr_sem.at[a, t, k], seq, head)

        def to_core(a, t, k):
            at = whole.at[a, rows_of(place(t)), lanes_of(2 * lane_from(k) + core)]
            return remote(at, at, cs_sem.at[a, t, k], cr_sem.at[a, t, k], seq, 2 * lane + 1 - core)

        def from_core(a, t, k):
            at = whole.at[a, rows_of(place(t)), lanes_of(2 * lane_from(k) + 1 - core)]
            return remote(at, at, cs_sem.at[a, t, k], cr_sem.at[a, t, k], seq, head)

        def forward(a, t):
            for k in range(half_heads - 1):
                to_lane(a, t, k).start()
            to_core(a, t, half_heads - 1).start()

        def collect(a, t):
            for k in range(half_heads - 1):
                from_lane(a, t, k).wait_recv()
                to_core(a, t, k).start()
            for k in range(half_heads):
                from_core(a, t, k).wait_recv()

        def outputs(t):
            at = rows_of(place(t))
            pairs = ((xn, xn_o), (z, z_o), (xr, xr_o), (bc, bc_o))
            return [
                pltpu.make_async_copy(src.at[at], dst.at[at], o_sem.at[i, t])
                for i, (src, dst) in enumerate(pairs)
            ]

        def late_outputs(t):
            at = rows_of(place(t))
            return [
                pltpu.make_async_copy(dn.at[at], dn_o.at[at], o_sem.at[4, t]),
                pltpu.make_async_copy(whole.at[1, at], cot_o.at[at], o_sem.at[5, t]),
                pltpu.make_async_copy(whole.at[0, at, lanes_of(head)], mine_o.at[at], o_sem.at[6, t]),
            ]

        def project(t):
            at = rows_of(place(t))
            squares = jnp.zeros((length, LANES), F32)
            for q in range(width // LANES):
                part = whole[0, at, q * LANES : (q + 1) * LANES].astype(F32)
                squares += part * part
            mean = jnp.sum(squares, axis=1, keepdims=True) * (1.0 / width)
            rstd = lax.rsqrt(mean + EPSILON)
            rstd_o[at] = rstd
            wide = jnp.broadcast_to(rstd, (length, LANES))
            for q in range(width // LANES):
                cols = slice(q * LANES, (q + 1) * LANES)
                xn[at, cols] = (whole[0, at, cols].astype(F32) * wide * gain[:, cols]).astype(BF16)
            normal = xn[at]
            if t == 0:
                for load in loads[:3]:
                    load.wait()
            xr[at] = dot(normal, value[...])
            z[at] = dot(normal, gate[...])
            bc[at] = dot(normal, state_m[...])
            dtr_o[at] = dot(normal, step_m[...])
            for copy in outputs(t):
                copy.start()

        def edges(there):
            tail = pl.ds(rows - EDGE, EDGE)
            return [
                remote(xr.at[tail], xedge_o, e_sem.at[0], e_sem.at[1], there, head),
                remote(bc.at[tail], bedge_o, e_sem.at[2], e_sem.at[3], there, head),
            ]

        def pass_on(there):
            return remote(leaving, carry_o, e_sem.at[4], e_sem.at[5], there, head)

        def block_outputs(i):
            at = rows_of(i)
            pairs = ((xs, xs_o), (xdt, xdt_o), (xw, xw_o))
            return [
                pltpu.make_async_copy(src.at[at], dst.at[at], o_sem.at[7 + n, i])
                for n, (src, dst) in enumerate(pairs)
            ] + [pltpu.make_async_copy(hin.at[i], hin_o.at[i], o_sem.at[10, i])]

        def prepare(i):
            at = slice(i * length, (i + 1) * length)
            if i == 0:
                padded[0:EDGE] = xedge_o[...]
                padded_bc[0:EDGE] = bedge_o[...]
                state[...] = jnp.zeros_like(state)
                ahead[...] = jnp.ones_like(ahead)
            else:
                padded[0:EDGE] = xr[i * length - EDGE : i * length]
                padded_bc[0:EDGE] = bc[i * length - EDGE : i * length]
            padded[EDGE:] = xr[at]
            padded_bc[EDGE:] = bc[at]
            summed = sb[...] + sk[0:1] * padded_bc[pl.ds(margin, length)]
            for k in range(1, taps):
                summed = summed + sk[k : k + 1] * padded_bc[pl.ds(margin + k, length)]
            basis = silu(summed).astype(BF16)
            bcs_o[at] = basis
            dt = softplus(dtr_o[at] + tb[...])
            da = dt * -jnp.exp(lr[...])
            lower = ones_where((length, length), lambda r, c: r >= c).astype(F32)
            upper = ones_where((length, length), lambda r, c: r <= c).astype(F32)
            cum = dot(lower, da, precision=HIGH)
            cumt = dot(da, upper, TN, precision=HIGH)
            dt_o[at] = dt
            cum_o[at] = cum
            cumt_o[:, at] = cumt
            factor = jnp.exp(cum[length - 1 : length] - cum) * dt
            decay = jnp.exp(jnp.broadcast_to(cumt[:, length - 1 : length], (heads, LANES)))
            dec_o[i] = decay
            pre_o[i] = ahead[...]
            ahead[...] = ahead[...] * decay
            hin[i] = state[...]
            for j in range(channels // LANES):
                cols = slice(j * LANES, (j + 1) * LANES)
                total = vb[:, cols] + vk[0:1, cols] * padded[pl.ds(margin, length), cols]
                for k in range(1, taps):
                    total = total + vk[k : k + 1, cols] * padded[pl.ds(margin + k, length), cols]
                value_low = silu(total).astype(BF16)
                xs[at, cols] = value_low
                plain = value_low.astype(F32)
                xdt[at, cols] = (plain * pair_spread(dt, j, length)).astype(BF16)
                xw[at, cols] = (plain * pair_spread(factor, j, length)).astype(BF16)
            local = dot(xw[at], basis[:, :states], TN)
            for h in range(heads):
                span = slice(h * wide, (h + 1) * wide)
                state[span] = decay[h : h + 1] * state[span] + local[span]
            for copy in block_outputs(i):
                copy.start()

        for t in range(1, members):
            to_group(0, t).start()
        own[0].wait()
        forward(0, 0)
        for t in range(1, members):
            from_group(0, t).wait_recv()
            forward(0, t)
        for t in range(1, members):
            to_group(1, t).start()
        own[1].wait()
        forward(1, 0)
        for t in range(members):
            collect(0, t)
            project(t)
            if t < members - 1:
                from_group(1, t + 1).wait_recv()
                forward(1, t + 1)
        @pl.when(group < groups - 1)
        def _():
            for copy in edges(seq + members):
                copy.start()

        @pl.when(group == 0)
        def _():
            xedge_o[...] = jnp.zeros_like(xedge_o)
            bedge_o[...] = jnp.zeros_like(bedge_o)
            carry_o[...] = jnp.zeros_like(carry_o)

        def gradient(t):
            collect(1, t)
            at = rows_of(place(t))
            dn[at] = dot(whole[1, at], out_m[...], NT)
            for copy in late_outputs(t):
                copy.start()

        loads[3].wait()
        gradient(0)

        @pl.when(group > 0)
        def _():
            for copy in edges(seq):
                copy.wait_recv()

        for i in range(members):
            prepare(i)
        leaving[...] = state[...].astype(BF16)

        @pl.when(group == 0)
        def _():
            pass_on(seq + members).start()

        for t in range(1, members):
            gradient(t)

        @pl.when(group > 0)
        def _():
            pass_on(seq).wait_recv()

            @pl.when(group < groups - 1)
            def _():
                for h in range(heads):
                    span = slice(h * wide, (h + 1) * wide)
                    leaving[span] = (
                        state[span] + ahead[h : h + 1] * carry_o[span].astype(F32)
                    ).astype(BF16)
                pass_on(seq + members).start()

        @pl.when(group < groups - 1)
        def _():
            for copy in edges(seq + members):
                copy.wait_send()
            pass_on(seq + members).wait_send()

        for t in range(members):
            for copy in outputs(t) + late_outputs(t) + block_outputs(t):
                copy.wait()
        for a in range(2):
            for t in range(1, members):
                to_group(a, t).wait_send()
            for t in range(members):
                for k in range(half_heads):
                    to_core(a, t, k).wait_send()
                    if k < half_heads - 1:
                        to_lane(a, t, k).wait_send()

    vmem = pl.BlockSpec(memory_space=pltpu.VMEM)
    anywhere = pl.BlockSpec(memory_space=pl.ANY)
    dma = pltpu.SemaphoreType.DMA
    args = (tokens, cotangent, norm_gain, gate_matrix, value_matrix, state_matrix, step_matrix,
            output_matrix, value_kernel, value_bias, state_kernel, state_bias, step_bias, log_rate)
    far = {0, 1, 3, 4, 5, 7}
    return pl.pallas_call(
        kernel,
        in_specs=[anywhere if i in far else vmem for i in range(len(args))],
        out_specs=[anywhere] * 11 + [vmem] * 11,
        out_shape=[
            shape((rows, width), BF16), shape((rows, width), BF16), shape((rows, share), BF16),
            shape((rows, channels), F32), shape((rows, channels), F32), shape((rows, both), F32),
            shape((rows, channels), F32), shape((rows, channels), BF16), shape((rows, channels), BF16),
            shape((rows, channels), BF16), shape((members, channels, states), F32),
            shape((rows, 1), F32), shape((rows, heads), F32), shape((rows, both), BF16),
            shape((rows, heads), F32), shape((rows, heads), F32), shape((heads, rows), F32),
            shape((members, heads, LANES), F32), shape((members, heads, LANES), F32),
            shape((EDGE, channels), F32), shape((EDGE, both), F32), shape((channels, states), BF16),
        ],
        scratch_shapes=[
            pltpu.VMEM((2, rows, width), BF16), pltpu.VMEM((rows, width), BF16),
            pltpu.VMEM((rows, channels), F32), pltpu.VMEM((rows, channels), F32),
            pltpu.VMEM((rows, both), F32), pltpu.VMEM((rows, channels), F32),
            pltpu.VMEM((width, channels), BF16), pltpu.VMEM((width, channels), BF16),
            pltpu.VMEM((width, both), BF16), pltpu.VMEM((channels, width), BF16),
            pltpu.VMEM((length + EDGE, channels), F32), pltpu.VMEM((length + EDGE, both), F32),
            pltpu.VMEM((rows, channels), BF16), pltpu.VMEM((rows, channels), BF16),
            pltpu.VMEM((rows, channels), BF16), pltpu.VMEM((members, channels, states), F32),
            pltpu.VMEM((channels, states), F32), pltpu.VMEM((heads, LANES), F32),
            pltpu.VMEM((channels, states), BF16),
            dma((2, members - 1)), dma((2, members - 1)),
            dma((2, members, max(half_heads - 1, 1))), dma((2, members, max(half_heads - 1, 1))),
            dma((2, members, half_heads)), dma((2, members, half_heads)),
            dma((4,)), dma((11, members)), dma((2,)), dma((6,)),
        ],
        compiler_params=pltpu.CompilerParams(
            collective_id=2, has_side_effects=True, vmem_limit_bytes=VMEM_BYTES
        ),
        cost_estimate=pl.CostEstimate(
            flops=2 * rows * width * (3 * channels + both), bytes_accessed=60_000_000, transcendentals=0
        ),
        name="opening_products",
    )(*args)

def closing(normal_in, dz, dxr, tail, head_rows, gate_matrix, value_matrix, state_matrix, step_matrix,
            value_kernel, state_kernel, state_bias, state_pre, state_edge, dbc, ddtr, vectors, small,
            part, mine, rstd, gain_share, gate_half, length, seq_size, head_size):
    rows, width = normal_in.shape
    channels = dz.shape[1]
    heads = ddtr.shape[1]
    both = dbc.shape[1]
    share = mine.shape[1]
    taps = value_kernel.shape[0]
    members = rows // length
    outer = seq_size // 2
    half_heads = head_size // 2
    strip = width // seq_size
    chunk = rows // head_size
    per = head_size // members
    packed = channels + both + LANES + share
    low_rows = share + heads * width // both
    steps = seq_size.bit_length() - 1
    groups = seq_size // members

    def kernel(xn, dz_r, dxr_h, tail_r, head_r, gate_h, value_h, state_m, step_m, vk, sk, sb, bc_h,
               bc_edge, dbc_h, ddtr_r, vec, small_r, part_h, mine_r, rstd_r, gain, half_h,
               gate_o, value_o, state_o, step_o, vkern_o, vbias_o, ggain_o, skern_o, sbias_o, norm_o,
               tbias_o, rate_o, skip_o, up_o, branch_o,
               dxr_r, duo, xrecv, zrecv, gown, grecv, weights, weight, csend, cown, crecv, yrecv, rsend,
               rrecv, up, norms, nrecv,
               pown, precv, pyrecv, drecv, dsum, ext, hrecv, hbrecv, low,
               full_sum, full_send, full_recv, low_sum, low_send, low_recv,
               xs_sem, xr_sem, zs_sem, zr_sem, cs_sem, cr_sem, ys_sem, yr_sem, rs_sem, rr_sem,
               us_sem, ur_sem, ns_sem, nr_sem, ps_sem, pr_sem, pys_sem, pyr_sem, ds_sem, dr_sem,
               as_sem, ar_sem, h_sem, hb_sem, fs_sem, fr_sem, ls_sem, lr_sem, bs_sem, br_sem, gs_sem, gr_sem, w_sem, copy_sem):
        seq, head = lax.axis_index("seq"), lax.axis_index("head")
        place, side = seq // 2, lax.rem(seq, 2)
        lane, core = head // 2, lax.rem(head, 2)
        group, member = seq // members, lax.rem(seq, members)
        base = seq - member
        load_dxr = pltpu.make_async_copy(dxr_h, dxr_r, copy_sem.at[0])
        load_dxr.start()
        load_bc = pltpu.make_async_copy(bc_h, low.at[pl.ds(EDGE, rows)], copy_sem.at[1 + half_heads])
        load_bc.start()
        low[0:EDGE] = bc_edge[...]

        def outer_at(k):
            other, result, bit = outer - 1 - k, 0, 1
            while bit < outer:
                result = result + bit * lax.rem(place // bit + other // bit, 2)
                bit *= 2
            return result

        def lane_at(k):
            return lax.rem(lane + 1 + k, half_heads)

        def seq_at(d):
            return lax.rem(seq + d, seq_size)

        def head_at(d):
            return lax.rem(head + d, head_size)

        loads = [
            pltpu.make_async_copy(part_h.at[2 * lane_at(k) + core], pown.at[k], copy_sem.at[1 + k])
            for k in range(half_heads)
        ]
        for load in loads:
            load.start()
        own_rows = pl.ds(pl.multiple_of(head * chunk, chunk), chunk)
        load_dbc = pltpu.make_async_copy(
            dbc_h.at[own_rows], dsum.at[own_rows], copy_sem.at[2 + half_heads]
        )
        load_dbc.start()
        load_half = pltpu.make_async_copy(half_h.at[place], gown, copy_sem.at[3 + half_heads])
        load_half.start()
        greet(seq, head, seq_size, head_size)

        def cross(k):
            return remote(duo.at[k, 1 - side], xrecv.at[k], xs_sem.at[k], xr_sem.at[k],
                          2 * place + 1 - side, head)

        def along(k):
            return remote(duo.at[k, side], zrecv.at[k], zs_sem.at[k], zr_sem.at[k],
                          2 * outer_at(k) + side, head)

        def along_gate(k):
            return remote(half_h.at[outer_at(k)], grecv.at[k], gs_sem.at[k], gr_sem.at[k],
                          2 * outer_at(k) + side, head)

        def edge_back(src, dst, sems):
            return remote(src, dst, sems.at[0], sems.at[1], seq - members, head)

        def part_core(k):
            return remote(part_h.at[2 * lane_at(k) + 1 - core], precv.at[k], ps_sem.at[k], pr_sem.at[k],
                          seq, 2 * lane + 1 - core)

        def part_lane(k):
            return remote(pown.at[k], pyrecv.at[k], pys_sem.at[k], pyr_sem.at[k],
                          seq, 2 * lane_at(k) + core)

        def rows_of(c):
            return pl.ds(pl.multiple_of(c * chunk, chunk), chunk)

        def basis_sum(d):
            return remote(dbc_h.at[rows_of(head_at(d))], drecv.at[d - 1], ds_sem.at[d - 1],
                          dr_sem.at[d - 1], seq, head_at(d))

        def basis_share(d):
            at = rows_of(head)
            return remote(dsum.at[at], dsum.at[at], as_sem.at[d - 1], ar_sem.at[d - 1], seq, head_at(d))

        @pl.when(group > 0)
        def _():
            edge_back(head_r, hrecv, h_sem).start()

        for d in range(1, head_size):
            basis_sum(d).start()
        for k in range(half_heads):
            part_core(k).start()

        for k in range(outer - 1):
            along_gate(k).start()

        load_dxr.wait()
        ext[...] = jnp.zeros_like(ext)

        @pl.when(group < groups - 1)
        def _():
            remote(head_r, hrecv, h_sem.at[0], h_sem.at[1], seq, head).wait_recv()
            ext[EDGE:] = hrecv[...]

        fixed = tail_r[...]
        for k in range(taps):
            fixed = fixed + vk[k : k + 1] * ext[pl.ds(taps - 1 - k, EDGE)]
        last = dxr_r[rows - 2 * EDGE :].astype(F32)
        dxr_r[rows - 2 * EDGE :] = jnp.concatenate([last[:EDGE], fixed], axis=0).astype(BF16)

        def multiply(k, _):
            at = pl.ds(pl.multiple_of(outer_at(k) * 2 * strip, 2 * strip), 2 * strip)
            product = dot(xn[:, at], dxr_r[...], TN).astype(BF16)
            duo[k, 0] = product[:strip]
            duo[k, 1] = product[strip:]
            cross(k).start()
            return 0

        lax.fori_loop(0, outer, multiply, 0)

        step_part = dot(ddtr_r[...], xn[...], TN)
        for q in range(width // both):
            low_sum[share + q * heads : share + (q + 1) * heads] = step_part[
                :, q * both : (q + 1) * both
            ]

        load_dbc.wait()
        total = dsum[own_rows]
        for d in range(1, head_size):
            basis_sum(d).wait_recv()
            total = total + drecv[d - 1]
        dsum[own_rows] = total
        for d in range(1, head_size):
            basis_share(d).start()

        def arrived(k, send=True):
            cross(k).wait_recv()
            duo[k, side] = (duo[k, side].astype(F32) + xrecv[k].astype(F32)).astype(BF16)
            if send:
                along(k).start()

        def arrived_loop(first, last):
            def one(k, _):
                arrived(k)
                return 0

            lax.fori_loop(first, last, one, 0)

        for k in range(half_heads):
            loads[k].wait()
            part_core(k).wait_recv()
            for r in range(members):
                at = slice(r * length, (r + 1) * length)
                pown[k, at] = (pown[k, at].astype(F32) + precv[k, at].astype(F32)).astype(BF16)
            if k < half_heads - 1:
                part_lane(k).start()

        for d in range(1, head_size):
            at = rows_of(head_at(d))
            remote(dsum.at[at], dsum.at[at], as_sem.at[d - 1], ar_sem.at[head_size - 1 - d],
                   seq, head).wait_recv()

        start = EDGE - taps + 1
        load_bc.wait()
        pre_bc = sb[...]
        for k in range(taps):
            pre_bc = pre_bc + sk[k : k + 1] * low[pl.ds(start + k, rows)]
        dpre = dsum[...] * slope(pre_bc)
        full_sum[...] = jnp.zeros_like(full_sum)
        full_sum[:, :channels] = vec[...]
        full_sum[:, channels + both : channels + both + heads] = small_r[...]
        for k in range(taps):
            full_sum[k : k + 1, channels : channels + both] = jnp.sum(
                dpre * low[pl.ds(start + k, rows)], axis=0, keepdims=True
            )
        full_sum[taps : taps + 1, channels : channels + both] = jnp.sum(dpre, axis=0, keepdims=True)
        low[0:rows] = dpre
        low[rows:] = jnp.zeros((EDGE, both), F32)

        @pl.when(group > 0)
        def _():
            edge_back(low.at[pl.ds(0, EDGE)], hbrecv, hb_sem).start()

        arrived_loop(0, outer // 4)

        @pl.when(group < groups - 1)
        def _():
            remote(low.at[pl.ds(0, EDGE)], hbrecv, hb_sem.at[0], hb_sem.at[1], seq, head).wait_recv()
            low[rows:] = hbrecv[...]

        dbc_v = sk[0:1] * low[pl.ds(taps - 1, rows)]
        for k in range(1, taps):
            dbc_v = dbc_v + sk[k : k + 1] * low[pl.ds(taps - 1 - k, rows)]
        dbc_low = dbc_v.astype(BF16)
        own_at = pl.ds(pl.multiple_of(head * share, share), share)
        low_sum[:share] = dot(xn[:, own_at], dbc_low, TN)
        for d in range(1, head_size):
            basis_share(d).wait_send()
        dsum[...] = dbc_low.astype(F32)

        def to_core(k):
            return remote(csend.at[k], crecv.at[k], cs_sem.at[k], cr_sem.at[k], seq, 2 * lane + 1 - core)

        def to_lane(k):
            return remote(cown.at[k], yrecv.at[k], ys_sem.at[k], yr_sem.at[k],
                          seq, 2 * lane_at(k) + core)

        def columns_of(step):
            which = 1 - core if step < half_heads else core
            at = (2 * lane_at(step % half_heads) + which) * share
            return pl.ds(pl.multiple_of(at, share), share)

        def fetch(step):
            at, slot = columns_of(step), step % 2
            return [
                pltpu.make_async_copy(gate_h.at[at], weights.at[slot, 0], w_sem.at[slot, 0]),
                pltpu.make_async_copy(value_h.at[at], weights.at[slot, 1], w_sem.at[slot, 1]),
            ]

        norms[...] = jnp.zeros_like(norms)
        for step in range(head_size):
            slot, at, k = step % 2, columns_of(step), step % half_heads
            keep = csend if step < half_heads else cown
            if step == 0:
                for load in fetch(0):
                    load.start()
            if step < head_size - 1:
                for load in fetch(step + 1):
                    load.start()
            for load in fetch(step):
                load.wait()

            def back_rows(c, _, slot=slot, at=at, k=k, keep=keep, first=step == 0, step=step):
                at_rows = rows_of(c)
                basis = jnp.where(c == head, dsum[at_rows], 0.0).astype(BF16)
                grad = (
                    dot(dz_r[at_rows], weights[slot, 0], NT) + dot(dxr_r[at_rows], weights[slot, 1], NT)
                    + dot(basis, state_m[at], NT) + dot(ddtr_r[at_rows], step_m[at], NT)
                )
                keep[k, at_rows] = grad.astype(BF16)
                weighed = grad * xn[at_rows, at].astype(F32)
                total = weighed[:, :LANES] if first else weight[at_rows] + weighed[:, :LANES]
                for q in range(1, share // LANES):
                    total += weighed[:, q * LANES : (q + 1) * LANES]
                weight[at_rows] = total
                norms[step] += jnp.broadcast_to(jnp.sum(weighed, axis=0, keepdims=True), (8, share))
                return 0

            lax.fori_loop(0, head_size, back_rows, 0)
            if step < half_heads:
                to_core(k).start()
            else:
                to_core(k).wait_recv()

                def add_rows(c, _, k=k):
                    at_rows = rows_of(c)
                    cown[k, at_rows] = (
                        cown[k, at_rows].astype(F32) + crecv[k, at_rows].astype(F32)
                    ).astype(BF16)
                    return 0

                lax.fori_loop(0, head_size, add_rows, 0)
                if k < half_heads - 1:
                    to_lane(k).start()
            if step == 0:
                arrived_loop(outer // 4, outer // 2)
            if step == head_size - 2:
                arrived_loop(outer // 2, outer - 1)

        rsend[...] = dot(jnp.ones((8, LANES), F32), weight[...], NT, precision=HIGH)

        def row_sums(d):
            return remote(rsend, rrecv.at[d - 1], rs_sem.at[d - 1], rr_sem.at[d - 1], seq, head_at(d))

        for d in range(1, head_size):
            row_sums(d).start()

        def share_norm(step):
            which = 1 - core if step < half_heads else core
            return remote(norms.at[step], nrecv.at[step], ns_sem.at[step], nr_sem.at[step],
                          seq, 2 * lane_at(step % half_heads) + which)

        for step in range(head_size - 1):
            share_norm(step).start()

        def give(src, out, r, sems_s, sems_r):
            return remote(src.at[r], out.at[member], sems_s.at[r], sems_r.at[member], base + r, head)

        for k in range(half_heads - 1):
            part_lane(k).wait_recv()
        for r in range(members):
            at = slice(r * length, (r + 1) * length)
            total = pown[half_heads - 1, at].astype(F32)
            for k in range(half_heads - 1):
                total = total + pyrecv[k, at].astype(F32)
            precv[0, at] = total.astype(BF16)

        def branch_rows(r):
            return precv.at[0, pl.ds(r * length, length)]

        for r in range(members):
            @pl.when(r != member)
            def _(r=r):
                remote(branch_rows(r), branch_o.at[member], bs_sem.at[r], br_sem.at[member],
                       base + r, head).start()

            @pl.when(r == member)
            def _(r=r):
                pltpu.make_async_copy(branch_rows(r), branch_o.at[r], copy_sem.at[0]).start()

        norm = norms[head_size - 1]
        for step in range(head_size - 1):
            share_norm(step).wait_recv()
            norm = norm + nrecv[step]
        full_sum[:, packed - share :] = norm / gain[...]

        def doubling(b):
            distance = 1 << b
            partner = seq + distance - 2 * distance * lax.rem(seq // distance, 2)
            return [
                remote(full_send.at[b], full_recv.at[b], fs_sem.at[b], fr_sem.at[b], partner, head),
                remote(low_send.at[b], low_recv.at[b], ls_sem.at[b], lr_sem.at[b], partner, head),
            ]

        def double(b):
            full_send[b] = full_sum[...]
            low_send[b] = low_sum[...].astype(BF16)
            for copy in doubling(b):
                copy.start()

        def doubled(b):
            for copy in doubling(b):
                copy.wait_recv()
            full_sum[...] = full_sum[...] + full_recv[b]
            low_sum[...] = low_send[b].astype(F32) + low_recv[b].astype(F32)

        double(0)
        arrived(outer - 1, False)
        for d in range(1, head_size):
            row_sums(d).wait_recv()
        sums = rsend[...]
        for d in range(1, head_size):
            sums = sums + rrecv[d - 1]
        pick = (lax.broadcasted_iota(jnp.int32, (8, LANES), 0) == 0).astype(F32)
        rrecv[0] = sums * (1.0 / width)
        for k in range(half_heads - 1):
            to_lane(k).wait_recv()

        def finish_rows(c, _):
            at_rows = rows_of(c)
            grad = cown[half_heads - 1, at_rows].astype(F32)
            for k in range(half_heads - 1):
                grad = grad + yrecv[k, at_rows].astype(F32)
            scale = rstd_r[at_rows]
            hat = mine_r[at_rows].astype(F32) * scale
            mean = dot(rrecv[0, :, at_rows], pick, TN, precision=HIGH)
            inside = pl.ds(pl.multiple_of(lax.rem(c, per) * chunk, chunk), chunk)
            for q in range(share // LANES):
                at = slice(q * LANES, (q + 1) * LANES)
                up[c // per, inside, at] = (
                    scale * (grad[:, at] * gain[:, at] - hat[:, at] * mean)
                ).astype(BF16)
            return 0

        lax.fori_loop(0, head_size, finish_rows, 0)
        for r in range(members):
            @pl.when(r != member)
            def _(r=r):
                give(up, up_o, r, us_sem, ur_sem).start()

        keep_up = pltpu.make_async_copy(up.at[member], up_o.at[member], copy_sem.at[1])
        keep_up.start()


        def settle(out, own, copy, landed):
            def one(k, total):
                copy(k).wait_recv()
                return total + landed[k].astype(F32)

            out[...] = lax.fori_loop(0, outer - 1, one, own.astype(F32))

        doubled(0)
        if steps > 1:
            double(1)
        load_half.wait()
        settle(gate_o, gown[...], along_gate, grecv)
        for b in range(1, steps - 1):
            doubled(b)
            double(b + 1)
        settle(value_o, duo[outer - 1, side], along, zrecv)
        if steps > 1:
            doubled(steps - 1)
        state_o[...] = low_sum[:share]
        step_o[...] = low_sum[share:]
        vkern_o[...] = full_sum[:taps, :channels]
        vbias_o[...] = full_sum[taps : taps + 1, :channels]
        ggain_o[...] = full_sum[taps + 1 : taps + 2, :channels]
        skern_o[...] = full_sum[:taps, channels : channels + both]
        sbias_o[...] = full_sum[taps : taps + 1, channels : channels + both]
        small_at = slice(channels + both, channels + both + heads)
        tbias_o[...] = full_sum[0:1, small_at]
        rate_o[...] = full_sum[1:2, small_at]
        skip_o[...] = full_sum[2:3, small_at]
        norm_o[...] = full_sum[0:1, packed - share :]

        for r in range(members):
            @pl.when(r != member)
            def _(r=r):
                remote(up.at[r], up_o.at[r], us_sem.at[r], ur_sem.at[r], base + r, head).wait()
                remote(branch_rows(r), branch_o.at[r], bs_sem.at[r], br_sem.at[r], base + r, head).wait()

            @pl.when(r == member)
            def _(r=r):
                pltpu.make_async_copy(branch_rows(r), branch_o.at[r], copy_sem.at[0]).wait()

        keep_up.wait()

        def drain(k, _):
            cross(k).wait_send()
            return 0

        def drain_along(k, _):
            along(k).wait_send()
            along_gate(k).wait_send()
            return 0

        lax.fori_loop(0, outer, drain, 0)
        lax.fori_loop(0, outer - 1, drain_along, 0)
        for k in range(half_heads):
            to_core(k).wait_send()
            if k < half_heads - 1:
                to_lane(k).wait_send()

        @pl.when(group > 0)
        def _():
            edge_back(head_r, hrecv, h_sem).wait_send()
            edge_back(low.at[pl.ds(0, EDGE)], hbrecv, hb_sem).wait_send()

        for k in range(half_heads):
            part_core(k).wait_send()
            if k < half_heads - 1:
                part_lane(k).wait_send()
        for d in range(1, head_size):
            row_sums(d).wait_send()
            basis_sum(d).wait_send()
        for step in range(head_size - 1):
            share_norm(step).wait_send()
        for b in range(steps):
            for copy in doubling(b):
                copy.wait_send()

    vmem = pl.BlockSpec(memory_space=pltpu.VMEM)
    anywhere = pl.BlockSpec(memory_space=pl.ANY)
    dma = pltpu.SemaphoreType.DMA
    args = (normal_in, dz, dxr, tail, head_rows, gate_matrix, value_matrix, state_matrix, step_matrix,
            value_kernel, state_kernel, state_bias, state_pre, state_edge, dbc, ddtr, vectors, small,
            part, mine, rstd, gain_share, gate_half)
    far = {2, 5, 6, 12, 14, 18, 22}
    moves = lambda *dims: pltpu.VMEM(dims, BF16)
    plain = lambda *dims: pltpu.VMEM(dims, F32)
    return pl.pallas_call(
        kernel,
        in_specs=[anywhere if i in far else vmem for i in range(len(args))],
        out_specs=[vmem] * 13 + [anywhere, anywhere],
        out_shape=[
            shape((strip, channels), F32), shape((strip, channels), F32),
            shape((share, both), F32), shape((low_rows - share, both), F32),
            shape((taps, channels), F32), shape((1, channels), F32), shape((1, channels), F32),
            shape((taps, both), F32), shape((1, both), F32), shape((1, share), F32),
            shape((1, heads), F32), shape((1, heads), F32), shape((1, heads), F32),
            shape((members, length, share), BF16), shape((members, length, share), BF16),
        ],
        scratch_shapes=[
            moves(rows, channels), moves(outer, 2, strip, channels), moves(outer, strip, channels),
            moves(outer - 1, strip, channels), moves(strip, channels),
            moves(outer - 1, strip, channels), moves(2, 2, share, channels), plain(rows, LANES),
            moves(half_heads, rows, share), moves(half_heads, rows, share),
            moves(half_heads, rows, share), moves(half_heads - 1, rows, share),
            plain(8, rows), plain(head_size - 1, 8, rows), moves(members, length, share),
            plain(head_size, 8, share), plain(head_size - 1, 8, share),
            moves(half_heads, rows, share), moves(half_heads, rows, share),
            moves(half_heads - 1, rows, share),
            plain(head_size - 1, chunk, both), plain(rows, both), plain(2 * EDGE, channels),
            plain(EDGE, channels), plain(EDGE, both), plain(rows + EDGE, both),
            plain(8, packed), plain(steps, 8, packed), plain(steps, 8, packed),
            plain(low_rows, both), moves(steps, low_rows, both), moves(steps, low_rows, both),
            dma((outer,)), dma((outer,)), dma((outer - 1,)), dma((outer - 1,)),
            dma((half_heads,)), dma((half_heads,)), dma((half_heads - 1,)), dma((half_heads - 1,)),
            dma((head_size - 1,)), dma((head_size - 1,)),
            dma((members,)), dma((members,)), dma((head_size - 1,)), dma((head_size - 1,)),
            dma((half_heads,)), dma((half_heads,)), dma((half_heads - 1,)), dma((half_heads - 1,)),
            dma((head_size - 1,)), dma((head_size - 1,)), dma((head_size - 1,)), dma((head_size - 1,)),
            dma((2,)), dma((2,)),
            dma((steps,)), dma((steps,)), dma((steps,)), dma((steps,)),
            dma((members,)), dma((members,)), dma((outer - 1,)), dma((outer - 1,)), dma((2, 2)),
            dma((4 + half_heads,)),
        ],
        compiler_params=pltpu.CompilerParams(
            collective_id=1, has_side_effects=True, vmem_limit_bytes=VMEM_BYTES
        ),
        cost_estimate=pl.CostEstimate(
            flops=60_000_000_000, bytes_accessed=300_000_000, transcendentals=0
        ),
        name="closing_sums",
    )(*args)

def shifted(block, axis, distance):
    devices = range(lax.axis_size(axis))
    route = [(i - distance, i) for i in devices if i - distance in devices]
    return lax.ppermute(block, axis, route)


def carried(part, decay, hops, distance):
    carry = shifted(part, "seq", distance)
    for _ in range(hops - 1):
        leaving = decay * carry.astype(F32) + part.astype(F32)
        carry = shifted(leaving.astype(BF16), "seq", distance)
    return carry


def summed_low(part, dim):
    low = part.astype(BF16)
    return lax.psum_scatter(low, "seq", scatter_dimension=dim, tiled=True).astype(F32)


def local(
    tokens,
    cotangent,
    norm_gain,
    gate_matrix,
    value_matrix,
    state_matrix,
    step_matrix,
    value_kernel,
    value_bias,
    state_kernel,
    state_bias,
    step_bias,
    log_rate,
    skip_gain,
    gate_gain,
    output_matrix,
):
    seq_count, length, share = tokens.shape
    hops = lax.axis_size("seq") // seq_count - 1
    width, channels = gate_matrix.shape
    heads = step_bias.shape[0]
    wide = channels // heads
    both = state_matrix.shape[1]
    taps = value_kernel.shape[0]
    rows = seq_count * length
    head_count = lax.axis_size("head")
    head_rank = lax.axis_index("head")
    row = lambda v: v.reshape(1, -1)

    (
        normal_in, flat_cot, mine, gate_pre, value_pre, state_pre, normed_grad, xs, xdt, xw, hin0,
        rstd, step_pre, bcs, dt, cum, cumt, pre, dec, value_edge, state_edge, carry,
    ) = opening(
        tokens, cotangent, row(norm_gain), gate_matrix, value_matrix, state_matrix, step_matrix,
        output_matrix, value_kernel, row(value_bias), state_kernel, row(state_bias), row(step_bias),
        row(log_rate), lax.axis_size("seq"), head_count,
    )
    whole_decay = jnp.repeat(pre[-1] * dec[-1], wide, axis=0)
    skip_row = row(jnp.repeat(skip_gain, wide))
    hin_low, normed, part, dy, dz, dv, ab, ds0, post, starting, gate_gain_part = forward(
        xdt, xs, bcs, gate_pre, normed_grad, cum, cumt, hin0, pre, dec, carry, skip_row,
        row(gate_gain), output_matrix, length, lax.axis_size("seq"), head_count,
    )
    back = carried(starting, whole_decay, hops, -seq_count)
    output_partial = dot(normed, flat_cot, TN)
    seq_size = lax.axis_size("seq")
    gate_keep, gate_give = halves(normal_in, dz, seq_size // 2)
    gate_half = lax.ppermute(gate_give, "seq", [(i, i ^ 1) for i in range(seq_size)])
    gate_half = (gate_keep.astype(F32) + gate_half.astype(F32)).astype(BF16)
    g, dbc_intra = intra_back(bcs, xdt, dy, cum, cumt, length)
    dxr, tail, head_rows, value_kernel_part, value_bias_part, ddtr, dbc, small = finish_back(
        value_pre, value_edge, value_kernel, row(value_bias), xs, xdt, xw, g, dy, dv, bcs, step_pre, dt, cum,
        ab, hin0, pre, carry, hin_low, ds0, post, back, dec, dbc_intra, skip_row, row(skip_gain),
        row(step_bias), row(log_rate), length,
    )
    vectors = jnp.concatenate(
        [value_kernel_part, value_bias_part, gate_gain_part, jnp.zeros((2, channels), F32)], axis=0
    )
    gain_share = lax.dynamic_slice_in_dim(norm_gain, head_rank * share, share, 0)
    (
        gate_grad, value_grad, state_grad, step_grad, value_kernel_grad, value_bias_grad,
        gate_gain_grad, state_kernel_grad, state_bias_grad, norm_grad, step_bias_grad, log_rate_grad,
        skip_gain_grad, up, branch,
    ) = closing(
        normal_in, dz, dxr, tail, head_rows, gate_matrix, value_matrix, state_matrix, step_matrix,
        value_kernel, state_kernel, row(state_bias), state_pre, state_edge, dbc, ddtr, vectors, small,
        part, mine, rstd, row(gain_share), gate_half, length, seq_size, head_count,
    )
    token_grad = cotangent.astype(F32) + up.astype(F32)
    layer_out = (tokens.astype(F32) + branch.astype(F32)).astype(BF16)
    output_grad = summed_low(output_partial, 1)
    strip = width // seq_size
    step_grad = jnp.transpose(step_grad.reshape(width // both, heads, both), (0, 2, 1))
    step_grad = lax.dynamic_slice_in_dim(
        step_grad.reshape(width, heads), lax.axis_index("seq") * strip, strip, 0
    )
    return (
        layer_out,
        token_grad,
        norm_grad[0],
        gate_grad,
        value_grad,
        state_grad,
        step_grad,
        value_kernel_grad,
        value_bias_grad[0],
        state_kernel_grad,
        state_bias_grad[0],
        step_bias_grad[0],
        log_rate_grad[0],
        skip_gain_grad[0],
        gate_gain_grad[0],
        output_grad,
    )


def solution(mesh):
    in_specs = (
        P(None, "seq", "head"),
        P(None, "seq", "head"),
        P(),
        P(None, "head"),
        P(None, "head"),
        P(),
        P(None, "head"),
        P(None, "head"),
        P("head"),
        P(),
        P(),
        P("head"),
        P("head"),
        P("head"),
        P("head"),
        P("head", None),
    )
    out_specs = (
        P(None, "seq", "head"),
        P(None, "seq", "head"),
        P("head"),
        P("seq", "head"),
        P("seq", "head"),
        P("head", None),
        P("seq", "head"),
        P(None, "head"),
        P("head"),
        P(),
        P(),
        P("head"),
        P("head"),
        P("head"),
        P("head"),
        P("head", "seq"),
    )
    return jax.shard_map(local, mesh=mesh, in_specs=in_specs, out_specs=out_specs, check_vma=False)
```

```python
import jax
import jax.numpy as jnp
from jax import lax
from jax.experimental import pallas as pl
from jax.experimental.pallas import tpu as pltpu
from jax.sharding import PartitionSpec as P

HIGH = lax.Precision.HIGHEST
EPSILON = 1e-05
F32 = jnp.float32
BF16 = jnp.bfloat16
LANES = 128
EDGE = 8
VMEM_BYTES = 56 * 1024 * 1024

NN = (((1,), (0,)), ((), ()))
NT = (((1,), (1,)), ((), ()))
TN = (((0,), (0,)), ((), ()))


def dot(a, b, dims=NN, precision=None):
    return lax.dot_general(a, b, dims, precision=precision, preferred_element_type=F32)


def dot_split(a, b, dims=NN):
    high = a.astype(BF16)
    rest = (a - high.astype(F32)).astype(BF16)
    return dot(high, b, dims) + dot(rest, b, dims)


def sigmoid(v):
    return 1.0 / (1.0 + jnp.exp(-v))


def silu(v):
    return v * sigmoid(v)


def slope(v):
    sigma = sigmoid(v)
    return sigma * (1.0 + v * (1.0 - sigma))


def softplus(v):
    return jnp.maximum(v, 0.0) + jnp.log1p(jnp.exp(-jnp.abs(v)))


def ones_where(shape, rule):
    rows = lax.broadcasted_iota(jnp.int32, shape, 0)
    cols = lax.broadcasted_iota(jnp.int32, shape, 1)
    return rule(rows, cols)


def head_picker(channels, heads):
    wide = channels // heads
    return ones_where((channels, heads), lambda r, c: r // wide == c).astype(F32).astype(BF16)


def pair_spread(cols, j, rows):
    lane = lax.broadcasted_iota(jnp.int32, (rows, LANES), 1)
    first = jnp.broadcast_to(cols[:, 2 * j : 2 * j + 1], (rows, LANES))
    second = jnp.broadcast_to(cols[:, 2 * j + 1 : 2 * j + 2], (rows, LANES))
    return jnp.where(lane < LANES // 2, first, second)


def spread(cols, rows, heads):
    return jnp.concatenate([pair_spread(cols, j, rows) for j in range(heads // 2)], axis=1)


def call(kernel, name, grid, in_specs, out_specs, out_shape, scratch, flops, args, transcendentals=0):
    moved = sum(a.size * a.dtype.itemsize for a in args) + sum(
        o.size * o.dtype.itemsize for o in out_shape
    )
    return pl.pallas_call(
        kernel,
        grid=grid,
        in_specs=in_specs,
        out_specs=out_specs,
        out_shape=out_shape,
        scratch_shapes=scratch,
        compiler_params=pltpu.CompilerParams(
            dimension_semantics=("arbitrary",) * len(grid), vmem_limit_bytes=VMEM_BYTES
        ),
        cost_estimate=pl.CostEstimate(
            flops=int(flops), bytes_accessed=int(moved), transcendentals=int(transcendentals)
        ),
        name=name,
    )(*args)


def shape(dims, dtype):
    return jax.ShapeDtypeStruct(dims, dtype)


def decays(cum, cumt, h, half):
    top = jnp.exp(jnp.minimum(cum[:half, h : h + 1] - cumt[h : h + 1, :half], 0.0))
    low = jnp.exp(jnp.minimum(cum[half:, h : h + 1] - cumt[h : h + 1, :], 0.0))
    return top, low


def lower_scores(basis, states, length):
    scores = dot(basis[:, states:], basis[:, :states], NT)
    return jnp.where(ones_where((length, length), lambda r, c: r >= c), scores, 0.0)


def intra_back(bcs, xdt, dy, cum, cumt, length):
    rows, channels = xdt.shape
    heads = cum.shape[1]
    both = bcs.shape[1]
    states = both // 2
    half = length // 2

    def kernel(bcs_r, xdt_r, dy_r, cum_r, cumt_r, g_o, dbc_o, grad):
        scores = lower_scores(bcs_r[...], states, length)
        cum_v, cumt_v = cum_r[...], cumt_r[...]
        lane = lax.broadcasted_iota(jnp.int32, (length, LANES), 1)
        grad[...] = jnp.zeros_like(grad)
        for j in range(heads // 2):
            at = slice(j * LANES, (j + 1) * LANES)
            pair, dpair = xdt_r[:, at], dy_r[:, at]
            g_top = jnp.zeros((half, LANES), F32)
            g_low = jnp.zeros((half, LANES), F32)
            for s in range(2):
                own = jnp.where((lane < LANES // 2) == (s == 0), dpair, jnp.zeros_like(dpair))
                top, low = decays(cum_v, cumt_v, 2 * j + s, half)
                grad[:half, :half] += dot(own[:half], pair[:half], NT) * top
                grad[half:] += dot(own[half:], pair, NT) * low
                w_top = (scores[:half, :half] * top).astype(BF16)
                w_low = (scores[half:] * low).astype(BF16)
                g_top += dot(w_top, own[:half], TN) + dot(w_low[:, :half], own[half:], TN)
                g_low += dot(w_low[:, half:], own[half:], TN)
            g_o[:half, at] = g_top
            g_o[half:, at] = g_low
        masked = jnp.where(ones_where((length, length), lambda r, c: r >= c), grad[...], 0.0)
        high = masked.astype(BF16)
        rest = (masked - high.astype(F32)).astype(BF16)
        in_b, out_b = bcs_r[:, :states], bcs_r[:, states:]
        dbc_o[:, :states] = dot(high, out_b, TN) + dot(rest, out_b, TN)
        dbc_o[:, states:] = dot(high, in_b) + dot(rest, in_b)

    tokens = lambda n: pl.BlockSpec((length, n), lambda i: (i, 0))
    return call(
        kernel, "within_blocks_back", (rows // length,),
        [tokens(both), tokens(channels), tokens(channels), tokens(heads),
         pl.BlockSpec((heads, length), lambda i: (0, i))],
        [tokens(channels), tokens(both)],
        [shape((rows, channels), F32), shape((rows, both), F32)],
        [pltpu.VMEM((length, length), F32)],
        2 * rows * length * channels * 8, (bcs, xdt, dy, cum, cumt), rows * length * heads,
    )


def finish_back(value_pre, value_edge, value_kernel, value_bias, xs, xdt, xw, g, dy, dv, bcs, step_pre, dt,
                cum, ab, hin0, pre, carry, hin_low, ds0, post, back, dec, dbc_intra, skip_row, skip_gain,
                step_bias, log_rate, length):
    rows, channels = xs.shape
    heads = cum.shape[1]
    both = bcs.shape[1]
    states = both // 2
    wide = channels // heads
    count = rows // length
    taps = value_kernel.shape[0]
    unit = length // EDGE

    def kernel(xr, xr_before, xr_edge, vk, vb, xs_r, xdt_r, xw_r, g_r, dy_r, dv_r, bcs_r, dtr, dt_r, cum_r,
               ab_r, hin_r, pre_r, carry_r, low_r, ds_r, post_r, back_r, dec_r, dbci, skip, skipg, tb,
               lr, dxr_o, tail_o, head_o, vkg_o, vbg_o, ddtr_o, dbc_o, small_o,
               padded, ext, ds_low, inner_sums):
        i = pl.program_id(0)
        block = count - 1 - i

        @pl.when(i == 0)
        def _():
            vkg_o[...] = jnp.zeros_like(vkg_o)
            vbg_o[...] = jnp.zeros_like(vbg_o)
            small_o[...] = jnp.zeros_like(small_o)
            ext[0:EDGE] = jnp.zeros((EDGE, channels), F32)

        @pl.when(block == 0)
        def _():
            padded[0:EDGE] = xr_edge[...]

        @pl.when(block > 0)
        def _():
            padded[0:EDGE] = xr_before[...]

        padded[EDGE:] = xr[...]
        ext[length:] = ext[0:EDGE]
        for h in range(heads):
            at = slice(h * wide, (h + 1) * wide)
            ds = ds_r[0, at] + post_r[0, h : h + 1] * back_r[at].astype(F32)
            ds_low[at] = ds.astype(BF16)
            hin = hin_r[0, at] + pre_r[0, h : h + 1] * carry_r[at].astype(F32)
            inner_sums[h : h + 1] = jnp.sum(ds * hin, axis=0, keepdims=True) * dec_r[0, h : h + 1]
        in_b = bcs_r[:, :states]
        dt_v, cum_v = dt_r[...], cum_r[...]
        fade = jnp.exp(cum_v[length - 1 : length] - cum_v)
        factor = fade * dt_v
        start = EDGE - taps + 1
        picker = head_picker(channels, heads)
        c_sum = jnp.zeros((length, heads), F32)
        d_sum = jnp.zeros((length, heads), F32)
        w_sum = jnp.zeros((length, heads), F32)
        for j in range(channels // LANES):
            at = slice(j * LANES, (j + 1) * LANES)
            xs_v = xs_r[:, at].astype(F32)
            dxw = dot(in_b, ds_low[at], NT)
            g_v = g_r[:, at]
            c_sum += dot_split(xs_v * g_v, picker[at])
            d_sum += dot_split(xs_v * dxw, picker[at])
            w_sum += dot_split(xdt_r[:, at].astype(F32) * g_v, picker[at])
            dxs = (
                pair_spread(dt_v, j, length) * g_v
                + pair_spread(factor, j, length) * dxw
                + skip[:, at] * dy_r[:, at].astype(F32)
            )
            total = vb[:, at] + vk[0:1, at] * padded[pl.ds(start, length), at]
            for k in range(1, taps):
                total = total + vk[k : k + 1, at] * padded[pl.ds(start + k, length), at]
            dpre = dxs * slope(total)
            ext[0:length, at] = dpre
            vbg_o[:, at] += jnp.sum(dpre, axis=0, keepdims=True)
            for k in range(taps):
                vkg_o[k : k + 1, at] += jnp.sum(
                    dpre * padded[pl.ds(start + k, length), at], axis=0, keepdims=True
                )
            dxr = vk[0:1, at] * ext[pl.ds(taps - 1, length), at]
            for k in range(1, taps):
                dxr = dxr + vk[k : k + 1, at] * ext[pl.ds(taps - 1 - k, length), at]
            dxr_o[:, at] = dxr.astype(BF16)

            @pl.when(i == 0)
            def _():
                tail_o[:, at] = dxr[length - EDGE :]

        head_o[...] = ext[0:EDGE]
        dbc_o[:, :states] = dbci[:, :states] + dot(xw_r[...], ds_low[...])
        dbc_o[:, states:] = dbci[:, states:] + dot(dv_r[...], low_r[0])
        rate = -jnp.exp(lr[...])
        a_sum, b_sum = ab_r[:, :heads], ab_r[:, heads:]
        e_sum = d_sum * factor
        ones = jnp.ones((1, LANES), F32)
        dtotal = jnp.sum(e_sum, axis=0, keepdims=True) + dot(ones, inner_sums[...], NT, precision=HIGH)
        row = lax.broadcasted_iota(jnp.int32, (length, heads), 0)
        dcum = a_sum - skipg[...] * b_sum - w_sum - e_sum
        dcum = dcum + jnp.where(row == length - 1, dtotal, 0.0)
        upper = ones_where((length, length), lambda r, c: r <= c).astype(F32)
        dda = dot(upper, dcum, precision=HIGH)
        ddt = c_sum + d_sum * fade + dda * rate
        dpre_dt = ddt * sigmoid(dtr[...] + tb[...])
        ddtr_o[...] = dpre_dt.astype(BF16)
        small_o[0:1] += jnp.sum(dpre_dt, axis=0, keepdims=True)
        small_o[1:2] += jnp.sum(dda * dt_v, axis=0, keepdims=True) * rate
        small_o[2:3] += jnp.sum(b_sum, axis=0, keepdims=True)

    last = count - 1
    whole = lambda *dims: pl.BlockSpec(dims, lambda i: (0,) * len(dims))
    tokens = lambda n: pl.BlockSpec((length, n), lambda i: (last - i, 0))
    before = lambda n: pl.BlockSpec((EDGE, n), lambda i: (jnp.maximum((last - i) * unit - 1, 0), 0))
    per = lambda *dims: pl.BlockSpec((1,) + dims, lambda i: (last - i, 0, 0))
    return call(
        kernel, "across_blocks_back", (count,),
        [tokens(channels), before(channels), whole(EDGE, channels), whole(taps, channels),
         whole(1, channels), tokens(channels), tokens(channels), tokens(channels), tokens(channels),
         tokens(channels), tokens(channels), tokens(both), tokens(heads), tokens(heads), tokens(heads),
         tokens(2 * heads), per(channels, states), per(heads, LANES), whole(channels, states),
         per(channels, states), per(channels, states), per(heads, LANES), whole(channels, states),
         per(heads, LANES), tokens(both), whole(1, channels), whole(1, heads), whole(1, heads),
         whole(1, heads)],
        [tokens(channels), whole(EDGE, channels), whole(EDGE, channels), whole(taps, channels),
         whole(1, channels), tokens(heads), tokens(both), whole(EDGE, heads)],
        [shape((rows, channels), BF16), shape((EDGE, channels), F32), shape((EDGE, channels), F32),
         shape((taps, channels), F32), shape((1, channels), F32), shape((rows, heads), BF16),
         shape((rows, both), F32), shape((EDGE, heads), F32)],
        [pltpu.VMEM((length + EDGE, channels), F32), pltpu.VMEM((length + EDGE, channels), F32),
         pltpu.VMEM((channels, states), BF16), pltpu.VMEM((heads, LANES), F32)],
        2 * rows * channels * states * 3,
        (value_pre, value_pre, value_edge, value_kernel, value_bias, xs, xdt, xw, g, dy, dv, bcs, step_pre,
         dt, cum, ab, hin0, pre, carry, hin_low, ds0, post, back, dec, dbc_intra, skip_row, skip_gain,
         step_bias, log_rate),
        2 * rows * channels,
    )


def halves(normal_in, grad, outer):
    rows, width = normal_in.shape
    channels = grad.shape[1]
    strip = width // (2 * outer)

    def kernel(xn, grad_r, keep_o, give_o):
        side = lax.rem(lax.axis_index("seq"), 2)
        product = dot(xn[...], grad_r[...], TN).astype(BF16)

        @pl.when(side == 0)
        def _():
            keep_o[0] = product[:strip]
            give_o[0] = product[strip:]

        @pl.when(side == 1)
        def _():
            keep_o[0] = product[strip:]
            give_o[0] = product[:strip]

    out = pl.BlockSpec((1, strip, channels), lambda i: (i, 0, 0))
    return call(
        kernel, "gate_strips", (outer,),
        [pl.BlockSpec((rows, 2 * strip), lambda i: (0, i)),
         pl.BlockSpec((rows, channels), lambda i: (0, 0))],
        [out, out], [shape((outer, strip, channels), BF16)] * 2, [], 2 * rows * width * channels,
        (normal_in, grad),
    )


def parities(normed, cotangent, outer):
    rows, width = cotangent.shape
    channels = normed.shape[1]
    strip = width // (2 * outer)

    def kernel(normed_r, cot, keep_o, give_o):
        parity = lax.rem(lax.axis_index("seq") // 2, 2)
        product = dot(normed_r[...], cot[...], TN).astype(BF16)
        for own in range(2):
            @pl.when(parity == own)
            def _(own=own):
                for side in range(2):
                    at, to = 2 * own + side, 2 * (1 - own) + side
                    keep_o[0, side] = product[:, at * strip : (at + 1) * strip]
                    give_o[0, side] = product[:, to * strip : (to + 1) * strip]

    out = pl.BlockSpec((1, 2, channels, strip), lambda i: (i, 0, 0, 0))
    return call(
        kernel, "output_strips", (outer // 2,),
        [pl.BlockSpec((rows, channels), lambda i: (0, 0)),
         pl.BlockSpec((rows, 4 * strip), lambda i: (0, i))],
        [out, out], [shape((outer // 2, 2, channels, strip), BF16)] * 2, [],
        2 * rows * width * channels, (normed, cotangent),
    )


def remote(src, dst, send, recv, seq, head):
    return pltpu.make_async_remote_copy(
        src_ref=src, dst_ref=dst, send_sem=send, recv_sem=recv, device_id=(seq, head),
        device_id_type=pl.DeviceIdType.MESH,
    )


def greet(seq, head, seq_size, head_size):
    barrier = pltpu.get_barrier_semaphore()
    for d in range(1, seq_size):
        pl.semaphore_signal(
            barrier, inc=1, device_id=(lax.rem(seq + d, seq_size), head),
            device_id_type=pl.DeviceIdType.MESH,
        )
    for d in range(1, head_size):
        pl.semaphore_signal(
            barrier, inc=1, device_id=(seq, lax.rem(head + d, head_size)),
            device_id_type=pl.DeviceIdType.MESH,
        )
    pl.semaphore_wait(barrier, seq_size - 1 + head_size - 1)


def forward(xdt, xs, bcs, gate_pre, normed_grad, cum, cumt, hin0, pre, dec, carry, skip_row, gate_gain,
            output_matrix, length, seq_size, head_size):
    rows, channels = xs.shape
    heads = cum.shape[1]
    both = bcs.shape[1]
    states = both // 2
    wide = channels // heads
    count = rows // length
    half = length // 2
    width = output_matrix.shape[1]
    inner = channels * head_size

    def kernel(xdt_r, xs_r, bcs_r, z_r, dn_r, cum_r, cumt_r, hin_r, pre_r, dec_r, carry_r, skip, gain, wo,
               low_o, normed_o, part_o, dy_o, dz_o, dv_o, ab_o, ds_o, post_o, start_o, ggain_o,
               y_s, sums, others, state, behind, prod_a, prod_b, s_sem, r_sem):
        i = pl.program_id(0)
        seq, head = lax.axis_index("seq"), lax.axis_index("head")
        barrier = pltpu.get_barrier_semaphore()

        def head_at(d):
            return lax.rem(head + d, head_size)

        def share_sums(d):
            return remote(sums, others.at[d - 1], s_sem.at[d - 1], r_sem.at[d - 1], seq, head_at(d))

        @pl.when(i == 0)
        def _():
            for d in range(1, head_size):
                pl.semaphore_signal(
                    barrier, inc=1, device_id=(seq, head_at(d)), device_id_type=pl.DeviceIdType.MESH
                )

        @pl.when(i < count)
        def _():
            at_rows = pl.ds(pl.multiple_of(i * length, length), length)
            for h in range(heads):
                at = slice(h * wide, (h + 1) * wide)
                low_o[0, at] = (
                    hin_r[0, at] + pre_r[0, h : h + 1] * carry_r[at].astype(F32)
                ).astype(BF16)
            scores = lower_scores(bcs_r[...], states, length)
            cum_v, cumt_v = cum_r[...], cumt_r[...]
            growth = jnp.exp(cum_v)
            lane = lax.broadcasted_iota(jnp.int32, (length, LANES), 1)
            squares = jnp.zeros((length, LANES), F32)
            crosses = jnp.zeros((length, LANES), F32)
            out_basis = bcs_r[:, states:]
            for j in range(channels // LANES):
                at = slice(j * LANES, (j + 1) * LANES)
                pair = xdt_r[:, at]
                y_top = jnp.zeros((half, LANES), F32)
                y_low = jnp.zeros((half, LANES), F32)
                for s in range(2):
                    own = jnp.where((lane < LANES // 2) == (s == 0), pair, jnp.zeros_like(pair))
                    top, low = decays(cum_v, cumt_v, 2 * j + s, half)
                    y_top += dot((scores[:half, :half] * top).astype(BF16), own[:half])
                    y_low += dot((scores[half:] * low).astype(BF16), own)
                v = dot(out_basis, low_o[0, at], NT)
                y = (
                    jnp.concatenate([y_top, y_low], axis=0)
                    + pair_spread(growth, j, length) * v
                    + skip[:, at] * xs_r[:, at].astype(F32)
                )
                y_s[at_rows, at] = y
                gated = y * silu(z_r[:, at])
                squares += gated * gated
                crosses += dn_r[:, at] * gain[:, at] * gated
            first = ones_where((8, LANES), lambda r, c: r == 0).astype(F32)
            second = ones_where((8, LANES), lambda r, c: r == 1).astype(F32)
            sums[:, at_rows] = dot(first, squares, NT, HIGH) + dot(second, crosses, NT, HIGH)

        @pl.when(i == count)
        def _():
            pl.semaphore_wait(barrier, head_size - 1)
            for d in range(1, head_size):
                share_sums(d).start()
            state[...] = jnp.zeros_like(state)
            behind[...] = jnp.ones_like(behind)
            ggain_o[...] = jnp.zeros_like(ggain_o)
            for d in range(1, head_size):
                share_sums(d).wait()
            total = sums[...]
            for d in range(1, head_size):
                total = total + others[d - 1]
            others[0] = total

        @pl.when(i >= count)
        def _():
            at_rows = pl.ds(pl.multiple_of((2 * count - 1 - i) * length, length), length)
            both_sums = others[0, :, at_rows]
            first = ones_where((8, LANES), lambda r, c: r == 0).astype(F32)
            second = ones_where((8, LANES), lambda r, c: r == 1).astype(F32)
            grstd = lax.rsqrt(dot(both_sums, first, TN, HIGH) * (1.0 / inner) + EPSILON)
            cross = (grstd * grstd * grstd) * (dot(both_sums, second, TN, HIGH) * (1.0 / inner))
            growth = jnp.exp(cum_r[...])
            for j in range(channels // LANES):
                at = slice(j * LANES, (j + 1) * LANES)
                y, z, dn = y_s[at_rows, at], z_r[:, at], dn_r[:, at]
                sigma = sigmoid(z)
                act = z * sigma
                gated = y * act
                scaled = gated * grstd
                normed_o[:, at] = (scaled * gain[:, at]).astype(BF16)
                ggain_o[:, at] += jnp.sum(dn * scaled, axis=0, keepdims=True)
                dgated = grstd * (dn * gain[:, at]) - gated * cross
                dy = (dgated * act).astype(BF16)
                dy_o[:, at] = dy
                dz_o[:, at] = (dgated * y * (sigma * (1.0 + z * (1.0 - sigma)))).astype(BF16)
                plain = dy.astype(F32)
                dv_o[:, at] = (plain * pair_spread(growth, j, length)).astype(BF16)
                prod_a[:, at] = plain * y
                prod_b[:, at] = plain * xs_r[:, at].astype(F32)
            picker = head_picker(channels, heads)
            ab_o[:, :heads] = dot_split(prod_a[...], picker)
            ab_o[:, heads:] = dot_split(prod_b[...], picker)
            part_o[...] = dot(normed_o[...], wo[...]).astype(BF16)
            dhin = dot(dv_o[...], bcs_r[:, states:], TN)
            ds_o[0] = state[...]
            post_o[0] = behind[...]
            behind[...] = behind[...] * dec_r[0]
            for h in range(heads):
                at = slice(h * wide, (h + 1) * wide)
                state[at] = dec_r[0, h : h + 1] * state[at] + dhin[at]
            start_o[...] = state[...].astype(BF16)

    last = count - 1
    ways = {
        "both": lambda i: jnp.where(i < count, i, 2 * count - 1 - i),
        "up": lambda i: jnp.minimum(i, last),
        "down": lambda i: jnp.minimum(2 * count - 1 - i, last),
    }
    whole = lambda *dims: pl.BlockSpec(dims, lambda i: (0,) * len(dims))
    tokens = lambda n, way: pl.BlockSpec((length, n), lambda i: (ways[way](i), 0))
    per = lambda way, *dims: pl.BlockSpec((1,) + dims, lambda i: (ways[way](i), 0, 0))
    args = (xdt, xs, bcs, gate_pre, normed_grad, cum, cumt, hin0, pre, dec, carry, skip_row, gate_gain,
            output_matrix)
    return pl.pallas_call(
        kernel,
        grid=(2 * count,),
        in_specs=[
            tokens(channels, "up"), tokens(channels, "both"), tokens(both, "both"),
            tokens(channels, "both"), tokens(channels, "both"), tokens(heads, "both"),
            pl.BlockSpec((heads, length), lambda i: (0, ways["up"](i))), per("up", channels, states),
            per("up", heads, LANES), per("down", heads, LANES), whole(channels, states),
            whole(1, channels), whole(1, channels), whole(channels, width),
        ],
        out_specs=[
            per("up", channels, states), tokens(channels, "down"), tokens(width, "down"),
            tokens(channels, "down"), tokens(channels, "down"), tokens(channels, "down"),
            tokens(2 * heads, "down"), per("down", channels, states), per("down", heads, LANES),
            whole(channels, states), whole(1, channels),
        ],
        out_shape=[
            shape((count, channels, states), BF16), shape((rows, channels), BF16),
            shape((rows, width), BF16), shape((rows, channels), BF16),
            shape((rows, channels), BF16), shape((rows, channels), BF16), shape((rows, 2 * heads), F32),
            shape((count, channels, states), F32), shape((count, heads, LANES), F32),
            shape((channels, states), BF16), shape((1, channels), F32),
        ],
        scratch_shapes=[
            pltpu.VMEM((rows, channels), F32), pltpu.VMEM((8, rows), F32),
            pltpu.VMEM((head_size - 1, 8, rows), F32), pltpu.VMEM((channels, states), F32),
            pltpu.VMEM((heads, LANES), F32), pltpu.VMEM((length, channels), F32),
            pltpu.VMEM((length, channels), F32),
            pltpu.SemaphoreType.DMA((head_size - 1,)), pltpu.SemaphoreType.DMA((head_size - 1,)),
        ],
        compiler_params=pltpu.CompilerParams(
            dimension_semantics=("arbitrary",), collective_id=3, has_side_effects=True,
            vmem_limit_bytes=VMEM_BYTES,
        ),
        cost_estimate=pl.CostEstimate(
            flops=2 * rows * channels * (width + 6 * length), bytes_accessed=60_000_000,
            transcendentals=rows * (length * heads + 2 * channels),
        ),
        name="blocks_and_gate",
    )(*args)


def opening(tokens, cotangent, norm_gain, gate_matrix, value_matrix, state_matrix, step_matrix,
            output_matrix, value_kernel, value_bias, state_kernel, state_bias, step_bias, log_rate,
            seq_size, head_size):
    members, length, share = tokens.shape
    rows = members * length
    width, channels = gate_matrix.shape
    both = state_matrix.shape[1]
    heads = step_matrix.shape[1]
    half_heads = head_size // 2
    states = both // 2
    wide = channels // heads
    taps = value_kernel.shape[0]
    groups = seq_size // members
    margin = EDGE - taps + 1

    def kernel(tokens_h, cot_h, gain, gate_h, value_h, state_h, step_m, out_h, vk, vb, sk, sb, tb, lr,
               xn_o, cot_o, mine_o, z_o, xr_o, bc_o, dn_o, xs_o, xdt_o, xw_o, hin_o,
               rstd_o, dtr_o, bcs_o, dt_o, cum_o, cumt_o, pre_o, dec_o, xedge_o, bedge_o, carry_o,
               whole, xn, z, xr, bc, dn, gate, value, state_m, out_m,
               padded, padded_bc, xs, xdt, xw, hin, state, ahead, leaving,
               gs_sem, gr_sem, ys_sem, yr_sem, cs_sem, cr_sem, w_sem, o_sem, l_sem, e_sem):
        seq, head = lax.axis_index("seq"), lax.axis_index("head")
        lane, core = head // 2, lax.rem(head, 2)
        group, member = seq // members, lax.rem(seq, members)
        base = seq - member
        sources = (tokens_h, cot_h)

        def rows_of(j):
            return pl.ds(pl.multiple_of(j * length, length), length)

        def lanes_of(h):
            return pl.ds(pl.multiple_of(h * share, share), share)

        own = [
            pltpu.make_async_copy(
                sources[a].at[member], whole.at[a, rows_of(member), lanes_of(head)], l_sem.at[a]
            )
            for a in range(2)
        ]
        loads = [
            pltpu.make_async_copy(src, dst, w_sem.at[i])
            for i, (src, dst) in enumerate(
                ((gate_h, gate), (value_h, value), (state_h, state_m), (out_h, out_m))
            )
        ]
        own[0].start()
        own[1].start()
        for load in loads:
            load.start()
        greet(seq, head, seq_size, head_size)

        def place(t):
            return lax.rem(member + t, members)

        def to_group(a, t):
            return remote(sources[a].at[place(t)], whole.at[a, rows_of(member), lanes_of(head)],
                          gs_sem.at[a, t - 1], gr_sem.at[a, members - 1 - t], base + place(t), head)

        def from_group(a, t):
            return remote(sources[a].at[place(t)], whole.at[a, rows_of(place(t)), lanes_of(head)],
                          gs_sem.at[a, t - 1], gr_sem.at[a, t - 1], seq, head)

        def to_lane(a, t, k):
            at = whole.at[a, rows_of(place(t)), lanes_of(head)]
            return remote(at, at, ys_sem.at[a, t, k], yr_sem.at[a, t, k],
                          seq, 2 * lax.rem(lane + 1 + k, half_heads) + core)

        def lane_from(k):
            return lax.rem(lane + half_heads - 1 - k, half_heads)

        def from_lane(a, t, k):
            at = whole.at[a, rows_of(place(t)), lanes_of(2 * lane_from(k) + core)]
            return remote(at, at, ys_sem.at[a, t, k], yr_sem.at[a, t, k], seq, head)

        def to_core(a, t, k):
            at = whole.at[a, rows_of(place(t)), lanes_of(2 * lane_from(k) + core)]
            return remote(at, at, cs_sem.at[a, t, k], cr_sem.at[a, t, k], seq, 2 * lane + 1 - core)

        def from_core(a, t, k):
            at = whole.at[a, rows_of(place(t)), lanes_of(2 * lane_from(k) + 1 - core)]
            return remote(at, at, cs_sem.at[a, t, k], cr_sem.at[a, t, k], seq, head)

        def forward(a, t):
            for k in range(half_heads - 1):
                to_lane(a, t, k).start()
            to_core(a, t, half_heads - 1).start()

        def collect(a, t):
            for k in range(half_heads - 1):
                from_lane(a, t, k).wait_recv()
                to_core(a, t, k).start()
            for k in range(half_heads):
                from_core(a, t, k).wait_recv()

        def outputs(t):
            at = rows_of(place(t))
            pairs = ((xn, xn_o), (z, z_o), (xr, xr_o), (bc, bc_o))
            return [
                pltpu.make_async_copy(src.at[at], dst.at[at], o_sem.at[i, t])
                for i, (src, dst) in enumerate(pairs)
            ]

        def late_outputs(t):
            at = rows_of(place(t))
            return [
                pltpu.make_async_copy(dn.at[at], dn_o.at[at], o_sem.at[4, t]),
                pltpu.make_async_copy(whole.at[1, at], cot_o.at[at], o_sem.at[5, t]),
                pltpu.make_async_copy(whole.at[0, at, lanes_of(head)], mine_o.at[at], o_sem.at[6, t]),
            ]

        def project(t):
            at = rows_of(place(t))
            squares = jnp.zeros((length, LANES), F32)
            for q in range(width // LANES):
                part = whole[0, at, q * LANES : (q + 1) * LANES].astype(F32)
                squares += part * part
            mean = jnp.sum(squares, axis=1, keepdims=True) * (1.0 / width)
            rstd = lax.rsqrt(mean + EPSILON)
            rstd_o[at] = rstd
            wide = jnp.broadcast_to(rstd, (length, LANES))
            for q in range(width // LANES):
                cols = slice(q * LANES, (q + 1) * LANES)
                xn[at, cols] = (whole[0, at, cols].astype(F32) * wide * gain[:, cols]).astype(BF16)
            normal = xn[at]
            if t == 0:
                for load in loads[:3]:
                    load.wait()
            xr[at] = dot(normal, value[...])
            z[at] = dot(normal, gate[...])
            bc[at] = dot(normal, state_m[...])
            dtr_o[at] = dot(normal, step_m[...])
            for copy in outputs(t):
                copy.start()

        def edges(there):
            tail = pl.ds(rows - EDGE, EDGE)
            return [
                remote(xr.at[tail], xedge_o, e_sem.at[0], e_sem.at[1], there, head),
                remote(bc.at[tail], bedge_o, e_sem.at[2], e_sem.at[3], there, head),
            ]

        def pass_on(there):
            return remote(leaving, carry_o, e_sem.at[4], e_sem.at[5], there, head)

        def block_outputs(i):
            at = rows_of(i)
            pairs = ((xs, xs_o), (xdt, xdt_o), (xw, xw_o))
            return [
                pltpu.make_async_copy(src.at[at], dst.at[at], o_sem.at[7 + n, i])
                for n, (src, dst) in enumerate(pairs)
            ] + [pltpu.make_async_copy(hin.at[i], hin_o.at[i], o_sem.at[10, i])]

        def prepare(i):
            at = slice(i * length, (i + 1) * length)
            if i == 0:
                padded[0:EDGE] = xedge_o[...]
                padded_bc[0:EDGE] = bedge_o[...]
                state[...] = jnp.zeros_like(state)
                ahead[...] = jnp.ones_like(ahead)
            else:
                padded[0:EDGE] = xr[i * length - EDGE : i * length]
                padded_bc[0:EDGE] = bc[i * length - EDGE : i * length]
            padded[EDGE:] = xr[at]
            padded_bc[EDGE:] = bc[at]
            summed = sb[...] + sk[0:1] * padded_bc[pl.ds(margin, length)]
            for k in range(1, taps):
                summed = summed + sk[k : k + 1] * padded_bc[pl.ds(margin + k, length)]
            basis = silu(summed).astype(BF16)
            bcs_o[at] = basis
            dt = softplus(dtr_o[at] + tb[...])
            da = dt * -jnp.exp(lr[...])
            lower = ones_where((length, length), lambda r, c: r >= c).astype(F32)
            upper = ones_where((length, length), lambda r, c: r <= c).astype(F32)
            cum = dot(lower, da, precision=HIGH)
            cumt = dot(da, upper, TN, precision=HIGH)
            dt_o[at] = dt
            cum_o[at] = cum
            cumt_o[:, at] = cumt
            factor = jnp.exp(cum[length - 1 : length] - cum) * dt
            decay = jnp.exp(jnp.broadcast_to(cumt[:, length - 1 : length], (heads, LANES)))
            dec_o[i] = decay
            pre_o[i] = ahead[...]
            ahead[...] = ahead[...] * decay
            hin[i] = state[...]
            for j in range(channels // LANES):
                cols = slice(j * LANES, (j + 1) * LANES)
                total = vb[:, cols] + vk[0:1, cols] * padded[pl.ds(margin, length), cols]
                for k in range(1, taps):
                    total = total + vk[k : k + 1, cols] * padded[pl.ds(margin + k, length), cols]
                value_low = silu(total).astype(BF16)
                xs[at, cols] = value_low
                plain = value_low.astype(F32)
                xdt[at, cols] = (plain * pair_spread(dt, j, length)).astype(BF16)
                xw[at, cols] = (plain * pair_spread(factor, j, length)).astype(BF16)
            local = dot(xw[at], basis[:, :states], TN)
            for h in range(heads):
                span = slice(h * wide, (h + 1) * wide)
                state[span] = decay[h : h + 1] * state[span] + local[span]
            for copy in block_outputs(i):
                copy.start()

        for t in range(1, members):
            to_group(0, t).start()
        own[0].wait()
        forward(0, 0)
        for t in range(1, members):
            from_group(0, t).wait_recv()
            forward(0, t)
        for t in range(1, members):
            to_group(1, t).start()
        own[1].wait()
        forward(1, 0)
        for t in range(members):
            collect(0, t)
            project(t)
            if t < members - 1:
                from_group(1, t + 1).wait_recv()
                forward(1, t + 1)
        @pl.when(group < groups - 1)
        def _():
            for copy in edges(seq + members):
                copy.start()

        @pl.when(group == 0)
        def _():
            xedge_o[...] = jnp.zeros_like(xedge_o)
            bedge_o[...] = jnp.zeros_like(bedge_o)
            carry_o[...] = jnp.zeros_like(carry_o)

        def gradient(t):
            collect(1, t)
            at = rows_of(place(t))
            dn[at] = dot(whole[1, at], out_m[...], NT)
            for copy in late_outputs(t):
                copy.start()

        loads[3].wait()
        gradient(0)

        @pl.when(group > 0)
        def _():
            for copy in edges(seq):
                copy.wait_recv()

        for i in range(members):
            prepare(i)
        leaving[...] = state[...].astype(BF16)

        @pl.when(group == 0)
        def _():
            pass_on(seq + members).start()

        for t in range(1, members):
            gradient(t)

        @pl.when(group > 0)
        def _():
            pass_on(seq).wait_recv()

            @pl.when(group < groups - 1)
            def _():
                for h in range(heads):
                    span = slice(h * wide, (h + 1) * wide)
                    leaving[span] = (
                        state[span] + ahead[h : h + 1] * carry_o[span].astype(F32)
                    ).astype(BF16)
                pass_on(seq + members).start()

        @pl.when(group < groups - 1)
        def _():
            for copy in edges(seq + members):
                copy.wait_send()
            pass_on(seq + members).wait_send()

        for t in range(members):
            for copy in outputs(t) + late_outputs(t) + block_outputs(t):
                copy.wait()
        for a in range(2):
            for t in range(1, members):
                to_group(a, t).wait_send()
            for t in range(members):
                for k in range(half_heads):
                    to_core(a, t, k).wait_send()
                    if k < half_heads - 1:
                        to_lane(a, t, k).wait_send()

    vmem = pl.BlockSpec(memory_space=pltpu.VMEM)
    anywhere = pl.BlockSpec(memory_space=pl.ANY)
    dma = pltpu.SemaphoreType.DMA
    args = (tokens, cotangent, norm_gain, gate_matrix, value_matrix, state_matrix, step_matrix,
            output_matrix, value_kernel, value_bias, state_kernel, state_bias, step_bias, log_rate)
    far = {0, 1, 3, 4, 5, 7}
    return pl.pallas_call(
        kernel,
        in_specs=[anywhere if i in far else vmem for i in range(len(args))],
        out_specs=[anywhere] * 11 + [vmem] * 11,
        out_shape=[
            shape((rows, width), BF16), shape((rows, width), BF16), shape((rows, share), BF16),
            shape((rows, channels), F32), shape((rows, channels), F32), shape((rows, both), F32),
            shape((rows, channels), F32), shape((rows, channels), BF16), shape((rows, channels), BF16),
            shape((rows, channels), BF16), shape((members, channels, states), F32),
            shape((rows, 1), F32), shape((rows, heads), F32), shape((rows, both), BF16),
            shape((rows, heads), F32), shape((rows, heads), F32), shape((heads, rows), F32),
            shape((members, heads, LANES), F32), shape((members, heads, LANES), F32),
            shape((EDGE, channels), F32), shape((EDGE, both), F32), shape((channels, states), BF16),
        ],
        scratch_shapes=[
            pltpu.VMEM((2, rows, width), BF16), pltpu.VMEM((rows, width), BF16),
            pltpu.VMEM((rows, channels), F32), pltpu.VMEM((rows, channels), F32),
            pltpu.VMEM((rows, both), F32), pltpu.VMEM((rows, channels), F32),
            pltpu.VMEM((width, channels), BF16), pltpu.VMEM((width, channels), BF16),
            pltpu.VMEM((width, both), BF16), pltpu.VMEM((channels, width), BF16),
            pltpu.VMEM((length + EDGE, channels), F32), pltpu.VMEM((length + EDGE, both), F32),
            pltpu.VMEM((rows, channels), BF16), pltpu.VMEM((rows, channels), BF16),
            pltpu.VMEM((rows, channels), BF16), pltpu.VMEM((members, channels, states), F32),
            pltpu.VMEM((channels, states), F32), pltpu.VMEM((heads, LANES), F32),
            pltpu.VMEM((channels, states), BF16),
            dma((2, members - 1)), dma((2, members - 1)),
            dma((2, members, max(half_heads - 1, 1))), dma((2, members, max(half_heads - 1, 1))),
            dma((2, members, half_heads)), dma((2, members, half_heads)),
            dma((4,)), dma((11, members)), dma((2,)), dma((6,)),
        ],
        compiler_params=pltpu.CompilerParams(
            collective_id=2, has_side_effects=True, vmem_limit_bytes=VMEM_BYTES
        ),
        cost_estimate=pl.CostEstimate(
            flops=2 * rows * width * (3 * channels + both), bytes_accessed=60_000_000, transcendentals=0
        ),
        name="opening_products",
    )(*args)

def closing(normal_in, dz, dxr, tail, head_rows, gate_matrix, value_matrix, state_matrix, step_matrix,
            value_kernel, state_kernel, state_bias, state_pre, state_edge, dbc, ddtr, vectors, small,
            branch, mine, rstd, gain_share, gate_half, output_half, length, seq_size, head_size):
    rows, width = normal_in.shape
    channels = dz.shape[1]
    heads = ddtr.shape[1]
    both = dbc.shape[1]
    share = mine.shape[1]
    taps = value_kernel.shape[0]
    members = rows // length
    outer = seq_size // 2
    half_heads = head_size // 2
    strip = width // seq_size
    chunk = rows // head_size
    per = head_size // members
    packed = channels + both + LANES + share
    low_rows = share + heads * width // both
    steps = seq_size.bit_length() - 1
    groups = seq_size // members

    def kernel(xn, dz_r, dxr_h, tail_r, head_r, gate_h, value_h, state_m, step_m, vk, sk, sb, bc_h,
               bc_edge, dbc_h, ddtr_r, vec, small_r, branch_h, mine_r, rstd_r, gain, gate_half_h,
               out_half_h,
               gate_o, value_o, out_o, state_o, step_o, vkern_o, vbias_o, ggain_o, skern_o, sbias_o, norm_o,
               tbias_o, rate_o, skip_o, up_o, branch_o,
               dxr_r, duo, xrecv, zrecv, gbuf, grecv, obuf, orecv, oxrecv, bpart, weights, weight, csend, cown, crecv, yrecv, rsend,
               rrecv, up, norms, nrecv, nlast, blow,
               drecv, dsum, ext, hrecv, hbrecv, low,
               full_sum, full_send, full_recv, low_sum, low_send, low_recv,
               xs_sem, xr_sem, zs_sem, zr_sem, cs_sem, cr_sem, ys_sem, yr_sem, rs_sem, rr_sem,
               us_sem, ur_sem, ns_sem, nr_sem, ds_sem, dr_sem,
               as_sem, ar_sem, h_sem, hb_sem, fs_sem, fr_sem, ls_sem, lr_sem, nl_sem, bs_sem, br_sem, gs_sem, gr_sem, os_sem, or_sem, ox_sem, half_sem, w_sem, copy_sem):
        seq, head = lax.axis_index("seq"), lax.axis_index("head")
        place, side = seq // 2, lax.rem(seq, 2)
        lane, core = head // 2, lax.rem(head, 2)
        group, member = seq // members, lax.rem(seq, members)
        base = seq - member
        load_dxr = pltpu.make_async_copy(dxr_h, dxr_r, copy_sem.at[0])
        load_dxr.start()
        load_bc = pltpu.make_async_copy(bc_h, low.at[pl.ds(EDGE, rows)], copy_sem.at[1])
        load_bc.start()
        low[0:EDGE] = bc_edge[...]

        def crossed(index, other, size):
            result, bit = 0, 1
            while bit < size:
                result = result + bit * lax.rem(index // bit + other // bit, 2)
                bit *= 2
            return result

        def outer_at(k):
            return crossed(place, outer - 1 - k, outer)

        def lane_at(k):
            return lax.rem(lane + 1 + k, half_heads)

        def seq_at(d):
            return lax.rem(seq + d, seq_size)

        def head_at(d):
            return lax.rem(head + d, head_size)

        own_rows = pl.ds(pl.multiple_of(head * chunk, chunk), chunk)
        load_dbc = pltpu.make_async_copy(
            dbc_h.at[own_rows], dsum.at[own_rows], copy_sem.at[2]
        )
        load_dbc.start()
        keep_branch = pltpu.make_async_copy(
            branch_h.at[member], branch_o.at[member], copy_sem.at[3]
        )
        keep_branch.start()
        gate_loads = [
            pltpu.make_async_copy(gate_half_h.at[crossed(place, c, outer)], gbuf.at[c], half_sem.at[c])
            for c in range(outer)
        ]
        out_loads = [
            pltpu.make_async_copy(
                out_half_h.at[crossed(place // 2, c, outer // 2)], obuf.at[c], half_sem.at[outer + c]
            )
            for c in range(outer // 2)
        ]
        for load in reversed(out_loads + gate_loads):
            load.start()
        greet(seq, head, seq_size, head_size)

        def cross(k):
            return remote(duo.at[k, 1 - side], xrecv.at[k], xs_sem.at[k], xr_sem.at[k],
                          2 * place + 1 - side, head)

        def zeros_of(c, size):
            count = 0
            while c % 2 == 0 and 1 << count < size:
                c, count = c // 2, count + 1
            return count

        def pass_along(held, landed, send, recv, c, span, size):
            bit = 1 << zeros_of(c, size)
            far = crossed(place, span * bit, outer)
            return remote(held, landed.at[c - 1], send.at[c - 1], recv.at[c - 1], 2 * far + side, head)

        def along(c):
            return pass_along(duo.at[outer - 1 - c, side], zrecv, zs_sem, zr_sem, c, 1, outer)

        def along_gate(c):
            return pass_along(gbuf.at[c], grecv, gs_sem, gr_sem, c, 1, outer)

        def along_out(c):
            return pass_along(obuf.at[c, side], orecv, os_sem, or_sem, c, 2, outer // 2)

        def gather_in(copy, landed, c, size):
            total = 0.0
            for b in range(zeros_of(c, size)):
                copy(c + (1 << b)).wait_recv()
                total = total + landed[c + (1 << b) - 1].astype(F32)
            return total

        def gate_step(c):
            gate_loads[c].wait()
            if zeros_of(c, outer):
                gbuf[c] = (gbuf[c].astype(F32) + gather_in(along_gate, grecv, c, outer)).astype(BF16)
            along_gate(c).start()

        def cross_out(c):
            return remote(obuf.at[c, 1 - side], oxrecv.at[c], ox_sem.at[0, c], ox_sem.at[1, c],
                          2 * place + 1 - side, head)

        def out_step(c):
            cross_out(c).wait_recv()
            total = obuf[c, side].astype(F32) + oxrecv[c].astype(F32)
            if c:
                total = total + gather_in(along_out, orecv, c, outer // 2)
            obuf[c, side] = total.astype(BF16)
            if c:
                along_out(c).start()

        def branch_give(r):
            return remote(branch_h.at[r], branch_o.at[member], bs_sem.at[r], br_sem.at[member],
                          base + r, head)

        def edge_back(src, dst, sems):
            return remote(src, dst, sems.at[0], sems.at[1], seq - members, head)

        def rows_of(c):
            return pl.ds(pl.multiple_of(c * chunk, chunk), chunk)

        def basis_sum(d):
            return remote(dbc_h.at[rows_of(head_at(d))], drecv.at[d - 1], ds_sem.at[d - 1],
                          dr_sem.at[d - 1], seq, head_at(d))

        def basis_share(d):
            at = rows_of(head)
            return remote(dsum.at[at], dsum.at[at], as_sem.at[d - 1], ar_sem.at[d - 1], seq, head_at(d))

        @pl.when(group > 0)
        def _():
            edge_back(head_r, hrecv, h_sem).start()

        for d in range(1, head_size):
            basis_sum(d).start()
        for c in range(outer // 2 - 1, -1, -1):
            out_loads[c].wait()
            cross_out(c).start()
        for c in range(outer - 1, 0, -1):
            if c % 2:
                gate_step(c)

        load_dxr.wait()
        ext[...] = jnp.zeros_like(ext)

        @pl.when(group < groups - 1)
        def _():
            remote(head_r, hrecv, h_sem.at[0], h_sem.at[1], seq, head).wait_recv()
            ext[EDGE:] = hrecv[...]

        fixed = tail_r[...]
        for k in range(taps):
            fixed = fixed + vk[k : k + 1] * ext[pl.ds(taps - 1 - k, EDGE)]
        last = dxr_r[rows - 2 * EDGE :].astype(F32)
        dxr_r[rows - 2 * EDGE :] = jnp.concatenate([last[:EDGE], fixed], axis=0).astype(BF16)

        def multiply(k, _):
            at = pl.ds(pl.multiple_of(outer_at(k) * 2 * strip, 2 * strip), 2 * strip)
            product = dot(xn[:, at], dxr_r[...], TN).astype(BF16)
            duo[k, 0] = product[:strip]
            duo[k, 1] = product[strip:]

            @pl.when(k < outer // 2)
            def _():
                cross(k).start()

            return 0

        lax.fori_loop(0, outer, multiply, 0)
        for r in range(members):
            @pl.when(r != member)
            def _(r=r):
                branch_give(r).start()


        step_part = dot(ddtr_r[...], xn[...], TN)
        for q in range(width // both):
            low_sum[share + q * heads : share + (q + 1) * heads] = step_part[
                :, q * both : (q + 1) * both
            ]

        load_dbc.wait()
        total = dsum[own_rows]
        for d in range(1, head_size):
            basis_sum(d).wait_recv()
            total = total + drecv[d - 1]
        dsum[own_rows] = total
        for d in range(1, head_size):
            basis_share(d).start()

        def arrived(k):
            c = outer - 1 - k
            cross(k).wait_recv()
            total = duo[k, side].astype(F32) + xrecv[k].astype(F32)
            if c:
                total = total + gather_in(along, zrecv, c, outer)
            duo[k, side] = total.astype(BF16)
            if c:
                along(c).start()

        def arrived_loop(first, last):
            for k in range(first, last):
                arrived(k)

        def to_core(k):
            return remote(csend.at[k], crecv.at[k], cs_sem.at[k], cr_sem.at[k], seq, 2 * lane + 1 - core)

        def to_lane(k):
            return remote(cown.at[k], yrecv.at[k], ys_sem.at[k], yr_sem.at[k],
                          seq, 2 * lane_at(k) + core)

        def columns_of(step):
            which = 1 - core if step < half_heads else core
            at = (2 * lane_at(step % half_heads) + which) * share
            return pl.ds(pl.multiple_of(at, share), share)

        def fetch(step):
            at, slot = columns_of(step), step % 2
            return [
                pltpu.make_async_copy(gate_h.at[at], weights.at[slot, 0], w_sem.at[slot, 0]),
                pltpu.make_async_copy(value_h.at[at], weights.at[slot, 1], w_sem.at[slot, 1]),
            ]

        norms[...] = jnp.zeros_like(norms)
        for step in range(head_size):
            slot, at, k = step % 2, columns_of(step), step % half_heads
            keep = csend if step < half_heads else cown
            if step == 0:
                for load in fetch(0):
                    load.start()
            if step < head_size - 1:
                for load in fetch(step + 1):
                    load.start()
            for load in fetch(step):
                load.wait()

            def back_rows(c, _, slot=slot, at=at, k=k, keep=keep, first=step == 0, step=step):
                at_rows = rows_of(c)
                grad = (
                    dot(dz_r[at_rows], weights[slot, 0], NT) + dot(dxr_r[at_rows], weights[slot, 1], NT)
                    + dot(ddtr_r[at_rows], step_m[at], NT)
                )
                keep[k, at_rows] = grad.astype(BF16)
                weighed = grad * xn[at_rows, at].astype(F32)
                total = weighed[:, :LANES] if first else weight[at_rows] + weighed[:, :LANES]
                for q in range(1, share // LANES):
                    total += weighed[:, q * LANES : (q + 1) * LANES]
                weight[at_rows] = total
                norms[step] += jnp.broadcast_to(jnp.sum(weighed, axis=0, keepdims=True), (8, share))
                return 0

            lax.fori_loop(0, head_size, back_rows, 0)
            if step < half_heads:
                to_core(k).start()
            else:
                to_core(k).wait_recv()

                def add_rows(c, _, k=k):
                    at_rows = rows_of(c)
                    cown[k, at_rows] = (
                        cown[k, at_rows].astype(F32) + crecv[k, at_rows].astype(F32)
                    ).astype(BF16)
                    return 0

                lax.fori_loop(0, head_size, add_rows, 0)
                if k < half_heads - 1:
                    to_lane(k).start()
            if step == 0:
                for c in range(outer - 1, 0, -1):
                    if c % 2 == 0:
                        gate_step(c)
            if step == head_size - 2:
                for c in range(outer // 2 - 1, 0, -1):
                    out_step(c)

        for d in range(1, head_size):
            at = rows_of(head_at(d))
            remote(dsum.at[at], dsum.at[at], as_sem.at[d - 1], ar_sem.at[head_size - 1 - d],
                   seq, head).wait_recv()

        start = EDGE - taps + 1
        load_bc.wait()
        pre_bc = sb[...]
        for k in range(taps):
            pre_bc = pre_bc + sk[k : k + 1] * low[pl.ds(start + k, rows)]
        dpre = dsum[...] * slope(pre_bc)
        full_sum[...] = jnp.zeros_like(full_sum)
        full_sum[:, :channels] = vec[...]
        full_sum[:, channels + both : channels + both + heads] = small_r[...]
        for k in range(taps):
            full_sum[k : k + 1, channels : channels + both] = jnp.sum(
                dpre * low[pl.ds(start + k, rows)], axis=0, keepdims=True
            )
        full_sum[taps : taps + 1, channels : channels + both] = jnp.sum(dpre, axis=0, keepdims=True)
        low[0:rows] = dpre
        low[rows:] = jnp.zeros((EDGE, both), F32)

        @pl.when(group > 0)
        def _():
            edge_back(low.at[pl.ds(0, EDGE)], hbrecv, hb_sem).start()

        arrived_loop(0, outer // 4)

        @pl.when(group < groups - 1)
        def _():
            remote(low.at[pl.ds(0, EDGE)], hbrecv, hb_sem.at[0], hb_sem.at[1], seq, head).wait_recv()
            low[rows:] = hbrecv[...]

        dbc_v = sk[0:1] * low[pl.ds(taps - 1, rows)]
        for k in range(1, taps):
            dbc_v = dbc_v + sk[k : k + 1] * low[pl.ds(taps - 1 - k, rows)]
        dbc_low = dbc_v.astype(BF16)
        own_at = pl.ds(pl.multiple_of(head * share, share), share)
        low_sum[:share] = dot(xn[:, own_at], dbc_low, TN)
        blow[...] = dbc_low

        def doubling(b):
            distance = 1 << b
            partner = seq + distance - 2 * distance * lax.rem(seq // distance, 2)
            return [
                remote(full_send.at[b], full_recv.at[b], fs_sem.at[b], fr_sem.at[b], partner, head),
                remote(low_send.at[b], low_recv.at[b], ls_sem.at[b], lr_sem.at[b], partner, head),
            ]

        def double(b):
            full_send[b] = full_sum[...]
            low_send[b] = low_sum[...].astype(BF16)
            for copy in doubling(b):
                copy.start()

        def doubled(b):
            for copy in doubling(b):
                copy.wait_recv()
            full_sum[...] = full_sum[...] + full_recv[b]
            low_sum[...] = low_send[b].astype(F32) + low_recv[b].astype(F32)

        double(0)

        def send_rest(k, _):
            cross(k).start()
            return 0

        lax.fori_loop(outer // 2, outer, send_rest, 0)

        def basis_rows(c, _):
            at_rows = rows_of(c)
            grad = dot(blow[at_rows], state_m[own_at], NT)
            bpart[at_rows] = grad.astype(BF16)
            weighed = grad * xn[at_rows, own_at].astype(F32)
            total = weight[at_rows]
            for q in range(share // LANES):
                total += weighed[:, q * LANES : (q + 1) * LANES]
            weight[at_rows] = total
            norms[head_size - 1] += jnp.broadcast_to(
                jnp.sum(weighed, axis=0, keepdims=True), (8, share)
            )
            return 0

        lax.fori_loop(0, head_size, basis_rows, 0)
        rsend[...] = dot(jnp.ones((8, LANES), F32), weight[...], NT, precision=HIGH)

        def row_sums(d):
            return remote(rsend, rrecv.at[d - 1], rs_sem.at[d - 1], rr_sem.at[d - 1], seq, head_at(d))

        for d in range(1, head_size):
            row_sums(d).start()

        def share_norm(step):
            which = 1 - core if step < half_heads else core
            return remote(norms.at[step], nrecv.at[step], ns_sem.at[step], nr_sem.at[step],
                          seq, 2 * lane_at(step % half_heads) + which)

        for step in range(head_size - 1):
            share_norm(step).start()

        arrived_loop(outer // 4, outer // 2)

        def give(r):
            return remote(up.at[r], up_o.at[member], us_sem.at[r], ur_sem.at[member], base + r, head)

        for d in range(1, head_size):
            row_sums(d).wait_recv()
        sums = rsend[...]
        for d in range(1, head_size):
            sums = sums + rrecv[d - 1]
        pick = (lax.broadcasted_iota(jnp.int32, (8, LANES), 0) == 0).astype(F32)
        rrecv[0] = sums * (1.0 / width)
        for k in range(half_heads - 1):
            to_lane(k).wait_recv()

        def finish_rows(c, _):
            at_rows = rows_of(c)
            grad = cown[half_heads - 1, at_rows].astype(F32) + bpart[at_rows].astype(F32)
            for k in range(half_heads - 1):
                grad = grad + yrecv[k, at_rows].astype(F32)
            scale = rstd_r[at_rows]
            hat = mine_r[at_rows].astype(F32) * scale
            mean = dot(rrecv[0, :, at_rows], pick, TN, precision=HIGH)
            inside = pl.ds(pl.multiple_of(lax.rem(c, per) * chunk, chunk), chunk)
            for q in range(share // LANES):
                at = slice(q * LANES, (q + 1) * LANES)
                up[c // per, inside, at] = (
                    scale * (grad[:, at] * gain[:, at] - hat[:, at] * mean)
                ).astype(BF16)
            return 0

        lax.fori_loop(0, head_size, finish_rows, 0)
        for r in range(members):
            @pl.when(r != member)
            def _(r=r):
                give(r).start()

        keep_up = pltpu.make_async_copy(up.at[member], up_o.at[member], copy_sem.at[0])
        keep_up.start()

        norm = norms[head_size - 1]
        for step in range(head_size - 1):
            share_norm(step).wait_recv()
            norm = norm + nrecv[step]
        doubled(0)
        full_sum[:, packed - share :] = norm / gain[...]

        double(1)
        arrived_loop(outer // 2, outer)
        out_step(0)
        gate_loads[0].wait()
        gate_o[...] = gbuf[0].astype(F32) + gather_in(along_gate, grecv, 0, outer)
        out_o[...] = obuf[0, side].astype(F32) + gather_in(along_out, orecv, 0, outer // 2)
        for b in range(1, steps - 1):
            doubled(b)
            double(b + 1)
        value_o[...] = duo[outer - 1, side].astype(F32) + gather_in(along, zrecv, 0, outer)
        doubled(steps - 1)
        for step in range(head_size - 1):
            share_norm(step).wait_send()
        norms[0] = full_sum[:, packed - share :]
        last_norm = remote(norms.at[0], nlast, nl_sem.at[0], nl_sem.at[1], 2 * place + 1 - side, head)
        last_norm.start()
        state_o[...] = low_sum[:share]
        step_o[...] = low_sum[share:]
        vkern_o[...] = full_sum[:taps, :channels]
        vbias_o[...] = full_sum[taps : taps + 1, :channels]
        ggain_o[...] = full_sum[taps + 1 : taps + 2, :channels]
        skern_o[...] = full_sum[:taps, channels : channels + both]
        sbias_o[...] = full_sum[taps : taps + 1, channels : channels + both]
        small_at = slice(channels + both, channels + both + heads)
        tbias_o[...] = full_sum[0:1, small_at]
        rate_o[...] = full_sum[1:2, small_at]
        skip_o[...] = full_sum[2:3, small_at]
        last_norm.wait()
        norm_o[...] = norms[0, 0:1] + nlast[0:1]

        for r in range(members):
            @pl.when(r != member)
            def _(r=r):
                remote(up.at[r], up_o.at[r], us_sem.at[r], ur_sem.at[r], base + r, head).wait()
                remote(branch_h.at[r], branch_o.at[r], bs_sem.at[r], br_sem.at[r], base + r, head).wait()

        keep_branch.wait()
        keep_up.wait()

        def drain(k, _):
            cross(k).wait_send()
            return 0

        lax.fori_loop(0, outer, drain, 0)
        for c in range(1, outer):
            along(c).wait_send()
            along_gate(c).wait_send()
        for c in range(1, outer // 2):
            along_out(c).wait_send()
        for c in range(outer // 2):
            cross_out(c).wait_send()
        for k in range(half_heads):
            to_core(k).wait_send()
            if k < half_heads - 1:
                to_lane(k).wait_send()

        @pl.when(group > 0)
        def _():
            edge_back(head_r, hrecv, h_sem).wait_send()
            edge_back(low.at[pl.ds(0, EDGE)], hbrecv, hb_sem).wait_send()

        for d in range(1, head_size):
            row_sums(d).wait_send()
            basis_sum(d).wait_send()
            basis_share(d).wait_send()
        for b in range(steps):
            for copy in doubling(b):
                copy.wait_send()

    vmem = pl.BlockSpec(memory_space=pltpu.VMEM)
    anywhere = pl.BlockSpec(memory_space=pl.ANY)
    dma = pltpu.SemaphoreType.DMA
    args = (normal_in, dz, dxr, tail, head_rows, gate_matrix, value_matrix, state_matrix, step_matrix,
            value_kernel, state_kernel, state_bias, state_pre, state_edge, dbc, ddtr, vectors, small,
            branch, mine, rstd, gain_share, gate_half, output_half)
    far = {2, 5, 6, 12, 14, 18, 22, 23}
    moves = lambda *dims: pltpu.VMEM(dims, BF16)
    plain = lambda *dims: pltpu.VMEM(dims, F32)
    return pl.pallas_call(
        kernel,
        in_specs=[anywhere if i in far else vmem for i in range(len(args))],
        out_specs=[vmem] * 14 + [anywhere, anywhere],
        out_shape=[
            shape((strip, channels), F32), shape((strip, channels), F32), shape((channels, strip), F32),
            shape((share, both), F32), shape((low_rows - share, both), F32),
            shape((taps, channels), F32), shape((1, channels), F32), shape((1, channels), F32),
            shape((taps, both), F32), shape((1, both), F32), shape((1, share), F32),
            shape((1, heads), F32), shape((1, heads), F32), shape((1, heads), F32),
            shape((members, length, share), BF16), shape((members, length, share), BF16),
        ],
        scratch_shapes=[
            moves(rows, channels), moves(outer, 2, strip, channels), moves(outer, strip, channels),
            moves(outer - 1, strip, channels), moves(outer, strip, channels),
            moves(outer - 1, strip, channels), moves(outer // 2, 2, channels, strip),
            moves(outer // 2 - 1, channels, strip), moves(outer // 2, channels, strip),
            moves(rows, share), moves(2, 2, share, channels), plain(rows, LANES),
            moves(half_heads, rows, share), moves(half_heads, rows, share),
            moves(half_heads, rows, share), moves(half_heads - 1, rows, share),
            plain(8, rows), plain(head_size - 1, 8, rows), moves(members, length, share),
            plain(head_size, 8, share), plain(head_size - 1, 8, share), plain(8, share),
            moves(rows, both),
            plain(head_size - 1, chunk, both), plain(rows, both), plain(2 * EDGE, channels),
            plain(EDGE, channels), plain(EDGE, both), plain(rows + EDGE, both),
            plain(8, packed), plain(steps, 8, packed), plain(steps, 8, packed),
            plain(low_rows, both), moves(steps, low_rows, both), moves(steps, low_rows, both),
            dma((outer,)), dma((outer,)), dma((outer - 1,)), dma((outer - 1,)),
            dma((half_heads,)), dma((half_heads,)), dma((half_heads - 1,)), dma((half_heads - 1,)),
            dma((head_size - 1,)), dma((head_size - 1,)),
            dma((members,)), dma((members,)), dma((head_size - 1,)), dma((head_size - 1,)),
            dma((head_size - 1,)), dma((head_size - 1,)), dma((head_size - 1,)), dma((head_size - 1,)),
            dma((2,)), dma((2,)),
            dma((steps,)), dma((steps,)), dma((steps,)), dma((steps,)), dma((2,)),
            dma((members,)), dma((members,)), dma((outer - 1,)), dma((outer - 1,)),
            dma((outer // 2 - 1,)), dma((outer // 2 - 1,)), dma((2, outer // 2)), dma((outer + outer // 2,)),
            dma((2, 2)), dma((4,)),
        ],
        compiler_params=pltpu.CompilerParams(
            collective_id=1, has_side_effects=True, vmem_limit_bytes=VMEM_BYTES
        ),
        cost_estimate=pl.CostEstimate(
            flops=60_000_000_000, bytes_accessed=300_000_000, transcendentals=0
        ),
        name="closing_sums",
    )(*args)

def shifted(block, axis, distance):
    devices = range(lax.axis_size(axis))
    route = [(i - distance, i) for i in devices if i - distance in devices]
    return lax.ppermute(block, axis, route)


def carried(part, decay, hops, distance):
    carry = shifted(part, "seq", distance)
    for _ in range(hops - 1):
        leaving = decay * carry.astype(F32) + part.astype(F32)
        carry = shifted(leaving.astype(BF16), "seq", distance)
    return carry


def swapped(block, distance):
    size = lax.axis_size("seq")
    return lax.ppermute(block, "seq", [(i, i ^ distance) for i in range(size)])


def local(
    tokens,
    cotangent,
    norm_gain,
    gate_matrix,
    value_matrix,
    state_matrix,
    step_matrix,
    value_kernel,
    value_bias,
    state_kernel,
    state_bias,
    step_bias,
    log_rate,
    skip_gain,
    gate_gain,
    output_matrix,
):
    seq_count, length, share = tokens.shape
    hops = lax.axis_size("seq") // seq_count - 1
    width, channels = gate_matrix.shape
    heads = step_bias.shape[0]
    wide = channels // heads
    both = state_matrix.shape[1]
    taps = value_kernel.shape[0]
    rows = seq_count * length
    head_count = lax.axis_size("head")
    head_rank = lax.axis_index("head")
    row = lambda v: v.reshape(1, -1)

    (
        normal_in, flat_cot, mine, gate_pre, value_pre, state_pre, normed_grad, xs, xdt, xw, hin0,
        rstd, step_pre, bcs, dt, cum, cumt, pre, dec, value_edge, state_edge, carry,
    ) = opening(
        tokens, cotangent, row(norm_gain), gate_matrix, value_matrix, state_matrix, step_matrix,
        output_matrix, value_kernel, row(value_bias), state_kernel, row(state_bias), row(step_bias),
        row(log_rate), lax.axis_size("seq"), head_count,
    )
    whole_decay = jnp.repeat(pre[-1] * dec[-1], wide, axis=0)
    skip_row = row(jnp.repeat(skip_gain, wide))
    hin_low, normed, part, dy, dz, dv, ab, ds0, post, starting, gate_gain_part = forward(
        xdt, xs, bcs, gate_pre, normed_grad, cum, cumt, hin0, pre, dec, carry, skip_row,
        row(gate_gain), output_matrix, length, lax.axis_size("seq"), head_count,
    )
    back = carried(starting, whole_decay, hops, -seq_count)
    seq_size = lax.axis_size("seq")
    gate_keep, gate_give = halves(normal_in, dz, seq_size // 2)
    gate_got = swapped(gate_give, 1)
    output_keep, output_give = parities(normed, flat_cot, seq_size // 2)
    output_give, back = lax.optimization_barrier((output_give, back))
    output_got = swapped(output_give, 2)
    branch = lax.psum_scatter(part, "head", scatter_dimension=1, tiled=True).reshape(tokens.shape)
    g, dbc_intra = intra_back(bcs, xdt, dy, cum, cumt, length)
    dxr, tail, head_rows, value_kernel_part, value_bias_part, ddtr, dbc, small = finish_back(
        value_pre, value_edge, value_kernel, row(value_bias), xs, xdt, xw, g, dy, dv, bcs, step_pre, dt, cum,
        ab, hin0, pre, carry, hin_low, ds0, post, back, dec, dbc_intra, skip_row, row(skip_gain),
        row(step_bias), row(log_rate), length,
    )
    gate_half = (gate_keep.astype(F32) + gate_got.astype(F32)).astype(BF16)
    output_half = (output_keep.astype(F32) + output_got.astype(F32)).astype(BF16)
    vectors = jnp.concatenate(
        [value_kernel_part, value_bias_part, gate_gain_part, jnp.zeros((2, channels), F32)], axis=0
    )
    gain_share = lax.dynamic_slice_in_dim(norm_gain, head_rank * share, share, 0)
    (
        gate_grad, value_grad, output_grad, state_grad, step_grad, value_kernel_grad, value_bias_grad,
        gate_gain_grad, state_kernel_grad, state_bias_grad, norm_grad, step_bias_grad, log_rate_grad,
        skip_gain_grad, up, branch,
    ) = closing(
        normal_in, dz, dxr, tail, head_rows, gate_matrix, value_matrix, state_matrix, step_matrix,
        value_kernel, state_kernel, row(state_bias), state_pre, state_edge, dbc, ddtr, vectors, small,
        branch, mine, rstd, row(gain_share), gate_half, output_half, length, seq_size, head_count,
    )
    token_grad = cotangent.astype(F32) + up.astype(F32)
    layer_out = (tokens.astype(F32) + branch.astype(F32)).astype(BF16)
    strip = width // seq_size
    step_grad = jnp.transpose(step_grad.reshape(width // both, heads, both), (0, 2, 1))
    step_grad = lax.dynamic_slice_in_dim(
        step_grad.reshape(width, heads), lax.axis_index("seq") * strip, strip, 0
    )
    return (
        layer_out,
        token_grad,
        norm_grad[0],
        gate_grad,
        value_grad,
        state_grad,
        step_grad,
        value_kernel_grad,
        value_bias_grad[0],
        state_kernel_grad,
        state_bias_grad[0],
        step_bias_grad[0],
        log_rate_grad[0],
        skip_gain_grad[0],
        gate_gain_grad[0],
        output_grad,
    )


def solution(mesh):
    in_specs = (
        P(None, "seq", "head"),
        P(None, "seq", "head"),
        P(),
        P(None, "head"),
        P(None, "head"),
        P(),
        P(None, "head"),
        P(None, "head"),
        P("head"),
        P(),
        P(),
        P("head"),
        P("head"),
        P("head"),
        P("head"),
        P("head", None),
    )
    out_specs = (
        P(None, "seq", "head"),
        P(None, "seq", "head"),
        P("head"),
        P("seq", "head"),
        P("seq", "head"),
        P("head", None),
        P("seq", "head"),
        P(None, "head"),
        P("head"),
        P(),
        P(),
        P("head"),
        P("head"),
        P("head"),
        P("head"),
        P("head", "seq"),
    )
    return jax.shard_map(local, mesh=mesh, in_specs=in_specs, out_specs=out_specs, check_vma=False)
```

```python
import jax
import jax.numpy as jnp
from jax import lax
from jax.experimental import pallas as pl
from jax.experimental.pallas import tpu as pltpu
from jax.sharding import PartitionSpec as P

HIGH = lax.Precision.HIGHEST
EPSILON = 1e-05
F32 = jnp.float32
BF16 = jnp.bfloat16
LANES = 128
EDGE = 8
VMEM_BYTES = 56 * 1024 * 1024

NN = (((1,), (0,)), ((), ()))
NT = (((1,), (1,)), ((), ()))
TN = (((0,), (0,)), ((), ()))


def dot(a, b, dims=NN, precision=None):
    return lax.dot_general(a, b, dims, precision=precision, preferred_element_type=F32)


def dot_split(a, b, dims=NN):
    high = a.astype(BF16)
    rest = (a - high.astype(F32)).astype(BF16)
    return dot(high, b, dims) + dot(rest, b, dims)


def sigmoid(v):
    return 1.0 / (1.0 + jnp.exp(-v))


def silu(v):
    return v * sigmoid(v)


def slope(v):
    sigma = sigmoid(v)
    return sigma * (1.0 + v * (1.0 - sigma))


def softplus(v):
    return jnp.maximum(v, 0.0) + jnp.log1p(jnp.exp(-jnp.abs(v)))


def ones_where(shape, rule):
    rows = lax.broadcasted_iota(jnp.int32, shape, 0)
    cols = lax.broadcasted_iota(jnp.int32, shape, 1)
    return rule(rows, cols)


def head_picker(channels, heads):
    wide = channels // heads
    return ones_where((channels, heads), lambda r, c: r // wide == c).astype(F32).astype(BF16)


def pair_spread(cols, j, rows):
    lane = lax.broadcasted_iota(jnp.int32, (rows, LANES), 1)
    first = jnp.broadcast_to(cols[:, 2 * j : 2 * j + 1], (rows, LANES))
    second = jnp.broadcast_to(cols[:, 2 * j + 1 : 2 * j + 2], (rows, LANES))
    return jnp.where(lane < LANES // 2, first, second)


def spread(cols, rows, heads):
    return jnp.concatenate([pair_spread(cols, j, rows) for j in range(heads // 2)], axis=1)


def call(kernel, name, grid, in_specs, out_specs, out_shape, scratch, flops, args, transcendentals=0):
    moved = sum(a.size * a.dtype.itemsize for a in args) + sum(
        o.size * o.dtype.itemsize for o in out_shape
    )
    return pl.pallas_call(
        kernel,
        grid=grid,
        in_specs=in_specs,
        out_specs=out_specs,
        out_shape=out_shape,
        scratch_shapes=scratch,
        compiler_params=pltpu.CompilerParams(
            dimension_semantics=("arbitrary",) * len(grid), vmem_limit_bytes=VMEM_BYTES
        ),
        cost_estimate=pl.CostEstimate(
            flops=int(flops), bytes_accessed=int(moved), transcendentals=int(transcendentals)
        ),
        name=name,
    )(*args)


def shape(dims, dtype):
    return jax.ShapeDtypeStruct(dims, dtype)


def decays(cum, cumt, h, half):
    top = jnp.exp(jnp.minimum(cum[:half, h : h + 1] - cumt[h : h + 1, :half], 0.0))
    low = jnp.exp(jnp.minimum(cum[half:, h : h + 1] - cumt[h : h + 1, :], 0.0))
    return top, low


def lower_scores(basis, states, length):
    scores = dot(basis[:, states:], basis[:, :states], NT)
    return jnp.where(ones_where((length, length), lambda r, c: r >= c), scores, 0.0)


def intra_back(bcs, xdt, dy, cum, cumt, length):
    rows, channels = xdt.shape
    heads = cum.shape[1]
    both = bcs.shape[1]
    states = both // 2
    half = length // 2

    def kernel(bcs_r, xdt_r, dy_r, cum_r, cumt_r, g_o, dbc_o, grad):
        scores = lower_scores(bcs_r[...], states, length)
        cum_v, cumt_v = cum_r[...], cumt_r[...]
        lane = lax.broadcasted_iota(jnp.int32, (length, LANES), 1)
        grad[...] = jnp.zeros_like(grad)
        for j in range(heads // 2):
            at = slice(j * LANES, (j + 1) * LANES)
            pair, dpair = xdt_r[:, at], dy_r[:, at]
            g_top = jnp.zeros((half, LANES), F32)
            g_low = jnp.zeros((half, LANES), F32)
            for s in range(2):
                own = jnp.where((lane < LANES // 2) == (s == 0), dpair, jnp.zeros_like(dpair))
                top, low = decays(cum_v, cumt_v, 2 * j + s, half)
                grad[:half, :half] += dot(own[:half], pair[:half], NT) * top
                grad[half:] += dot(own[half:], pair, NT) * low
                w_top = (scores[:half, :half] * top).astype(BF16)
                w_low = (scores[half:] * low).astype(BF16)
                g_top += dot(w_top, own[:half], TN) + dot(w_low[:, :half], own[half:], TN)
                g_low += dot(w_low[:, half:], own[half:], TN)
            g_o[:half, at] = g_top
            g_o[half:, at] = g_low
        masked = jnp.where(ones_where((length, length), lambda r, c: r >= c), grad[...], 0.0)
        high = masked.astype(BF16)
        rest = (masked - high.astype(F32)).astype(BF16)
        in_b, out_b = bcs_r[:, :states], bcs_r[:, states:]
        dbc_o[:, :states] = dot(high, out_b, TN) + dot(rest, out_b, TN)
        dbc_o[:, states:] = dot(high, in_b) + dot(rest, in_b)

    tokens = lambda n: pl.BlockSpec((length, n), lambda i: (i, 0))
    return call(
        kernel, "within_blocks_back", (rows // length,),
        [tokens(both), tokens(channels), tokens(channels), tokens(heads),
         pl.BlockSpec((heads, length), lambda i: (0, i))],
        [tokens(channels), tokens(both)],
        [shape((rows, channels), F32), shape((rows, both), F32)],
        [pltpu.VMEM((length, length), F32)],
        2 * rows * length * channels * 8, (bcs, xdt, dy, cum, cumt), rows * length * heads,
    )


def finish_back(value_pre, value_edge, value_kernel, value_bias, xs, xdt, xw, g, dy, dv, bcs, step_pre, dt,
                cum, ab, hin0, pre, carry, hin_low, ds0, post, back, dec, dbc_intra, skip_row, skip_gain,
                step_bias, log_rate, length):
    rows, channels = xs.shape
    heads = cum.shape[1]
    both = bcs.shape[1]
    states = both // 2
    wide = channels // heads
    count = rows // length
    taps = value_kernel.shape[0]
    unit = length // EDGE

    def kernel(xr, xr_before, xr_edge, vk, vb, xs_r, xdt_r, xw_r, g_r, dy_r, dv_r, bcs_r, dtr, dt_r, cum_r,
               ab_r, hin_r, pre_r, carry_r, low_r, ds_r, post_r, back_r, dec_r, dbci, skip, skipg, tb,
               lr, dxr_o, tail_o, head_o, vkg_o, vbg_o, ddtr_o, dbc_o, small_o,
               padded, ext, ds_low, inner_sums):
        i = pl.program_id(0)
        block = count - 1 - i

        @pl.when(i == 0)
        def _():
            vkg_o[...] = jnp.zeros_like(vkg_o)
            vbg_o[...] = jnp.zeros_like(vbg_o)
            small_o[...] = jnp.zeros_like(small_o)
            ext[0:EDGE] = jnp.zeros((EDGE, channels), F32)

        @pl.when(block == 0)
        def _():
            padded[0:EDGE] = xr_edge[...]

        @pl.when(block > 0)
        def _():
            padded[0:EDGE] = xr_before[...]

        padded[EDGE:] = xr[...]
        ext[length:] = ext[0:EDGE]
        for h in range(heads):
            at = slice(h * wide, (h + 1) * wide)
            ds = ds_r[0, at] + post_r[0, h : h + 1] * back_r[at].astype(F32)
            ds_low[at] = ds.astype(BF16)
            hin = hin_r[0, at] + pre_r[0, h : h + 1] * carry_r[at].astype(F32)
            inner_sums[h : h + 1] = jnp.sum(ds * hin, axis=0, keepdims=True) * dec_r[0, h : h + 1]
        in_b = bcs_r[:, :states]
        dt_v, cum_v = dt_r[...], cum_r[...]
        fade = jnp.exp(cum_v[length - 1 : length] - cum_v)
        factor = fade * dt_v
        start = EDGE - taps + 1
        picker = head_picker(channels, heads)
        c_sum = jnp.zeros((length, heads), F32)
        d_sum = jnp.zeros((length, heads), F32)
        w_sum = jnp.zeros((length, heads), F32)
        for j in range(channels // LANES):
            at = slice(j * LANES, (j + 1) * LANES)
            xs_v = xs_r[:, at].astype(F32)
            dxw = dot(in_b, ds_low[at], NT)
            g_v = g_r[:, at]
            c_sum += dot_split(xs_v * g_v, picker[at])
            d_sum += dot_split(xs_v * dxw, picker[at])
            w_sum += dot_split(xdt_r[:, at].astype(F32) * g_v, picker[at])
            dxs = (
                pair_spread(dt_v, j, length) * g_v
                + pair_spread(factor, j, length) * dxw
                + skip[:, at] * dy_r[:, at].astype(F32)
            )
            total = vb[:, at] + vk[0:1, at] * padded[pl.ds(start, length), at]
            for k in range(1, taps):
                total = total + vk[k : k + 1, at] * padded[pl.ds(start + k, length), at]
            dpre = dxs * slope(total)
            ext[0:length, at] = dpre
            vbg_o[:, at] += jnp.sum(dpre, axis=0, keepdims=True)
            for k in range(taps):
                vkg_o[k : k + 1, at] += jnp.sum(
                    dpre * padded[pl.ds(start + k, length), at], axis=0, keepdims=True
                )
            dxr = vk[0:1, at] * ext[pl.ds(taps - 1, length), at]
            for k in range(1, taps):
                dxr = dxr + vk[k : k + 1, at] * ext[pl.ds(taps - 1 - k, length), at]
            dxr_o[:, at] = dxr.astype(BF16)

            @pl.when(i == 0)
            def _():
                tail_o[:, at] = dxr[length - EDGE :]

        head_o[...] = ext[0:EDGE]
        dbc_o[:, :states] = dbci[:, :states] + dot(xw_r[...], ds_low[...])
        dbc_o[:, states:] = dbci[:, states:] + dot(dv_r[...], low_r[0])
        rate = -jnp.exp(lr[...])
        a_sum, b_sum = ab_r[:, :heads], ab_r[:, heads:]
        e_sum = d_sum * factor
        ones = jnp.ones((1, LANES), F32)
        dtotal = jnp.sum(e_sum, axis=0, keepdims=True) + dot(ones, inner_sums[...], NT, precision=HIGH)
        row = lax.broadcasted_iota(jnp.int32, (length, heads), 0)
        dcum = a_sum - skipg[...] * b_sum - w_sum - e_sum
        dcum = dcum + jnp.where(row == length - 1, dtotal, 0.0)
        upper = ones_where((length, length), lambda r, c: r <= c).astype(F32)
        dda = dot(upper, dcum, precision=HIGH)
        ddt = c_sum + d_sum * fade + dda * rate
        dpre_dt = ddt * sigmoid(dtr[...] + tb[...])
        ddtr_o[...] = dpre_dt.astype(BF16)
        small_o[0:1] += jnp.sum(dpre_dt, axis=0, keepdims=True)
        small_o[1:2] += jnp.sum(dda * dt_v, axis=0, keepdims=True) * rate
        small_o[2:3] += jnp.sum(b_sum, axis=0, keepdims=True)

    last = count - 1
    whole = lambda *dims: pl.BlockSpec(dims, lambda i: (0,) * len(dims))
    tokens = lambda n: pl.BlockSpec((length, n), lambda i: (last - i, 0))
    before = lambda n: pl.BlockSpec((EDGE, n), lambda i: (jnp.maximum((last - i) * unit - 1, 0), 0))
    per = lambda *dims: pl.BlockSpec((1,) + dims, lambda i: (last - i, 0, 0))
    return call(
        kernel, "across_blocks_back", (count,),
        [tokens(channels), before(channels), whole(EDGE, channels), whole(taps, channels),
         whole(1, channels), tokens(channels), tokens(channels), tokens(channels), tokens(channels),
         tokens(channels), tokens(channels), tokens(both), tokens(heads), tokens(heads), tokens(heads),
         tokens(2 * heads), per(channels, states), per(heads, LANES), whole(channels, states),
         per(channels, states), per(channels, states), per(heads, LANES), whole(channels, states),
         per(heads, LANES), tokens(both), whole(1, channels), whole(1, heads), whole(1, heads),
         whole(1, heads)],
        [tokens(channels), whole(EDGE, channels), whole(EDGE, channels), whole(taps, channels),
         whole(1, channels), tokens(heads), tokens(both), whole(EDGE, heads)],
        [shape((rows, channels), BF16), shape((EDGE, channels), F32), shape((EDGE, channels), F32),
         shape((taps, channels), F32), shape((1, channels), F32), shape((rows, heads), BF16),
         shape((rows, both), F32), shape((EDGE, heads), F32)],
        [pltpu.VMEM((length + EDGE, channels), F32), pltpu.VMEM((length + EDGE, channels), F32),
         pltpu.VMEM((channels, states), BF16), pltpu.VMEM((heads, LANES), F32)],
        2 * rows * channels * states * 3,
        (value_pre, value_pre, value_edge, value_kernel, value_bias, xs, xdt, xw, g, dy, dv, bcs, step_pre,
         dt, cum, ab, hin0, pre, carry, hin_low, ds0, post, back, dec, dbc_intra, skip_row, skip_gain,
         step_bias, log_rate),
        2 * rows * channels,
    )


def halves(normal_in, grad, outer):
    rows, width = normal_in.shape
    channels = grad.shape[1]
    strip = width // (2 * outer)

    def kernel(xn, grad_r, keep_o, give_o):
        side = lax.rem(lax.axis_index("seq"), 2)
        product = dot(xn[...], grad_r[...], TN).astype(BF16)

        @pl.when(side == 0)
        def _():
            keep_o[0] = product[:strip]
            give_o[0] = product[strip:]

        @pl.when(side == 1)
        def _():
            keep_o[0] = product[strip:]
            give_o[0] = product[:strip]

    out = pl.BlockSpec((1, strip, channels), lambda i: (i, 0, 0))
    return call(
        kernel, "gate_strips", (outer,),
        [pl.BlockSpec((rows, 2 * strip), lambda i: (0, i)),
         pl.BlockSpec((rows, channels), lambda i: (0, 0))],
        [out, out], [shape((outer, strip, channels), BF16)] * 2, [], 2 * rows * width * channels,
        (normal_in, grad),
    )


def parities(normed, cotangent, outer):
    rows, width = cotangent.shape
    channels = normed.shape[1]
    strip = width // (2 * outer)

    def kernel(normed_r, cot, keep_o, give_o):
        parity = lax.rem(lax.axis_index("seq") // 2, 2)
        product = dot(normed_r[...], cot[...], TN).astype(BF16)
        for own in range(2):
            @pl.when(parity == own)
            def _(own=own):
                for side in range(2):
                    at, to = 2 * own + side, 2 * (1 - own) + side
                    keep_o[0, side] = product[:, at * strip : (at + 1) * strip]
                    give_o[0, side] = product[:, to * strip : (to + 1) * strip]

    out = pl.BlockSpec((1, 2, channels, strip), lambda i: (i, 0, 0, 0))
    return call(
        kernel, "output_strips", (outer // 2,),
        [pl.BlockSpec((rows, channels), lambda i: (0, 0)),
         pl.BlockSpec((rows, 4 * strip), lambda i: (0, i))],
        [out, out], [shape((outer // 2, 2, channels, strip), BF16)] * 2, [],
        2 * rows * width * channels, (normed, cotangent),
    )


def remote(src, dst, send, recv, seq, head):
    return pltpu.make_async_remote_copy(
        src_ref=src, dst_ref=dst, send_sem=send, recv_sem=recv, device_id=(seq, head),
        device_id_type=pl.DeviceIdType.MESH,
    )


def greet(seq, head, seq_size, head_size):
    barrier = pltpu.get_barrier_semaphore()
    for d in range(1, seq_size):
        pl.semaphore_signal(
            barrier, inc=1, device_id=(lax.rem(seq + d, seq_size), head),
            device_id_type=pl.DeviceIdType.MESH,
        )
    for d in range(1, head_size):
        pl.semaphore_signal(
            barrier, inc=1, device_id=(seq, lax.rem(head + d, head_size)),
            device_id_type=pl.DeviceIdType.MESH,
        )
    pl.semaphore_wait(barrier, seq_size - 1 + head_size - 1)


def forward(xdt, xs, bcs, gate_pre, normed_grad, cum, cumt, hin0, pre, dec, carry, skip_row, gate_gain,
            output_matrix, length, seq_size, head_size):
    rows, channels = xs.shape
    heads = cum.shape[1]
    both = bcs.shape[1]
    states = both // 2
    wide = channels // heads
    count = rows // length
    half = length // 2
    width = output_matrix.shape[1]
    inner = channels * head_size

    def kernel(xdt_r, xs_r, bcs_r, z_r, dn_r, cum_r, cumt_r, hin_r, pre_r, dec_r, carry_r, skip, gain, wo,
               low_o, normed_o, part_o, dy_o, dz_o, dv_o, ab_o, ds_o, post_o, start_o, ggain_o,
               y_s, sums, others, state, behind, prod_a, prod_b, s_sem, r_sem):
        i = pl.program_id(0)
        seq, head = lax.axis_index("seq"), lax.axis_index("head")
        barrier = pltpu.get_barrier_semaphore()

        def head_at(d):
            return lax.rem(head + d, head_size)

        def share_sums(d):
            return remote(sums, others.at[d - 1], s_sem.at[d - 1], r_sem.at[d - 1], seq, head_at(d))

        @pl.when(i == 0)
        def _():
            for d in range(1, head_size):
                pl.semaphore_signal(
                    barrier, inc=1, device_id=(seq, head_at(d)), device_id_type=pl.DeviceIdType.MESH
                )

        @pl.when(i < count)
        def _():
            at_rows = pl.ds(pl.multiple_of(i * length, length), length)
            for h in range(heads):
                at = slice(h * wide, (h + 1) * wide)
                low_o[0, at] = (
                    hin_r[0, at] + pre_r[0, h : h + 1] * carry_r[at].astype(F32)
                ).astype(BF16)
            scores = lower_scores(bcs_r[...], states, length)
            cum_v, cumt_v = cum_r[...], cumt_r[...]
            growth = jnp.exp(cum_v)
            lane = lax.broadcasted_iota(jnp.int32, (length, LANES), 1)
            squares = jnp.zeros((length, LANES), F32)
            crosses = jnp.zeros((length, LANES), F32)
            out_basis = bcs_r[:, states:]
            for j in range(channels // LANES):
                at = slice(j * LANES, (j + 1) * LANES)
                pair = xdt_r[:, at]
                y_top = jnp.zeros((half, LANES), F32)
                y_low = jnp.zeros((half, LANES), F32)
                for s in range(2):
                    own = jnp.where((lane < LANES // 2) == (s == 0), pair, jnp.zeros_like(pair))
                    top, low = decays(cum_v, cumt_v, 2 * j + s, half)
                    y_top += dot((scores[:half, :half] * top).astype(BF16), own[:half])
                    y_low += dot((scores[half:] * low).astype(BF16), own)
                v = dot(out_basis, low_o[0, at], NT)
                y = (
                    jnp.concatenate([y_top, y_low], axis=0)
                    + pair_spread(growth, j, length) * v
                    + skip[:, at] * xs_r[:, at].astype(F32)
                )
                y_s[at_rows, at] = y
                gated = y * silu(z_r[:, at])
                squares += gated * gated
                crosses += dn_r[:, at] * gain[:, at] * gated
            first = ones_where((8, LANES), lambda r, c: r == 0).astype(F32)
            second = ones_where((8, LANES), lambda r, c: r == 1).astype(F32)
            sums[:, at_rows] = dot(first, squares, NT, HIGH) + dot(second, crosses, NT, HIGH)

        @pl.when(i == count)
        def _():
            pl.semaphore_wait(barrier, head_size - 1)
            for d in range(1, head_size):
                share_sums(d).start()
            state[...] = jnp.zeros_like(state)
            behind[...] = jnp.ones_like(behind)
            ggain_o[...] = jnp.zeros_like(ggain_o)
            for d in range(1, head_size):
                share_sums(d).wait()
            total = sums[...]
            for d in range(1, head_size):
                total = total + others[d - 1]
            others[0] = total

        @pl.when(i >= count)
        def _():
            at_rows = pl.ds(pl.multiple_of((2 * count - 1 - i) * length, length), length)
            both_sums = others[0, :, at_rows]
            first = ones_where((8, LANES), lambda r, c: r == 0).astype(F32)
            second = ones_where((8, LANES), lambda r, c: r == 1).astype(F32)
            grstd = lax.rsqrt(dot(both_sums, first, TN, HIGH) * (1.0 / inner) + EPSILON)
            cross = (grstd * grstd * grstd) * (dot(both_sums, second, TN, HIGH) * (1.0 / inner))
            growth = jnp.exp(cum_r[...])
            for j in range(channels // LANES):
                at = slice(j * LANES, (j + 1) * LANES)
                y, z, dn = y_s[at_rows, at], z_r[:, at], dn_r[:, at]
                sigma = sigmoid(z)
                act = z * sigma
                gated = y * act
                scaled = gated * grstd
                normed_o[:, at] = (scaled * gain[:, at]).astype(BF16)
                ggain_o[:, at] += jnp.sum(dn * scaled, axis=0, keepdims=True)
                dgated = grstd * (dn * gain[:, at]) - gated * cross
                dy = (dgated * act).astype(BF16)
                dy_o[:, at] = dy
                dz_o[:, at] = (dgated * y * (sigma * (1.0 + z * (1.0 - sigma)))).astype(BF16)
                plain = dy.astype(F32)
                dv_o[:, at] = (plain * pair_spread(growth, j, length)).astype(BF16)
                prod_a[:, at] = plain * y
                prod_b[:, at] = plain * xs_r[:, at].astype(F32)
            picker = head_picker(channels, heads)
            ab_o[:, :heads] = dot_split(prod_a[...], picker)
            ab_o[:, heads:] = dot_split(prod_b[...], picker)
            part_o[...] = dot(normed_o[...], wo[...]).astype(BF16)
            dhin = dot(dv_o[...], bcs_r[:, states:], TN)
            ds_o[0] = state[...]
            post_o[0] = behind[...]
            behind[...] = behind[...] * dec_r[0]
            for h in range(heads):
                at = slice(h * wide, (h + 1) * wide)
                state[at] = dec_r[0, h : h + 1] * state[at] + dhin[at]
            start_o[...] = state[...].astype(BF16)

    last = count - 1
    ways = {
        "both": lambda i: jnp.where(i < count, i, 2 * count - 1 - i),
        "up": lambda i: jnp.minimum(i, last),
        "down": lambda i: jnp.minimum(2 * count - 1 - i, last),
    }
    whole = lambda *dims: pl.BlockSpec(dims, lambda i: (0,) * len(dims))
    tokens = lambda n, way: pl.BlockSpec((length, n), lambda i: (ways[way](i), 0))
    per = lambda way, *dims: pl.BlockSpec((1,) + dims, lambda i: (ways[way](i), 0, 0))
    args = (xdt, xs, bcs, gate_pre, normed_grad, cum, cumt, hin0, pre, dec, carry, skip_row, gate_gain,
            output_matrix)
    return pl.pallas_call(
        kernel,
        grid=(2 * count,),
        in_specs=[
            tokens(channels, "up"), tokens(channels, "both"), tokens(both, "both"),
            tokens(channels, "both"), tokens(channels, "both"), tokens(heads, "both"),
            pl.BlockSpec((heads, length), lambda i: (0, ways["up"](i))), per("up", channels, states),
            per("up", heads, LANES), per("down", heads, LANES), whole(channels, states),
            whole(1, channels), whole(1, channels), whole(channels, width),
        ],
        out_specs=[
            per("up", channels, states), tokens(channels, "down"), tokens(width, "down"),
            tokens(channels, "down"), tokens(channels, "down"), tokens(channels, "down"),
            tokens(2 * heads, "down"), per("down", channels, states), per("down", heads, LANES),
            whole(channels, states), whole(1, channels),
        ],
        out_shape=[
            shape((count, channels, states), BF16), shape((rows, channels), BF16),
            shape((rows, width), BF16), shape((rows, channels), BF16),
            shape((rows, channels), BF16), shape((rows, channels), BF16), shape((rows, 2 * heads), F32),
            shape((count, channels, states), F32), shape((count, heads, LANES), F32),
            shape((channels, states), BF16), shape((1, channels), F32),
        ],
        scratch_shapes=[
            pltpu.VMEM((rows, channels), F32), pltpu.VMEM((8, rows), F32),
            pltpu.VMEM((head_size - 1, 8, rows), F32), pltpu.VMEM((channels, states), F32),
            pltpu.VMEM((heads, LANES), F32), pltpu.VMEM((length, channels), F32),
            pltpu.VMEM((length, channels), F32),
            pltpu.SemaphoreType.DMA((head_size - 1,)), pltpu.SemaphoreType.DMA((head_size - 1,)),
        ],
        compiler_params=pltpu.CompilerParams(
            dimension_semantics=("arbitrary",), collective_id=3, has_side_effects=True,
            vmem_limit_bytes=VMEM_BYTES,
        ),
        cost_estimate=pl.CostEstimate(
            flops=2 * rows * channels * (width + 6 * length), bytes_accessed=60_000_000,
            transcendentals=rows * (length * heads + 2 * channels),
        ),
        name="blocks_and_gate",
    )(*args)


def opening(tokens, cotangent, norm_gain, gate_matrix, value_matrix, state_matrix, step_matrix,
            output_matrix, value_kernel, value_bias, state_kernel, state_bias, step_bias, log_rate,
            seq_size, head_size):
    members, length, share = tokens.shape
    rows = members * length
    width, channels = gate_matrix.shape
    both = state_matrix.shape[1]
    heads = step_matrix.shape[0]
    half_heads = head_size // 2
    states = both // 2
    wide = channels // heads
    taps = value_kernel.shape[0]
    groups = seq_size // members
    margin = EDGE - taps + 1

    def kernel(tokens_h, cot_h, gain, gate_h, value_h, state_h, step_m, out_h, vk, vb, sk, sb, tb, lr,
               xn_o, cot_o, mine_o, z_o, xr_o, bc_o, dn_o, xs_o, xdt_o, xw_o, hin_o,
               rstd_o, dtr_o, bcs_o, dt_o, cum_o, cumt_o, pre_o, dec_o, xedge_o, bedge_o, carry_o,
               whole, xn, z, xr, bc, dn, gate, value, state_m, out_m,
               padded, padded_bc, xs, xdt, xw, hin, state, ahead, leaving,
               gs_sem, gr_sem, ys_sem, yr_sem, cs_sem, cr_sem, w_sem, o_sem, l_sem, e_sem):
        seq, head = lax.axis_index("seq"), lax.axis_index("head")
        lane, core = head // 2, lax.rem(head, 2)
        group, member = seq // members, lax.rem(seq, members)
        base = seq - member
        sources = (tokens_h, cot_h)

        def rows_of(j):
            return pl.ds(pl.multiple_of(j * length, length), length)

        def lanes_of(h):
            return pl.ds(pl.multiple_of(h * share, share), share)

        own = [
            pltpu.make_async_copy(
                sources[a].at[member], whole.at[a, rows_of(member), lanes_of(head)], l_sem.at[a]
            )
            for a in range(2)
        ]
        loads = [
            pltpu.make_async_copy(src, dst, w_sem.at[i])
            for i, (src, dst) in enumerate(
                ((gate_h, gate), (value_h, value), (state_h, state_m), (out_h, out_m))
            )
        ]
        own[0].start()
        own[1].start()
        for load in loads:
            load.start()
        greet(seq, head, seq_size, head_size)

        order = [0, *range(members - 1, 0, -1)]

        def place(t):
            return lax.rem(member + t, members)

        def to_group(a, t):
            return remote(sources[a].at[place(t)], whole.at[a, rows_of(member), lanes_of(head)],
                          gs_sem.at[a, t - 1], gr_sem.at[a, members - 1 - t], base + place(t), head)

        def from_group(a, t):
            return remote(sources[a].at[place(t)], whole.at[a, rows_of(place(t)), lanes_of(head)],
                          gs_sem.at[a, t - 1], gr_sem.at[a, t - 1], seq, head)

        def to_lane(a, t, k):
            at = whole.at[a, rows_of(place(t)), lanes_of(head)]
            return remote(at, at, ys_sem.at[a, t, k], yr_sem.at[a, t, k],
                          seq, 2 * lax.rem(lane + 1 + k, half_heads) + core)

        def lane_from(k):
            return lax.rem(lane + half_heads - 1 - k, half_heads)

        def from_lane(a, t, k):
            at = whole.at[a, rows_of(place(t)), lanes_of(2 * lane_from(k) + core)]
            return remote(at, at, ys_sem.at[a, t, k], yr_sem.at[a, t, k], seq, head)

        def to_core(a, t, k):
            at = whole.at[a, rows_of(place(t)), lanes_of(2 * lane_from(k) + core)]
            return remote(at, at, cs_sem.at[a, t, k], cr_sem.at[a, t, k], seq, 2 * lane + 1 - core)

        def from_core(a, t, k):
            at = whole.at[a, rows_of(place(t)), lanes_of(2 * lane_from(k) + 1 - core)]
            return remote(at, at, cs_sem.at[a, t, k], cr_sem.at[a, t, k], seq, head)

        def forward(a, t):
            for k in range(half_heads - 1):
                to_lane(a, t, k).start()
            to_core(a, t, half_heads - 1).start()

        def collect(a, t):
            for k in range(half_heads - 1):
                from_lane(a, t, k).wait_recv()
                to_core(a, t, k).start()
            for k in range(half_heads):
                from_core(a, t, k).wait_recv()

        def outputs(t):
            at = rows_of(place(t))
            pairs = ((xn, xn_o), (z, z_o), (xr, xr_o), (bc, bc_o))
            return [
                pltpu.make_async_copy(src.at[at], dst.at[at], o_sem.at[i, t])
                for i, (src, dst) in enumerate(pairs)
            ]

        def late_outputs(t):
            at = rows_of(place(t))
            return [
                pltpu.make_async_copy(dn.at[at], dn_o.at[at], o_sem.at[4, t]),
                pltpu.make_async_copy(whole.at[1, at], cot_o.at[at], o_sem.at[5, t]),
                pltpu.make_async_copy(whole.at[0, at, lanes_of(head)], mine_o.at[at], o_sem.at[6, t]),
            ]

        def project(t):
            at = rows_of(place(t))
            squares = jnp.zeros((length, LANES), F32)
            for q in range(width // LANES):
                part = whole[0, at, q * LANES : (q + 1) * LANES].astype(F32)
                squares += part * part
            mean = jnp.sum(squares, axis=1, keepdims=True) * (1.0 / width)
            rstd = lax.rsqrt(mean + EPSILON)
            rstd_o[at] = rstd
            wide = jnp.broadcast_to(rstd, (length, LANES))
            for q in range(width // LANES):
                cols = slice(q * LANES, (q + 1) * LANES)
                xn[at, cols] = (whole[0, at, cols].astype(F32) * wide * gain[:, cols]).astype(BF16)
            normal = xn[at]
            if t == 0:
                for load in loads[:3]:
                    load.wait()
            xr[at] = dot(normal, value[...])
            z[at] = dot(normal, gate[...])
            bc[at] = dot(normal, state_m[...])
            dtr_o[at] = dot(normal, step_m[...], NT)
            for copy in outputs(t):
                copy.start()

        def edges(there):
            tail = pl.ds(rows - EDGE, EDGE)
            return [
                remote(xr.at[tail], xedge_o, e_sem.at[0], e_sem.at[1], there, head),
                remote(bc.at[tail], bedge_o, e_sem.at[2], e_sem.at[3], there, head),
            ]

        def pass_on(there):
            return remote(leaving, carry_o, e_sem.at[4], e_sem.at[5], there, head)

        def block_outputs(i):
            at = rows_of(i)
            pairs = ((xs, xs_o), (xdt, xdt_o), (xw, xw_o))
            return [
                pltpu.make_async_copy(src.at[at], dst.at[at], o_sem.at[7 + n, i])
                for n, (src, dst) in enumerate(pairs)
            ] + [pltpu.make_async_copy(hin.at[i], hin_o.at[i], o_sem.at[10, i])]

        def prepare(i):
            at = slice(i * length, (i + 1) * length)
            if i == 0:
                padded[0:EDGE] = xedge_o[...]
                padded_bc[0:EDGE] = bedge_o[...]
                state[...] = jnp.zeros_like(state)
                ahead[...] = jnp.ones_like(ahead)
            else:
                padded[0:EDGE] = xr[i * length - EDGE : i * length]
                padded_bc[0:EDGE] = bc[i * length - EDGE : i * length]
            padded[EDGE:] = xr[at]
            padded_bc[EDGE:] = bc[at]
            summed = sb[...] + sk[0:1] * padded_bc[pl.ds(margin, length)]
            for k in range(1, taps):
                summed = summed + sk[k : k + 1] * padded_bc[pl.ds(margin + k, length)]
            basis = silu(summed).astype(BF16)
            bcs_o[at] = basis
            dt = softplus(dtr_o[at] + tb[...])
            da = dt * -jnp.exp(lr[...])
            lower = ones_where((length, length), lambda r, c: r >= c).astype(F32)
            upper = ones_where((length, length), lambda r, c: r <= c).astype(F32)
            cum = dot(lower, da, precision=HIGH)
            cumt = dot(da, upper, TN, precision=HIGH)
            dt_o[at] = dt
            cum_o[at] = cum
            cumt_o[:, at] = cumt
            factor = jnp.exp(cum[length - 1 : length] - cum) * dt
            decay = jnp.exp(jnp.broadcast_to(cumt[:, length - 1 : length], (heads, LANES)))
            dec_o[i] = decay
            pre_o[i] = ahead[...]
            ahead[...] = ahead[...] * decay
            hin[i] = state[...]
            for j in range(channels // LANES):
                cols = slice(j * LANES, (j + 1) * LANES)
                total = vb[:, cols] + vk[0:1, cols] * padded[pl.ds(margin, length), cols]
                for k in range(1, taps):
                    total = total + vk[k : k + 1, cols] * padded[pl.ds(margin + k, length), cols]
                value_low = silu(total).astype(BF16)
                xs[at, cols] = value_low
                plain = value_low.astype(F32)
                xdt[at, cols] = (plain * pair_spread(dt, j, length)).astype(BF16)
                xw[at, cols] = (plain * pair_spread(factor, j, length)).astype(BF16)
            local = dot(xw[at], basis[:, :states], TN)
            for h in range(heads):
                span = slice(h * wide, (h + 1) * wide)
                state[span] = decay[h : h + 1] * state[span] + local[span]
            for copy in block_outputs(i):
                copy.start()

        for t in range(1, members):
            to_group(0, t).start()
        own[0].wait()
        forward(0, 0)
        for t in order[1:]:
            from_group(0, t).wait_recv()
            forward(0, t)
        for t in range(1, members):
            to_group(1, t).start()
        own[1].wait()
        forward(1, 0)
        for n, t in enumerate(order):
            collect(0, t)
            project(t)
            if n < members - 1:
                from_group(1, order[n + 1]).wait_recv()
                forward(1, order[n + 1])
        @pl.when(group < groups - 1)
        def _():
            for copy in edges(seq + members):
                copy.start()

        @pl.when(group == 0)
        def _():
            xedge_o[...] = jnp.zeros_like(xedge_o)
            bedge_o[...] = jnp.zeros_like(bedge_o)
            carry_o[...] = jnp.zeros_like(carry_o)

        def gradient(t):
            collect(1, t)
            at = rows_of(place(t))
            dn[at] = dot(whole[1, at], out_m[...], NT)
            for copy in late_outputs(t):
                copy.start()

        loads[3].wait()
        gradient(0)

        @pl.when(group > 0)
        def _():
            for copy in edges(seq):
                copy.wait_recv()

        for i in range(members):
            prepare(i)
        leaving[...] = state[...].astype(BF16)

        @pl.when(group == 0)
        def _():
            pass_on(seq + members).start()

        for t in order[1:]:
            gradient(t)

        @pl.when(group > 0)
        def _():
            pass_on(seq).wait_recv()

            @pl.when(group < groups - 1)
            def _():
                for h in range(heads):
                    span = slice(h * wide, (h + 1) * wide)
                    leaving[span] = (
                        state[span] + ahead[h : h + 1] * carry_o[span].astype(F32)
                    ).astype(BF16)
                pass_on(seq + members).start()

        @pl.when(group < groups - 1)
        def _():
            for copy in edges(seq + members):
                copy.wait_send()
            pass_on(seq + members).wait_send()

        for t in range(members):
            for copy in outputs(t) + late_outputs(t) + block_outputs(t):
                copy.wait()
        for a in range(2):
            for t in range(1, members):
                to_group(a, t).wait_send()
            for t in range(members):
                for k in range(half_heads):
                    to_core(a, t, k).wait_send()
                    if k < half_heads - 1:
                        to_lane(a, t, k).wait_send()

    vmem = pl.BlockSpec(memory_space=pltpu.VMEM)
    anywhere = pl.BlockSpec(memory_space=pl.ANY)
    dma = pltpu.SemaphoreType.DMA
    args = (tokens, cotangent, norm_gain, gate_matrix, value_matrix, state_matrix, step_matrix,
            output_matrix, value_kernel, value_bias, state_kernel, state_bias, step_bias, log_rate)
    far = {0, 1, 3, 4, 5, 7}
    return pl.pallas_call(
        kernel,
        in_specs=[anywhere if i in far else vmem for i in range(len(args))],
        out_specs=[anywhere] * 11 + [vmem] * 11,
        out_shape=[
            shape((rows, width), BF16), shape((rows, width), BF16), shape((rows, share), BF16),
            shape((rows, channels), F32), shape((rows, channels), F32), shape((rows, both), F32),
            shape((rows, channels), F32), shape((rows, channels), BF16), shape((rows, channels), BF16),
            shape((rows, channels), BF16), shape((members, channels, states), F32),
            shape((rows, 1), F32), shape((rows, heads), F32), shape((rows, both), BF16),
            shape((rows, heads), F32), shape((rows, heads), F32), shape((heads, rows), F32),
            shape((members, heads, LANES), F32), shape((members, heads, LANES), F32),
            shape((EDGE, channels), F32), shape((EDGE, both), F32), shape((channels, states), BF16),
        ],
        scratch_shapes=[
            pltpu.VMEM((2, rows, width), BF16), pltpu.VMEM((rows, width), BF16),
            pltpu.VMEM((rows, channels), F32), pltpu.VMEM((rows, channels), F32),
            pltpu.VMEM((rows, both), F32), pltpu.VMEM((rows, channels), F32),
            pltpu.VMEM((width, channels), BF16), pltpu.VMEM((width, channels), BF16),
            pltpu.VMEM((width, both), BF16), pltpu.VMEM((channels, width), BF16),
            pltpu.VMEM((length + EDGE, channels), F32), pltpu.VMEM((length + EDGE, both), F32),
            pltpu.VMEM((rows, channels), BF16), pltpu.VMEM((rows, channels), BF16),
            pltpu.VMEM((rows, channels), BF16), pltpu.VMEM((members, channels, states), F32),
            pltpu.VMEM((channels, states), F32), pltpu.VMEM((heads, LANES), F32),
            pltpu.VMEM((channels, states), BF16),
            dma((2, members - 1)), dma((2, members - 1)),
            dma((2, members, max(half_heads - 1, 1))), dma((2, members, max(half_heads - 1, 1))),
            dma((2, members, half_heads)), dma((2, members, half_heads)),
            dma((4,)), dma((11, members)), dma((2,)), dma((6,)),
        ],
        compiler_params=pltpu.CompilerParams(
            collective_id=2, has_side_effects=True, vmem_limit_bytes=VMEM_BYTES
        ),
        cost_estimate=pl.CostEstimate(
            flops=2 * rows * width * (3 * channels + both), bytes_accessed=60_000_000, transcendentals=0
        ),
        name="opening_products",
    )(*args)

def closing(normal_in, dz, dxr, tail, head_rows, gate_matrix, value_matrix, state_matrix, step_matrix,
            value_kernel, state_kernel, state_bias, state_pre, state_edge, dbc, ddtr, vectors, small,
            branch, mine, rstd, gain_share, gate_half, output_half, length, seq_size, head_size):
    rows, width = normal_in.shape
    channels = dz.shape[1]
    heads = ddtr.shape[1]
    both = dbc.shape[1]
    share = mine.shape[1]
    taps = value_kernel.shape[0]
    members = rows // length
    outer = seq_size // 2
    half_heads = head_size // 2
    strip = width // seq_size
    chunk = rows // head_size
    per = head_size // members
    packed = channels + both + LANES + share
    low_rows = share + heads * width // both
    steps = seq_size.bit_length() - 1
    groups = seq_size // members

    def kernel(xn, dz_r, dxr_h, tail_r, head_r, gate_h, value_h, state_m, step_m, vk, sk, sb, bc_h,
               bc_edge, dbc_h, ddtr_r, vec, small_r, branch_h, mine_r, rstd_r, gain, gate_half_h,
               out_half_h,
               gate_o, value_o, out_o, state_o, step_o, vkern_o, vbias_o, ggain_o, skern_o, sbias_o, norm_o,
               tbias_o, rate_o, skip_o, up_o, branch_o,
               dxr_r, duo, xrecv, zrecv, gbuf, grecv, obuf, orecv, oxrecv, bpart, weights, weight, csend, cown, crecv, yrecv, rsend,
               rrecv, up, norms, nrecv, nlast, blow,
               drecv, dsum, ext, hrecv, hbrecv, low,
               full_sum, full_send, full_recv, low_sum, low_send, low_recv,
               xs_sem, xr_sem, zs_sem, zr_sem, cs_sem, cr_sem, ys_sem, yr_sem, rs_sem, rr_sem,
               us_sem, ur_sem, ns_sem, nr_sem, ds_sem, dr_sem,
               as_sem, ar_sem, h_sem, hb_sem, fs_sem, fr_sem, ls_sem, lr_sem, nl_sem, bs_sem, br_sem, gs_sem, gr_sem, os_sem, or_sem, ox_sem, half_sem, w_sem, copy_sem):
        seq, head = lax.axis_index("seq"), lax.axis_index("head")
        place, side = seq // 2, lax.rem(seq, 2)
        lane, core = head // 2, lax.rem(head, 2)
        group, member = seq // members, lax.rem(seq, members)
        base = seq - member
        load_dxr = pltpu.make_async_copy(dxr_h, dxr_r, copy_sem.at[0])
        load_dxr.start()
        load_bc = pltpu.make_async_copy(bc_h, low.at[pl.ds(EDGE, rows)], copy_sem.at[1])
        load_bc.start()
        low[0:EDGE] = bc_edge[...]

        def crossed(index, other, size):
            result, bit = 0, 1
            while bit < size:
                result = result + bit * lax.rem(index // bit + other // bit, 2)
                bit *= 2
            return result

        def outer_at(k):
            return crossed(place, outer - 1 - k, outer)

        def lane_at(k):
            return lax.rem(lane + 1 + k, half_heads)

        def seq_at(d):
            return lax.rem(seq + d, seq_size)

        def head_at(d):
            return lax.rem(head + d, head_size)

        own_rows = pl.ds(pl.multiple_of(head * chunk, chunk), chunk)
        load_dbc = pltpu.make_async_copy(
            dbc_h.at[own_rows], dsum.at[own_rows], copy_sem.at[2]
        )
        load_dbc.start()
        keep_branch = pltpu.make_async_copy(
            branch_h.at[member], branch_o.at[member], copy_sem.at[3]
        )
        keep_branch.start()
        gate_loads = [
            pltpu.make_async_copy(gate_half_h.at[crossed(place, c, outer)], gbuf.at[c], half_sem.at[c])
            for c in range(outer)
        ]
        out_loads = [
            pltpu.make_async_copy(
                out_half_h.at[crossed(place // 2, c, outer // 2)], obuf.at[c], half_sem.at[outer + c]
            )
            for c in range(outer // 2)
        ]
        for load in reversed(out_loads + gate_loads):
            load.start()
        greet(seq, head, seq_size, head_size)

        def cross(k):
            return remote(duo.at[k, 1 - side], xrecv.at[k], xs_sem.at[k], xr_sem.at[k],
                          2 * place + 1 - side, head)

        def zeros_of(c, size):
            count = 0
            while c % 2 == 0 and 1 << count < size:
                c, count = c // 2, count + 1
            return count

        def pass_along(held, landed, send, recv, c, span, size):
            bit = 1 << zeros_of(c, size)
            far = crossed(place, span * bit, outer)
            return remote(held, landed.at[c - 1], send.at[c - 1], recv.at[c - 1], 2 * far + side, head)

        def along(c):
            return pass_along(duo.at[outer - 1 - c, side], zrecv, zs_sem, zr_sem, c, 1, outer)

        def along_gate(c):
            return pass_along(gbuf.at[c], grecv, gs_sem, gr_sem, c, 1, outer)

        def along_out(c):
            return pass_along(obuf.at[c, side], orecv, os_sem, or_sem, c, 2, outer // 2)

        def gather_in(copy, landed, c, size):
            total = 0.0
            for b in range(zeros_of(c, size)):
                copy(c + (1 << b)).wait_recv()
                total = total + landed[c + (1 << b) - 1].astype(F32)
            return total

        def gate_step(c):
            gate_loads[c].wait()
            if zeros_of(c, outer):
                gbuf[c] = (gbuf[c].astype(F32) + gather_in(along_gate, grecv, c, outer)).astype(BF16)
            along_gate(c).start()

        def cross_out(c):
            return remote(obuf.at[c, 1 - side], oxrecv.at[c], ox_sem.at[0, c], ox_sem.at[1, c],
                          2 * place + 1 - side, head)

        def out_step(c):
            cross_out(c).wait_recv()
            total = obuf[c, side].astype(F32) + oxrecv[c].astype(F32)
            if c:
                total = total + gather_in(along_out, orecv, c, outer // 2)
            obuf[c, side] = total.astype(BF16)
            if c:
                along_out(c).start()

        def branch_give(r):
            return remote(branch_h.at[r], branch_o.at[member], bs_sem.at[r], br_sem.at[member],
                          base + r, head)

        def edge_back(src, dst, sems):
            return remote(src, dst, sems.at[0], sems.at[1], seq - members, head)

        def rows_of(c):
            return pl.ds(pl.multiple_of(c * chunk, chunk), chunk)

        def basis_sum(d):
            return remote(dbc_h.at[rows_of(head_at(d))], drecv.at[d - 1], ds_sem.at[d - 1],
                          dr_sem.at[d - 1], seq, head_at(d))

        def basis_share(d):
            at = rows_of(head)
            return remote(dsum.at[at], dsum.at[at], as_sem.at[d - 1], ar_sem.at[d - 1], seq, head_at(d))

        @pl.when(group > 0)
        def _():
            edge_back(head_r, hrecv, h_sem).start()

        for d in range(1, head_size):
            basis_sum(d).start()
        for c in range(outer // 2 - 1, -1, -1):
            out_loads[c].wait()
            cross_out(c).start()
        for c in range(outer - 1, 0, -1):
            if c % 2:
                gate_step(c)

        load_dxr.wait()
        ext[...] = jnp.zeros_like(ext)

        @pl.when(group < groups - 1)
        def _():
            remote(head_r, hrecv, h_sem.at[0], h_sem.at[1], seq, head).wait_recv()
            ext[EDGE:] = hrecv[...]

        fixed = tail_r[...]
        for k in range(taps):
            fixed = fixed + vk[k : k + 1] * ext[pl.ds(taps - 1 - k, EDGE)]
        last = dxr_r[rows - 2 * EDGE :].astype(F32)
        dxr_r[rows - 2 * EDGE :] = jnp.concatenate([last[:EDGE], fixed], axis=0).astype(BF16)

        def multiply(k, _):
            at = pl.ds(pl.multiple_of(outer_at(k) * 2 * strip, 2 * strip), 2 * strip)
            product = dot(xn[:, at], dxr_r[...], TN).astype(BF16)
            duo[k, 0] = product[:strip]
            duo[k, 1] = product[strip:]

            @pl.when(k < outer // 2)
            def _():
                cross(k).start()

            return 0

        lax.fori_loop(0, outer, multiply, 0)
        for r in range(members):
            @pl.when(r != member)
            def _(r=r):
                branch_give(r).start()


        step_part = dot(ddtr_r[...], xn[...], TN)
        for q in range(width // both):
            low_sum[share + q * heads : share + (q + 1) * heads] = step_part[
                :, q * both : (q + 1) * both
            ]

        load_dbc.wait()
        total = dsum[own_rows]
        for d in range(1, head_size):
            basis_sum(d).wait_recv()
            total = total + drecv[d - 1]
        dsum[own_rows] = total
        for d in range(1, head_size):
            basis_share(d).start()

        def arrived(k):
            c = outer - 1 - k
            cross(k).wait_recv()
            total = duo[k, side].astype(F32) + xrecv[k].astype(F32)
            if c:
                total = total + gather_in(along, zrecv, c, outer)
            duo[k, side] = total.astype(BF16)
            if c:
                along(c).start()

        def arrived_loop(first, last):
            for k in range(first, last):
                arrived(k)

        def to_core(k):
            return remote(csend.at[k], crecv.at[k], cs_sem.at[k], cr_sem.at[k], seq, 2 * lane + 1 - core)

        def to_lane(k):
            return remote(cown.at[k], yrecv.at[k], ys_sem.at[k], yr_sem.at[k],
                          seq, 2 * lane_at(k) + core)

        def columns_of(step):
            which = 1 - core if step < half_heads else core
            at = (2 * lane_at(step % half_heads) + which) * share
            return pl.ds(pl.multiple_of(at, share), share)

        def fetch(step):
            at, slot = columns_of(step), step % 2
            return [
                pltpu.make_async_copy(gate_h.at[at], weights.at[slot, 0], w_sem.at[slot, 0]),
                pltpu.make_async_copy(value_h.at[at], weights.at[slot, 1], w_sem.at[slot, 1]),
            ]

        norms[...] = jnp.zeros_like(norms)
        for step in range(head_size):
            slot, at, k = step % 2, columns_of(step), step % half_heads
            keep = csend if step < half_heads else cown
            if step == 0:
                for load in fetch(0):
                    load.start()
            if step < head_size - 1:
                for load in fetch(step + 1):
                    load.start()
            for load in fetch(step):
                load.wait()

            def back_rows(c, _, slot=slot, at=at, k=k, keep=keep, first=step == 0, step=step):
                at_rows = rows_of(c)
                grad = (
                    dot(dz_r[at_rows], weights[slot, 0], NT) + dot(dxr_r[at_rows], weights[slot, 1], NT)
                    + dot(ddtr_r[at_rows], step_m[:, at])
                )
                keep[k, at_rows] = grad.astype(BF16)
                weighed = grad * xn[at_rows, at].astype(F32)
                total = weighed[:, :LANES] if first else weight[at_rows] + weighed[:, :LANES]
                for q in range(1, share // LANES):
                    total += weighed[:, q * LANES : (q + 1) * LANES]
                weight[at_rows] = total
                norms[step] += jnp.broadcast_to(jnp.sum(weighed, axis=0, keepdims=True), (8, share))
                return 0

            lax.fori_loop(0, head_size, back_rows, 0)
            if step < half_heads:
                to_core(k).start()
            else:
                to_core(k).wait_recv()

                def add_rows(c, _, k=k):
                    at_rows = rows_of(c)
                    cown[k, at_rows] = (
                        cown[k, at_rows].astype(F32) + crecv[k, at_rows].astype(F32)
                    ).astype(BF16)
                    return 0

                lax.fori_loop(0, head_size, add_rows, 0)
                if k < half_heads - 1:
                    to_lane(k).start()
            if step == 0:
                for c in range(outer - 1, 0, -1):
                    if c % 2 == 0:
                        gate_step(c)
            if step == head_size - 2:
                for c in range(outer // 2 - 1, 0, -1):
                    out_step(c)

        for d in range(1, head_size):
            at = rows_of(head_at(d))
            remote(dsum.at[at], dsum.at[at], as_sem.at[d - 1], ar_sem.at[head_size - 1 - d],
                   seq, head).wait_recv()

        start = EDGE - taps + 1
        load_bc.wait()
        pre_bc = sb[...]
        for k in range(taps):
            pre_bc = pre_bc + sk[k : k + 1] * low[pl.ds(start + k, rows)]
        dpre = dsum[...] * slope(pre_bc)
        full_sum[...] = jnp.zeros_like(full_sum)
        full_sum[:, :channels] = vec[...]
        full_sum[:, channels + both : channels + both + heads] = small_r[...]
        for k in range(taps):
            full_sum[k : k + 1, channels : channels + both] = jnp.sum(
                dpre * low[pl.ds(start + k, rows)], axis=0, keepdims=True
            )
        full_sum[taps : taps + 1, channels : channels + both] = jnp.sum(dpre, axis=0, keepdims=True)
        low[0:rows] = dpre
        low[rows:] = jnp.zeros((EDGE, both), F32)

        @pl.when(group > 0)
        def _():
            edge_back(low.at[pl.ds(0, EDGE)], hbrecv, hb_sem).start()

        arrived_loop(0, outer // 4)

        @pl.when(group < groups - 1)
        def _():
            remote(low.at[pl.ds(0, EDGE)], hbrecv, hb_sem.at[0], hb_sem.at[1], seq, head).wait_recv()
            low[rows:] = hbrecv[...]

        dbc_v = sk[0:1] * low[pl.ds(taps - 1, rows)]
        for k in range(1, taps):
            dbc_v = dbc_v + sk[k : k + 1] * low[pl.ds(taps - 1 - k, rows)]
        dbc_low = dbc_v.astype(BF16)
        own_at = pl.ds(pl.multiple_of(head * share, share), share)
        low_sum[:share] = dot(xn[:, own_at], dbc_low, TN)
        blow[...] = dbc_low

        def doubling(b):
            distance = 1 << b
            partner = seq + distance - 2 * distance * lax.rem(seq // distance, 2)
            return [
                remote(full_send.at[b], full_recv.at[b], fs_sem.at[b], fr_sem.at[b], partner, head),
                remote(low_send.at[b], low_recv.at[b], ls_sem.at[b], lr_sem.at[b], partner, head),
            ]

        def double(b):
            full_send[b] = full_sum[...]
            low_send[b] = low_sum[...].astype(BF16)
            for copy in doubling(b):
                copy.start()

        def doubled(b):
            for copy in doubling(b):
                copy.wait_recv()
            full_sum[...] = full_sum[...] + full_recv[b]
            low_sum[...] = low_send[b].astype(F32) + low_recv[b].astype(F32)

        double(0)

        def send_rest(k, _):
            cross(k).start()
            return 0

        lax.fori_loop(outer // 2, outer, send_rest, 0)

        def basis_rows(c, _):
            at_rows = rows_of(c)
            grad = dot(blow[at_rows], state_m[own_at], NT)
            bpart[at_rows] = grad.astype(BF16)
            weighed = grad * xn[at_rows, own_at].astype(F32)
            total = weight[at_rows]
            for q in range(share // LANES):
                total += weighed[:, q * LANES : (q + 1) * LANES]
            weight[at_rows] = total
            norms[head_size - 1] += jnp.broadcast_to(
                jnp.sum(weighed, axis=0, keepdims=True), (8, share)
            )
            return 0

        lax.fori_loop(0, head_size, basis_rows, 0)
        rsend[...] = dot(jnp.ones((8, LANES), F32), weight[...], NT, precision=HIGH)

        def row_sums(d):
            return remote(rsend, rrecv.at[d - 1], rs_sem.at[d - 1], rr_sem.at[d - 1], seq, head_at(d))

        for d in range(1, head_size):
            row_sums(d).start()

        def share_norm(step):
            which = 1 - core if step < half_heads else core
            return remote(norms.at[step], nrecv.at[step], ns_sem.at[step], nr_sem.at[step],
                          seq, 2 * lane_at(step % half_heads) + which)

        for step in range(head_size - 1):
            share_norm(step).start()

        arrived_loop(outer // 4, outer // 2)

        def give(r):
            return remote(up.at[r], up_o.at[member], us_sem.at[r], ur_sem.at[member], base + r, head)

        for d in range(1, head_size):
            row_sums(d).wait_recv()
        sums = rsend[...]
        for d in range(1, head_size):
            sums = sums + rrecv[d - 1]
        pick = (lax.broadcasted_iota(jnp.int32, (8, LANES), 0) == 0).astype(F32)
        rrecv[0] = sums * (1.0 / width)
        for k in range(half_heads - 1):
            to_lane(k).wait_recv()

        def finish_rows(c, _):
            at_rows = rows_of(c)
            grad = cown[half_heads - 1, at_rows].astype(F32) + bpart[at_rows].astype(F32)
            for k in range(half_heads - 1):
                grad = grad + yrecv[k, at_rows].astype(F32)
            scale = rstd_r[at_rows]
            hat = mine_r[at_rows].astype(F32) * scale
            mean = dot(rrecv[0, :, at_rows], pick, TN, precision=HIGH)
            inside = pl.ds(pl.multiple_of(lax.rem(c, per) * chunk, chunk), chunk)
            for q in range(share // LANES):
                at = slice(q * LANES, (q + 1) * LANES)
                up[c // per, inside, at] = (
                    scale * (grad[:, at] * gain[:, at] - hat[:, at] * mean)
                ).astype(BF16)
            return 0

        lax.fori_loop(0, head_size, finish_rows, 0)
        for r in range(members):
            @pl.when(r != member)
            def _(r=r):
                give(r).start()

        keep_up = pltpu.make_async_copy(up.at[member], up_o.at[member], copy_sem.at[0])
        keep_up.start()

        norm = norms[head_size - 1]
        for step in range(head_size - 1):
            share_norm(step).wait_recv()
            norm = norm + nrecv[step]
        doubled(0)
        full_sum[:, packed - share :] = norm / gain[...]

        double(1)
        arrived_loop(outer // 2, outer - 1)
        for b in range(1, steps - 1):
            doubled(b)
            double(b + 1)
        arrived(outer - 1)
        out_step(0)
        gate_loads[0].wait()
        gate_o[...] = gbuf[0].astype(F32) + gather_in(along_gate, grecv, 0, outer)
        out_o[...] = obuf[0, side].astype(F32) + gather_in(along_out, orecv, 0, outer // 2)
        value_o[...] = duo[outer - 1, side].astype(F32) + gather_in(along, zrecv, 0, outer)
        doubled(steps - 1)
        for step in range(head_size - 1):
            share_norm(step).wait_send()
        norms[0] = full_sum[:, packed - share :]
        last_norm = remote(norms.at[0], nlast, nl_sem.at[0], nl_sem.at[1], 2 * place + 1 - side, head)
        last_norm.start()
        state_o[...] = low_sum[:share]
        step_o[...] = low_sum[share:]
        vkern_o[...] = full_sum[:taps, :channels]
        vbias_o[...] = full_sum[taps : taps + 1, :channels]
        ggain_o[...] = full_sum[taps + 1 : taps + 2, :channels]
        skern_o[...] = full_sum[:taps, channels : channels + both]
        sbias_o[...] = full_sum[taps : taps + 1, channels : channels + both]
        small_at = slice(channels + both, channels + both + heads)
        tbias_o[...] = full_sum[0:1, small_at]
        rate_o[...] = full_sum[1:2, small_at]
        skip_o[...] = full_sum[2:3, small_at]
        last_norm.wait()
        norm_o[...] = norms[0, 0:1] + nlast[0:1]

        for r in range(members):
            @pl.when(r != member)
            def _(r=r):
                remote(up.at[r], up_o.at[r], us_sem.at[r], ur_sem.at[r], base + r, head).wait()
                remote(branch_h.at[r], branch_o.at[r], bs_sem.at[r], br_sem.at[r], base + r, head).wait()

        keep_branch.wait()
        keep_up.wait()

        def drain(k, _):
            cross(k).wait_send()
            return 0

        lax.fori_loop(0, outer, drain, 0)
        for c in range(1, outer):
            along(c).wait_send()
            along_gate(c).wait_send()
        for c in range(1, outer // 2):
            along_out(c).wait_send()
        for c in range(outer // 2):
            cross_out(c).wait_send()
        for k in range(half_heads):
            to_core(k).wait_send()
            if k < half_heads - 1:
                to_lane(k).wait_send()

        @pl.when(group > 0)
        def _():
            edge_back(head_r, hrecv, h_sem).wait_send()
            edge_back(low.at[pl.ds(0, EDGE)], hbrecv, hb_sem).wait_send()

        for d in range(1, head_size):
            row_sums(d).wait_send()
            basis_sum(d).wait_send()
            basis_share(d).wait_send()
        for b in range(steps):
            for copy in doubling(b):
                copy.wait_send()

    vmem = pl.BlockSpec(memory_space=pltpu.VMEM)
    anywhere = pl.BlockSpec(memory_space=pl.ANY)
    dma = pltpu.SemaphoreType.DMA
    args = (normal_in, dz, dxr, tail, head_rows, gate_matrix, value_matrix, state_matrix, step_matrix,
            value_kernel, state_kernel, state_bias, state_pre, state_edge, dbc, ddtr, vectors, small,
            branch, mine, rstd, gain_share, gate_half, output_half)
    far = {2, 5, 6, 12, 14, 18, 22, 23}
    moves = lambda *dims: pltpu.VMEM(dims, BF16)
    plain = lambda *dims: pltpu.VMEM(dims, F32)
    return pl.pallas_call(
        kernel,
        in_specs=[anywhere if i in far else vmem for i in range(len(args))],
        out_specs=[vmem] * 14 + [anywhere, anywhere],
        out_shape=[
            shape((strip, channels), F32), shape((strip, channels), F32), shape((channels, strip), F32),
            shape((share, both), F32), shape((low_rows - share, both), F32),
            shape((taps, channels), F32), shape((1, channels), F32), shape((1, channels), F32),
            shape((taps, both), F32), shape((1, both), F32), shape((1, share), F32),
            shape((1, heads), F32), shape((1, heads), F32), shape((1, heads), F32),
            shape((members, length, share), BF16), shape((members, length, share), BF16),
        ],
        scratch_shapes=[
            moves(rows, channels), moves(outer, 2, strip, channels), moves(outer, strip, channels),
            moves(outer - 1, strip, channels), moves(outer, strip, channels),
            moves(outer - 1, strip, channels), moves(outer // 2, 2, channels, strip),
            moves(outer // 2 - 1, channels, strip), moves(outer // 2, channels, strip),
            moves(rows, share), moves(2, 2, share, channels), plain(rows, LANES),
            moves(half_heads, rows, share), moves(half_heads, rows, share),
            moves(half_heads, rows, share), moves(half_heads - 1, rows, share),
            plain(8, rows), plain(head_size - 1, 8, rows), moves(members, length, share),
            plain(head_size, 8, share), plain(head_size - 1, 8, share), plain(8, share),
            moves(rows, both),
            plain(head_size - 1, chunk, both), plain(rows, both), plain(2 * EDGE, channels),
            plain(EDGE, channels), plain(EDGE, both), plain(rows + EDGE, both),
            plain(8, packed), plain(steps, 8, packed), plain(steps, 8, packed),
            plain(low_rows, both), moves(steps, low_rows, both), moves(steps, low_rows, both),
            dma((outer,)), dma((outer,)), dma((outer - 1,)), dma((outer - 1,)),
            dma((half_heads,)), dma((half_heads,)), dma((half_heads - 1,)), dma((half_heads - 1,)),
            dma((head_size - 1,)), dma((head_size - 1,)),
            dma((members,)), dma((members,)), dma((head_size - 1,)), dma((head_size - 1,)),
            dma((head_size - 1,)), dma((head_size - 1,)), dma((head_size - 1,)), dma((head_size - 1,)),
            dma((2,)), dma((2,)),
            dma((steps,)), dma((steps,)), dma((steps,)), dma((steps,)), dma((2,)),
            dma((members,)), dma((members,)), dma((outer - 1,)), dma((outer - 1,)),
            dma((outer // 2 - 1,)), dma((outer // 2 - 1,)), dma((2, outer // 2)), dma((outer + outer // 2,)),
            dma((2, 2)), dma((4,)),
        ],
        compiler_params=pltpu.CompilerParams(
            collective_id=1, has_side_effects=True, vmem_limit_bytes=VMEM_BYTES
        ),
        cost_estimate=pl.CostEstimate(
            flops=60_000_000_000, bytes_accessed=300_000_000, transcendentals=0
        ),
        name="closing_sums",
    )(*args)

def settle(tokens, cotangent, up, branch, wide_grads, small_grads):
    members, length, share = tokens.shape
    count = len(wide_grads) + len(small_grads)

    def kernel(tokens_r, cot_r, up_r, branch_r, *refs):
        grads, out_o, grad_o, given = refs[:count], refs[count], refs[count + 1], refs[count + 2 :]
        out_o[...] = (tokens_r[...].astype(F32) + branch_r[...].astype(F32)).astype(BF16)
        grad_o[...] = cot_r[...].astype(F32) + up_r[...].astype(F32)
        for source, target in zip(grads, given):
            target[...] = source[...]

    block = pl.BlockSpec((1, length, share), lambda i: (i, 0, 0))
    rest = [
        pl.BlockSpec((g.shape[0] // members, g.shape[1]), lambda i: (i, 0)) for g in wide_grads
    ] + [pl.BlockSpec(g.shape, lambda i: (0, 0)) for g in small_grads]
    return call(
        kernel, "first_layout", (members,), [block] * 4 + rest, [block, block] + rest,
        [shape(tokens.shape, BF16), shape(tokens.shape, F32)]
        + [shape(g.shape, F32) for g in (*wide_grads, *small_grads)],
        [], 1000, (tokens, cotangent, up, branch, *wide_grads, *small_grads),
    )


def shifted(block, axis, distance):
    devices = range(lax.axis_size(axis))
    route = [(i - distance, i) for i in devices if i - distance in devices]
    return lax.ppermute(block, axis, route)


def carried(part, decay, hops, distance):
    carry = shifted(part, "seq", distance)
    for _ in range(hops - 1):
        leaving = decay * carry.astype(F32) + part.astype(F32)
        carry = shifted(leaving.astype(BF16), "seq", distance)
    return carry


def swapped(block, distance):
    size = lax.axis_size("seq")
    return lax.ppermute(block, "seq", [(i, i ^ distance) for i in range(size)])


def local(
    tokens,
    cotangent,
    norm_gain,
    gate_matrix,
    value_matrix,
    state_matrix,
    step_matrix,
    value_kernel,
    value_bias,
    state_kernel,
    state_bias,
    step_bias,
    log_rate,
    skip_gain,
    gate_gain,
    output_matrix,
):
    seq_count, length, share = tokens.shape
    hops = lax.axis_size("seq") // seq_count - 1
    width, channels = gate_matrix.shape
    heads = step_bias.shape[0]
    wide = channels // heads
    both = state_matrix.shape[1]
    taps = value_kernel.shape[0]
    rows = seq_count * length
    head_count = lax.axis_size("head")
    head_rank = lax.axis_index("head")
    row = lambda v: v.reshape(1, -1)

    (
        normal_in, flat_cot, mine, gate_pre, value_pre, state_pre, normed_grad, xs, xdt, xw, hin0,
        rstd, step_pre, bcs, dt, cum, cumt, pre, dec, value_edge, state_edge, carry,
    ) = opening(
        tokens, cotangent, row(norm_gain), gate_matrix, value_matrix, state_matrix, step_matrix.T,
        output_matrix, value_kernel, row(value_bias), state_kernel, row(state_bias), row(step_bias),
        row(log_rate), lax.axis_size("seq"), head_count,
    )
    whole_decay = jnp.repeat(pre[-1] * dec[-1], wide, axis=0)
    skip_row = row(jnp.repeat(skip_gain, wide))
    hin_low, normed, part, dy, dz, dv, ab, ds0, post, starting, gate_gain_part = forward(
        xdt, xs, bcs, gate_pre, normed_grad, cum, cumt, hin0, pre, dec, carry, skip_row,
        row(gate_gain), output_matrix, length, lax.axis_size("seq"), head_count,
    )
    back = carried(starting, whole_decay, hops, -seq_count)
    seq_size = lax.axis_size("seq")
    gate_keep, gate_give = halves(normal_in, dz, seq_size // 2)
    gate_got = swapped(gate_give, 1)
    output_keep, output_give = parities(normed, flat_cot, seq_size // 2)
    output_give, back = lax.optimization_barrier((output_give, back))
    output_got = swapped(output_give, 2)
    branch = lax.psum_scatter(part, "head", scatter_dimension=1, tiled=True).reshape(tokens.shape)
    g, dbc_intra = intra_back(bcs, xdt, dy, cum, cumt, length)
    dxr, tail, head_rows, value_kernel_part, value_bias_part, ddtr, dbc, small = finish_back(
        value_pre, value_edge, value_kernel, row(value_bias), xs, xdt, xw, g, dy, dv, bcs, step_pre, dt, cum,
        ab, hin0, pre, carry, hin_low, ds0, post, back, dec, dbc_intra, skip_row, row(skip_gain),
        row(step_bias), row(log_rate), length,
    )
    gate_half = (gate_keep.astype(F32) + gate_got.astype(F32)).astype(BF16)
    output_half = (output_keep.astype(F32) + output_got.astype(F32)).astype(BF16)
    vectors = jnp.concatenate(
        [value_kernel_part, value_bias_part, gate_gain_part, jnp.zeros((2, channels), F32)], axis=0
    )
    gain_share = lax.dynamic_slice_in_dim(norm_gain, head_rank * share, share, 0)
    (
        gate_grad, value_grad, output_grad, state_grad, step_grad, value_kernel_grad, value_bias_grad,
        gate_gain_grad, state_kernel_grad, state_bias_grad, norm_grad, step_bias_grad, log_rate_grad,
        skip_gain_grad, up, branch,
    ) = closing(
        normal_in, dz, dxr, tail, head_rows, gate_matrix, value_matrix, state_matrix, step_matrix.T,
        value_kernel, state_kernel, row(state_bias), state_pre, state_edge, dbc, ddtr, vectors, small,
        branch, mine, rstd, row(gain_share), gate_half, output_half, length, seq_size, head_count,
    )
    (
        layer_out, token_grad, gate_grad, value_grad, output_grad, state_grad, value_kernel_grad,
        value_bias_grad, gate_gain_grad, state_kernel_grad, state_bias_grad, norm_grad,
        step_bias_grad, log_rate_grad, skip_gain_grad,
    ) = settle(
        tokens, cotangent, up, branch, (gate_grad, value_grad, output_grad, state_grad),
        (value_kernel_grad, value_bias_grad, gate_gain_grad, state_kernel_grad, state_bias_grad,
         norm_grad, step_bias_grad, log_rate_grad, skip_gain_grad),
    )
    strip = width // seq_size
    step_grad = jnp.transpose(step_grad.reshape(width // both, heads, both), (0, 2, 1))
    step_grad = lax.dynamic_slice_in_dim(
        step_grad.reshape(width, heads), lax.axis_index("seq") * strip, strip, 0
    )
    return (
        layer_out,
        token_grad,
        norm_grad[0],
        gate_grad,
        value_grad,
        state_grad,
        step_grad,
        value_kernel_grad,
        value_bias_grad[0],
        state_kernel_grad,
        state_bias_grad[0],
        step_bias_grad[0],
        log_rate_grad[0],
        skip_gain_grad[0],
        gate_gain_grad[0],
        output_grad,
    )


def solution(mesh):
    in_specs = (
        P(None, "seq", "head"),
        P(None, "seq", "head"),
        P(),
        P(None, "head"),
        P(None, "head"),
        P(),
        P(None, "head"),
        P(None, "head"),
        P("head"),
        P(),
        P(),
        P("head"),
        P("head"),
        P("head"),
        P("head"),
        P("head", None),
    )
    out_specs = (
        P(None, "seq", "head"),
        P(None, "seq", "head"),
        P("head"),
        P("seq", "head"),
        P("seq", "head"),
        P("head", None),
        P("seq", "head"),
        P(None, "head"),
        P("head"),
        P(),
        P(),
        P("head"),
        P("head"),
        P("head"),
        P("head"),
        P("head", "seq"),
    )
    return jax.shard_map(local, mesh=mesh, in_specs=in_specs, out_specs=out_specs, check_vma=False)
```

```python
import jax
import jax.numpy as jnp
from jax import lax
from jax.experimental import pallas as pl
from jax.experimental.pallas import tpu as pltpu
from jax.sharding import PartitionSpec as P

HIGH = lax.Precision.HIGHEST
EPSILON = 1e-05
F32 = jnp.float32
BF16 = jnp.bfloat16
LANES = 128
EDGE = 8
VMEM_BYTES = 56 * 1024 * 1024

NN = (((1,), (0,)), ((), ()))
NT = (((1,), (1,)), ((), ()))
TN = (((0,), (0,)), ((), ()))


def dot(a, b, dims=NN, precision=None):
    return lax.dot_general(a, b, dims, precision=precision, preferred_element_type=F32)


def dot_split(a, b, dims=NN):
    high = a.astype(BF16)
    rest = (a - high.astype(F32)).astype(BF16)
    return dot(high, b, dims) + dot(rest, b, dims)


def sigmoid(v):
    return 1.0 / (1.0 + jnp.exp(-v))


def silu(v):
    return v * sigmoid(v)


def slope(v):
    sigma = sigmoid(v)
    return sigma * (1.0 + v * (1.0 - sigma))


def softplus(v):
    return jnp.maximum(v, 0.0) + jnp.log1p(jnp.exp(-jnp.abs(v)))


def ones_where(shape, rule):
    rows = lax.broadcasted_iota(jnp.int32, shape, 0)
    cols = lax.broadcasted_iota(jnp.int32, shape, 1)
    return rule(rows, cols)


def head_picker(channels, heads):
    wide = channels // heads
    return ones_where((channels, heads), lambda r, c: r // wide == c).astype(F32).astype(BF16)


def pair_spread(cols, j, rows):
    lane = lax.broadcasted_iota(jnp.int32, (rows, LANES), 1)
    first = jnp.broadcast_to(cols[:, 2 * j : 2 * j + 1], (rows, LANES))
    second = jnp.broadcast_to(cols[:, 2 * j + 1 : 2 * j + 2], (rows, LANES))
    return jnp.where(lane < LANES // 2, first, second)


def spread(cols, rows, heads):
    return jnp.concatenate([pair_spread(cols, j, rows) for j in range(heads // 2)], axis=1)


def call(kernel, name, grid, in_specs, out_specs, out_shape, scratch, flops, args, transcendentals=0):
    moved = sum(a.size * a.dtype.itemsize for a in args) + sum(
        o.size * o.dtype.itemsize for o in out_shape
    )
    return pl.pallas_call(
        kernel,
        grid=grid,
        in_specs=in_specs,
        out_specs=out_specs,
        out_shape=out_shape,
        scratch_shapes=scratch,
        compiler_params=pltpu.CompilerParams(
            dimension_semantics=("arbitrary",) * len(grid), vmem_limit_bytes=VMEM_BYTES
        ),
        cost_estimate=pl.CostEstimate(
            flops=int(flops), bytes_accessed=int(moved), transcendentals=int(transcendentals)
        ),
        name=name,
    )(*args)


def shape(dims, dtype):
    return jax.ShapeDtypeStruct(dims, dtype)


def decays(cum, cumt, h, half):
    top = jnp.exp(jnp.minimum(cum[:half, h : h + 1] - cumt[h : h + 1, :half], 0.0))
    low = jnp.exp(jnp.minimum(cum[half:, h : h + 1] - cumt[h : h + 1, :], 0.0))
    return top, low


def lower_scores(basis, states, length):
    scores = dot(basis[:, states:], basis[:, :states], NT)
    return jnp.where(ones_where((length, length), lambda r, c: r >= c), scores, 0.0)


def intra_back(bcs, xdt, dy, cum, cumt, length):
    rows, channels = xdt.shape
    heads = cum.shape[1]
    both = bcs.shape[1]
    states = both // 2
    half = length // 2

    def kernel(bcs_r, xdt_r, dy_r, cum_r, cumt_r, g_o, dbc_o, grad):
        scores = lower_scores(bcs_r[...], states, length)
        cum_v, cumt_v = cum_r[...], cumt_r[...]
        lane = lax.broadcasted_iota(jnp.int32, (length, LANES), 1)
        grad[...] = jnp.zeros_like(grad)
        for j in range(heads // 2):
            at = slice(j * LANES, (j + 1) * LANES)
            pair, dpair = xdt_r[:, at], dy_r[:, at]
            g_top = jnp.zeros((half, LANES), F32)
            g_low = jnp.zeros((half, LANES), F32)
            for s in range(2):
                own = jnp.where((lane < LANES // 2) == (s == 0), dpair, jnp.zeros_like(dpair))
                top, low = decays(cum_v, cumt_v, 2 * j + s, half)
                grad[:half, :half] += dot(own[:half], pair[:half], NT) * top
                grad[half:] += dot(own[half:], pair, NT) * low
                w_top = (scores[:half, :half] * top).astype(BF16)
                w_low = (scores[half:] * low).astype(BF16)
                g_top += dot(w_top, own[:half], TN) + dot(w_low[:, :half], own[half:], TN)
                g_low += dot(w_low[:, half:], own[half:], TN)
            g_o[:half, at] = g_top
            g_o[half:, at] = g_low
        masked = jnp.where(ones_where((length, length), lambda r, c: r >= c), grad[...], 0.0)
        high = masked.astype(BF16)
        rest = (masked - high.astype(F32)).astype(BF16)
        in_b, out_b = bcs_r[:, :states], bcs_r[:, states:]
        dbc_o[:, :states] = dot(high, out_b, TN) + dot(rest, out_b, TN)
        dbc_o[:, states:] = dot(high, in_b) + dot(rest, in_b)

    tokens = lambda n: pl.BlockSpec((length, n), lambda i: (i, 0))
    return call(
        kernel, "within_blocks_back", (rows // length,),
        [tokens(both), tokens(channels), tokens(channels), tokens(heads),
         pl.BlockSpec((heads, length), lambda i: (0, i))],
        [tokens(channels), tokens(both)],
        [shape((rows, channels), F32), shape((rows, both), F32)],
        [pltpu.VMEM((length, length), F32)],
        2 * rows * length * channels * 8, (bcs, xdt, dy, cum, cumt), rows * length * heads,
    )


def finish_back(value_pre, value_edge, value_kernel, value_bias, xs, xdt, xw, g, dy, dv, bcs, step_pre, dt,
                cum, ab, hin0, pre, carry, hin_low, ds0, post, back, dec, dbc_intra, skip_row, skip_gain,
                step_bias, log_rate, gain_part, length):
    rows, channels = xs.shape
    heads = cum.shape[1]
    both = bcs.shape[1]
    states = both // 2
    wide = channels // heads
    count = rows // length
    taps = value_kernel.shape[0]
    unit = length // EDGE

    def kernel(xr, xr_before, xr_edge, vk, vb, xs_r, xdt_r, xw_r, g_r, dy_r, dv_r, bcs_r, dtr, dt_r, cum_r,
               ab_r, hin_r, pre_r, carry_r, low_r, ds_r, post_r, back_r, dec_r, dbci, skip, skipg, tb,
               lr, gain_r, dxr_o, tail_o, head_o, vec_o, ddtr_o, dbc_o, small_o,
               padded, ext, ds_low, inner_sums):
        i = pl.program_id(0)
        block = count - 1 - i

        @pl.when(i == 0)
        def _():
            vec_o[...] = jnp.zeros_like(vec_o)
            vec_o[taps + 1 : taps + 2] = gain_r[...]
            small_o[...] = jnp.zeros_like(small_o)
            ext[0:EDGE] = jnp.zeros((EDGE, channels), F32)

        @pl.when(block == 0)
        def _():
            padded[0:EDGE] = xr_edge[...]

        @pl.when(block > 0)
        def _():
            padded[0:EDGE] = xr_before[...]

        padded[EDGE:] = xr[...]
        ext[length:] = ext[0:EDGE]
        for h in range(heads):
            at = slice(h * wide, (h + 1) * wide)
            ds = ds_r[0, at] + post_r[0, h : h + 1] * back_r[at].astype(F32)
            ds_low[at] = ds.astype(BF16)
            hin = hin_r[0, at] + pre_r[0, h : h + 1] * carry_r[at].astype(F32)
            inner_sums[h : h + 1] = jnp.sum(ds * hin, axis=0, keepdims=True) * dec_r[0, h : h + 1]
        in_b = bcs_r[:, :states]
        dt_v, cum_v = dt_r[...], cum_r[...]
        fade = jnp.exp(cum_v[length - 1 : length] - cum_v)
        factor = fade * dt_v
        start = EDGE - taps + 1
        picker = head_picker(channels, heads)
        c_sum = jnp.zeros((length, heads), F32)
        d_sum = jnp.zeros((length, heads), F32)
        w_sum = jnp.zeros((length, heads), F32)
        for j in range(channels // LANES):
            at = slice(j * LANES, (j + 1) * LANES)
            xs_v = xs_r[:, at].astype(F32)
            dxw = dot(in_b, ds_low[at], NT)
            g_v = g_r[:, at]
            c_sum += dot_split(xs_v * g_v, picker[at])
            d_sum += dot_split(xs_v * dxw, picker[at])
            w_sum += dot_split(xdt_r[:, at].astype(F32) * g_v, picker[at])
            dxs = (
                pair_spread(dt_v, j, length) * g_v
                + pair_spread(factor, j, length) * dxw
                + skip[:, at] * dy_r[:, at].astype(F32)
            )
            total = vb[:, at] + vk[0:1, at] * padded[pl.ds(start, length), at]
            for k in range(1, taps):
                total = total + vk[k : k + 1, at] * padded[pl.ds(start + k, length), at]
            dpre = dxs * slope(total)
            ext[0:length, at] = dpre
            vec_o[taps : taps + 1, at] += jnp.sum(dpre, axis=0, keepdims=True)
            for k in range(taps):
                vec_o[k : k + 1, at] += jnp.sum(
                    dpre * padded[pl.ds(start + k, length), at], axis=0, keepdims=True
                )
            dxr = vk[0:1, at] * ext[pl.ds(taps - 1, length), at]
            for k in range(1, taps):
                dxr = dxr + vk[k : k + 1, at] * ext[pl.ds(taps - 1 - k, length), at]
            dxr_o[:, at] = dxr.astype(BF16)

            @pl.when(i == 0)
            def _():
                tail_o[:, at] = dxr[length - EDGE :]

        head_o[...] = ext[0:EDGE]
        dbc_o[:, :states] = dbci[:, :states] + dot(xw_r[...], ds_low[...])
        dbc_o[:, states:] = dbci[:, states:] + dot(dv_r[...], low_r[0])
        rate = -jnp.exp(lr[...])
        a_sum, b_sum = ab_r[:, :heads], ab_r[:, heads:]
        e_sum = d_sum * factor
        ones = jnp.ones((1, LANES), F32)
        dtotal = jnp.sum(e_sum, axis=0, keepdims=True) + dot(ones, inner_sums[...], NT, precision=HIGH)
        row = lax.broadcasted_iota(jnp.int32, (length, heads), 0)
        dcum = a_sum - skipg[...] * b_sum - w_sum - e_sum
        dcum = dcum + jnp.where(row == length - 1, dtotal, 0.0)
        upper = ones_where((length, length), lambda r, c: r <= c).astype(F32)
        dda = dot(upper, dcum, precision=HIGH)
        ddt = c_sum + d_sum * fade + dda * rate
        dpre_dt = ddt * sigmoid(dtr[...] + tb[...])
        ddtr_o[...] = dpre_dt.astype(BF16)
        small_o[0:1] += jnp.sum(dpre_dt, axis=0, keepdims=True)
        small_o[1:2] += jnp.sum(dda * dt_v, axis=0, keepdims=True) * rate
        small_o[2:3] += jnp.sum(b_sum, axis=0, keepdims=True)

    last = count - 1
    whole = lambda *dims: pl.BlockSpec(dims, lambda i: (0,) * len(dims))
    tokens = lambda n: pl.BlockSpec((length, n), lambda i: (last - i, 0))
    before = lambda n: pl.BlockSpec((EDGE, n), lambda i: (jnp.maximum((last - i) * unit - 1, 0), 0))
    per = lambda *dims: pl.BlockSpec((1,) + dims, lambda i: (last - i, 0, 0))
    return call(
        kernel, "across_blocks_back", (count,),
        [tokens(channels), before(channels), whole(EDGE, channels), whole(taps, channels),
         whole(1, channels), tokens(channels), tokens(channels), tokens(channels), tokens(channels),
         tokens(channels), tokens(channels), tokens(both), tokens(heads), tokens(heads), tokens(heads),
         tokens(2 * heads), per(channels, states), per(heads, LANES), whole(channels, states),
         per(channels, states), per(channels, states), per(heads, LANES), whole(channels, states),
         per(heads, LANES), tokens(both), whole(1, channels), whole(1, heads), whole(1, heads),
         whole(1, heads), whole(1, channels)],
        [tokens(channels), whole(EDGE, channels), whole(EDGE, channels), whole(EDGE, channels),
         tokens(heads), tokens(both), whole(EDGE, heads)],
        [shape((rows, channels), BF16), shape((EDGE, channels), F32), shape((EDGE, channels), F32),
         shape((EDGE, channels), F32), shape((rows, heads), BF16),
         shape((rows, both), F32), shape((EDGE, heads), F32)],
        [pltpu.VMEM((length + EDGE, channels), F32), pltpu.VMEM((length + EDGE, channels), F32),
         pltpu.VMEM((channels, states), BF16), pltpu.VMEM((heads, LANES), F32)],
        2 * rows * channels * states * 3,
        (value_pre, value_pre, value_edge, value_kernel, value_bias, xs, xdt, xw, g, dy, dv, bcs, step_pre,
         dt, cum, ab, hin0, pre, carry, hin_low, ds0, post, back, dec, dbc_intra, skip_row, skip_gain,
         step_bias, log_rate, gain_part),
        2 * rows * channels,
    )


def halves(normal_in, grad, outer):
    rows, width = normal_in.shape
    channels = grad.shape[1]
    strip = width // (2 * outer)

    def kernel(xn, grad_r, keep_o, give_o):
        side = lax.rem(lax.axis_index("seq"), 2)
        product = dot(xn[...], grad_r[...], TN).astype(BF16)

        @pl.when(side == 0)
        def _():
            keep_o[0] = product[:strip]
            give_o[0] = product[strip:]

        @pl.when(side == 1)
        def _():
            keep_o[0] = product[strip:]
            give_o[0] = product[:strip]

    out = pl.BlockSpec((1, strip, channels), lambda i: (i, 0, 0))
    return call(
        kernel, "gate_strips", (outer,),
        [pl.BlockSpec((rows, 2 * strip), lambda i: (0, i)),
         pl.BlockSpec((rows, channels), lambda i: (0, 0))],
        [out, out], [shape((outer, strip, channels), BF16)] * 2, [], 2 * rows * width * channels,
        (normal_in, grad),
    )


def parities(normed, cotangent, outer):
    rows, width = cotangent.shape
    channels = normed.shape[1]
    strip = width // (2 * outer)

    def kernel(normed_r, cot, keep_o, give_o):
        parity = lax.rem(lax.axis_index("seq") // 2, 2)
        product = dot(normed_r[...], cot[...], TN).astype(BF16)
        for own in range(2):
            @pl.when(parity == own)
            def _(own=own):
                for side in range(2):
                    at, to = 2 * own + side, 2 * (1 - own) + side
                    keep_o[0, side] = product[:, at * strip : (at + 1) * strip]
                    give_o[0, side] = product[:, to * strip : (to + 1) * strip]

    out = pl.BlockSpec((1, 2, channels, strip), lambda i: (i, 0, 0, 0))
    return call(
        kernel, "output_strips", (outer // 2,),
        [pl.BlockSpec((rows, channels), lambda i: (0, 0)),
         pl.BlockSpec((rows, 4 * strip), lambda i: (0, i))],
        [out, out], [shape((outer // 2, 2, channels, strip), BF16)] * 2, [],
        2 * rows * width * channels, (normed, cotangent),
    )


def remote(src, dst, send, recv, seq, head):
    return pltpu.make_async_remote_copy(
        src_ref=src, dst_ref=dst, send_sem=send, recv_sem=recv, device_id=(seq, head),
        device_id_type=pl.DeviceIdType.MESH,
    )


def greet(seq, head, seq_size, head_size):
    barrier = pltpu.get_barrier_semaphore()
    for d in range(1, seq_size):
        pl.semaphore_signal(
            barrier, inc=1, device_id=(lax.rem(seq + d, seq_size), head),
            device_id_type=pl.DeviceIdType.MESH,
        )
    for d in range(1, head_size):
        pl.semaphore_signal(
            barrier, inc=1, device_id=(seq, lax.rem(head + d, head_size)),
            device_id_type=pl.DeviceIdType.MESH,
        )
    pl.semaphore_wait(barrier, seq_size - 1 + head_size - 1)


def forward(xdt, xs, bcs, gate_pre, normed_grad, cum, cumt, hin0, pre, dec, carry, skip_row, gate_gain,
            output_matrix, length, seq_size, head_size):
    rows, channels = xs.shape
    heads = cum.shape[1]
    both = bcs.shape[1]
    states = both // 2
    wide = channels // heads
    count = rows // length
    half = length // 2
    width = output_matrix.shape[1]
    inner = channels * head_size

    def kernel(xdt_r, xs_r, bcs_r, z_r, dn_r, cum_r, cumt_r, hin_r, pre_r, dec_r, carry_r, skip, gain, wo,
               low_o, normed_o, part_o, dy_o, dz_o, dv_o, ab_o, ds_o, post_o, start_o, ggain_o,
               y_s, sums, others, state, behind, prod_a, prod_b, s_sem, r_sem):
        i = pl.program_id(0)
        seq, head = lax.axis_index("seq"), lax.axis_index("head")
        barrier = pltpu.get_barrier_semaphore()

        def head_at(d):
            return lax.rem(head + d, head_size)

        def share_sums(d):
            return remote(sums, others.at[d - 1], s_sem.at[d - 1], r_sem.at[d - 1], seq, head_at(d))

        @pl.when(i == 0)
        def _():
            for d in range(1, head_size):
                pl.semaphore_signal(
                    barrier, inc=1, device_id=(seq, head_at(d)), device_id_type=pl.DeviceIdType.MESH
                )

        @pl.when(i < count)
        def _():
            at_rows = pl.ds(pl.multiple_of(i * length, length), length)
            for h in range(heads):
                at = slice(h * wide, (h + 1) * wide)
                low_o[0, at] = (
                    hin_r[0, at] + pre_r[0, h : h + 1] * carry_r[at].astype(F32)
                ).astype(BF16)
            scores = lower_scores(bcs_r[...], states, length)
            cum_v, cumt_v = cum_r[...], cumt_r[...]
            growth = jnp.exp(cum_v)
            lane = lax.broadcasted_iota(jnp.int32, (length, LANES), 1)
            squares = jnp.zeros((length, LANES), F32)
            crosses = jnp.zeros((length, LANES), F32)
            out_basis = bcs_r[:, states:]
            for j in range(channels // LANES):
                at = slice(j * LANES, (j + 1) * LANES)
                pair = xdt_r[:, at]
                y_top = jnp.zeros((half, LANES), F32)
                y_low = jnp.zeros((half, LANES), F32)
                for s in range(2):
                    own = jnp.where((lane < LANES // 2) == (s == 0), pair, jnp.zeros_like(pair))
                    top, low = decays(cum_v, cumt_v, 2 * j + s, half)
                    y_top += dot((scores[:half, :half] * top).astype(BF16), own[:half])
                    y_low += dot((scores[half:] * low).astype(BF16), own)
                v = dot(out_basis, low_o[0, at], NT)
                y = (
                    jnp.concatenate([y_top, y_low], axis=0)
                    + pair_spread(growth, j, length) * v
                    + skip[:, at] * xs_r[:, at].astype(F32)
                )
                y_s[at_rows, at] = y
                gated = y * silu(z_r[:, at])
                squares += gated * gated
                crosses += dn_r[:, at] * gain[:, at] * gated
            first = ones_where((8, LANES), lambda r, c: r == 0).astype(F32)
            second = ones_where((8, LANES), lambda r, c: r == 1).astype(F32)
            sums[:, at_rows] = dot(first, squares, NT, HIGH) + dot(second, crosses, NT, HIGH)

        @pl.when(i == count)
        def _():
            pl.semaphore_wait(barrier, head_size - 1)
            for d in range(1, head_size):
                share_sums(d).start()
            state[...] = jnp.zeros_like(state)
            behind[...] = jnp.ones_like(behind)
            ggain_o[...] = jnp.zeros_like(ggain_o)
            for d in range(1, head_size):
                share_sums(d).wait()
            total = sums[...]
            for d in range(1, head_size):
                total = total + others[d - 1]
            others[0] = total

        @pl.when(i >= count)
        def _():
            at_rows = pl.ds(pl.multiple_of((2 * count - 1 - i) * length, length), length)
            both_sums = others[0, :, at_rows]
            first = ones_where((8, LANES), lambda r, c: r == 0).astype(F32)
            second = ones_where((8, LANES), lambda r, c: r == 1).astype(F32)
            grstd = lax.rsqrt(dot(both_sums, first, TN, HIGH) * (1.0 / inner) + EPSILON)
            cross = (grstd * grstd * grstd) * (dot(both_sums, second, TN, HIGH) * (1.0 / inner))
            growth = jnp.exp(cum_r[...])
            for j in range(channels // LANES):
                at = slice(j * LANES, (j + 1) * LANES)
                y, z, dn = y_s[at_rows, at], z_r[:, at], dn_r[:, at]
                sigma = sigmoid(z)
                act = z * sigma
                gated = y * act
                scaled = gated * grstd
                normed_o[:, at] = (scaled * gain[:, at]).astype(BF16)
                ggain_o[:, at] += jnp.sum(dn * scaled, axis=0, keepdims=True)
                dgated = grstd * (dn * gain[:, at]) - gated * cross
                dy = (dgated * act).astype(BF16)
                dy_o[:, at] = dy
                dz_o[:, at] = (dgated * y * (sigma * (1.0 + z * (1.0 - sigma)))).astype(BF16)
                plain = dy.astype(F32)
                dv_o[:, at] = (plain * pair_spread(growth, j, length)).astype(BF16)
                prod_a[:, at] = plain * y
                prod_b[:, at] = plain * xs_r[:, at].astype(F32)
            picker = head_picker(channels, heads)
            ab_o[:, :heads] = dot_split(prod_a[...], picker)
            ab_o[:, heads:] = dot_split(prod_b[...], picker)
            part_o[...] = dot(normed_o[...], wo[...]).astype(BF16)
            dhin = dot(dv_o[...], bcs_r[:, states:], TN)
            ds_o[0] = state[...]
            post_o[0] = behind[...]
            behind[...] = behind[...] * dec_r[0]
            for h in range(heads):
                at = slice(h * wide, (h + 1) * wide)
                state[at] = dec_r[0, h : h + 1] * state[at] + dhin[at]
            start_o[...] = state[...].astype(BF16)

    last = count - 1
    ways = {
        "both": lambda i: jnp.where(i < count, i, 2 * count - 1 - i),
        "up": lambda i: jnp.minimum(i, last),
        "down": lambda i: jnp.minimum(2 * count - 1 - i, last),
    }
    whole = lambda *dims: pl.BlockSpec(dims, lambda i: (0,) * len(dims))
    tokens = lambda n, way: pl.BlockSpec((length, n), lambda i: (ways[way](i), 0))
    per = lambda way, *dims: pl.BlockSpec((1,) + dims, lambda i: (ways[way](i), 0, 0))
    args = (xdt, xs, bcs, gate_pre, normed_grad, cum, cumt, hin0, pre, dec, carry, skip_row, gate_gain,
            output_matrix)
    return pl.pallas_call(
        kernel,
        grid=(2 * count,),
        in_specs=[
            tokens(channels, "up"), tokens(channels, "both"), tokens(both, "both"),
            tokens(channels, "both"), tokens(channels, "both"), tokens(heads, "both"),
            pl.BlockSpec((heads, length), lambda i: (0, ways["up"](i))), per("up", channels, states),
            per("up", heads, LANES), per("down", heads, LANES), whole(channels, states),
            whole(1, channels), whole(1, channels), whole(channels, width),
        ],
        out_specs=[
            per("up", channels, states), tokens(channels, "down"), tokens(width, "down"),
            tokens(channels, "down"), tokens(channels, "down"), tokens(channels, "down"),
            tokens(2 * heads, "down"), per("down", channels, states), per("down", heads, LANES),
            whole(channels, states), whole(1, channels),
        ],
        out_shape=[
            shape((count, channels, states), BF16), shape((rows, channels), BF16),
            shape((rows, width), BF16), shape((rows, channels), BF16),
            shape((rows, channels), BF16), shape((rows, channels), BF16), shape((rows, 2 * heads), F32),
            shape((count, channels, states), F32), shape((count, heads, LANES), F32),
            shape((channels, states), BF16), shape((1, channels), F32),
        ],
        scratch_shapes=[
            pltpu.VMEM((rows, channels), F32), pltpu.VMEM((8, rows), F32),
            pltpu.VMEM((head_size - 1, 8, rows), F32), pltpu.VMEM((channels, states), F32),
            pltpu.VMEM((heads, LANES), F32), pltpu.VMEM((length, channels), F32),
            pltpu.VMEM((length, channels), F32),
            pltpu.SemaphoreType.DMA((head_size - 1,)), pltpu.SemaphoreType.DMA((head_size - 1,)),
        ],
        compiler_params=pltpu.CompilerParams(
            dimension_semantics=("arbitrary",), collective_id=3, has_side_effects=True,
            vmem_limit_bytes=VMEM_BYTES,
        ),
        cost_estimate=pl.CostEstimate(
            flops=2 * rows * channels * (width + 6 * length), bytes_accessed=60_000_000,
            transcendentals=rows * (length * heads + 2 * channels),
        ),
        name="blocks_and_gate",
    )(*args)


def opening(tokens, cotangent, norm_gain, gate_matrix, value_matrix, state_matrix, step_matrix,
            output_matrix, value_kernel, value_bias, state_kernel, state_bias, step_bias, log_rate,
            seq_size, head_size):
    members, length, share = tokens.shape
    rows = members * length
    width, channels = gate_matrix.shape
    both = state_matrix.shape[1]
    heads = step_matrix.shape[0]
    half_heads = head_size // 2
    states = both // 2
    wide = channels // heads
    taps = value_kernel.shape[0]
    groups = seq_size // members
    margin = EDGE - taps + 1

    def kernel(tokens_h, cot_h, gain, gate_h, value_h, state_h, step_m, out_h, vk, vb, sk, sb, tb, lr,
               xn_o, cot_o, mine_o, z_o, xr_o, bc_o, dn_o, xs_o, xdt_o, xw_o, hin_o,
               rstd_o, dtr_o, bcs_o, dt_o, cum_o, cumt_o, pre_o, dec_o, xedge_o, bedge_o, carry_o,
               whole, xn, z, xr, bc, dn, gate, value, state_m, out_m,
               padded, padded_bc, xs, xdt, xw, hin, state, ahead, leaving,
               gs_sem, gr_sem, ys_sem, yr_sem, cs_sem, cr_sem, w_sem, o_sem, l_sem, e_sem):
        seq, head = lax.axis_index("seq"), lax.axis_index("head")
        lane, core = head // 2, lax.rem(head, 2)
        group, member = seq // members, lax.rem(seq, members)
        base = seq - member
        sources = (tokens_h, cot_h)

        def rows_of(j):
            return pl.ds(pl.multiple_of(j * length, length), length)

        def lanes_of(h):
            return pl.ds(pl.multiple_of(h * share, share), share)

        own = [
            pltpu.make_async_copy(
                sources[a].at[member], whole.at[a, rows_of(member), lanes_of(head)], l_sem.at[a]
            )
            for a in range(2)
        ]
        loads = [
            pltpu.make_async_copy(src, dst, w_sem.at[i])
            for i, (src, dst) in enumerate(
                ((gate_h, gate), (value_h, value), (state_h, state_m), (out_h, out_m))
            )
        ]
        own[0].start()
        own[1].start()
        for load in loads:
            load.start()
        greet(seq, head, seq_size, head_size)

        order = [0, *range(members - 1, 0, -1)]

        def place(t):
            return lax.rem(member + t, members)

        def to_group(a, t):
            return remote(sources[a].at[place(t)], whole.at[a, rows_of(member), lanes_of(head)],
                          gs_sem.at[a, t - 1], gr_sem.at[a, members - 1 - t], base + place(t), head)

        def from_group(a, t):
            return remote(sources[a].at[place(t)], whole.at[a, rows_of(place(t)), lanes_of(head)],
                          gs_sem.at[a, t - 1], gr_sem.at[a, t - 1], seq, head)

        def to_lane(a, t, k):
            at = whole.at[a, rows_of(place(t)), lanes_of(head)]
            return remote(at, at, ys_sem.at[a, t, k], yr_sem.at[a, t, k],
                          seq, 2 * lax.rem(lane + 1 + k, half_heads) + core)

        def lane_from(k):
            return lax.rem(lane + half_heads - 1 - k, half_heads)

        def from_lane(a, t, k):
            at = whole.at[a, rows_of(place(t)), lanes_of(2 * lane_from(k) + core)]
            return remote(at, at, ys_sem.at[a, t, k], yr_sem.at[a, t, k], seq, head)

        def to_core(a, t, k):
            at = whole.at[a, rows_of(place(t)), lanes_of(2 * lane_from(k) + core)]
            return remote(at, at, cs_sem.at[a, t, k], cr_sem.at[a, t, k], seq, 2 * lane + 1 - core)

        def from_core(a, t, k):
            at = whole.at[a, rows_of(place(t)), lanes_of(2 * lane_from(k) + 1 - core)]
            return remote(at, at, cs_sem.at[a, t, k], cr_sem.at[a, t, k], seq, head)

        def forward(a, t):
            for k in range(half_heads - 1):
                to_lane(a, t, k).start()
            to_core(a, t, half_heads - 1).start()

        def collect(a, t):
            for k in range(half_heads - 1):
                from_lane(a, t, k).wait_recv()
                to_core(a, t, k).start()
            for k in range(half_heads):
                from_core(a, t, k).wait_recv()

        def outputs(t):
            at = rows_of(place(t))
            pairs = ((xn, xn_o), (z, z_o), (xr, xr_o), (bc, bc_o))
            return [
                pltpu.make_async_copy(src.at[at], dst.at[at], o_sem.at[i, t])
                for i, (src, dst) in enumerate(pairs)
            ]

        def late_outputs(t):
            at = rows_of(place(t))
            return [
                pltpu.make_async_copy(dn.at[at], dn_o.at[at], o_sem.at[4, t]),
                pltpu.make_async_copy(whole.at[1, at], cot_o.at[at], o_sem.at[5, t]),
                pltpu.make_async_copy(whole.at[0, at, lanes_of(head)], mine_o.at[at], o_sem.at[6, t]),
            ]

        def project(t):
            at = rows_of(place(t))
            squares = jnp.zeros((length, LANES), F32)
            for q in range(width // LANES):
                part = whole[0, at, q * LANES : (q + 1) * LANES].astype(F32)
                squares += part * part
            mean = jnp.sum(squares, axis=1, keepdims=True) * (1.0 / width)
            rstd = lax.rsqrt(mean + EPSILON)
            rstd_o[at] = rstd
            wide = jnp.broadcast_to(rstd, (length, LANES))
            for q in range(width // LANES):
                cols = slice(q * LANES, (q + 1) * LANES)
                xn[at, cols] = (whole[0, at, cols].astype(F32) * wide * gain[:, cols]).astype(BF16)
            normal = xn[at]
            if t == 0:
                for load in loads[:3]:
                    load.wait()
            xr[at] = dot(normal, value[...])
            z[at] = dot(normal, gate[...])
            bc[at] = dot(normal, state_m[...])
            dtr_o[at] = dot(normal, step_m[...], NT)
            for copy in outputs(t):
                copy.start()

        def edges(there):
            tail = pl.ds(rows - EDGE, EDGE)
            return [
                remote(xr.at[tail], xedge_o, e_sem.at[0], e_sem.at[1], there, head),
                remote(bc.at[tail], bedge_o, e_sem.at[2], e_sem.at[3], there, head),
            ]

        def pass_on(there):
            return remote(leaving, carry_o, e_sem.at[4], e_sem.at[5], there, head)

        def block_outputs(i):
            at = rows_of(i)
            pairs = ((xs, xs_o), (xdt, xdt_o), (xw, xw_o))
            return [
                pltpu.make_async_copy(src.at[at], dst.at[at], o_sem.at[7 + n, i])
                for n, (src, dst) in enumerate(pairs)
            ] + [pltpu.make_async_copy(hin.at[i], hin_o.at[i], o_sem.at[10, i])]

        def prepare(i):
            at = slice(i * length, (i + 1) * length)
            if i == 0:
                padded[0:EDGE] = xedge_o[...]
                padded_bc[0:EDGE] = bedge_o[...]
                state[...] = jnp.zeros_like(state)
                ahead[...] = jnp.ones_like(ahead)
            else:
                padded[0:EDGE] = xr[i * length - EDGE : i * length]
                padded_bc[0:EDGE] = bc[i * length - EDGE : i * length]
            padded[EDGE:] = xr[at]
            padded_bc[EDGE:] = bc[at]
            summed = sb[...] + sk[0:1] * padded_bc[pl.ds(margin, length)]
            for k in range(1, taps):
                summed = summed + sk[k : k + 1] * padded_bc[pl.ds(margin + k, length)]
            basis = silu(summed).astype(BF16)
            bcs_o[at] = basis
            dt = softplus(dtr_o[at] + tb[...])
            da = dt * -jnp.exp(lr[...])
            lower = ones_where((length, length), lambda r, c: r >= c).astype(F32)
            upper = ones_where((length, length), lambda r, c: r <= c).astype(F32)
            cum = dot(lower, da, precision=HIGH)
            cumt = dot(da, upper, TN, precision=HIGH)
            dt_o[at] = dt
            cum_o[at] = cum
            cumt_o[:, at] = cumt
            factor = jnp.exp(cum[length - 1 : length] - cum) * dt
            decay = jnp.exp(jnp.broadcast_to(cumt[:, length - 1 : length], (heads, LANES)))
            dec_o[i] = decay
            pre_o[i] = ahead[...]
            ahead[...] = ahead[...] * decay
            hin[i] = state[...]
            for j in range(channels // LANES):
                cols = slice(j * LANES, (j + 1) * LANES)
                total = vb[:, cols] + vk[0:1, cols] * padded[pl.ds(margin, length), cols]
                for k in range(1, taps):
                    total = total + vk[k : k + 1, cols] * padded[pl.ds(margin + k, length), cols]
                value_low = silu(total).astype(BF16)
                xs[at, cols] = value_low
                plain = value_low.astype(F32)
                xdt[at, cols] = (plain * pair_spread(dt, j, length)).astype(BF16)
                xw[at, cols] = (plain * pair_spread(factor, j, length)).astype(BF16)
            local = dot(xw[at], basis[:, :states], TN)
            for h in range(heads):
                span = slice(h * wide, (h + 1) * wide)
                state[span] = decay[h : h + 1] * state[span] + local[span]
            for copy in block_outputs(i):
                copy.start()

        for t in range(1, members):
            to_group(0, t).start()
        own[0].wait()
        forward(0, 0)
        for t in order[1:]:
            from_group(0, t).wait_recv()
            forward(0, t)
        for t in range(1, members):
            to_group(1, t).start()
        own[1].wait()
        forward(1, 0)
        for n, t in enumerate(order):
            collect(0, t)
            project(t)
            if n < members - 1:
                from_group(1, order[n + 1]).wait_recv()
                forward(1, order[n + 1])
        @pl.when(group < groups - 1)
        def _():
            for copy in edges(seq + members):
                copy.start()

        @pl.when(group == 0)
        def _():
            xedge_o[...] = jnp.zeros_like(xedge_o)
            bedge_o[...] = jnp.zeros_like(bedge_o)
            carry_o[...] = jnp.zeros_like(carry_o)

        def gradient(t):
            collect(1, t)
            at = rows_of(place(t))
            dn[at] = dot(whole[1, at], out_m[...], NT)
            for copy in late_outputs(t):
                copy.start()

        loads[3].wait()
        gradient(0)

        @pl.when(group > 0)
        def _():
            for copy in edges(seq):
                copy.wait_recv()

        for i in range(members):
            prepare(i)
        leaving[...] = state[...].astype(BF16)

        @pl.when(group == 0)
        def _():
            pass_on(seq + members).start()

        for t in order[1:]:
            gradient(t)

        @pl.when(group > 0)
        def _():
            pass_on(seq).wait_recv()

            @pl.when(group < groups - 1)
            def _():
                for h in range(heads):
                    span = slice(h * wide, (h + 1) * wide)
                    leaving[span] = (
                        state[span] + ahead[h : h + 1] * carry_o[span].astype(F32)
                    ).astype(BF16)
                pass_on(seq + members).start()

        @pl.when(group < groups - 1)
        def _():
            for copy in edges(seq + members):
                copy.wait_send()
            pass_on(seq + members).wait_send()

        for t in range(members):
            for copy in outputs(t) + late_outputs(t) + block_outputs(t):
                copy.wait()
        for a in range(2):
            for t in range(1, members):
                to_group(a, t).wait_send()
            for t in range(members):
                for k in range(half_heads):
                    to_core(a, t, k).wait_send()
                    if k < half_heads - 1:
                        to_lane(a, t, k).wait_send()

    vmem = pl.BlockSpec(memory_space=pltpu.VMEM)
    anywhere = pl.BlockSpec(memory_space=pl.ANY)
    dma = pltpu.SemaphoreType.DMA
    args = (tokens, cotangent, norm_gain, gate_matrix, value_matrix, state_matrix, step_matrix,
            output_matrix, value_kernel, value_bias, state_kernel, state_bias, step_bias, log_rate)
    far = {0, 1, 3, 4, 5, 7}
    return pl.pallas_call(
        kernel,
        in_specs=[anywhere if i in far else vmem for i in range(len(args))],
        out_specs=[anywhere] * 11 + [vmem] * 11,
        out_shape=[
            shape((rows, width), BF16), shape((rows, width), BF16), shape((rows, share), BF16),
            shape((rows, channels), F32), shape((rows, channels), F32), shape((rows, both), F32),
            shape((rows, channels), F32), shape((rows, channels), BF16), shape((rows, channels), BF16),
            shape((rows, channels), BF16), shape((members, channels, states), F32),
            shape((rows, 1), F32), shape((rows, heads), F32), shape((rows, both), BF16),
            shape((rows, heads), F32), shape((rows, heads), F32), shape((heads, rows), F32),
            shape((members, heads, LANES), F32), shape((members, heads, LANES), F32),
            shape((EDGE, channels), F32), shape((EDGE, both), F32), shape((channels, states), BF16),
        ],
        scratch_shapes=[
            pltpu.VMEM((2, rows, width), BF16), pltpu.VMEM((rows, width), BF16),
            pltpu.VMEM((rows, channels), F32), pltpu.VMEM((rows, channels), F32),
            pltpu.VMEM((rows, both), F32), pltpu.VMEM((rows, channels), F32),
            pltpu.VMEM((width, channels), BF16), pltpu.VMEM((width, channels), BF16),
            pltpu.VMEM((width, both), BF16), pltpu.VMEM((channels, width), BF16),
            pltpu.VMEM((length + EDGE, channels), F32), pltpu.VMEM((length + EDGE, both), F32),
            pltpu.VMEM((rows, channels), BF16), pltpu.VMEM((rows, channels), BF16),
            pltpu.VMEM((rows, channels), BF16), pltpu.VMEM((members, channels, states), F32),
            pltpu.VMEM((channels, states), F32), pltpu.VMEM((heads, LANES), F32),
            pltpu.VMEM((channels, states), BF16),
            dma((2, members - 1)), dma((2, members - 1)),
            dma((2, members, max(half_heads - 1, 1))), dma((2, members, max(half_heads - 1, 1))),
            dma((2, members, half_heads)), dma((2, members, half_heads)),
            dma((4,)), dma((11, members)), dma((2,)), dma((6,)),
        ],
        compiler_params=pltpu.CompilerParams(
            collective_id=2, has_side_effects=True, vmem_limit_bytes=VMEM_BYTES
        ),
        cost_estimate=pl.CostEstimate(
            flops=2 * rows * width * (3 * channels + both), bytes_accessed=60_000_000, transcendentals=0
        ),
        name="opening_products",
    )(*args)

def closing(normal_in, dz, dxr, tail, head_rows, gate_matrix, value_matrix, state_matrix, step_matrix,
            value_kernel, state_kernel, state_bias, state_pre, state_edge, dbc, ddtr, vectors, small,
            branch, mine, rstd, gain_share, gate_half, output_half, length, seq_size, head_size):
    rows, width = normal_in.shape
    channels = dz.shape[1]
    heads = ddtr.shape[1]
    both = dbc.shape[1]
    share = mine.shape[1]
    taps = value_kernel.shape[0]
    members = rows // length
    outer = seq_size // 2
    half_heads = head_size // 2
    strip = width // seq_size
    chunk = rows // head_size
    per = head_size // members
    packed = channels + both + LANES + share
    low_rows = share + heads * width // both
    steps = seq_size.bit_length() - 1
    groups = seq_size // members

    def kernel(xn, dz_r, dxr_h, tail_r, head_r, gate_h, value_h, state_m, step_m, vk, sk, sb, bc_h,
               bc_edge, dbc_h, ddtr_r, vec, small_r, branch_h, mine_r, rstd_r, gain, gate_half_h,
               out_half_h,
               gate_o, value_o, out_o, state_o, step_o, vkern_o, vbias_o, ggain_o, skern_o, sbias_o, norm_o,
               tbias_o, rate_o, skip_o, up_o, branch_o,
               dxr_r, duo, xrecv, zrecv, gbuf, grecv, obuf, orecv, oxrecv, bpart, weights, weight, csend, cown, crecv, yrecv, rsend,
               rrecv, up, norms, nrecv, nlast, blow,
               drecv, dsum, ext, hrecv, hbrecv, low,
               full_sum, full_send, full_recv, low_sum, low_send, low_recv,
               xs_sem, xr_sem, zs_sem, zr_sem, cs_sem, cr_sem, ys_sem, yr_sem, rs_sem, rr_sem,
               us_sem, ur_sem, ns_sem, nr_sem, ds_sem, dr_sem,
               as_sem, ar_sem, h_sem, hb_sem, fs_sem, fr_sem, ls_sem, lr_sem, nl_sem, bs_sem, br_sem, gs_sem, gr_sem, os_sem, or_sem, ox_sem, half_sem, w_sem, copy_sem):
        seq, head = lax.axis_index("seq"), lax.axis_index("head")
        place, side = seq // 2, lax.rem(seq, 2)
        lane, core = head // 2, lax.rem(head, 2)
        group, member = seq // members, lax.rem(seq, members)
        base = seq - member
        load_dxr = pltpu.make_async_copy(dxr_h, dxr_r, copy_sem.at[0])
        load_dxr.start()
        load_bc = pltpu.make_async_copy(bc_h, low.at[pl.ds(EDGE, rows)], copy_sem.at[1])
        load_bc.start()
        low[0:EDGE] = bc_edge[...]

        def crossed(index, other, size):
            result, bit = 0, 1
            while bit < size:
                result = result + bit * lax.rem(index // bit + other // bit, 2)
                bit *= 2
            return result

        def outer_at(k):
            return crossed(place, outer - 1 - k, outer)

        def lane_at(k):
            return lax.rem(lane + 1 + k, half_heads)

        def seq_at(d):
            return lax.rem(seq + d, seq_size)

        def head_at(d):
            return lax.rem(head + d, head_size)

        own_rows = pl.ds(pl.multiple_of(head * chunk, chunk), chunk)
        load_dbc = pltpu.make_async_copy(
            dbc_h.at[own_rows], dsum.at[own_rows], copy_sem.at[2]
        )
        load_dbc.start()
        keep_branch = pltpu.make_async_copy(
            branch_h.at[member], branch_o.at[member], copy_sem.at[3]
        )
        keep_branch.start()
        gate_loads = [
            pltpu.make_async_copy(gate_half_h.at[crossed(place, c, outer)], gbuf.at[c], half_sem.at[c])
            for c in range(outer)
        ]
        out_loads = [
            pltpu.make_async_copy(
                out_half_h.at[crossed(place // 2, c, outer // 2)], obuf.at[c], half_sem.at[outer + c]
            )
            for c in range(outer // 2)
        ]
        for load in reversed(out_loads + gate_loads):
            load.start()
        greet(seq, head, seq_size, head_size)

        def cross(k):
            return remote(duo.at[k, 1 - side], xrecv.at[k], xs_sem.at[k], xr_sem.at[k],
                          2 * place + 1 - side, head)

        def zeros_of(c, size):
            count = 0
            while c % 2 == 0 and 1 << count < size:
                c, count = c // 2, count + 1
            return count

        def pass_along(held, landed, send, recv, c, span, size):
            bit = 1 << zeros_of(c, size)
            far = crossed(place, span * bit, outer)
            return remote(held, landed.at[c - 1], send.at[c - 1], recv.at[c - 1], 2 * far + side, head)

        def along(c):
            return pass_along(duo.at[outer - 1 - c, side], zrecv, zs_sem, zr_sem, c, 1, outer)

        def along_gate(c):
            return pass_along(gbuf.at[c], grecv, gs_sem, gr_sem, c, 1, outer)

        def along_out(c):
            return pass_along(obuf.at[c, side], orecv, os_sem, or_sem, c, 2, outer // 2)

        def gather_in(copy, landed, c, size):
            total = 0.0
            for b in range(zeros_of(c, size)):
                copy(c + (1 << b)).wait_recv()
                total = total + landed[c + (1 << b) - 1].astype(F32)
            return total

        def gate_step(c):
            gate_loads[c].wait()
            if zeros_of(c, outer):
                gbuf[c] = (gbuf[c].astype(F32) + gather_in(along_gate, grecv, c, outer)).astype(BF16)
            along_gate(c).start()

        def cross_out(c):
            return remote(obuf.at[c, 1 - side], oxrecv.at[c], ox_sem.at[0, c], ox_sem.at[1, c],
                          2 * place + 1 - side, head)

        def out_step(c):
            cross_out(c).wait_recv()
            total = obuf[c, side].astype(F32) + oxrecv[c].astype(F32)
            if c:
                total = total + gather_in(along_out, orecv, c, outer // 2)
            obuf[c, side] = total.astype(BF16)
            if c:
                along_out(c).start()

        def branch_give(r):
            return remote(branch_h.at[r], branch_o.at[member], bs_sem.at[r], br_sem.at[member],
                          base + r, head)

        def edge_back(src, dst, sems):
            return remote(src, dst, sems.at[0], sems.at[1], seq - members, head)

        def rows_of(c):
            return pl.ds(pl.multiple_of(c * chunk, chunk), chunk)

        def basis_sum(d):
            return remote(dbc_h.at[rows_of(head_at(d))], drecv.at[d - 1], ds_sem.at[d - 1],
                          dr_sem.at[d - 1], seq, head_at(d))

        def basis_share(d):
            at = rows_of(head)
            return remote(dsum.at[at], dsum.at[at], as_sem.at[d - 1], ar_sem.at[d - 1], seq, head_at(d))

        @pl.when(group > 0)
        def _():
            edge_back(head_r, hrecv, h_sem).start()

        for d in range(1, head_size):
            basis_sum(d).start()
        for c in range(outer // 2 - 1, -1, -1):
            out_loads[c].wait()
            cross_out(c).start()
        for c in range(outer - 1, 0, -1):
            if c % 2:
                gate_step(c)

        load_dxr.wait()
        ext[...] = jnp.zeros_like(ext)

        @pl.when(group < groups - 1)
        def _():
            remote(head_r, hrecv, h_sem.at[0], h_sem.at[1], seq, head).wait_recv()
            ext[EDGE:] = hrecv[...]

        fixed = tail_r[...]
        for k in range(taps):
            fixed = fixed + vk[k : k + 1] * ext[pl.ds(taps - 1 - k, EDGE)]
        last = dxr_r[rows - 2 * EDGE :].astype(F32)
        dxr_r[rows - 2 * EDGE :] = jnp.concatenate([last[:EDGE], fixed], axis=0).astype(BF16)

        def multiply(k, _):
            at = pl.ds(pl.multiple_of(outer_at(k) * 2 * strip, 2 * strip), 2 * strip)
            product = dot(xn[:, at], dxr_r[...], TN).astype(BF16)
            duo[k, 0] = product[:strip]
            duo[k, 1] = product[strip:]

            @pl.when(k < outer // 2)
            def _():
                cross(k).start()

            return 0

        lax.fori_loop(0, outer, multiply, 0)
        for r in range(members):
            @pl.when(r != member)
            def _(r=r):
                branch_give(r).start()


        step_part = dot(ddtr_r[...], xn[...], TN)
        for q in range(width // both):
            low_sum[share + q * heads : share + (q + 1) * heads] = step_part[
                :, q * both : (q + 1) * both
            ]

        load_dbc.wait()
        total = dsum[own_rows]
        for d in range(1, head_size):
            basis_sum(d).wait_recv()
            total = total + drecv[d - 1]
        dsum[own_rows] = total
        for d in range(1, head_size):
            basis_share(d).start()

        def arrived(k):
            c = outer - 1 - k
            cross(k).wait_recv()
            total = duo[k, side].astype(F32) + xrecv[k].astype(F32)
            if c:
                total = total + gather_in(along, zrecv, c, outer)
            duo[k, side] = total.astype(BF16)
            if c:
                along(c).start()

        def arrived_loop(first, last):
            for k in range(first, last):
                arrived(k)

        def to_core(k):
            return remote(csend.at[k], crecv.at[k], cs_sem.at[k], cr_sem.at[k], seq, 2 * lane + 1 - core)

        def to_lane(k):
            return remote(cown.at[k], yrecv.at[k], ys_sem.at[k], yr_sem.at[k],
                          seq, 2 * lane_at(k) + core)

        def columns_of(step):
            which = 1 - core if step < half_heads else core
            at = (2 * lane_at(step % half_heads) + which) * share
            return pl.ds(pl.multiple_of(at, share), share)

        def fetch(step):
            at, slot = columns_of(step), step % 2
            return [
                pltpu.make_async_copy(gate_h.at[at], weights.at[slot, 0], w_sem.at[slot, 0]),
                pltpu.make_async_copy(value_h.at[at], weights.at[slot, 1], w_sem.at[slot, 1]),
            ]

        norms[...] = jnp.zeros_like(norms)
        for step in range(head_size):
            slot, at, k = step % 2, columns_of(step), step % half_heads
            keep = csend if step < half_heads else cown
            if step == 0:
                for load in fetch(0):
                    load.start()
            if step < head_size - 1:
                for load in fetch(step + 1):
                    load.start()
            for load in fetch(step):
                load.wait()

            def back_rows(c, _, slot=slot, at=at, k=k, keep=keep, first=step == 0, step=step):
                at_rows = rows_of(c)
                grad = (
                    dot(dz_r[at_rows], weights[slot, 0], NT) + dot(dxr_r[at_rows], weights[slot, 1], NT)
                    + dot(ddtr_r[at_rows], step_m[:, at])
                )
                keep[k, at_rows] = grad.astype(BF16)
                weighed = grad * xn[at_rows, at].astype(F32)
                total = weighed[:, :LANES] if first else weight[at_rows] + weighed[:, :LANES]
                for q in range(1, share // LANES):
                    total += weighed[:, q * LANES : (q + 1) * LANES]
                weight[at_rows] = total
                norms[step] += jnp.broadcast_to(jnp.sum(weighed, axis=0, keepdims=True), (8, share))
                return 0

            lax.fori_loop(0, head_size, back_rows, 0)
            if step < half_heads:
                to_core(k).start()
            else:
                to_core(k).wait_recv()

                def add_rows(c, _, k=k):
                    at_rows = rows_of(c)
                    cown[k, at_rows] = (
                        cown[k, at_rows].astype(F32) + crecv[k, at_rows].astype(F32)
                    ).astype(BF16)
                    return 0

                lax.fori_loop(0, head_size, add_rows, 0)
                if k < half_heads - 1:
                    to_lane(k).start()
            if step == 0:
                for c in range(outer - 1, 0, -1):
                    if c % 2 == 0:
                        gate_step(c)
            if step == head_size - 2:
                for c in range(outer // 2 - 1, 0, -1):
                    out_step(c)

        for d in range(1, head_size):
            at = rows_of(head_at(d))
            remote(dsum.at[at], dsum.at[at], as_sem.at[d - 1], ar_sem.at[head_size - 1 - d],
                   seq, head).wait_recv()

        start = EDGE - taps + 1
        load_bc.wait()
        pre_bc = sb[...]
        for k in range(taps):
            pre_bc = pre_bc + sk[k : k + 1] * low[pl.ds(start + k, rows)]
        dpre = dsum[...] * slope(pre_bc)
        full_sum[...] = jnp.zeros_like(full_sum)
        full_sum[:, :channels] = vec[...]
        full_sum[:, channels + both : channels + both + heads] = small_r[...]
        for k in range(taps):
            full_sum[k : k + 1, channels : channels + both] = jnp.sum(
                dpre * low[pl.ds(start + k, rows)], axis=0, keepdims=True
            )
        full_sum[taps : taps + 1, channels : channels + both] = jnp.sum(dpre, axis=0, keepdims=True)
        low[0:rows] = dpre
        low[rows:] = jnp.zeros((EDGE, both), F32)

        @pl.when(group > 0)
        def _():
            edge_back(low.at[pl.ds(0, EDGE)], hbrecv, hb_sem).start()

        arrived_loop(0, outer // 4)

        @pl.when(group < groups - 1)
        def _():
            remote(low.at[pl.ds(0, EDGE)], hbrecv, hb_sem.at[0], hb_sem.at[1], seq, head).wait_recv()
            low[rows:] = hbrecv[...]

        dbc_v = sk[0:1] * low[pl.ds(taps - 1, rows)]
        for k in range(1, taps):
            dbc_v = dbc_v + sk[k : k + 1] * low[pl.ds(taps - 1 - k, rows)]
        dbc_low = dbc_v.astype(BF16)
        own_at = pl.ds(pl.multiple_of(head * share, share), share)
        low_sum[:share] = dot(xn[:, own_at], dbc_low, TN)
        blow[...] = dbc_low

        def doubling(b):
            distance = 1 << b
            partner = seq + distance - 2 * distance * lax.rem(seq // distance, 2)
            return [
                remote(full_send.at[b], full_recv.at[b], fs_sem.at[b], fr_sem.at[b], partner, head),
                remote(low_send.at[b], low_recv.at[b], ls_sem.at[b], lr_sem.at[b], partner, head),
            ]

        def double(b):
            full_send[b] = full_sum[...]
            low_send[b] = low_sum[...].astype(BF16)
            for copy in doubling(b):
                copy.start()

        def doubled(b):
            for copy in doubling(b):
                copy.wait_recv()
            full_sum[...] = full_sum[...] + full_recv[b]
            low_sum[...] = low_send[b].astype(F32) + low_recv[b].astype(F32)

        double(0)

        def send_rest(k, _):
            cross(k).start()
            return 0

        lax.fori_loop(outer // 2, outer, send_rest, 0)

        def basis_rows(c, _):
            at_rows = rows_of(c)
            grad = dot(blow[at_rows], state_m[own_at], NT)
            bpart[at_rows] = grad.astype(BF16)
            weighed = grad * xn[at_rows, own_at].astype(F32)
            total = weight[at_rows]
            for q in range(share // LANES):
                total += weighed[:, q * LANES : (q + 1) * LANES]
            weight[at_rows] = total
            norms[head_size - 1] += jnp.broadcast_to(
                jnp.sum(weighed, axis=0, keepdims=True), (8, share)
            )
            return 0

        lax.fori_loop(0, head_size, basis_rows, 0)
        rsend[...] = dot(jnp.ones((8, LANES), F32), weight[...], NT, precision=HIGH)

        def row_sums(d):
            return remote(rsend, rrecv.at[d - 1], rs_sem.at[d - 1], rr_sem.at[d - 1], seq, head_at(d))

        for d in range(1, head_size):
            row_sums(d).start()

        def share_norm(step):
            which = 1 - core if step < half_heads else core
            return remote(norms.at[step], nrecv.at[step], ns_sem.at[step], nr_sem.at[step],
                          seq, 2 * lane_at(step % half_heads) + which)

        for step in range(head_size - 1):
            share_norm(step).start()

        arrived_loop(outer // 4, outer // 2)

        def give(r):
            return remote(up.at[r], up_o.at[member], us_sem.at[r], ur_sem.at[member], base + r, head)

        for d in range(1, head_size):
            row_sums(d).wait_recv()
        sums = rsend[...]
        for d in range(1, head_size):
            sums = sums + rrecv[d - 1]
        pick = (lax.broadcasted_iota(jnp.int32, (8, LANES), 0) == 0).astype(F32)
        rrecv[0] = sums * (1.0 / width)
        for k in range(half_heads - 1):
            to_lane(k).wait_recv()

        def finish_rows(c, _):
            at_rows = rows_of(c)
            grad = cown[half_heads - 1, at_rows].astype(F32) + bpart[at_rows].astype(F32)
            for k in range(half_heads - 1):
                grad = grad + yrecv[k, at_rows].astype(F32)
            scale = rstd_r[at_rows]
            hat = mine_r[at_rows].astype(F32) * scale
            mean = dot(rrecv[0, :, at_rows], pick, TN, precision=HIGH)
            inside = pl.ds(pl.multiple_of(lax.rem(c, per) * chunk, chunk), chunk)
            for q in range(share // LANES):
                at = slice(q * LANES, (q + 1) * LANES)
                up[c // per, inside, at] = (
                    scale * (grad[:, at] * gain[:, at] - hat[:, at] * mean)
                ).astype(BF16)
            return 0

        lax.fori_loop(0, head_size, finish_rows, 0)
        for r in range(members):
            @pl.when(r != member)
            def _(r=r):
                give(r).start()

        keep_up = pltpu.make_async_copy(up.at[member], up_o.at[member], copy_sem.at[0])
        keep_up.start()

        norm = norms[head_size - 1]
        for step in range(head_size - 1):
            share_norm(step).wait_recv()
            norm = norm + nrecv[step]
        doubled(0)
        full_sum[:, packed - share :] = norm / gain[...]

        double(1)
        arrived_loop(outer // 2, outer - 1)
        for b in range(1, steps - 1):
            doubled(b)
            double(b + 1)
        arrived(outer - 1)
        out_step(0)
        gate_loads[0].wait()
        gate_o[...] = gbuf[0].astype(F32) + gather_in(along_gate, grecv, 0, outer)
        out_o[...] = obuf[0, side].astype(F32) + gather_in(along_out, orecv, 0, outer // 2)
        value_o[...] = duo[outer - 1, side].astype(F32) + gather_in(along, zrecv, 0, outer)
        doubled(steps - 1)
        for step in range(head_size - 1):
            share_norm(step).wait_send()
        norms[0] = full_sum[:, packed - share :]
        last_norm = remote(norms.at[0], nlast, nl_sem.at[0], nl_sem.at[1], 2 * place + 1 - side, head)
        last_norm.start()
        state_o[...] = low_sum[:share]
        step_o[...] = low_sum[share:]
        vkern_o[...] = full_sum[:taps, :channels]
        vbias_o[...] = full_sum[taps : taps + 1, :channels]
        ggain_o[...] = full_sum[taps + 1 : taps + 2, :channels]
        skern_o[...] = full_sum[:taps, channels : channels + both]
        sbias_o[...] = full_sum[taps : taps + 1, channels : channels + both]
        small_at = slice(channels + both, channels + both + heads)
        tbias_o[...] = full_sum[0:1, small_at]
        rate_o[...] = full_sum[1:2, small_at]
        skip_o[...] = full_sum[2:3, small_at]
        last_norm.wait()
        norm_o[...] = norms[0, 0:1] + nlast[0:1]

        for r in range(members):
            @pl.when(r != member)
            def _(r=r):
                remote(up.at[r], up_o.at[r], us_sem.at[r], ur_sem.at[r], base + r, head).wait()
                remote(branch_h.at[r], branch_o.at[r], bs_sem.at[r], br_sem.at[r], base + r, head).wait()

        keep_branch.wait()
        keep_up.wait()

        def drain(k, _):
            cross(k).wait_send()
            return 0

        lax.fori_loop(0, outer, drain, 0)
        for c in range(1, outer):
            along(c).wait_send()
            along_gate(c).wait_send()
        for c in range(1, outer // 2):
            along_out(c).wait_send()
        for c in range(outer // 2):
            cross_out(c).wait_send()
        for k in range(half_heads):
            to_core(k).wait_send()
            if k < half_heads - 1:
                to_lane(k).wait_send()

        @pl.when(group > 0)
        def _():
            edge_back(head_r, hrecv, h_sem).wait_send()
            edge_back(low.at[pl.ds(0, EDGE)], hbrecv, hb_sem).wait_send()

        for d in range(1, head_size):
            row_sums(d).wait_send()
            basis_sum(d).wait_send()
            basis_share(d).wait_send()
        for b in range(steps):
            for copy in doubling(b):
                copy.wait_send()

    vmem = pl.BlockSpec(memory_space=pltpu.VMEM)
    anywhere = pl.BlockSpec(memory_space=pl.ANY)
    dma = pltpu.SemaphoreType.DMA
    args = (normal_in, dz, dxr, tail, head_rows, gate_matrix, value_matrix, state_matrix, step_matrix,
            value_kernel, state_kernel, state_bias, state_pre, state_edge, dbc, ddtr, vectors, small,
            branch, mine, rstd, gain_share, gate_half, output_half)
    far = {2, 5, 6, 12, 14, 18, 22, 23}
    moves = lambda *dims: pltpu.VMEM(dims, BF16)
    plain = lambda *dims: pltpu.VMEM(dims, F32)
    return pl.pallas_call(
        kernel,
        in_specs=[anywhere if i in far else vmem for i in range(len(args))],
        out_specs=[vmem] * 14 + [anywhere, anywhere],
        out_shape=[
            shape((strip, channels), F32), shape((strip, channels), F32), shape((channels, strip), F32),
            shape((share, both), F32), shape((low_rows - share, both), F32),
            shape((taps, channels), F32), shape((1, channels), F32), shape((1, channels), F32),
            shape((taps, both), F32), shape((1, both), F32), shape((1, share), F32),
            shape((1, heads), F32), shape((1, heads), F32), shape((1, heads), F32),
            shape((members, length, share), BF16), shape((members, length, share), BF16),
        ],
        scratch_shapes=[
            moves(rows, channels), moves(outer, 2, strip, channels), moves(outer, strip, channels),
            moves(outer - 1, strip, channels), moves(outer, strip, channels),
            moves(outer - 1, strip, channels), moves(outer // 2, 2, channels, strip),
            moves(outer // 2 - 1, channels, strip), moves(outer // 2, channels, strip),
            moves(rows, share), moves(2, 2, share, channels), plain(rows, LANES),
            moves(half_heads, rows, share), moves(half_heads, rows, share),
            moves(half_heads, rows, share), moves(half_heads - 1, rows, share),
            plain(8, rows), plain(head_size - 1, 8, rows), moves(members, length, share),
            plain(head_size, 8, share), plain(head_size - 1, 8, share), plain(8, share),
            moves(rows, both),
            plain(head_size - 1, chunk, both), plain(rows, both), plain(2 * EDGE, channels),
            plain(EDGE, channels), plain(EDGE, both), plain(rows + EDGE, both),
            plain(8, packed), plain(steps, 8, packed), plain(steps, 8, packed),
            plain(low_rows, both), moves(steps, low_rows, both), moves(steps, low_rows, both),
            dma((outer,)), dma((outer,)), dma((outer - 1,)), dma((outer - 1,)),
            dma((half_heads,)), dma((half_heads,)), dma((half_heads - 1,)), dma((half_heads - 1,)),
            dma((head_size - 1,)), dma((head_size - 1,)),
            dma((members,)), dma((members,)), dma((head_size - 1,)), dma((head_size - 1,)),
            dma((head_size - 1,)), dma((head_size - 1,)), dma((head_size - 1,)), dma((head_size - 1,)),
            dma((2,)), dma((2,)),
            dma((steps,)), dma((steps,)), dma((steps,)), dma((steps,)), dma((2,)),
            dma((members,)), dma((members,)), dma((outer - 1,)), dma((outer - 1,)),
            dma((outer // 2 - 1,)), dma((outer // 2 - 1,)), dma((2, outer // 2)), dma((outer + outer // 2,)),
            dma((2, 2)), dma((4,)),
        ],
        compiler_params=pltpu.CompilerParams(
            collective_id=1, has_side_effects=True, vmem_limit_bytes=VMEM_BYTES
        ),
        cost_estimate=pl.CostEstimate(
            flops=60_000_000_000, bytes_accessed=300_000_000, transcendentals=0
        ),
        name="closing_sums",
    )(*args)

def settle(tokens, cotangent, up, branch, wide_grads, small_grads):
    members, length, share = tokens.shape
    count = len(wide_grads) + len(small_grads)

    def kernel(tokens_r, cot_r, up_r, branch_r, *refs):
        grads, out_o, grad_o, given = refs[:count], refs[count], refs[count + 1], refs[count + 2 :]
        out_o[...] = (tokens_r[...].astype(F32) + branch_r[...].astype(F32)).astype(BF16)
        grad_o[...] = cot_r[...].astype(F32) + up_r[...].astype(F32)
        for source, target in zip(grads, given):
            target[...] = source[...]

    block = pl.BlockSpec((1, length, share), lambda i: (i, 0, 0))
    rest = [
        pl.BlockSpec((g.shape[0] // members, g.shape[1]), lambda i: (i, 0)) for g in wide_grads
    ] + [pl.BlockSpec(g.shape, lambda i: (0, 0)) for g in small_grads]
    return call(
        kernel, "first_layout", (members,), [block] * 4 + rest, [block, block] + rest,
        [shape(tokens.shape, BF16), shape(tokens.shape, F32)]
        + [shape(g.shape, F32) for g in (*wide_grads, *small_grads)],
        [], 1000, (tokens, cotangent, up, branch, *wide_grads, *small_grads),
    )


def shifted(block, axis, distance):
    devices = range(lax.axis_size(axis))
    route = [(i - distance, i) for i in devices if i - distance in devices]
    return lax.ppermute(block, axis, route)


def carried(part, decay, hops, distance):
    carry = shifted(part, "seq", distance)
    for _ in range(hops - 1):
        leaving = decay * carry.astype(F32) + part.astype(F32)
        carry = shifted(leaving.astype(BF16), "seq", distance)
    return carry


def swapped(block, distance):
    size = lax.axis_size("seq")
    return lax.ppermute(block, "seq", [(i, i ^ distance) for i in range(size)])


def local(
    tokens,
    cotangent,
    norm_gain,
    gate_matrix,
    value_matrix,
    state_matrix,
    step_matrix,
    value_kernel,
    value_bias,
    state_kernel,
    state_bias,
    step_bias,
    log_rate,
    skip_gain,
    gate_gain,
    output_matrix,
):
    seq_count, length, share = tokens.shape
    hops = lax.axis_size("seq") // seq_count - 1
    width, channels = gate_matrix.shape
    heads = step_bias.shape[0]
    wide = channels // heads
    both = state_matrix.shape[1]
    taps = value_kernel.shape[0]
    rows = seq_count * length
    head_count = lax.axis_size("head")
    head_rank = lax.axis_index("head")
    row = lambda v: v.reshape(1, -1)

    (
        normal_in, flat_cot, mine, gate_pre, value_pre, state_pre, normed_grad, xs, xdt, xw, hin0,
        rstd, step_pre, bcs, dt, cum, cumt, pre, dec, value_edge, state_edge, carry,
    ) = opening(
        tokens, cotangent, row(norm_gain), gate_matrix, value_matrix, state_matrix, step_matrix.T,
        output_matrix, value_kernel, row(value_bias), state_kernel, row(state_bias), row(step_bias),
        row(log_rate), lax.axis_size("seq"), head_count,
    )
    whole_decay = jnp.repeat(pre[-1] * dec[-1], wide, axis=0)
    skip_row = row(jnp.repeat(skip_gain, wide))
    hin_low, normed, part, dy, dz, dv, ab, ds0, post, starting, gate_gain_part = forward(
        xdt, xs, bcs, gate_pre, normed_grad, cum, cumt, hin0, pre, dec, carry, skip_row,
        row(gate_gain), output_matrix, length, lax.axis_size("seq"), head_count,
    )
    back = carried(starting, whole_decay, hops, -seq_count)
    seq_size = lax.axis_size("seq")
    gate_keep, gate_give = halves(normal_in, dz, seq_size // 2)
    gate_got = swapped(gate_give, 1)
    output_keep, output_give = parities(normed, flat_cot, seq_size // 2)
    output_give, back = lax.optimization_barrier((output_give, back))
    output_got = swapped(output_give, 2)
    branch = lax.psum_scatter(part, "head", scatter_dimension=1, tiled=True).reshape(tokens.shape)
    g, dbc_intra = intra_back(bcs, xdt, dy, cum, cumt, length)
    dxr, tail, head_rows, vectors, ddtr, dbc, small = finish_back(
        value_pre, value_edge, value_kernel, row(value_bias), xs, xdt, xw, g, dy, dv, bcs, step_pre, dt, cum,
        ab, hin0, pre, carry, hin_low, ds0, post, back, dec, dbc_intra, skip_row, row(skip_gain),
        row(step_bias), row(log_rate), gate_gain_part, length,
    )
    gate_half = (gate_keep.astype(F32) + gate_got.astype(F32)).astype(BF16)
    output_half = (output_keep.astype(F32) + output_got.astype(F32)).astype(BF16)
    gain_share = lax.dynamic_slice_in_dim(norm_gain, head_rank * share, share, 0)
    (
        gate_grad, value_grad, output_grad, state_grad, step_grad, value_kernel_grad, value_bias_grad,
        gate_gain_grad, state_kernel_grad, state_bias_grad, norm_grad, step_bias_grad, log_rate_grad,
        skip_gain_grad, up, branch,
    ) = closing(
        normal_in, dz, dxr, tail, head_rows, gate_matrix, value_matrix, state_matrix, step_matrix.T,
        value_kernel, state_kernel, row(state_bias), state_pre, state_edge, dbc, ddtr, vectors, small,
        branch, mine, rstd, row(gain_share), gate_half, output_half, length, seq_size, head_count,
    )
    (
        layer_out, token_grad, gate_grad, value_grad, output_grad, state_grad, value_kernel_grad,
        value_bias_grad, gate_gain_grad, state_kernel_grad, state_bias_grad, norm_grad,
        step_bias_grad, log_rate_grad, skip_gain_grad,
    ) = settle(
        tokens, cotangent, up, branch, (gate_grad, value_grad, output_grad, state_grad),
        (value_kernel_grad, value_bias_grad, gate_gain_grad, state_kernel_grad, state_bias_grad,
         norm_grad, step_bias_grad, log_rate_grad, skip_gain_grad),
    )
    strip = width // seq_size
    step_grad = jnp.transpose(step_grad.reshape(width // both, heads, both), (0, 2, 1))
    step_grad = lax.dynamic_slice_in_dim(
        step_grad.reshape(width, heads), lax.axis_index("seq") * strip, strip, 0
    )
    return (
        layer_out,
        token_grad,
        norm_grad[0],
        gate_grad,
        value_grad,
        state_grad,
        step_grad,
        value_kernel_grad,
        value_bias_grad[0],
        state_kernel_grad,
        state_bias_grad[0],
        step_bias_grad[0],
        log_rate_grad[0],
        skip_gain_grad[0],
        gate_gain_grad[0],
        output_grad,
    )


def solution(mesh):
    in_specs = (
        P(None, "seq", "head"),
        P(None, "seq", "head"),
        P(),
        P(None, "head"),
        P(None, "head"),
        P(),
        P(None, "head"),
        P(None, "head"),
        P("head"),
        P(),
        P(),
        P("head"),
        P("head"),
        P("head"),
        P("head"),
        P("head", None),
    )
    out_specs = (
        P(None, "seq", "head"),
        P(None, "seq", "head"),
        P("head"),
        P("seq", "head"),
        P("seq", "head"),
        P("head", None),
        P("seq", "head"),
        P(None, "head"),
        P("head"),
        P(),
        P(),
        P("head"),
        P("head"),
        P("head"),
        P("head"),
        P("head", "seq"),
    )
    return jax.shard_map(local, mesh=mesh, in_specs=in_specs, out_specs=out_specs, check_vma=False)
```
